32 devices in a mesh: groups: 2 (over y), pts: 4 (over z), comp: 2 (over x), sub: 2 (over core).
Axes of the slice: x: 2, y: 2, z: 4, core: 2. Of those that a mesh axis runs over, the one named last changes fastest.
Arguments:
- spectra: float32 [5120, 768], P(('groups', 'pts', 'comp'), 'sub'), parts along dimension 0, may hold values from 0.2 to 2
- wind: float32 [5120], P(('groups', 'pts', 'comp')), parts along dimension 0, may hold values from 0.2 to 1
- growth: float32 [768], P('sub'), may hold values from -0.6 to 0.6
- damping: float32 [768], P('sub'), may hold values from 0.05 to 0.5
- row_cell: int32 [5120], P(('groups', 'pts', 'comp')), parts along dimension 0, may hold values from 0 to 4095, as said below
- land_mask: int32 [64, 128], P(('groups', 'pts', 'comp')), parts along dimension 0, may hold values from 0 to 1, as said below
- group_speed: float32 [64, 32, 128], P(('groups', 'sub'), ('pts', 'comp')), parts along dimension 0, may hold values from 0.4 to 1
- current: float32 [4, 32, 128], P('groups', ('pts', 'comp')), parts along dimension 0, may hold values from -0.3 to 0.3
- turning: float32 [64, 128], P(('groups', 'pts', 'comp')), parts along dimension 0, may hold values from -0.4 to 0.4
Outputs:
- advanced: float32 [2, 384, 64, 128], P('sub', ('pts', 'comp'), 'groups'), parts along dimension 2
The draws below stay inside these ranges and needn't reach their ends.
There are 2 independent parts, one for each index of `groups`. The reference program is written for one: setup_inputs(seed, part) draws one part's arguments, and reference() takes and returns one part's arrays. A program takes and returns all parts, laid end to end along the dimension named above; an argument that names none is the same for every part. Nothing has to cross between parts.
Inputs may be any that keep to these rules, and one draw needn't show every extreme that they name: `row_cell`: 2560 distinct cells, exactly the cells where land_mask is 1. Tile t holds the cells of rows t * 4 to (t + 1) * 4 - 1; the sea cells of one tile are spread over the 8 owners, whose rows are the consecutive blocks of 320 rows, as evenly as possible, so at most 64 rows of one owner lie in one tile, and some tile is all sea. `land_mask`: 2560 sea cells; every tile holds 128 to 512 of them, some tile all sea.
All inputs are finite; a program needn't handle non-finite values.
Results may differ from the reference program's by a relative error of at most 0.00002.
Values sent between devices are 32-bit elements; how exact they have to be, the bound alone decides.
No kernel may reach another device: no remote copies, remote signals or barrier semaphores. Data moves between devices by JAX's collectives and lax.ppermute only.
A program may use at most 128 MiB of HBM per device.

```python
import math
import jax
import jax.numpy as jnp
from jax import lax

DIR = 24
F = 32
NY = 128
SUBSTEPS = 2
COMPS = 768
TILES = 8
G = 512
NX = 32
NSEA_DEV = 320
NSEA = 2560
N_SUB = 2


def ocean_layout(key):
    tile_count = TILES
    cell_count = G
    per_device = NSEA_DEV
    spare_room = cell_count - per_device
    pair_key, amount_key, place_key, row_key = jax.random.split(key, 4)
    pairing = jax.random.permutation(pair_key, tile_count)
    amount = jax.random.randint(amount_key, (tile_count // 2,), 0, spare_room + 1)
    amount = amount.at[0].set(spare_room)
    shifts = jnp.concatenate([amount, -amount])
    sea_count = jnp.zeros((tile_count,), jnp.int32).at[pairing].set(per_device + shifts)
    scores = jax.vmap(lambda sub_key: jax.random.permutation(sub_key, cell_count))(jax.random.split(place_key, tile_count))
    sea_cells = (scores < sea_count[:, None]).astype(jnp.int32)
    flat_mask = sea_cells.reshape(-1)
    sea_rank = jnp.cumsum(flat_mask) - 1
    owner_dev = sea_rank % tile_count
    local_rank = jnp.clip(sea_rank // tile_count, 0, per_device - 1)
    row_orders = jax.vmap(lambda sub_key: jax.random.permutation(sub_key, per_device))(jax.random.split(row_key, tile_count))
    row_index = owner_dev * per_device + row_orders[owner_dev, local_rank]
    target = jnp.where(flat_mask == 1, row_index, tile_count * per_device)
    cell_ids = jnp.arange(tile_count * cell_count, dtype=jnp.int32)
    row_cell = jnp.zeros((tile_count * per_device,), jnp.int32).at[target].set(cell_ids, mode='drop')
    return (sea_cells.reshape(NX, NY), row_cell)


def draw_land_mask(key, part):
    sea_cells, row_cell = ocean_layout(key)
    return sea_cells


def draw_row_cell(key, part):
    sea_cells, row_cell = ocean_layout(key)
    return row_cell


def block_scale(rng, shape, cuts, low, high):
    gain = 1.0
    for position, parts in cuts:
        steps = jax.random.uniform(jax.random.fold_in(jax.random.fold_in(rng, 6), position), (parts,), jnp.float32, low / len(cuts), high / len(cuts))
        gain = gain * jnp.repeat(jnp.exp(steps), shape[position] // parts).reshape((-1,) + (1,) * (len(shape) - 1 - position))
    return gain


def setup_inputs(seed: int = 0, part: int = 0) -> dict:
    key_of = jax.random.split(jax.random.key(seed), 10)
    part_keys = jax.random.split(jax.random.fold_in(key_of[9], part), 10)
    return {
        "spectra": jnp.clip(jnp.exp(math.log(2.0) - 2.3025851 * jax.random.uniform(part_keys[0], (NSEA, COMPS), jnp.float32) ** block_scale(part_keys[0], (NSEA, COMPS), ((0, 8), (1, 2)), -0.2, 0.2)), 0.2, 2.0),
        "wind": jnp.clip(jnp.exp(math.log(1.0) - 1.609438 * jax.random.uniform(part_keys[1], (NSEA,), jnp.float32) ** block_scale(part_keys[1], (NSEA,), ((0, 8),), -0.2, 0.2)), 0.2, 1.0),
        "growth": jnp.clip(jax.random.uniform(key_of[2], (COMPS,), jnp.float32, -0.6, 0.6) * block_scale(key_of[2], (COMPS,), ((0, 2),), -0.4, 0.0), -0.6, 0.6),
        "damping": jnp.clip(jnp.exp(math.log(0.5) - 2.3025851 * jax.random.uniform(key_of[3], (COMPS,), jnp.float32) ** block_scale(key_of[3], (COMPS,), ((0, 2),), -0.2, 0.2)), 0.05, 0.5),
        "row_cell": draw_row_cell(jax.random.fold_in(jax.random.fold_in(key_of[9], part), 71), part),
        "land_mask": draw_land_mask(jax.random.fold_in(jax.random.fold_in(key_of[9], part), 71), part),
        "group_speed": jnp.clip(0.4 + 0.6 * jax.random.uniform(part_keys[6], (F, NX, NY), jnp.float32) ** block_scale(part_keys[6], (F, NX, NY), ((0, 2), (1, 8)), -0.2, 0.2), 0.4, 1.0),
        "current": jnp.clip(jax.random.uniform(part_keys[7], (2, NX, NY), jnp.float32, -0.3, 0.3) * block_scale(part_keys[7], (2, NX, NY), ((1, 8),), -0.4, 0.0), -0.3, 0.3),
        "turning": jnp.clip(jax.random.uniform(part_keys[8], (NX, NY), jnp.float32, -0.4, 0.4) * block_scale(part_keys[8], (NX, NY), ((0, 8),), -0.4, 0.0), -0.4, 0.4),
    }


courant = 0.35


def take_slice(values, first_index, extent, along_axis):
    return lax.slice_in_dim(values, first_index, first_index + extent, axis=along_axis)


def upwind_divergence(padded, motion, along_axis):
    length = padded.shape[along_axis] - 4
    face_count = length + 1
    behind = take_slice(padded, 0, face_count, along_axis)
    centre = take_slice(padded, 1, face_count, along_axis)
    onward = take_slice(padded, 2, face_count, along_axis)
    beyond = take_slice(padded, 3, face_count, along_axis)
    left_face = (6.0 * centre + 3.0 * onward - behind) * 0.125
    right_face = (3.0 * centre + 6.0 * onward - beyond) * 0.125
    face_speed = 0.5 * (take_slice(motion, 1, face_count, along_axis) + take_slice(motion, 2, face_count, along_axis))
    fluxes = jnp.maximum(face_speed, 0.0) * left_face + jnp.minimum(face_speed, 0.0) * right_face
    return take_slice(fluxes, 1, length, along_axis) - take_slice(fluxes, 0, length, along_axis)


def substep(extended, speed_x, speed_y, sea_mask):
    across = upwind_divergence(extended, speed_x, 1)
    centre_part = extended[:, 2:-2]
    padding = ((0, 0), (0, 0), (2, 2))
    sideways = upwind_divergence(jnp.pad(centre_part, padding), jnp.pad(speed_y, padding), 2)
    return (centre_part - courant * (across + sideways)) * sea_mask


def direction_tables(directions):
    angles = jnp.arange(directions, dtype=jnp.float32) * (2.0 * jnp.pi / directions)
    return jnp.cos(angles), jnp.sin(angles)


def source_term(values, wind_speed, growth, damping):
    return values * jnp.exp(wind_speed[:, None] * growth[None, :] - damping[None, :])


def reference(spectra, wind, growth, damping, row_cell, land_mask, group_speed, current, turning):
    source = source_term(spectra, wind, growth, damping)
    scattered = jnp.zeros((NX * NY, COMPS), jnp.float32).at[row_cell].set(source)
    field_all = scattered.T.reshape(F, DIR, NX, NY)
    sea_mask = land_mask.astype(jnp.float32)
    cosine_table, sine_table = direction_tables(DIR)
    x_padding = ((0, 0), (2, 2), (0, 0))

    def advance(inputs):
        spectrum, celerity = inputs
        speed_x = celerity[None] * cosine_table[:, None, None] + current[0][None]
        speed_y = celerity[None] * sine_table[:, None, None] + current[1][None]
        for repeat in range(SUBSTEPS):
            spectrum = substep(jnp.pad(spectrum, x_padding), jnp.pad(speed_x, x_padding), speed_y, sea_mask)
        wrapped = jnp.concatenate([spectrum[-2:], spectrum, spectrum[:2]], axis=0)
        turning_full = jnp.broadcast_to(turning[None], wrapped.shape)
        return spectrum - upwind_divergence(wrapped, turning_full, 0)

    result = lax.map(advance, (field_all, group_speed))
    return result.reshape(N_SUB, COMPS // N_SUB, NX, NY)
```

```python
import functools
import jax
import jax.numpy as jnp
from jax import lax
from jax.experimental import pallas as pl
from jax.experimental.pallas import tpu as pltpu
from jax.sharding import PartitionSpec as P

DIR = 24
SUBSTEPS = 2
LANES = 128
GROUP = ("pts", "comp")


courant = 0.35


def with_halo(cells, sides, width):
    for axis, dim in sides:
        count = lax.axis_size(axis)
        ends = count - 1
        head = lax.slice_in_dim(cells, 0, width, axis=dim)
        tail = lax.slice_in_dim(cells, cells.shape[dim] - width, cells.shape[dim], axis=dim)
        cells = jnp.concatenate(
            [
                lax.ppermute(tail, axis, [(i, (i + 1) % count) for i in range(ends)]),
                cells,
                lax.ppermute(head, axis, [((i + 1) % count, i) for i in range(ends)]),
            ],
            axis=dim,
        )
    return cells


def take_slice(values, first_index, extent, along_axis):
    return lax.slice_in_dim(values, first_index, first_index + extent, axis=along_axis)


def upwind_divergence(padded, motion, along_axis):
    length = padded.shape[along_axis] - 4
    face_count = length + 1
    behind = take_slice(padded, 0, face_count, along_axis)
    centre = take_slice(padded, 1, face_count, along_axis)
    onward = take_slice(padded, 2, face_count, along_axis)
    beyond = take_slice(padded, 3, face_count, along_axis)
    left_face = (6.0 * centre + 3.0 * onward - behind) * 0.125
    right_face = (3.0 * centre + 6.0 * onward - beyond) * 0.125
    face_speed = 0.5 * (
        take_slice(motion, 1, face_count, along_axis)
        + take_slice(motion, 2, face_count, along_axis)
    )
    fluxes = jnp.maximum(face_speed, 0.0) * left_face + jnp.minimum(face_speed, 0.0) * right_face
    return take_slice(fluxes, 1, length, along_axis) - take_slice(fluxes, 0, length, along_axis)


def substep(extended, speed_x, speed_y, sea_mask):
    across = upwind_divergence(extended, speed_x, 1)
    centre_part = extended[:, 2:-2]
    padding = ((0, 0), (0, 0), (2, 2))
    sideways = upwind_divergence(jnp.pad(centre_part, padding), jnp.pad(speed_y, padding), 2)
    return (centre_part - courant * (across + sideways)) * sea_mask


def direction_tables(directions):
    angles = jnp.arange(directions, dtype=jnp.float32) * (2.0 * jnp.pi / directions)
    return (jnp.cos(angles), jnp.sin(angles))


def source_term(values, wind_speed, growth, damping):
    return values * jnp.exp(wind_speed[:, None] * growth[None, :] - damping[None, :])


def velocities(stacked, freq_count):
    cosine_table, sine_table = direction_tables(DIR)
    celerity = stacked[:freq_count][:, None]
    shape_out = (freq_count * DIR,) + stacked.shape[1:]
    speed_x = (
        celerity * cosine_table[None, :, None, None] + stacked[freq_count][None, None]
    ).reshape(shape_out)
    speed_y = (
        celerity * sine_table[None, :, None, None] + stacked[freq_count + 1][None, None]
    ).reshape(shape_out)
    return (speed_x, speed_y)


def deliver(bulk_rows, small_rows):
    return (
        lax.all_to_all(bulk_rows, GROUP, split_axis=0, concat_axis=0, tiled=True),
        lax.all_to_all(small_rows, GROUP, split_axis=0, concat_axis=0, tiled=True),
    )


def tile_plan(spectra, wind, growth, damping, row_cell, land_mask, group_speed, current, turning):
    tile_count = lax.axis_size(GROUP)
    comp_width = spectra.shape[1]
    tile_rows, tile_cols = land_mask.shape
    cell_count = tile_rows * tile_cols
    capacity = cell_count // tile_count
    target = row_cell // cell_count
    local_cell = (row_cell - target * cell_count).astype(jnp.float32)
    matches = (target[:, None] == jnp.arange(tile_count, dtype=jnp.int32)[None, :]).astype(
        jnp.int32
    )
    bucket_slot = jnp.sum((jnp.cumsum(matches, axis=0) - 1) * matches, axis=1)

    def bucket(values, filler):
        shape_out = (tile_count, capacity) + values.shape[1:]
        return jnp.full(shape_out, filler, jnp.float32).at[target, bucket_slot].set(values)

    bulk_rows = bucket(source_term(spectra, wind, growth, damping), 0.0)
    small_rows = bucket(local_cell[:, None], float(cell_count))
    bulk_back, small_back = deliver(bulk_rows, small_rows)
    cell_index = small_back[:, :, 0].reshape(-1).astype(jnp.int32)
    flat_values = bulk_back.reshape((tile_count * capacity,) + bulk_back.shape[2:])
    tile_field = (
        jnp.zeros((cell_count,) + bulk_back.shape[2:], jnp.float32)
        .at[cell_index]
        .set(flat_values, mode="drop")
    )
    spectrum = tile_field.T.reshape(comp_width, tile_rows, tile_cols)
    freq_count = comp_width // DIR
    reach = 2 * SUBSTEPS
    stacked = jnp.concatenate([group_speed, current, land_mask.astype(jnp.float32)[None]], axis=0)
    rimmed = with_halo(stacked, ((GROUP, 1),), 2 * SUBSTEPS)
    speed_x, speed_y = velocities(rimmed, freq_count)
    sea_rim = rimmed[freq_count + 2 :]

    def window(values, margin):
        return lax.slice_in_dim(values, reach - margin, reach + tile_rows + margin, axis=1)

    for repeat in range(SUBSTEPS):
        extended = with_halo(spectrum, ((GROUP, 1),), 2)
        spectrum = substep(extended, window(speed_x, 2), window(speed_y, 0), window(sea_rim, 0)[0])
    blocks = spectrum.reshape(freq_count, DIR, tile_rows, tile_cols)
    wrapped = jnp.concatenate([blocks[:, -2:], blocks, blocks[:, :2]], axis=1)
    turning_full = jnp.broadcast_to(turning[None, None], wrapped.shape)
    blocks = blocks - upwind_divergence(wrapped, turning_full, 1)
    spectrum = blocks.reshape(comp_width, tile_rows, tile_cols)
    shipped = lax.all_to_all(spectrum, GROUP, split_axis=0, concat_axis=1, tiled=True)
    return shipped[None]


def pack_kernel(parts, spectra_ref, wind_ref, growth_ref, damping_ref, speed_ref, out_ref):
    rows, comps = spectra_ref.shape
    half = LANES // 2
    full = rows // LANES
    width = comps // parts
    wind_cols = jnp.broadcast_to(wind_ref[...], (LANES, wind_ref.shape[1])).T
    low = lax.broadcasted_iota(jnp.int32, (8, LANES), 1) < half
    groups = []
    for block in range(comps // LANES):
        lanes = pl.ds(block * LANES, LANES)
        growth = growth_ref[:, lanes]
        damping = damping_ref[:, lanes]

        def source(first, count):
            span = pl.ds(first, count)
            return spectra_ref[span, lanes] * jnp.exp(
                wind_cols[first : first + count] * growth - damping
            )

        for chunk in range(full):
            turned = source(chunk * LANES, LANES).T
            for g in range(LANES // 8):
                part, within = divmod(block * LANES + g * 8, width)
                out_ref[part, pl.ds(chunk * width + within, 8), :] = turned[g * 8 : g * 8 + 8]
        tail = source(full * LANES, half)
        turned = jnp.concatenate([tail, tail], axis=0).T
        groups += [turned[g * 8 : g * 8 + 8] for g in range(LANES // 8)]
    for part in range(parts):
        for g in range(DIR // 8):
            first = groups[part * width // 8 + g]
            second = groups[(part * width + DIR) // 8 + g]
            out_ref[part, pl.ds(full * width + g * 8, 8), :] = jnp.where(low, first, second)
        out_ref[part, pl.ds(full * width + DIR, 8), :] = speed_ref[pl.ds(part * 8, 8), :]


def slab_kernel(
    parts, tile_rows, full, recv_ref, small_ref, trig_ref, out_ref, onehot, spread, first, second, table
):
    slab_rows = parts * tile_rows
    freqs = 2
    width = freqs * DIR
    half = LANES // 2
    small_rows = small_ref.shape[0] // parts
    highs = slab_rows // 2
    depth = onehot.shape[1] // 2
    low_lane = lax.broadcasted_iota(jnp.int32, (1, LANES), 1) < half
    low_lane_wide = lax.broadcasted_iota(jnp.int32, (DIR, LANES), 1) < half
    cell_iota = lax.broadcasted_iota(jnp.int32, (2 * LANES, LANES), 0)

    def cells_of(owner, chunk):
        return small_ref[pl.ds(owner * small_rows + 4 * tile_rows + chunk, 1), :].astype(jnp.int32)

    def place(chunk_index, cells, values):
        high = cells // (2 * LANES)
        low = cells - high * (2 * LANES)
        hot = (cell_iota == low).astype(jnp.float32).astype(jnp.bfloat16)
        onehot[:, pl.ds(chunk_index * LANES, LANES)] = hot
        onehot[:, pl.ds(depth + chunk_index * LANES, LANES)] = hot
        head = values.astype(jnp.bfloat16)
        rest = (values - head.astype(jnp.float32)).astype(jnp.bfloat16)
        for h in range(highs):
            pick = jnp.broadcast_to((high == h).astype(jnp.float32), (width, LANES)).astype(jnp.bfloat16)
            spread[pl.ds(h * width, width), pl.ds(chunk_index * LANES, LANES)] = head * pick
            spread[pl.ds(h * width, width), pl.ds(depth + chunk_index * LANES, LANES)] = rest * pick

    per_pair = 2 * full + 1
    for pair in range(parts // 2):
        even, odd = 2 * pair, 2 * pair + 1
        for side, owner in enumerate((even, odd)):
            for chunk in range(full):
                values = recv_ref[owner, pl.ds(chunk * width, width), :]
                place(pair * per_pair + side * full + chunk, cells_of(owner, chunk), values)
        tail_even = recv_ref[even, pl.ds(full * width, DIR), :]
        tail_odd = recv_ref[odd, pl.ds(full * width, DIR), :]
        swapped_even = pltpu.roll(tail_even, half, 1)
        swapped_odd = pltpu.roll(tail_odd, half, 1)
        values = jnp.concatenate(
            [
                jnp.where(low_lane_wide, tail_even, swapped_odd),
                jnp.where(low_lane_wide, swapped_even, tail_odd),
            ],
            axis=0,
        )
        cells_even, cells_odd = cells_of(even, full), cells_of(odd, full)
        cells = jnp.where(low_lane, cells_even, pltpu.roll(cells_odd, half, 1))
        place(pair * per_pair + 2 * full, cells, values)

    scattered = lax.dot_general(
        spread[...], onehot[...], (((1,), (1,)), ((), ())), preferred_element_type=jnp.float32
    )
    nothing = jnp.zeros((DIR, LANES), jnp.float32)
    for field in (first, second):
        for f in range(freqs):
            for edge in (0, 1, slab_rows + 2, slab_rows + 3):
                field[f, edge] = nothing
    for h in range(highs):
        for f in range(freqs):
            span = scattered[h * width + f * DIR : h * width + (f + 1) * DIR]
            first[f, 2 * h + 2] = span[:, :LANES]
            first[f, 2 * h + 3] = span[:, LANES:]

    lane = lax.broadcasted_iota(jnp.int32, (slab_rows, LANES), 1)
    zero_rows = jnp.zeros((8, LANES), jnp.float32)

    def gather(read):
        return jnp.concatenate([read(owner) for owner in range(parts)], axis=0)

    def small(kind):
        return gather(lambda owner: small_ref[pl.ds(owner * small_rows + kind * tile_rows, tile_rows), :])

    gain = 0.5 * courant / 8.0
    slots = iter(range(table.shape[0]))

    def keep(rows):
        slot = next(slots)
        table[slot, pl.ds(8, slab_rows), :] = rows
        return slot

    def face_x(rows):
        slot = next(slots)
        table[slot, pl.ds(0, 8), :] = zero_rows
        table[slot, pl.ds(8 + slab_rows, 8), :] = zero_rows
        table[slot, pl.ds(8, slab_rows), :] = rows
        faces = gain * (table[slot, pl.ds(7, slab_rows + 8), :] + table[slot, pl.ds(8, slab_rows + 8), :])
        table[slot, pl.ds(7, slab_rows + 8), :] = faces
        return slot

    def face_y(rows):
        after = jnp.where(lane < LANES - 1, pltpu.roll(rows, LANES - 1, 1), 0.0)
        before = jnp.where(lane > 0, pltpu.roll(rows, 1, 1), 0.0)
        return keep(gain * (rows + after)), keep(gain * (rows + before))

    current_x, current_y, turning, land = (small(kind) for kind in range(4))
    current_x_face = face_x(current_x)
    current_y_faces = face_y(current_y)
    speeds = [
        gather(lambda owner: recv_ref[owner, pl.ds(full * width + DIR + f * tile_rows, tile_rows), :])
        for f in range(freqs)
    ]
    speed_x_face = [face_x(s) for s in speeds]
    speed_y_faces = [face_y(s) for s in speeds]
    land_slot = keep(land)
    ahead = jnp.maximum(turning, 0.0) * 0.125
    back = jnp.minimum(turning, 0.0) * 0.125
    bend_slots = [
        keep(rows)
        for rows in (
            -ahead,
            7.0 * ahead + 3.0 * back,
            1.0 - 3.0 * (ahead - back),
            -3.0 * ahead - 7.0 * back,
            back,
        )
    ]

    cosine = trig_ref[0]
    sine = trig_ref[1]
    lane_wide = lax.broadcasted_iota(jnp.int32, (DIR, LANES), 1)

    def row(slot, x):
        return table[slot, pl.ds(8 + x, 1), :]

    def flux(speed, behind, centre, onward, beyond):
        shared = 3.0 * (centre + onward)
        return jnp.maximum(speed, 0.0) * (shared + 3.0 * centre - behind) + jnp.minimum(speed, 0.0) * (
            shared + 3.0 * onward - beyond
        )

    def flux_x(field, f, x):
        speed = row(speed_x_face[f], x) * cosine + row(current_x_face, x)
        return flux(speed, field[f, x + 1], field[f, x + 2], field[f, x + 3], field[f, x + 4])

    def advance(field, f, x, entering):
        leaving = flux_x(field, f, x)
        centre = field[f, x + 2]
        up1 = jnp.where(lane_wide < LANES - 1, pltpu.roll(centre, LANES - 1, 1), 0.0)
        up2 = jnp.where(lane_wide < LANES - 2, pltpu.roll(centre, LANES - 2, 1), 0.0)
        down1 = jnp.where(lane_wide > 0, pltpu.roll(centre, 1, 1), 0.0)
        down2 = jnp.where(lane_wide > 1, pltpu.roll(centre, 2, 1), 0.0)
        right = flux(
            row(speed_y_faces[f][0], x) * sine + row(current_y_faces[0], x), down1, centre, up1, up2
        )
        left = flux(
            row(speed_y_faces[f][1], x) * sine + row(current_y_faces[1], x), down2, down1, centre, up1
        )
        moved = (centre - (leaving - entering) - (right - left)) * row(land_slot, x)
        return moved, leaving

    def sweep(field, finish):
        def body(x, carry):
            out = []
            for f in range(freqs):
                moved, leaving = advance(field, f, x, carry[f])
                finish(f, x, moved)
                out.append(leaving)
            return tuple(out)

        lax.fori_loop(0, slab_rows, body, tuple(flux_x(field, f, -1) for f in range(freqs)))

    def store(f, x, moved):
        second[f, x + 2] = moved

    def refract(f, x, moved):
        bent = row(bend_slots[2], x) * moved
        for slot, shift in zip(bend_slots, (2, 1, 0, DIR - 1, DIR - 2)):
            if shift:
                bent = bent + row(slot, x) * jnp.roll(moved, shift, axis=0)
        for g in range(DIR // 8):
            out_ref[pl.ds((f * DIR + g * 8) * slab_rows + x, 8, stride=slab_rows), :] = bent[g * 8 : g * 8 + 8]

    sweep(first, store)
    sweep(second, refract)


def slab_plan(spectra, wind, growth, damping, row_cell, land_mask, group_speed, current, turning):
    parts = lax.axis_size(GROUP)
    rows, comps = spectra.shape
    tile_rows = land_mask.shape[0]
    width = comps // parts
    full = rows // LANES
    slab_rows = parts * tile_rows
    spare = -(-rows // LANES) * LANES - rows
    cells = jnp.pad(row_cell.astype(jnp.float32), (0, spare)).reshape(-1, LANES)
    small = jnp.concatenate(
        [current.reshape(-1, LANES), turning, land_mask.astype(jnp.float32), cells], axis=0
    )
    small = jnp.pad(small, ((0, -small.shape[0] % 8), (0, 0)))
    small_all = lax.all_gather(small, GROUP, axis=0, tiled=True)
    block_rows = full * width + DIR + 2 * tile_rows
    vmem = pltpu.CompilerParams(vmem_limit_bytes=48 * 1024 * 1024)
    packed = pl.pallas_call(
        functools.partial(pack_kernel, parts),
        out_shape=jax.ShapeDtypeStruct((parts, block_rows, LANES), jnp.float32),
        compiler_params=vmem,
        name="pack",
    )(
        spectra,
        jnp.pad(wind, (0, spare))[None],
        growth[None],
        damping[None],
        group_speed.reshape(-1, LANES),
    )
    recv = lax.all_to_all(packed, GROUP, split_axis=0, concat_axis=0, tiled=True)
    trig = jnp.stack([jnp.broadcast_to(t[:, None], (DIR, LANES)) for t in direction_tables(DIR)])
    depth = parts * rows
    out = pl.pallas_call(
        functools.partial(slab_kernel, parts, tile_rows, full),
        out_shape=jax.ShapeDtypeStruct((width * slab_rows, LANES), jnp.float32),
        scratch_shapes=[
            pltpu.VMEM((2 * LANES, 2 * depth), jnp.bfloat16),
            pltpu.VMEM((slab_rows // 2 * width, 2 * depth), jnp.bfloat16),
            pltpu.VMEM((2, slab_rows + 4, DIR, LANES), jnp.float32),
            pltpu.VMEM((2, slab_rows + 4, DIR, LANES), jnp.float32),
            pltpu.VMEM((15, slab_rows + 16, LANES), jnp.float32),
        ],
        compiler_params=vmem,
        name="slab",
    )(recv, small_all, trig)
    return out.reshape(1, width, slab_rows, LANES)


def shards(*arrays):
    spectra, land_mask = arrays[0], arrays[5]
    parts = lax.axis_size(GROUP)
    rows, comps = spectra.shape
    whole_frequencies = comps == parts * 2 * DIR
    fits = rows % LANES == LANES // 2 and land_mask.shape == (4, LANES) and parts % 2 == 0
    if whole_frequencies and fits:
        return slab_plan(*arrays)
    return tile_plan(*arrays)


def solution(mesh):
    placed = (
        P(("groups", "pts", "comp"), "sub"),
        P(("groups", "pts", "comp")),
        P("sub"),
        P("sub"),
        P(("groups", "pts", "comp")),
        P(("groups", "pts", "comp"), None),
        P(("groups", "sub"), ("pts", "comp"), None),
        P("groups", ("pts", "comp"), None),
        P(("groups", "pts", "comp"), None),
    )
    return jax.shard_map(
        shards,
        mesh=mesh,
        in_specs=placed,
        out_specs=P("sub", ("pts", "comp"), "groups", None),
        check_vma=False,
    )
```

```python
import functools
import math
import jax
import jax.numpy as jnp
from jax import lax
from jax.experimental import pallas as pl
from jax.experimental.pallas import tpu as pltpu
from jax.sharding import PartitionSpec as P

DIR = 24
SUBSTEPS = 2
LANES = 128
GROUP = ("pts", "comp")


courant = 0.35


def with_halo(cells, sides, width):
    for axis, dim in sides:
        count = lax.axis_size(axis)
        ends = count - 1
        head = lax.slice_in_dim(cells, 0, width, axis=dim)
        tail = lax.slice_in_dim(cells, cells.shape[dim] - width, cells.shape[dim], axis=dim)
        cells = jnp.concatenate(
            [
                lax.ppermute(tail, axis, [(i, (i + 1) % count) for i in range(ends)]),
                cells,
                lax.ppermute(head, axis, [((i + 1) % count, i) for i in range(ends)]),
            ],
            axis=dim,
        )
    return cells


def take_slice(values, first_index, extent, along_axis):
    return lax.slice_in_dim(values, first_index, first_index + extent, axis=along_axis)


def upwind_divergence(padded, motion, along_axis):
    length = padded.shape[along_axis] - 4
    face_count = length + 1
    behind = take_slice(padded, 0, face_count, along_axis)
    centre = take_slice(padded, 1, face_count, along_axis)
    onward = take_slice(padded, 2, face_count, along_axis)
    beyond = take_slice(padded, 3, face_count, along_axis)
    left_face = (6.0 * centre + 3.0 * onward - behind) * 0.125
    right_face = (3.0 * centre + 6.0 * onward - beyond) * 0.125
    face_speed = 0.5 * (
        take_slice(motion, 1, face_count, along_axis)
        + take_slice(motion, 2, face_count, along_axis)
    )
    fluxes = jnp.maximum(face_speed, 0.0) * left_face + jnp.minimum(face_speed, 0.0) * right_face
    return take_slice(fluxes, 1, length, along_axis) - take_slice(fluxes, 0, length, along_axis)


def substep(extended, speed_x, speed_y, sea_mask):
    across = upwind_divergence(extended, speed_x, 1)
    centre_part = extended[:, 2:-2]
    padding = ((0, 0), (0, 0), (2, 2))
    sideways = upwind_divergence(jnp.pad(centre_part, padding), jnp.pad(speed_y, padding), 2)
    return (centre_part - courant * (across + sideways)) * sea_mask


def direction_tables(directions):
    angles = jnp.arange(directions, dtype=jnp.float32) * (2.0 * jnp.pi / directions)
    return (jnp.cos(angles), jnp.sin(angles))


def source_term(values, wind_speed, growth, damping):
    return values * jnp.exp(wind_speed[:, None] * growth[None, :] - damping[None, :])


def velocities(stacked, freq_count):
    cosine_table, sine_table = direction_tables(DIR)
    celerity = stacked[:freq_count][:, None]
    shape_out = (freq_count * DIR,) + stacked.shape[1:]
    speed_x = (
        celerity * cosine_table[None, :, None, None] + stacked[freq_count][None, None]
    ).reshape(shape_out)
    speed_y = (
        celerity * sine_table[None, :, None, None] + stacked[freq_count + 1][None, None]
    ).reshape(shape_out)
    return (speed_x, speed_y)


def deliver(bulk_rows, small_rows):
    return (
        lax.all_to_all(bulk_rows, GROUP, split_axis=0, concat_axis=0, tiled=True),
        lax.all_to_all(small_rows, GROUP, split_axis=0, concat_axis=0, tiled=True),
    )


def tile_plan(spectra, wind, growth, damping, row_cell, land_mask, group_speed, current, turning):
    tile_count = lax.axis_size(GROUP)
    comp_width = spectra.shape[1]
    tile_rows, tile_cols = land_mask.shape
    cell_count = tile_rows * tile_cols
    capacity = cell_count // tile_count
    target = row_cell // cell_count
    local_cell = (row_cell - target * cell_count).astype(jnp.float32)
    matches = (target[:, None] == jnp.arange(tile_count, dtype=jnp.int32)[None, :]).astype(
        jnp.int32
    )
    bucket_slot = jnp.sum((jnp.cumsum(matches, axis=0) - 1) * matches, axis=1)

    def bucket(values, filler):
        shape_out = (tile_count, capacity) + values.shape[1:]
        return jnp.full(shape_out, filler, jnp.float32).at[target, bucket_slot].set(values)

    bulk_rows = bucket(source_term(spectra, wind, growth, damping), 0.0)
    small_rows = bucket(local_cell[:, None], float(cell_count))
    bulk_back, small_back = deliver(bulk_rows, small_rows)
    cell_index = small_back[:, :, 0].reshape(-1).astype(jnp.int32)
    flat_values = bulk_back.reshape((tile_count * capacity,) + bulk_back.shape[2:])
    tile_field = (
        jnp.zeros((cell_count,) + bulk_back.shape[2:], jnp.float32)
        .at[cell_index]
        .set(flat_values, mode="drop")
    )
    spectrum = tile_field.T.reshape(comp_width, tile_rows, tile_cols)
    freq_count = comp_width // DIR
    reach = 2 * SUBSTEPS
    stacked = jnp.concatenate([group_speed, current, land_mask.astype(jnp.float32)[None]], axis=0)
    rimmed = with_halo(stacked, ((GROUP, 1),), 2 * SUBSTEPS)
    speed_x, speed_y = velocities(rimmed, freq_count)
    sea_rim = rimmed[freq_count + 2 :]

    def window(values, margin):
        return lax.slice_in_dim(values, reach - margin, reach + tile_rows + margin, axis=1)

    for repeat in range(SUBSTEPS):
        extended = with_halo(spectrum, ((GROUP, 1),), 2)
        spectrum = substep(extended, window(speed_x, 2), window(speed_y, 0), window(sea_rim, 0)[0])
    blocks = spectrum.reshape(freq_count, DIR, tile_rows, tile_cols)
    wrapped = jnp.concatenate([blocks[:, -2:], blocks, blocks[:, :2]], axis=1)
    turning_full = jnp.broadcast_to(turning[None, None], wrapped.shape)
    blocks = blocks - upwind_divergence(wrapped, turning_full, 1)
    spectrum = blocks.reshape(comp_width, tile_rows, tile_cols)
    shipped = lax.all_to_all(spectrum, GROUP, split_axis=0, concat_axis=1, tiled=True)
    return shipped[None]


def pack_kernel(
    parts,
    spectra_ref,
    wind_ref,
    growth_ref,
    damping_ref,
    cell_ref,
    land_ref,
    speed_ref,
    current_ref,
    turning_ref,
    out_ref,
):
    rows, comps = spectra_ref.shape
    tile_rows = land_ref.shape[0]
    half = LANES // 2
    full = rows // LANES
    width = comps // parts
    spare = jnp.zeros((1, half), jnp.float32)
    wind_row = jnp.concatenate([wind_ref[...][None], spare], axis=1)
    wind_cols = jnp.broadcast_to(wind_row, (LANES, rows + half)).T
    low = lax.broadcasted_iota(jnp.int32, (8, LANES), 1) < half
    groups = []
    for block in range(comps // LANES):
        lanes = pl.ds(block * LANES, LANES)
        growth = growth_ref[lanes][None]
        damping = damping_ref[lanes][None]

        def source(first, count):
            span = pl.ds(first, count)
            return spectra_ref[span, lanes] * jnp.exp(
                wind_cols[first : first + count] * growth - damping
            )

        for chunk in range(full):
            turned = source(chunk * LANES, LANES).T
            for g in range(LANES // 8):
                part, within = divmod(block * LANES + g * 8, width)
                out_ref[part, pl.ds(chunk * width + within, 8), :] = turned[g * 8 : g * 8 + 8]
        tail = source(full * LANES, half)
        turned = jnp.concatenate([tail, tail], axis=0).T
        groups += [turned[g * 8 : g * 8 + 8] for g in range(LANES // 8)]
    cell_row = jnp.concatenate([cell_ref[...].astype(jnp.float32)[None], spare], axis=1)
    shared = jnp.concatenate(
        [current_ref[0], current_ref[1], turning_ref[...], land_ref[...].astype(jnp.float32)]
        + [cell_row[:, c * LANES : (c + 1) * LANES] for c in range(full + 1)],
        axis=0,
    )
    base = full * width + DIR
    for part in range(parts):
        for g in range(DIR // 8):
            first = groups[part * width // 8 + g]
            second = groups[(part * width + DIR) // 8 + g]
            out_ref[part, pl.ds(full * width + g * 8, 8), :] = jnp.where(low, first, second)
        for f in range(2):
            out_ref[part, pl.ds(base + f * tile_rows, tile_rows), :] = speed_ref[2 * part + f]
        out_ref[part, pl.ds(base + 2 * tile_rows, shared.shape[0]), :] = shared


def slab_kernel(
    parts, tile_rows, full, recv_ref, out_ref, onehot, spread, first, second, table
):
    slab_rows = parts * tile_rows
    freqs = 2
    width = freqs * DIR
    half = LANES // 2
    base = full * width + DIR
    highs = slab_rows // 2
    depth = onehot.shape[1] // 2
    low_lane = lax.broadcasted_iota(jnp.int32, (1, LANES), 1) < half
    low_lane_wide = lax.broadcasted_iota(jnp.int32, (DIR, LANES), 1) < half
    cell_iota = lax.broadcasted_iota(jnp.int32, (2 * LANES, LANES), 0)

    def cells_of(owner, chunk):
        return recv_ref[owner, pl.ds(base + 6 * tile_rows + chunk, 1), :].astype(jnp.int32)

    def place(chunk_index, cells, values):
        high = cells // (2 * LANES)
        low = cells - high * (2 * LANES)
        hot = (cell_iota == low).astype(jnp.float32).astype(jnp.bfloat16)
        onehot[:, pl.ds(chunk_index * LANES, LANES)] = hot
        onehot[:, pl.ds(depth + chunk_index * LANES, LANES)] = hot
        head = values.astype(jnp.bfloat16)
        rest = (values - head.astype(jnp.float32)).astype(jnp.bfloat16)
        for h in range(highs):
            pick = jnp.broadcast_to((high == h).astype(jnp.float32), (width, LANES)).astype(jnp.bfloat16)
            spread[pl.ds(h * width, width), pl.ds(chunk_index * LANES, LANES)] = head * pick
            spread[pl.ds(h * width, width), pl.ds(depth + chunk_index * LANES, LANES)] = rest * pick

    per_pair = 2 * full + 1
    for pair in range(parts // 2):
        even, odd = 2 * pair, 2 * pair + 1
        for side, owner in enumerate((even, odd)):
            for chunk in range(full):
                values = recv_ref[owner, pl.ds(chunk * width, width), :]
                place(pair * per_pair + side * full + chunk, cells_of(owner, chunk), values)
        tail_even = recv_ref[even, pl.ds(full * width, DIR), :]
        tail_odd = recv_ref[odd, pl.ds(full * width, DIR), :]
        swapped_even = pltpu.roll(tail_even, half, 1)
        swapped_odd = pltpu.roll(tail_odd, half, 1)
        values = jnp.concatenate(
            [
                jnp.where(low_lane_wide, tail_even, swapped_odd),
                jnp.where(low_lane_wide, swapped_even, tail_odd),
            ],
            axis=0,
        )
        cells_even, cells_odd = cells_of(even, full), cells_of(odd, full)
        cells = jnp.where(low_lane, cells_even, pltpu.roll(cells_odd, half, 1))
        place(pair * per_pair + 2 * full, cells, values)

    scattered = lax.dot_general(
        spread[...], onehot[...], (((1,), (1,)), ((), ())), preferred_element_type=jnp.float32
    )
    nothing = jnp.zeros((DIR, LANES), jnp.float32)
    for field in (first, second):
        for f in range(freqs):
            for edge in (0, 1, slab_rows + 2, slab_rows + 3):
                field[f, edge] = nothing
    for h in range(highs):
        for f in range(freqs):
            span = scattered[h * width + f * DIR : h * width + (f + 1) * DIR]
            first[f, 2 * h + 2] = span[:, :LANES]
            first[f, 2 * h + 3] = span[:, LANES:]

    lane = lax.broadcasted_iota(jnp.int32, (slab_rows, LANES), 1)
    zero_rows = jnp.zeros((8, LANES), jnp.float32)

    def gather(read):
        return jnp.concatenate([read(owner) for owner in range(parts)], axis=0)

    def small(kind):
        return gather(lambda owner: recv_ref[owner, pl.ds(base + kind * tile_rows, tile_rows), :])

    gain = 0.5 * courant / 8.0
    slots = iter(range(table.shape[0]))

    def keep(rows):
        slot = next(slots)
        table[slot, pl.ds(8, slab_rows), :] = rows
        return slot

    def face_x(rows):
        slot = next(slots)
        table[slot, pl.ds(0, 8), :] = zero_rows
        table[slot, pl.ds(8 + slab_rows, 8), :] = zero_rows
        table[slot, pl.ds(8, slab_rows), :] = rows
        faces = gain * (table[slot, pl.ds(7, slab_rows + 8), :] + table[slot, pl.ds(8, slab_rows + 8), :])
        table[slot, pl.ds(7, slab_rows + 8), :] = faces
        return slot

    def face_y(rows):
        after = jnp.where(lane < LANES - 1, pltpu.roll(rows, LANES - 1, 1), 0.0)
        before = jnp.where(lane > 0, pltpu.roll(rows, 1, 1), 0.0)
        return keep(gain * (rows + after)), keep(gain * (rows + before))

    speeds = [small(f) for f in range(freqs)]
    current_x, current_y, turning, land = (small(freqs + kind) for kind in range(4))
    current_x_face = face_x(current_x)
    current_y_faces = face_y(current_y)
    speed_x_face = [face_x(s) for s in speeds]
    speed_y_faces = [face_y(s) for s in speeds]
    land_slot = keep(land)
    ahead = jnp.maximum(turning, 0.0) * 0.125
    back = jnp.minimum(turning, 0.0) * 0.125
    bend_slots = [
        keep(rows)
        for rows in (
            -ahead,
            7.0 * ahead + 3.0 * back,
            1.0 - 3.0 * (ahead - back),
            -3.0 * ahead - 7.0 * back,
            back,
        )
    ]

    angles = lax.broadcasted_iota(jnp.int32, (DIR, LANES), 0).astype(jnp.float32) * (2.0 * math.pi / DIR)
    cosine = jnp.cos(angles)
    sine = jnp.sin(angles)
    lane_wide = lax.broadcasted_iota(jnp.int32, (DIR, LANES), 1)

    def row(slot, x):
        return table[slot, pl.ds(8 + x, 1), :]

    def flux(speed, behind, centre, onward, beyond):
        shared = 3.0 * (centre + onward)
        return jnp.maximum(speed, 0.0) * (shared + 3.0 * centre - behind) + jnp.minimum(speed, 0.0) * (
            shared + 3.0 * onward - beyond
        )

    def flux_x(field, f, x):
        speed = row(speed_x_face[f], x) * cosine + row(current_x_face, x)
        return flux(speed, field[f, x + 1], field[f, x + 2], field[f, x + 3], field[f, x + 4])

    def advance(field, f, x, entering):
        leaving = flux_x(field, f, x)
        centre = field[f, x + 2]
        up1 = jnp.where(lane_wide < LANES - 1, pltpu.roll(centre, LANES - 1, 1), 0.0)
        up2 = jnp.where(lane_wide < LANES - 2, pltpu.roll(centre, LANES - 2, 1), 0.0)
        down1 = jnp.where(lane_wide > 0, pltpu.roll(centre, 1, 1), 0.0)
        down2 = jnp.where(lane_wide > 1, pltpu.roll(centre, 2, 1), 0.0)
        right = flux(
            row(speed_y_faces[f][0], x) * sine + row(current_y_faces[0], x), down1, centre, up1, up2
        )
        left = flux(
            row(speed_y_faces[f][1], x) * sine + row(current_y_faces[1], x), down2, down1, centre, up1
        )
        moved = (centre - (leaving - entering) - (right - left)) * row(land_slot, x)
        return moved, leaving

    def sweep(field, finish):
        def body(x, carry):
            out = []
            for f in range(freqs):
                moved, leaving = advance(field, f, x, carry[f])
                finish(f, x, moved)
                out.append(leaving)
            return tuple(out)

        lax.fori_loop(0, slab_rows, body, tuple(flux_x(field, f, -1) for f in range(freqs)))

    def store(f, x, moved):
        second[f, x + 2] = moved

    def refract(f, x, moved):
        bent = row(bend_slots[2], x) * moved
        for slot, shift in zip(bend_slots, (2, 1, 0, DIR - 1, DIR - 2)):
            if shift:
                bent = bent + row(slot, x) * jnp.roll(moved, shift, axis=0)
        for g in range(DIR // 8):
            out_ref[pl.ds((f * DIR + g * 8) * slab_rows + x, 8, stride=slab_rows), :] = bent[g * 8 : g * 8 + 8]

    sweep(first, store)
    sweep(second, refract)


def slab_plan(spectra, wind, growth, damping, row_cell, land_mask, group_speed, current, turning):
    parts = lax.axis_size(GROUP)
    rows, comps = spectra.shape
    tile_rows = land_mask.shape[0]
    width = comps // parts
    full = rows // LANES
    slab_rows = parts * tile_rows
    shared_rows = 6 * tile_rows + full + 1
    block_rows = -(-(full * width + DIR + shared_rows) // 8) * 8
    vmem = pltpu.CompilerParams(vmem_limit_bytes=56 * 1024 * 1024)
    packed = pl.pallas_call(
        functools.partial(pack_kernel, parts),
        out_shape=jax.ShapeDtypeStruct((parts, block_rows, LANES), jnp.float32),
        compiler_params=vmem,
        name="pack",
    )(spectra, wind, growth, damping, row_cell, land_mask, group_speed, current, turning)
    recv = lax.all_to_all(packed, GROUP, split_axis=0, concat_axis=0, tiled=True)
    depth = parts * rows
    out = pl.pallas_call(
        functools.partial(slab_kernel, parts, tile_rows, full),
        out_shape=jax.ShapeDtypeStruct((width * slab_rows, LANES), jnp.float32),
        scratch_shapes=[
            pltpu.VMEM((2 * LANES, 2 * depth), jnp.bfloat16),
            pltpu.VMEM((slab_rows // 2 * width, 2 * depth), jnp.bfloat16),
            pltpu.VMEM((2, slab_rows + 4, DIR, LANES), jnp.float32),
            pltpu.VMEM((2, slab_rows + 4, DIR, LANES), jnp.float32),
            pltpu.VMEM((15, slab_rows + 16, LANES), jnp.float32),
        ],
        compiler_params=vmem,
        name="slab",
    )(recv)
    return out.reshape(1, width, slab_rows, LANES)


def shards(*arrays):
    spectra, land_mask = arrays[0], arrays[5]
    parts = lax.axis_size(GROUP)
    rows, comps = spectra.shape
    whole_frequencies = comps == parts * 2 * DIR
    fits = rows % LANES == LANES // 2 and land_mask.shape == (4, LANES) and parts % 2 == 0
    if whole_frequencies and fits:
        return slab_plan(*arrays)
    return tile_plan(*arrays)


def solution(mesh):
    placed = (
        P(("groups", "pts", "comp"), "sub"),
        P(("groups", "pts", "comp")),
        P("sub"),
        P("sub"),
        P(("groups", "pts", "comp")),
        P(("groups", "pts", "comp"), None),
        P(("groups", "sub"), ("pts", "comp"), None),
        P("groups", ("pts", "comp"), None),
        P(("groups", "pts", "comp"), None),
    )
    return jax.shard_map(
        shards,
        mesh=mesh,
        in_specs=placed,
        out_specs=P("sub", ("pts", "comp"), "groups", None),
        check_vma=False,
    )
```

```python
import functools
import math
import jax
import jax.numpy as jnp
from jax import lax
from jax.experimental import pallas as pl
from jax.experimental.pallas import tpu as pltpu
from jax.sharding import PartitionSpec as P

DIR = 24
SUBSTEPS = 2
LANES = 128
GROUP = ("pts", "comp")


courant = 0.35


def with_halo(cells, sides, width):
    for axis, dim in sides:
        count = lax.axis_size(axis)
        ends = count - 1
        head = lax.slice_in_dim(cells, 0, width, axis=dim)
        tail = lax.slice_in_dim(cells, cells.shape[dim] - width, cells.shape[dim], axis=dim)
        cells = jnp.concatenate(
            [
                lax.ppermute(tail, axis, [(i, (i + 1) % count) for i in range(ends)]),
                cells,
                lax.ppermute(head, axis, [((i + 1) % count, i) for i in range(ends)]),
            ],
            axis=dim,
        )
    return cells


def take_slice(values, first_index, extent, along_axis):
    return lax.slice_in_dim(values, first_index, first_index + extent, axis=along_axis)


def upwind_divergence(padded, motion, along_axis):
    length = padded.shape[along_axis] - 4
    face_count = length + 1
    behind = take_slice(padded, 0, face_count, along_axis)
    centre = take_slice(padded, 1, face_count, along_axis)
    onward = take_slice(padded, 2, face_count, along_axis)
    beyond = take_slice(padded, 3, face_count, along_axis)
    left_face = (6.0 * centre + 3.0 * onward - behind) * 0.125
    right_face = (3.0 * centre + 6.0 * onward - beyond) * 0.125
    face_speed = 0.5 * (
        take_slice(motion, 1, face_count, along_axis)
        + take_slice(motion, 2, face_count, along_axis)
    )
    fluxes = jnp.maximum(face_speed, 0.0) * left_face + jnp.minimum(face_speed, 0.0) * right_face
    return take_slice(fluxes, 1, length, along_axis) - take_slice(fluxes, 0, length, along_axis)


def substep(extended, speed_x, speed_y, sea_mask):
    across = upwind_divergence(extended, speed_x, 1)
    centre_part = extended[:, 2:-2]
    padding = ((0, 0), (0, 0), (2, 2))
    sideways = upwind_divergence(jnp.pad(centre_part, padding), jnp.pad(speed_y, padding), 2)
    return (centre_part - courant * (across + sideways)) * sea_mask


def direction_tables(directions):
    angles = jnp.arange(directions, dtype=jnp.float32) * (2.0 * jnp.pi / directions)
    return (jnp.cos(angles), jnp.sin(angles))


def source_term(values, wind_speed, growth, damping):
    return values * jnp.exp(wind_speed[:, None] * growth[None, :] - damping[None, :])


def velocities(stacked, freq_count):
    cosine_table, sine_table = direction_tables(DIR)
    celerity = stacked[:freq_count][:, None]
    shape_out = (freq_count * DIR,) + stacked.shape[1:]
    speed_x = (
        celerity * cosine_table[None, :, None, None] + stacked[freq_count][None, None]
    ).reshape(shape_out)
    speed_y = (
        celerity * sine_table[None, :, None, None] + stacked[freq_count + 1][None, None]
    ).reshape(shape_out)
    return (speed_x, speed_y)


def deliver(bulk_rows, small_rows):
    return (
        lax.all_to_all(bulk_rows, GROUP, split_axis=0, concat_axis=0, tiled=True),
        lax.all_to_all(small_rows, GROUP, split_axis=0, concat_axis=0, tiled=True),
    )


def tile_plan(spectra, wind, growth, damping, row_cell, land_mask, group_speed, current, turning):
    tile_count = lax.axis_size(GROUP)
    comp_width = spectra.shape[1]
    tile_rows, tile_cols = land_mask.shape
    cell_count = tile_rows * tile_cols
    capacity = cell_count // tile_count
    target = row_cell // cell_count
    local_cell = (row_cell - target * cell_count).astype(jnp.float32)
    matches = (target[:, None] == jnp.arange(tile_count, dtype=jnp.int32)[None, :]).astype(
        jnp.int32
    )
    bucket_slot = jnp.sum((jnp.cumsum(matches, axis=0) - 1) * matches, axis=1)

    def bucket(values, filler):
        shape_out = (tile_count, capacity) + values.shape[1:]
        return jnp.full(shape_out, filler, jnp.float32).at[target, bucket_slot].set(values)

    bulk_rows = bucket(source_term(spectra, wind, growth, damping), 0.0)
    small_rows = bucket(local_cell[:, None], float(cell_count))
    bulk_back, small_back = deliver(bulk_rows, small_rows)
    cell_index = small_back[:, :, 0].reshape(-1).astype(jnp.int32)
    flat_values = bulk_back.reshape((tile_count * capacity,) + bulk_back.shape[2:])
    tile_field = (
        jnp.zeros((cell_count,) + bulk_back.shape[2:], jnp.float32)
        .at[cell_index]
        .set(flat_values, mode="drop")
    )
    spectrum = tile_field.T.reshape(comp_width, tile_rows, tile_cols)
    freq_count = comp_width // DIR
    reach = 2 * SUBSTEPS
    stacked = jnp.concatenate([group_speed, current, land_mask.astype(jnp.float32)[None]], axis=0)
    rimmed = with_halo(stacked, ((GROUP, 1),), 2 * SUBSTEPS)
    speed_x, speed_y = velocities(rimmed, freq_count)
    sea_rim = rimmed[freq_count + 2 :]

    def window(values, margin):
        return lax.slice_in_dim(values, reach - margin, reach + tile_rows + margin, axis=1)

    for repeat in range(SUBSTEPS):
        extended = with_halo(spectrum, ((GROUP, 1),), 2)
        spectrum = substep(extended, window(speed_x, 2), window(speed_y, 0), window(sea_rim, 0)[0])
    blocks = spectrum.reshape(freq_count, DIR, tile_rows, tile_cols)
    wrapped = jnp.concatenate([blocks[:, -2:], blocks, blocks[:, :2]], axis=1)
    turning_full = jnp.broadcast_to(turning[None, None], wrapped.shape)
    blocks = blocks - upwind_divergence(wrapped, turning_full, 1)
    spectrum = blocks.reshape(comp_width, tile_rows, tile_cols)
    shipped = lax.all_to_all(spectrum, GROUP, split_axis=0, concat_axis=1, tiled=True)
    return shipped[None]


def pack_kernel(
    parts,
    spectra_ref,
    wind_ref,
    growth_ref,
    damping_ref,
    cell_ref,
    land_ref,
    speed_ref,
    current_ref,
    turning_ref,
    *out_refs,
):
    rows, comps = spectra_ref.shape
    tile_rows = land_ref.shape[0]
    half = LANES // 2
    full = rows // LANES
    spare = jnp.zeros((1, half), jnp.float32)
    wind_row = jnp.concatenate([wind_ref[...][None], spare], axis=1)
    wind_cols = jnp.broadcast_to(wind_row, (LANES, rows + half)).T
    low = lax.broadcasted_iota(jnp.int32, (8, LANES), 1) < half
    per_freq = DIR // 8
    tails = []
    for block in range(comps // LANES):
        lanes = pl.ds(block * LANES, LANES)
        growth = growth_ref[lanes][None]
        damping = damping_ref[lanes][None]

        def source(first, count):
            span = pl.ds(first, count)
            return spectra_ref[span, lanes] * jnp.exp(
                wind_cols[first : first + count] * growth - damping
            )

        for chunk in range(full):
            turned = source(chunk * LANES, LANES).T
            for g in range(LANES // 8):
                freq, within = divmod(block * (LANES // 8) + g, per_freq)
                part, f = divmod(freq, len(out_refs))
                out_refs[f][part, pl.ds(chunk * DIR + within * 8, 8), :] = turned[g * 8 : g * 8 + 8]
        tail = source(full * LANES, half)
        turned = jnp.concatenate([tail, tail], axis=0).T
        tails += [turned[g * 8 : g * 8 + 8] for g in range(LANES // 8)]
    cell_row = jnp.concatenate([cell_ref[...].astype(jnp.float32)[None], spare], axis=1)
    shared = jnp.concatenate(
        [current_ref[0], current_ref[1], turning_ref[...], land_ref[...].astype(jnp.float32)]
        + [cell_row[:, c * LANES : (c + 1) * LANES] for c in range(full + 1)],
        axis=0,
    )
    base = full * DIR
    for part in range(parts):
        for f, out_ref in enumerate(out_refs):
            freq = part * len(out_refs) + f
            one, two, three = tails[freq * per_freq : (freq + 1) * per_freq]
            out_ref[part, pl.ds(base, 8), :] = jnp.where(low, one, two)
            folded = jnp.where(low, three, pltpu.roll(three, 4, 0))
            out_ref[part, pl.ds(base + 8, 8), :] = jnp.concatenate([folded[:4], speed_ref[freq]], axis=0)
        out_refs[0][part, pl.ds(base + 16, shared.shape[0]), :] = shared


UNROLL = 8


def slab_kernel(parts, tile_rows, full, *refs):
    recv_ref, shared_ref, out_ref = refs[0], refs[-9], refs[-8]
    onehot, spread, first, second, table, faces_x, faces_r = refs[-7:]
    slab_rows = parts * tile_rows
    half = LANES // 2
    base = full * DIR
    shared_base = base + 16
    highs = slab_rows // 2
    low_lane = lax.broadcasted_iota(jnp.int32, (1, LANES), 1) < half
    low_lanes = lax.broadcasted_iota(jnp.int32, (8, LANES), 1) < half
    top_rows = lax.broadcasted_iota(jnp.int32, (8, LANES), 0) < 4
    cell_iota = lax.broadcasted_iota(jnp.int32, (2 * LANES, LANES), 0).astype(jnp.float32).astype(jnp.bfloat16)

    def cells_of(owner, chunk):
        return shared_ref[owner, pl.ds(shared_base + 4 * tile_rows + chunk, 1), :].astype(jnp.int32)

    def place(index, cells, values):
        span = pl.ds(index * LANES, LANES)
        high = cells // (2 * LANES)
        low = (cells - high * (2 * LANES)).astype(jnp.float32)
        low = jnp.broadcast_to(low, (2 * LANES, LANES)).astype(jnp.bfloat16)
        onehot[:, span] = jnp.where(cell_iota == low, 1.0, 0.0).astype(jnp.bfloat16)
        head = values.astype(jnp.bfloat16).astype(jnp.float32)
        both = jnp.concatenate([head, values - head], axis=0).astype(jnp.bfloat16)
        for h in range(highs):
            pick = jnp.broadcast_to((high == h).astype(jnp.float32), (2 * DIR, LANES)).astype(jnp.bfloat16)
            spread[pl.ds(h * 2 * DIR, 2 * DIR), span] = both * pick

    per_pair = 2 * full + 1
    for pair in range(parts // 2):
        even, odd = 2 * pair, 2 * pair + 1
        for side, owner in enumerate((even, odd)):
            for chunk in range(full):
                values = recv_ref[owner, pl.ds(chunk * DIR, DIR), :]
                place(pair * per_pair + side * full + chunk, cells_of(owner, chunk), values)

        def merged(offset):
            own, other = recv_ref[even, pl.ds(offset, 8), :], recv_ref[odd, pl.ds(offset, 8), :]
            return (
                jnp.where(low_lanes, own, pltpu.roll(other, half, 1)),
                jnp.where(low_lanes, pltpu.roll(own, half, 1), other),
            )

        one, two = merged(base)
        three, four = merged(base + 8)
        values = jnp.concatenate([one, two, jnp.where(top_rows, three, pltpu.roll(four, 4, 0))], axis=0)
        cells = jnp.where(low_lane, cells_of(even, full), pltpu.roll(cells_of(odd, full), half, 1))
        place(pair * per_pair + 2 * full, cells, values)

    scattered = lax.dot_general(
        spread[...], onehot[...], (((1,), (1,)), ((), ())), preferred_element_type=jnp.float32
    )
    nothing = jnp.zeros((DIR, LANES), jnp.float32)
    for field in (first, second):
        for edge in (0, 1, slab_rows + 2, slab_rows + 3):
            field[edge] = nothing
    for h in range(highs):
        at = h * 2 * DIR
        total = scattered[at : at + DIR] + scattered[at + DIR : at + 2 * DIR]
        first[2 * h + 2] = total[:, :LANES]
        first[2 * h + 3] = total[:, LANES:]

    lane = lax.broadcasted_iota(jnp.int32, (slab_rows, LANES), 1)
    zero_rows = jnp.zeros((8, LANES), jnp.float32)

    def gather(ref, offset):
        return jnp.concatenate([ref[owner, pl.ds(offset, tile_rows), :] for owner in range(parts)], axis=0)

    gain = 0.5 * courant / 8.0
    slots = iter(range(table.shape[0]))

    def keep(rows):
        slot = next(slots)
        table[slot, pl.ds(8, slab_rows), :] = rows
        return slot

    def face_x(rows):
        slot = next(slots)
        table[slot, pl.ds(0, 8), :] = zero_rows
        table[slot, pl.ds(8 + slab_rows, 8), :] = zero_rows
        table[slot, pl.ds(8, slab_rows), :] = rows
        faces = gain * (table[slot, pl.ds(7, slab_rows + 8), :] + table[slot, pl.ds(8, slab_rows + 8), :])
        table[slot, pl.ds(7, slab_rows + 8), :] = faces
        return slot

    def face_y(rows):
        after = jnp.where(lane < LANES - 1, pltpu.roll(rows, LANES - 1, 1), 0.0)
        before = jnp.where(lane > 0, pltpu.roll(rows, 1, 1), 0.0)
        return keep(gain * (rows + after)), keep(gain * (rows + before))

    speed = gather(recv_ref, base + 12)
    current_x, current_y, turning, land = (
        gather(shared_ref, shared_base + kind * tile_rows) for kind in range(4)
    )
    current_x_face, speed_x_face = face_x(current_x), face_x(speed)
    current_y_faces, speed_y_faces = face_y(current_y), face_y(speed)
    land_slot = keep(land)
    ahead = jnp.maximum(turning, 0.0) * 0.125
    back = jnp.minimum(turning, 0.0) * 0.125
    bend_slots = [
        keep(rows)
        for rows in (
            -ahead,
            7.0 * ahead + 3.0 * back,
            1.0 - 3.0 * (ahead - back),
            -3.0 * ahead - 7.0 * back,
            back,
        )
    ]

    angles = lax.broadcasted_iota(jnp.int32, (DIR, LANES), 0).astype(jnp.float32) * (2.0 * math.pi / DIR)
    cosine = jnp.cos(angles)
    sine = jnp.sin(angles)
    lane_wide = lax.broadcasted_iota(jnp.int32, (DIR, LANES), 1)

    def row(slot, x):
        return table[slot, pl.ds(8 + x, 1), :]

    def flux(speeds, behind, centre, centre3, onward3, beyond):
        both = centre3 + onward3
        return speeds[0] * (both + centre3 - behind) + speeds[1] * (both + onward3 - beyond)

    def split(speed):
        return jnp.maximum(speed, 0.0), jnp.minimum(speed, 0.0)

    def flux_x(field, x, speeds, centre3, onward3):
        return flux(speeds, field[x + 1], None, centre3, onward3, field[x + 4])

    def sweep(field, fresh, finish):
        def speeds_x(x):
            if fresh:
                speeds = split(row(speed_x_face, x) * cosine + row(current_x_face, x))
                faces_x[0, x + 1], faces_x[1, x + 1] = speeds
                return speeds
            return faces_x[0, x + 1], faces_x[1, x + 1]

        def speeds_y(side, x):
            if fresh:
                speeds = split(row(speed_y_faces[side], x) * sine + row(current_y_faces[side], x))
                faces_r[2 * side, x], faces_r[2 * side + 1, x] = speeds
                return speeds
            return faces_r[2 * side, x], faces_r[2 * side + 1, x]

        def body(step, carry):
            entering, centre3 = carry
            for i in range(UNROLL):
                x = step * UNROLL + i
                centre = field[x + 2]
                onward3 = 3.0 * field[x + 3]
                leaving = flux_x(field, x, speeds_x(x), centre3, onward3)
                up1 = jnp.where(lane_wide < LANES - 1, pltpu.roll(centre, LANES - 1, 1), 0.0)
                up2 = jnp.where(lane_wide < LANES - 2, pltpu.roll(centre, LANES - 2, 1), 0.0)
                down1 = jnp.where(lane_wide > 0, pltpu.roll(centre, 1, 1), 0.0)
                down2 = jnp.where(lane_wide > 1, pltpu.roll(centre, 2, 1), 0.0)
                right = flux(speeds_y(0, x), down1, centre, centre3, 3.0 * up1, up2)
                left = flux(speeds_y(1, x), down2, down1, 3.0 * down1, centre3, up1)
                finish(x, (centre - (leaving - entering) - (right - left)) * row(land_slot, x))
                entering, centre3 = leaving, onward3
            return entering, centre3

        start3 = 3.0 * field[2]
        entering = flux_x(field, -1, speeds_x(-1), nothing, start3)
        lax.fori_loop(0, slab_rows // UNROLL, body, (entering, start3))

    def store(x, moved):
        second[x + 2] = moved

    def refract(x, moved):
        bent = row(bend_slots[2], x) * moved
        for slot, shift in zip(bend_slots, (2, 1, 0, DIR - 1, DIR - 2)):
            if shift:
                bent = bent + row(slot, x) * jnp.roll(moved, shift, axis=0)
        for g in range(DIR // 8):
            out_ref[pl.ds(g * 8 * slab_rows + x, 8, stride=slab_rows), :] = bent[g * 8 : g * 8 + 8]

    sweep(first, True, store)
    sweep(second, False, refract)


def slab_plan(spectra, wind, growth, damping, row_cell, land_mask, group_speed, current, turning):
    parts = lax.axis_size(GROUP)
    rows, comps = spectra.shape
    tile_rows = land_mask.shape[0]
    freqs = comps // parts // DIR
    full = rows // LANES
    slab_rows = parts * tile_rows
    depth = parts * rows
    block_rows = full * DIR + 16
    shared_rows = -(-(4 * tile_rows + full + 1) // 8) * 8
    blocks = [block_rows + shared_rows * (f == 0) for f in range(freqs)]
    params = pltpu.CompilerParams(vmem_limit_bytes=56 * 1024 * 1024)
    packed = pl.pallas_call(
        functools.partial(pack_kernel, parts),
        out_shape=[jax.ShapeDtypeStruct((parts, block, LANES), jnp.float32) for block in blocks],
        compiler_params=params,
        name="pack",
    )(spectra, wind, growth, damping, row_cell, land_mask, group_speed, current, turning)
    arrived = [lax.all_to_all(p, GROUP, split_axis=0, concat_axis=0, tiled=True) for p in packed]
    whole = pl.BlockSpec(memory_space=pltpu.VMEM)
    field = None
    for f in range(freqs):
        operands = [arrived[f]] if f == 0 else [arrived[f], field, arrived[0]]
        field = pl.pallas_call(
            functools.partial(slab_kernel, parts, tile_rows, full),
            grid=(1,),
            out_shape=jax.ShapeDtypeStruct((freqs * DIR * slab_rows, LANES), jnp.float32),
            in_specs=[whole] if f == 0 else [whole, pl.BlockSpec(memory_space=pl.ANY), whole],
            out_specs=pl.BlockSpec((DIR * slab_rows, LANES), functools.partial(lambda f, i: (f, 0), f)),
            scratch_shapes=[
                pltpu.VMEM((2 * LANES, depth), jnp.bfloat16),
                pltpu.VMEM((slab_rows * DIR, depth), jnp.bfloat16),
                pltpu.VMEM((slab_rows + 4, DIR, LANES), jnp.float32),
                pltpu.VMEM((slab_rows + 4, DIR, LANES), jnp.float32),
                pltpu.VMEM((12, slab_rows + 16, LANES), jnp.float32),
                pltpu.VMEM((2, slab_rows + 1, DIR, LANES), jnp.float32),
                pltpu.VMEM((4, slab_rows, DIR, LANES), jnp.float32),
            ],
            input_output_aliases={} if f == 0 else {1: 0},
            cost_estimate=pl.CostEstimate(
                flops=100 * slab_rows * DIR * LANES * 10, bytes_accessed=1 << 20, transcendentals=0
            ),
            compiler_params=params,
            name="slab",
        )(*operands)
    return field.reshape(1, freqs * DIR, slab_rows, LANES)


def shards(*arrays):
    spectra, land_mask = arrays[0], arrays[5]
    parts = lax.axis_size(GROUP)
    rows, comps = spectra.shape
    whole_frequencies = comps == parts * 2 * DIR
    fits = rows % LANES == LANES // 2 and land_mask.shape == (4, LANES) and parts % 2 == 0
    if whole_frequencies and fits:
        return slab_plan(*arrays)
    return tile_plan(*arrays)


def solution(mesh):
    placed = (
        P(("groups", "pts", "comp"), "sub"),
        P(("groups", "pts", "comp")),
        P("sub"),
        P("sub"),
        P(("groups", "pts", "comp")),
        P(("groups", "pts", "comp"), None),
        P(("groups", "sub"), ("pts", "comp"), None),
        P("groups", ("pts", "comp"), None),
        P(("groups", "pts", "comp"), None),
    )
    return jax.shard_map(
        shards,
        mesh=mesh,
        in_specs=placed,
        out_specs=P("sub", ("pts", "comp"), "groups", None),
        check_vma=False,
    )
```

```python
import functools
import math
import jax
import jax.numpy as jnp
from jax import lax
from jax.experimental import pallas as pl
from jax.experimental.pallas import tpu as pltpu
from jax.sharding import PartitionSpec as P

DIR = 24
SUBSTEPS = 2
LANES = 128
GROUP = ("pts", "comp")


courant = 0.35


def with_halo(cells, sides, width):
    for axis, dim in sides:
        count = lax.axis_size(axis)
        ends = count - 1
        head = lax.slice_in_dim(cells, 0, width, axis=dim)
        tail = lax.slice_in_dim(cells, cells.shape[dim] - width, cells.shape[dim], axis=dim)
        cells = jnp.concatenate(
            [
                lax.ppermute(tail, axis, [(i, (i + 1) % count) for i in range(ends)]),
                cells,
                lax.ppermute(head, axis, [((i + 1) % count, i) for i in range(ends)]),
            ],
            axis=dim,
        )
    return cells


def take_slice(values, first_index, extent, along_axis):
    return lax.slice_in_dim(values, first_index, first_index + extent, axis=along_axis)


def upwind_divergence(padded, motion, along_axis):
    length = padded.shape[along_axis] - 4
    face_count = length + 1
    behind = take_slice(padded, 0, face_count, along_axis)
    centre = take_slice(padded, 1, face_count, along_axis)
    onward = take_slice(padded, 2, face_count, along_axis)
    beyond = take_slice(padded, 3, face_count, along_axis)
    left_face = (6.0 * centre + 3.0 * onward - behind) * 0.125
    right_face = (3.0 * centre + 6.0 * onward - beyond) * 0.125
    face_speed = 0.5 * (
        take_slice(motion, 1, face_count, along_axis)
        + take_slice(motion, 2, face_count, along_axis)
    )
    fluxes = jnp.maximum(face_speed, 0.0) * left_face + jnp.minimum(face_speed, 0.0) * right_face
    return take_slice(fluxes, 1, length, along_axis) - take_slice(fluxes, 0, length, along_axis)


def substep(extended, speed_x, speed_y, sea_mask):
    across = upwind_divergence(extended, speed_x, 1)
    centre_part = extended[:, 2:-2]
    padding = ((0, 0), (0, 0), (2, 2))
    sideways = upwind_divergence(jnp.pad(centre_part, padding), jnp.pad(speed_y, padding), 2)
    return (centre_part - courant * (across + sideways)) * sea_mask


def direction_tables(directions):
    angles = jnp.arange(directions, dtype=jnp.float32) * (2.0 * jnp.pi / directions)
    return (jnp.cos(angles), jnp.sin(angles))


def source_term(values, wind_speed, growth, damping):
    return values * jnp.exp(wind_speed[:, None] * growth[None, :] - damping[None, :])


def velocities(stacked, freq_count):
    cosine_table, sine_table = direction_tables(DIR)
    celerity = stacked[:freq_count][:, None]
    shape_out = (freq_count * DIR,) + stacked.shape[1:]
    speed_x = (
        celerity * cosine_table[None, :, None, None] + stacked[freq_count][None, None]
    ).reshape(shape_out)
    speed_y = (
        celerity * sine_table[None, :, None, None] + stacked[freq_count + 1][None, None]
    ).reshape(shape_out)
    return (speed_x, speed_y)


def deliver(bulk_rows, small_rows):
    return (
        lax.all_to_all(bulk_rows, GROUP, split_axis=0, concat_axis=0, tiled=True),
        lax.all_to_all(small_rows, GROUP, split_axis=0, concat_axis=0, tiled=True),
    )


def tile_plan(spectra, wind, growth, damping, row_cell, land_mask, group_speed, current, turning):
    tile_count = lax.axis_size(GROUP)
    comp_width = spectra.shape[1]
    tile_rows, tile_cols = land_mask.shape
    cell_count = tile_rows * tile_cols
    capacity = cell_count // tile_count
    target = row_cell // cell_count
    local_cell = (row_cell - target * cell_count).astype(jnp.float32)
    matches = (target[:, None] == jnp.arange(tile_count, dtype=jnp.int32)[None, :]).astype(
        jnp.int32
    )
    bucket_slot = jnp.sum((jnp.cumsum(matches, axis=0) - 1) * matches, axis=1)

    def bucket(values, filler):
        shape_out = (tile_count, capacity) + values.shape[1:]
        return jnp.full(shape_out, filler, jnp.float32).at[target, bucket_slot].set(values)

    bulk_rows = bucket(source_term(spectra, wind, growth, damping), 0.0)
    small_rows = bucket(local_cell[:, None], float(cell_count))
    bulk_back, small_back = deliver(bulk_rows, small_rows)
    cell_index = small_back[:, :, 0].reshape(-1).astype(jnp.int32)
    flat_values = bulk_back.reshape((tile_count * capacity,) + bulk_back.shape[2:])
    tile_field = (
        jnp.zeros((cell_count,) + bulk_back.shape[2:], jnp.float32)
        .at[cell_index]
        .set(flat_values, mode="drop")
    )
    spectrum = tile_field.T.reshape(comp_width, tile_rows, tile_cols)
    freq_count = comp_width // DIR
    reach = 2 * SUBSTEPS
    stacked = jnp.concatenate([group_speed, current, land_mask.astype(jnp.float32)[None]], axis=0)
    rimmed = with_halo(stacked, ((GROUP, 1),), 2 * SUBSTEPS)
    speed_x, speed_y = velocities(rimmed, freq_count)
    sea_rim = rimmed[freq_count + 2 :]

    def window(values, margin):
        return lax.slice_in_dim(values, reach - margin, reach + tile_rows + margin, axis=1)

    for repeat in range(SUBSTEPS):
        extended = with_halo(spectrum, ((GROUP, 1),), 2)
        spectrum = substep(extended, window(speed_x, 2), window(speed_y, 0), window(sea_rim, 0)[0])
    blocks = spectrum.reshape(freq_count, DIR, tile_rows, tile_cols)
    wrapped = jnp.concatenate([blocks[:, -2:], blocks, blocks[:, :2]], axis=1)
    turning_full = jnp.broadcast_to(turning[None, None], wrapped.shape)
    blocks = blocks - upwind_divergence(wrapped, turning_full, 1)
    spectrum = blocks.reshape(comp_width, tile_rows, tile_cols)
    shipped = lax.all_to_all(spectrum, GROUP, split_axis=0, concat_axis=1, tiled=True)
    return shipped[None]


def pack_kernel(
    parts,
    freqs,
    spectra_ref,
    wind_ref,
    growth_ref,
    damping_ref,
    cell_ref,
    speed_ref,
    current_ref,
    turning_ref,
    out_ref,
):
    rows, comps = spectra_ref.shape
    half = LANES // 2
    full = rows // LANES
    spare = jnp.zeros((1, half), jnp.float32)
    wind_row = jnp.concatenate([wind_ref[...][None], spare], axis=1)
    wind_cols = jnp.broadcast_to(wind_row, (LANES, rows + half)).T
    low = lax.broadcasted_iota(jnp.int32, (8, LANES), 1) < half
    per_freq = DIR // 8
    span_rows = full * DIR + 16
    tails = []
    for block in range(comps // LANES):
        lanes = pl.ds(block * LANES, LANES)
        growth = growth_ref[lanes][None]
        damping = damping_ref[lanes][None]

        def source(first, count):
            span = pl.ds(first, count)
            return spectra_ref[span, lanes] * jnp.exp(
                wind_cols[first : first + count] * growth - damping
            )

        for chunk in range(full):
            turned = source(chunk * LANES, LANES).T
            for g in range(LANES // 8):
                freq, within = divmod(block * (LANES // 8) + g, per_freq)
                part, f = divmod(freq, freqs)
                at = f * span_rows + chunk * DIR + within * 8
                out_ref[part, pl.ds(at, 8), :] = turned[g * 8 : g * 8 + 8]
        tail = source(full * LANES, half)
        turned = jnp.concatenate([tail, tail], axis=0).T
        tails += [turned[g * 8 : g * 8 + 8] for g in range(LANES // 8)]
    cell_row = jnp.concatenate([cell_ref[...].astype(jnp.float32)[None], spare], axis=1)
    shared = jnp.concatenate(
        [current_ref[0], current_ref[1], turning_ref[...]]
        + [cell_row[:, c * LANES : (c + 1) * LANES] for c in range(full + 1)],
        axis=0,
    )
    for part in range(parts):
        for f in range(freqs):
            freq = part * freqs + f
            one, two, three = tails[freq * per_freq : (freq + 1) * per_freq]
            at = f * span_rows + full * DIR
            out_ref[part, pl.ds(at, 8), :] = jnp.where(low, one, two)
            folded = jnp.where(low, three, pltpu.roll(three, 4, 0))
            out_ref[part, pl.ds(at + 8, 8), :] = jnp.concatenate([folded[:4], speed_ref[freq]], axis=0)
        out_ref[part, pl.ds(freqs * span_rows, shared.shape[0]), :] = shared


BLOCK = 8


def slab_kernel(
    parts,
    tile_rows,
    full,
    freqs,
    recv_ref,
    out_ref,
    onehot,
    spread,
    first,
    second,
    table,
    faces_x,
    faces_y,
    moved_ref,
    done_ref,
    sems,
):
    slab_rows = parts * tile_rows
    half = LANES // 2
    span_rows = full * DIR + 16
    shared_base = freqs * span_rows
    highs = slab_rows // 2
    width = freqs * 2 * DIR
    low_lane = lax.broadcasted_iota(jnp.int32, (1, LANES), 1) < half
    low_lanes = lax.broadcasted_iota(jnp.int32, (8, LANES), 1) < half
    top_rows = lax.broadcasted_iota(jnp.int32, (8, LANES), 0) < 4
    cell_iota = lax.broadcasted_iota(jnp.int32, (2 * LANES, LANES), 0).astype(jnp.float32).astype(jnp.bfloat16)
    high_iota = lax.broadcasted_iota(jnp.int32, (highs, LANES), 0)

    def cells_of(owner, chunk):
        return recv_ref[owner, pl.ds(shared_base + 3 * tile_rows + chunk, 1), :].astype(jnp.int32)

    def place(index, cells, values):
        span = pl.ds(index * LANES, LANES)
        high = cells // (2 * LANES)
        low = (cells - high * (2 * LANES)).astype(jnp.float32)
        low = jnp.broadcast_to(low, (2 * LANES, LANES)).astype(jnp.bfloat16)
        onehot[:, span] = jnp.where(cell_iota == low, 1.0, 0.0).astype(jnp.bfloat16)
        pieces = []
        for value in values:
            head = value.astype(jnp.bfloat16).astype(jnp.float32)
            pieces += [head, value - head]
        both = jnp.concatenate(pieces, axis=0).astype(jnp.bfloat16)
        for h in range(highs):
            pick = jnp.broadcast_to((high == h).astype(jnp.float32), (width, LANES)).astype(jnp.bfloat16)
            spread[pl.ds(h * width, width), span] = both * pick
        spread[pl.ds(highs * width, highs), span] = (
            (high_iota == high).astype(jnp.float32).astype(jnp.bfloat16)
        )

    per_pair = 2 * full + 1
    for pair in range(parts // 2):
        even, odd = 2 * pair, 2 * pair + 1
        for side, owner in enumerate((even, odd)):
            for chunk in range(full):
                values = [
                    recv_ref[owner, pl.ds(f * span_rows + chunk * DIR, DIR), :] for f in range(freqs)
                ]
                place(pair * per_pair + side * full + chunk, cells_of(owner, chunk), values)

        def merged(offset):
            own, other = recv_ref[even, pl.ds(offset, 8), :], recv_ref[odd, pl.ds(offset, 8), :]
            return (
                jnp.where(low_lanes, own, pltpu.roll(other, half, 1)),
                jnp.where(low_lanes, pltpu.roll(own, half, 1), other),
            )

        values = []
        for f in range(freqs):
            one, two = merged(f * span_rows + full * DIR)
            three, four = merged(f * span_rows + full * DIR + 8)
            values.append(
                jnp.concatenate([one, two, jnp.where(top_rows, three, pltpu.roll(four, 4, 0))], axis=0)
            )
        cells = jnp.where(low_lane, cells_of(even, full), pltpu.roll(cells_of(odd, full), half, 1))
        place(pair * per_pair + 2 * full, cells, values)

    scattered = lax.dot_general(
        spread[...], onehot[...], (((1,), (1,)), ((), ())), preferred_element_type=jnp.float32
    )
    nothing = jnp.zeros((DIR, LANES), jnp.float32)
    for f in range(freqs):
        for field in (first, second):
            for edge in (0, 1, slab_rows + 2, slab_rows + 3):
                field[f, edge] = nothing
        for h in range(highs):
            at = h * width + f * 2 * DIR
            total = scattered[at : at + DIR] + scattered[at + DIR : at + 2 * DIR]
            first[f, 2 * h + 2] = total[:, :LANES]
            first[f, 2 * h + 3] = total[:, LANES:]

    lane = lax.broadcasted_iota(jnp.int32, (slab_rows, LANES), 1)
    zero_rows = jnp.zeros((8, LANES), jnp.float32)

    def gather(offset):
        return jnp.concatenate(
            [recv_ref[owner, pl.ds(offset, tile_rows), :] for owner in range(parts)], axis=0
        )

    gain = 0.5 * courant / 8.0
    slots = iter(range(table.shape[0]))

    def keep(rows):
        slot = next(slots)
        table[slot, pl.ds(8, rows.shape[0]), :] = rows
        return slot

    def face_x(rows):
        slot = next(slots)
        table[slot, pl.ds(0, 8), :] = zero_rows
        table[slot, pl.ds(8 + slab_rows, 8), :] = zero_rows
        table[slot, pl.ds(8, slab_rows), :] = rows
        faces = gain * (table[slot, pl.ds(7, slab_rows + 8), :] + table[slot, pl.ds(8, slab_rows + 8), :])
        table[slot, pl.ds(7, slab_rows + 8), :] = faces
        return slot

    def face_y(rows):
        after = jnp.where(lane < LANES - 1, pltpu.roll(rows, LANES - 1, 1), 0.0)
        before = jnp.where(lane > 0, pltpu.roll(rows, 1, 1), 0.0)
        return keep(gain * (rows + after)), keep(gain * (rows + before))

    speeds = [gather(f * span_rows + full * DIR + 12) for f in range(freqs)]
    current_x, current_y, turning = (gather(shared_base + kind * tile_rows) for kind in range(3))
    current_x_face, speed_x_face = face_x(current_x), [face_x(s) for s in speeds]
    current_y_faces, speed_y_faces = face_y(current_y), [face_y(s) for s in speeds]
    named = scattered[highs * width : highs * width + highs]
    land_slots = keep(named[:, :LANES]), keep(named[:, LANES:])
    ahead = jnp.maximum(turning, 0.0) * 0.125
    back = jnp.minimum(turning, 0.0) * 0.125
    bend_slots = [
        keep(rows)
        for rows in (
            -ahead,
            7.0 * ahead + 3.0 * back,
            1.0 - 3.0 * (ahead - back),
            -3.0 * ahead - 7.0 * back,
            back,
        )
    ]

    angles = lax.broadcasted_iota(jnp.int32, (DIR, LANES), 0).astype(jnp.float32) * (2.0 * math.pi / DIR)
    cosine = jnp.cos(angles)
    sine = jnp.sin(angles)
    lane_wide = lax.broadcasted_iota(jnp.int32, (DIR, LANES), 1)

    def row(slot, x):
        return table[slot, pl.ds(8 + x, 1), :]

    def flux(speed, behind, centre3, onward3, beyond):
        positive = speed > 0.0
        near = jnp.where(positive, centre3, onward3)
        far = jnp.where(positive, behind, beyond)
        return speed * ((centre3 + onward3) + (near - far))

    def advance(field, fresh, step, carry, finish):
        def speed_x(f, x):
            if fresh:
                faces_x[f, x + 1] = row(speed_x_face[f], x) * cosine + row(current_x_face, x)
            return faces_x[f, x + 1]

        def speed_y(f, side, x):
            if fresh:
                faces_y[f, side, x] = row(speed_y_faces[f][side], x) * sine + row(current_y_faces[side], x)
            return faces_y[f, side, x]

        carry = list(carry)
        for i in range(BLOCK):
            x = step * BLOCK + i
            sea = row(land_slots[i % 2], step * (BLOCK // 2) + i // 2)
            for f in range(freqs):
                entering, centre3 = carry[f]
                centre = field[f, x + 2]
                onward3 = 3.0 * field[f, x + 3]
                leaving = flux(speed_x(f, x), field[f, x + 1], centre3, onward3, field[f, x + 4])
                up1 = jnp.where(lane_wide < LANES - 1, pltpu.roll(centre, LANES - 1, 1), 0.0)
                up2 = jnp.where(lane_wide < LANES - 2, pltpu.roll(centre, LANES - 2, 1), 0.0)
                down1 = jnp.where(lane_wide > 0, pltpu.roll(centre, 1, 1), 0.0)
                down2 = jnp.where(lane_wide > 1, pltpu.roll(centre, 2, 1), 0.0)
                right = flux(speed_y(f, 0, x), down1, centre3, 3.0 * up1, up2)
                left = flux(speed_y(f, 1, x), down2, 3.0 * down1, centre3, up1)
                finish(f, x, (centre - (leaving - entering) - (right - left)) * sea)
                carry[f] = leaving, onward3
        return tuple(carry)

    def enter(field, fresh):
        carry = []
        for f in range(freqs):
            if fresh:
                faces_x[f, 0] = row(speed_x_face[f], -1) * cosine + row(current_x_face, -1)
            start3 = 3.0 * field[f, 2]
            carry.append((flux(faces_x[f, 0], nothing, nothing, start3, field[f, 3]), start3))
        return tuple(carry)

    def store(f, x, moved):
        second[f, x + 2] = moved

    def turn(f, x, moved):
        for g in range(DIR // 8):
            at = (f * DIR + g * 8) * slab_rows + x
            moved_ref[pl.ds(at, 8, stride=slab_rows), :] = moved[g * 8 : g * 8 + 8]

    def copy_out(step):
        part = pl.ds(pl.multiple_of(step * BLOCK, BLOCK), BLOCK)
        return pltpu.make_async_copy(done_ref.at[:, part, :], out_ref.at[:, part, :], sems.at[step])

    def final(step, carry):
        carry = advance(second, False, step, carry, turn)
        at = pl.multiple_of(step * BLOCK, BLOCK)
        weights = [table[slot, pl.ds(8 + at, BLOCK), :] for slot in bend_slots]
        for f in range(freqs):
            ring = [moved_ref[pl.ds((f * DIR + d) * slab_rows + at, BLOCK), :] for d in range(DIR)]
            for d in range(DIR):
                bent = weights[2] * ring[d]
                for k in (0, 1, 3, 4):
                    bent = bent + weights[k] * ring[(d + k - 2) % DIR]
                done_ref[f * DIR + d, pl.ds(at, BLOCK), :] = bent
        copy_out(step).start()
        return carry

    steps = slab_rows // BLOCK
    lax.fori_loop(0, steps, lambda step, carry: advance(first, True, step, carry, store), enter(first, True))
    lax.fori_loop(0, steps, final, enter(second, False))
    for step in range(steps):
        copy_out(step).wait()


def slab_plan(spectra, wind, growth, damping, row_cell, group_speed, current, turning):
    parts = lax.axis_size(GROUP)
    rows, comps = spectra.shape
    tile_rows = turning.shape[0]
    freqs = comps // parts // DIR
    full = rows // LANES
    slab_rows = parts * tile_rows
    depth = parts * rows
    highs = slab_rows // 2
    block_rows = -(-(freqs * (full * DIR + 16) + 3 * tile_rows + full + 1) // 8) * 8
    packed = pl.pallas_call(
        functools.partial(pack_kernel, parts, freqs),
        out_shape=jax.ShapeDtypeStruct((parts, block_rows, LANES), jnp.float32),
        compiler_params=pltpu.CompilerParams(vmem_limit_bytes=56 * 1024 * 1024),
        name="pack",
    )(spectra, wind, growth, damping, row_cell, group_speed, current, turning)
    arrived = lax.all_to_all(packed, GROUP, split_axis=0, concat_axis=0, tiled=True)
    out = pl.pallas_call(
        functools.partial(slab_kernel, parts, tile_rows, full, freqs),
        out_shape=jax.ShapeDtypeStruct((freqs * DIR, slab_rows, LANES), jnp.float32),
        in_specs=[pl.BlockSpec(memory_space=pltpu.VMEM)],
        out_specs=pl.BlockSpec(memory_space=pl.ANY),
        scratch_shapes=[
            pltpu.VMEM((2 * LANES, depth), jnp.bfloat16),
            pltpu.VMEM((highs * (freqs * 2 * DIR + 1), depth), jnp.bfloat16),
            pltpu.VMEM((freqs, slab_rows + 4, DIR, LANES), jnp.float32),
            pltpu.VMEM((freqs, slab_rows + 4, DIR, LANES), jnp.float32),
            pltpu.VMEM((10 + 3 * freqs, slab_rows + 16, LANES), jnp.float32),
            pltpu.VMEM((freqs, slab_rows + 1, DIR, LANES), jnp.float32),
            pltpu.VMEM((freqs, 2, slab_rows, DIR, LANES), jnp.float32),
            pltpu.VMEM((freqs * DIR * slab_rows, LANES), jnp.float32),
            pltpu.VMEM((freqs * DIR, slab_rows, LANES), jnp.float32),
            pltpu.SemaphoreType.DMA((slab_rows // BLOCK,)),
        ],
        compiler_params=pltpu.CompilerParams(vmem_limit_bytes=32 * 1024 * 1024),
        name="slab",
    )(arrived)
    return out.reshape(1, freqs * DIR, slab_rows, LANES)


def shards(*arrays):
    spectra, land_mask = arrays[0], arrays[5]
    parts = lax.axis_size(GROUP)
    rows, comps = spectra.shape
    whole_frequencies = comps == parts * 2 * DIR
    fits = rows % LANES == LANES // 2 and land_mask.shape == (4, LANES) and parts % 2 == 0
    if whole_frequencies and fits:
        return slab_plan(*arrays[:5], *arrays[6:])
    return tile_plan(*arrays)


def solution(mesh):
    placed = (
        P(("groups", "pts", "comp"), "sub"),
        P(("groups", "pts", "comp")),
        P("sub"),
        P("sub"),
        P(("groups", "pts", "comp")),
        P(("groups", "pts", "comp"), None),
        P(("groups", "sub"), ("pts", "comp"), None),
        P("groups", ("pts", "comp"), None),
        P(("groups", "pts", "comp"), None),
    )
    return jax.shard_map(
        shards,
        mesh=mesh,
        in_specs=placed,
        out_specs=P("sub", ("pts", "comp"), "groups", None),
        check_vma=False,
    )
```

```python
import functools
import math
import jax
import jax.numpy as jnp
from jax import lax
from jax.experimental import pallas as pl
from jax.experimental.pallas import tpu as pltpu
from jax.sharding import PartitionSpec as P

DIR = 24
SUBSTEPS = 2
LANES = 128
GROUP = ("pts", "comp")


courant = 0.35


def with_halo(cells, sides, width):
    for axis, dim in sides:
        count = lax.axis_size(axis)
        ends = count - 1
        head = lax.slice_in_dim(cells, 0, width, axis=dim)
        tail = lax.slice_in_dim(cells, cells.shape[dim] - width, cells.shape[dim], axis=dim)
        cells = jnp.concatenate(
            [
                lax.ppermute(tail, axis, [(i, (i + 1) % count) for i in range(ends)]),
                cells,
                lax.ppermute(head, axis, [((i + 1) % count, i) for i in range(ends)]),
            ],
            axis=dim,
        )
    return cells


def take_slice(values, first_index, extent, along_axis):
    return lax.slice_in_dim(values, first_index, first_index + extent, axis=along_axis)


def upwind_divergence(padded, motion, along_axis):
    length = padded.shape[along_axis] - 4
    face_count = length + 1
    behind = take_slice(padded, 0, face_count, along_axis)
    centre = take_slice(padded, 1, face_count, along_axis)
    onward = take_slice(padded, 2, face_count, along_axis)
    beyond = take_slice(padded, 3, face_count, along_axis)
    left_face = (6.0 * centre + 3.0 * onward - behind) * 0.125
    right_face = (3.0 * centre + 6.0 * onward - beyond) * 0.125
    face_speed = 0.5 * (
        take_slice(motion, 1, face_count, along_axis)
        + take_slice(motion, 2, face_count, along_axis)
    )
    fluxes = jnp.maximum(face_speed, 0.0) * left_face + jnp.minimum(face_speed, 0.0) * right_face
    return take_slice(fluxes, 1, length, along_axis) - take_slice(fluxes, 0, length, along_axis)


def substep(extended, speed_x, speed_y, sea_mask):
    across = upwind_divergence(extended, speed_x, 1)
    centre_part = extended[:, 2:-2]
    padding = ((0, 0), (0, 0), (2, 2))
    sideways = upwind_divergence(jnp.pad(centre_part, padding), jnp.pad(speed_y, padding), 2)
    return (centre_part - courant * (across + sideways)) * sea_mask


def direction_tables(directions):
    angles = jnp.arange(directions, dtype=jnp.float32) * (2.0 * jnp.pi / directions)
    return (jnp.cos(angles), jnp.sin(angles))


def source_term(values, wind_speed, growth, damping):
    return values * jnp.exp(wind_speed[:, None] * growth[None, :] - damping[None, :])


def velocities(stacked, freq_count):
    cosine_table, sine_table = direction_tables(DIR)
    celerity = stacked[:freq_count][:, None]
    shape_out = (freq_count * DIR,) + stacked.shape[1:]
    speed_x = (
        celerity * cosine_table[None, :, None, None] + stacked[freq_count][None, None]
    ).reshape(shape_out)
    speed_y = (
        celerity * sine_table[None, :, None, None] + stacked[freq_count + 1][None, None]
    ).reshape(shape_out)
    return (speed_x, speed_y)


def deliver(bulk_rows, small_rows):
    return (
        lax.all_to_all(bulk_rows, GROUP, split_axis=0, concat_axis=0, tiled=True),
        lax.all_to_all(small_rows, GROUP, split_axis=0, concat_axis=0, tiled=True),
    )


def tile_plan(spectra, wind, growth, damping, row_cell, land_mask, group_speed, current, turning):
    tile_count = lax.axis_size(GROUP)
    comp_width = spectra.shape[1]
    tile_rows, tile_cols = land_mask.shape
    cell_count = tile_rows * tile_cols
    capacity = cell_count // tile_count
    target = row_cell // cell_count
    local_cell = (row_cell - target * cell_count).astype(jnp.float32)
    matches = (target[:, None] == jnp.arange(tile_count, dtype=jnp.int32)[None, :]).astype(
        jnp.int32
    )
    bucket_slot = jnp.sum((jnp.cumsum(matches, axis=0) - 1) * matches, axis=1)

    def bucket(values, filler):
        shape_out = (tile_count, capacity) + values.shape[1:]
        return jnp.full(shape_out, filler, jnp.float32).at[target, bucket_slot].set(values)

    bulk_rows = bucket(source_term(spectra, wind, growth, damping), 0.0)
    small_rows = bucket(local_cell[:, None], float(cell_count))
    bulk_back, small_back = deliver(bulk_rows, small_rows)
    cell_index = small_back[:, :, 0].reshape(-1).astype(jnp.int32)
    flat_values = bulk_back.reshape((tile_count * capacity,) + bulk_back.shape[2:])
    tile_field = (
        jnp.zeros((cell_count,) + bulk_back.shape[2:], jnp.float32)
        .at[cell_index]
        .set(flat_values, mode="drop")
    )
    spectrum = tile_field.T.reshape(comp_width, tile_rows, tile_cols)
    freq_count = comp_width // DIR
    reach = 2 * SUBSTEPS
    stacked = jnp.concatenate([group_speed, current, land_mask.astype(jnp.float32)[None]], axis=0)
    rimmed = with_halo(stacked, ((GROUP, 1),), 2 * SUBSTEPS)
    speed_x, speed_y = velocities(rimmed, freq_count)
    sea_rim = rimmed[freq_count + 2 :]

    def window(values, margin):
        return lax.slice_in_dim(values, reach - margin, reach + tile_rows + margin, axis=1)

    for repeat in range(SUBSTEPS):
        extended = with_halo(spectrum, ((GROUP, 1),), 2)
        spectrum = substep(extended, window(speed_x, 2), window(speed_y, 0), window(sea_rim, 0)[0])
    blocks = spectrum.reshape(freq_count, DIR, tile_rows, tile_cols)
    wrapped = jnp.concatenate([blocks[:, -2:], blocks, blocks[:, :2]], axis=1)
    turning_full = jnp.broadcast_to(turning[None, None], wrapped.shape)
    blocks = blocks - upwind_divergence(wrapped, turning_full, 1)
    spectrum = blocks.reshape(comp_width, tile_rows, tile_cols)
    shipped = lax.all_to_all(spectrum, GROUP, split_axis=0, concat_axis=1, tiled=True)
    return shipped[None]


def pack_kernel(
    parts,
    freqs,
    spectra_ref,
    wind_ref,
    growth_ref,
    damping_ref,
    cell_ref,
    speed_ref,
    current_ref,
    turning_ref,
    out_ref,
):
    rows, comps = spectra_ref.shape
    half = LANES // 2
    full = rows // LANES
    spare = jnp.zeros((1, half), jnp.float32)
    wind_row = jnp.concatenate([wind_ref[...][None], spare], axis=1)
    wind_cols = jnp.broadcast_to(wind_row, (LANES, rows + half)).T
    low = lax.broadcasted_iota(jnp.int32, (8, LANES), 1) < half
    per_freq = DIR // 8
    span_rows = full * DIR + 16
    tails = []
    for block in range(comps // LANES):
        lanes = pl.ds(block * LANES, LANES)
        growth = growth_ref[lanes][None]
        damping = damping_ref[lanes][None]

        def source(first, count):
            span = pl.ds(first, count)
            return spectra_ref[span, lanes] * jnp.exp(
                wind_cols[first : first + count] * growth - damping
            )

        for chunk in range(full):
            turned = source(chunk * LANES, LANES).T
            for g in range(LANES // 8):
                freq, within = divmod(block * (LANES // 8) + g, per_freq)
                part, f = divmod(freq, freqs)
                at = f * span_rows + chunk * DIR + within * 8
                out_ref[part, pl.ds(at, 8), :] = turned[g * 8 : g * 8 + 8]
        tail = source(full * LANES, half)
        turned = jnp.concatenate([tail, tail], axis=0).T
        tails += [turned[g * 8 : g * 8 + 8] for g in range(LANES // 8)]
    cell_row = jnp.concatenate([cell_ref[...].astype(jnp.float32)[None], spare], axis=1)
    shared = jnp.concatenate(
        [current_ref[0], current_ref[1], turning_ref[...]]
        + [cell_row[:, c * LANES : (c + 1) * LANES] for c in range(full + 1)],
        axis=0,
    )
    for part in range(parts):
        for f in range(freqs):
            freq = part * freqs + f
            one, two, three = tails[freq * per_freq : (freq + 1) * per_freq]
            at = f * span_rows + full * DIR
            out_ref[part, pl.ds(at, 8), :] = jnp.where(low, one, two)
            folded = jnp.where(low, three, pltpu.roll(three, 4, 0))
            out_ref[part, pl.ds(at + 8, 8), :] = jnp.concatenate([folded[:4], speed_ref[freq]], axis=0)
        out_ref[part, pl.ds(freqs * span_rows, shared.shape[0]), :] = shared


BLOCK = 8
SPAN = 4


def slab_kernel(
    parts,
    tile_rows,
    full,
    freqs,
    recv_ref,
    out_ref,
    onehot,
    masses,
    spread,
    first,
    second,
    table,
    faces_x,
    faces_y,
    moved_ref,
    done_ref,
    sems,
):
    slab_rows = parts * tile_rows
    half = LANES // 2
    span_rows = full * DIR + 16
    shared_base = freqs * span_rows
    highs = slab_rows // SPAN
    width = freqs * 2 * DIR
    half_rows = highs // 2 * width
    depth = onehot.shape[1]
    named_rows = spread.shape[0] - highs * width
    low_lane = lax.broadcasted_iota(jnp.int32, (1, LANES), 1) < half
    low_lanes = lax.broadcasted_iota(jnp.int32, (8, LANES), 1) < half
    top_rows = lax.broadcasted_iota(jnp.int32, (8, LANES), 0) < 4
    cell_iota = (
        lax.broadcasted_iota(jnp.int32, (2 * LANES, LANES), 0).astype(jnp.float32).astype(jnp.bfloat16)
    )
    high_iota = lax.broadcasted_iota(jnp.int32, (named_rows, LANES), 0)
    high_parts = []

    def cells_of(owner, chunk):
        return recv_ref[owner, pl.ds(shared_base + 3 * tile_rows + chunk, 1), :].astype(jnp.int32)

    def place(index, cells, values):
        span = pl.ds(index * LANES, LANES)
        high = cells // (SPAN * LANES)
        low = cells - high * (SPAN * LANES)
        for k in range(0, SPAN, 2):
            near = jnp.broadcast_to((low - k * LANES).astype(jnp.float32), (2 * LANES, LANES))
            hit = cell_iota == near.astype(jnp.bfloat16)
            onehot[pl.ds(k * LANES, 2 * LANES), span] = jnp.where(hit, 1.0, 0.0).astype(jnp.bfloat16)
        pieces = []
        for value in values:
            head = value.astype(jnp.bfloat16).astype(jnp.float32)
            pieces += [head, value - head]
        masses[:, span] = jnp.concatenate(pieces, axis=0).astype(jnp.bfloat16)
        spread[pl.ds(highs * width, named_rows), span] = (
            (high_iota == high).astype(jnp.float32).astype(jnp.bfloat16)
        )
        high_parts.append(high)

    per_pair = 2 * full + 1
    for pair in range(parts // 2):
        even, odd = 2 * pair, 2 * pair + 1
        for side, owner in enumerate((even, odd)):
            for chunk in range(full):
                values = [
                    recv_ref[owner, pl.ds(f * span_rows + chunk * DIR, DIR), :] for f in range(freqs)
                ]
                place(pair * per_pair + side * full + chunk, cells_of(owner, chunk), values)

        def merged(offset):
            own, other = recv_ref[even, pl.ds(offset, 8), :], recv_ref[odd, pl.ds(offset, 8), :]
            return (
                jnp.where(low_lanes, own, pltpu.roll(other, half, 1)),
                jnp.where(low_lanes, pltpu.roll(own, half, 1), other),
            )

        values = []
        for f in range(freqs):
            one, two = merged(f * span_rows + full * DIR)
            three, four = merged(f * span_rows + full * DIR + 8)
            values.append(
                jnp.concatenate([one, two, jnp.where(top_rows, three, pltpu.roll(four, 4, 0))], axis=0)
            )
        cells = jnp.where(low_lane, cells_of(even, full), pltpu.roll(cells_of(odd, full), half, 1))
        place(pair * per_pair + 2 * full, cells, values)

    def product(first_row, count):
        return lax.dot_general(
            spread[pl.ds(first_row, count), :],
            onehot[...],
            (((1,), (1,)), ((), ())),
            preferred_element_type=jnp.float32,
        )

    def build(h):
        for index, high in enumerate(high_parts):
            span = pl.ds(index * LANES, LANES)
            pick = jnp.broadcast_to((high == h).astype(jnp.float32), (width, LANES)).astype(jnp.bfloat16)
            spread[pl.ds(h * width, width), span] = masses[:, span] * pick

    nothing = jnp.zeros((DIR, LANES), jnp.float32)
    for f in range(freqs):
        for field in (first, second):
            for edge in (0, 1, slab_rows + 2, slab_rows + 3):
                field[f, edge] = nothing
    named = product(highs * width, named_rows)
    for part in range(2):
        some = range(part * highs // 2, (part + 1) * highs // 2)
        for h in some:
            build(h)
        scattered = product(part * half_rows, half_rows)
        for h in some:
            for f in range(freqs):
                at = (h - some[0]) * width + f * 2 * DIR
                total = scattered[at : at + DIR] + scattered[at + DIR : at + 2 * DIR]
                for k in range(SPAN):
                    first[f, SPAN * h + 2 + k] = total[:, k * LANES : (k + 1) * LANES]

    lane = lax.broadcasted_iota(jnp.int32, (slab_rows, LANES), 1)
    zero_rows = jnp.zeros((8, LANES), jnp.float32)

    def gather(offset):
        return jnp.concatenate(
            [recv_ref[owner, pl.ds(offset, tile_rows), :] for owner in range(parts)], axis=0
        )

    gain = 0.5 * courant / 8.0
    slots = iter(range(table.shape[0]))

    def keep(rows):
        slot = next(slots)
        table[slot, pl.ds(8, rows.shape[0]), :] = rows
        return slot

    def face_x(rows):
        slot = next(slots)
        table[slot, pl.ds(0, 8), :] = zero_rows
        table[slot, pl.ds(8 + slab_rows, 8), :] = zero_rows
        table[slot, pl.ds(8, slab_rows), :] = rows
        faces = gain * (table[slot, pl.ds(7, slab_rows + 8), :] + table[slot, pl.ds(8, slab_rows + 8), :])
        table[slot, pl.ds(7, slab_rows + 8), :] = faces
        return slot

    def face_y(rows):
        after = jnp.where(lane < LANES - 1, pltpu.roll(rows, LANES - 1, 1), 0.0)
        before = jnp.where(lane > 0, pltpu.roll(rows, 1, 1), 0.0)
        return keep(gain * (rows + after)), keep(gain * (rows + before))

    speeds = [gather(f * span_rows + full * DIR + 12) for f in range(freqs)]
    current_x, current_y, turning = (gather(shared_base + kind * tile_rows) for kind in range(3))
    current_x_face, speed_x_face = face_x(current_x), [face_x(s) for s in speeds]
    current_y_faces, speed_y_faces = face_y(current_y), [face_y(s) for s in speeds]
    land_slots = [keep(named[:highs, k * LANES : (k + 1) * LANES]) for k in range(SPAN)]
    ahead = jnp.maximum(turning, 0.0) * 0.125
    back = jnp.minimum(turning, 0.0) * 0.125
    bend_slots = [
        keep(rows)
        for rows in (
            -ahead,
            7.0 * ahead + 3.0 * back,
            1.0 - 3.0 * (ahead - back),
            -3.0 * ahead - 7.0 * back,
            back,
        )
    ]

    angles = lax.broadcasted_iota(jnp.int32, (DIR, LANES), 0).astype(jnp.float32) * (2.0 * math.pi / DIR)
    cosine = jnp.cos(angles)
    sine = jnp.sin(angles)
    lane_wide = lax.broadcasted_iota(jnp.int32, (DIR, LANES), 1)

    def row(slot, x):
        return table[slot, pl.ds(8 + x, 1), :]

    def flux(speed, behind, centre3, onward3, beyond):
        positive = speed > 0.0
        near = jnp.where(positive, centre3, onward3)
        far = jnp.where(positive, behind, beyond)
        return speed * ((centre3 + onward3) + (near - far))

    def advance(field, fresh, step, carry, finish):
        def speed_x(f, x):
            if fresh:
                faces_x[f, x + 1] = row(speed_x_face[f], x) * cosine + row(current_x_face, x)
            return faces_x[f, x + 1]

        def speed_y(f, side, x):
            if fresh:
                faces_y[f, side, x] = row(speed_y_faces[f][side], x) * sine + row(current_y_faces[side], x)
            return faces_y[f, side, x]

        carry = list(carry)
        for i in range(BLOCK):
            x = step * BLOCK + i
            sea = row(land_slots[i % SPAN], step * (BLOCK // SPAN) + i // SPAN)
            for f in range(freqs):
                entering, centre3 = carry[f]
                centre = field[f, x + 2]
                onward3 = 3.0 * field[f, x + 3]
                leaving = flux(speed_x(f, x), field[f, x + 1], centre3, onward3, field[f, x + 4])
                up1 = jnp.where(lane_wide < LANES - 1, pltpu.roll(centre, LANES - 1, 1), 0.0)
                up2 = jnp.where(lane_wide < LANES - 2, pltpu.roll(centre, LANES - 2, 1), 0.0)
                down1 = jnp.where(lane_wide > 0, pltpu.roll(centre, 1, 1), 0.0)
                down2 = jnp.where(lane_wide > 1, pltpu.roll(centre, 2, 1), 0.0)
                right = flux(speed_y(f, 0, x), down1, centre3, 3.0 * up1, up2)
                left = flux(speed_y(f, 1, x), down2, 3.0 * down1, centre3, up1)
                finish(f, x, (centre - (leaving - entering) - (right - left)) * sea)
                carry[f] = leaving, onward3
        return tuple(carry)

    def enter(field, fresh):
        carry = []
        for f in range(freqs):
            if fresh:
                faces_x[f, 0] = row(speed_x_face[f], -1) * cosine + row(current_x_face, -1)
            start3 = 3.0 * field[f, 2]
            carry.append((flux(faces_x[f, 0], nothing, nothing, start3, field[f, 3]), start3))
        return tuple(carry)

    def store(f, x, moved):
        second[f, x + 2] = moved

    def turn(f, x, moved):
        for g in range(DIR // 8):
            at = (f * DIR + g * 8) * slab_rows + x
            moved_ref[pl.ds(at, 8, stride=slab_rows), :] = moved[g * 8 : g * 8 + 8]

    def copy_out(step):
        part = pl.ds(pl.multiple_of(step * BLOCK, BLOCK), BLOCK)
        return pltpu.make_async_copy(done_ref.at[:, part, :], out_ref.at[:, part, :], sems.at[step])

    def final(step, carry):
        carry = advance(second, False, step, carry, turn)
        at = pl.multiple_of(step * BLOCK, BLOCK)
        weights = [table[slot, pl.ds(8 + at, BLOCK), :] for slot in bend_slots]
        for f in range(freqs):
            ring = [moved_ref[pl.ds((f * DIR + d) * slab_rows + at, BLOCK), :] for d in range(DIR)]
            for d in range(DIR):
                bent = weights[2] * ring[d]
                for k in (0, 1, 3, 4):
                    bent = bent + weights[k] * ring[(d + k - 2) % DIR]
                done_ref[f * DIR + d, pl.ds(at, BLOCK), :] = bent
        copy_out(step).start()
        return carry

    steps = slab_rows // BLOCK
    lax.fori_loop(0, steps, lambda step, carry: advance(first, True, step, carry, store), enter(first, True))
    lax.fori_loop(0, steps, final, enter(second, False))
    for step in range(steps):
        copy_out(step).wait()


def slab_plan(spectra, wind, growth, damping, row_cell, group_speed, current, turning):
    parts = lax.axis_size(GROUP)
    rows, comps = spectra.shape
    tile_rows = turning.shape[0]
    freqs = comps // parts // DIR
    full = rows // LANES
    slab_rows = parts * tile_rows
    depth = parts * rows
    highs = slab_rows // SPAN
    block_rows = -(-(freqs * (full * DIR + 16) + 3 * tile_rows + full + 1) // 8) * 8
    packed = pl.pallas_call(
        functools.partial(pack_kernel, parts, freqs),
        out_shape=pltpu.VMEM((parts, block_rows, LANES), jnp.float32),
        compiler_params=pltpu.CompilerParams(vmem_limit_bytes=56 * 1024 * 1024),
        name="pack",
    )(spectra, wind, growth, damping, row_cell, group_speed, current, turning)
    arrived = lax.all_to_all(packed, GROUP, split_axis=0, concat_axis=0, tiled=True)
    out = pl.pallas_call(
        functools.partial(slab_kernel, parts, tile_rows, full, freqs),
        out_shape=jax.ShapeDtypeStruct((freqs * DIR, slab_rows, LANES), jnp.float32),
        in_specs=[pl.BlockSpec(memory_space=pltpu.VMEM)],
        out_specs=pl.BlockSpec(memory_space=pl.ANY),
        scratch_shapes=[
            pltpu.VMEM((SPAN * LANES, depth), jnp.bfloat16),
            pltpu.VMEM((freqs * 2 * DIR, depth), jnp.bfloat16),
            pltpu.VMEM((highs * freqs * 2 * DIR + -(-highs // 16) * 16, depth), jnp.bfloat16),
            pltpu.VMEM((freqs, slab_rows + 4, DIR, LANES), jnp.float32),
            pltpu.VMEM((freqs, slab_rows + 4, DIR, LANES), jnp.float32),
            pltpu.VMEM((8 + SPAN + 3 * freqs, slab_rows + 16, LANES), jnp.float32),
            pltpu.VMEM((freqs, slab_rows + 1, DIR, LANES), jnp.float32),
            pltpu.VMEM((freqs, 2, slab_rows, DIR, LANES), jnp.float32),
            pltpu.VMEM((freqs * DIR * slab_rows, LANES), jnp.float32),
            pltpu.VMEM((freqs * DIR, slab_rows, LANES), jnp.float32),
            pltpu.SemaphoreType.DMA((slab_rows // BLOCK,)),
        ],
        compiler_params=pltpu.CompilerParams(vmem_limit_bytes=32 * 1024 * 1024),
        name="slab",
    )(arrived)
    return out.reshape(1, freqs * DIR, slab_rows, LANES)


def shards(*arrays):
    spectra, land_mask = arrays[0], arrays[5]
    parts = lax.axis_size(GROUP)
    rows, comps = spectra.shape
    whole_frequencies = comps == parts * 2 * DIR
    fits = rows % LANES == LANES // 2 and land_mask.shape == (4, LANES) and parts % 2 == 0
    if whole_frequencies and fits:
        return slab_plan(*arrays[:5], *arrays[6:])
    return tile_plan(*arrays)


def solution(mesh):
    placed = (
        P(("groups", "pts", "comp"), "sub"),
        P(("groups", "pts", "comp")),
        P("sub"),
        P("sub"),
        P(("groups", "pts", "comp")),
        P(("groups", "pts", "comp"), None),
        P(("groups", "sub"), ("pts", "comp"), None),
        P("groups", ("pts", "comp"), None),
        P(("groups", "pts", "comp"), None),
    )
    return jax.shard_map(
        shards,
        mesh=mesh,
        in_specs=placed,
        out_specs=P("sub", ("pts", "comp"), "groups", None),
        check_vma=False,
    )
```

```python
import functools
import math
import jax
import jax.numpy as jnp
from jax import lax
from jax.experimental import pallas as pl
from jax.experimental.pallas import tpu as pltpu
from jax.sharding import PartitionSpec as P

DIR = 24
SUBSTEPS = 2
LANES = 128
GROUP = ("pts", "comp")


courant = 0.35


def with_halo(cells, sides, width):
    for axis, dim in sides:
        count = lax.axis_size(axis)
        ends = count - 1
        head = lax.slice_in_dim(cells, 0, width, axis=dim)
        tail = lax.slice_in_dim(cells, cells.shape[dim] - width, cells.shape[dim], axis=dim)
        cells = jnp.concatenate(
            [
                lax.ppermute(tail, axis, [(i, (i + 1) % count) for i in range(ends)]),
                cells,
                lax.ppermute(head, axis, [((i + 1) % count, i) for i in range(ends)]),
            ],
            axis=dim,
        )
    return cells


def take_slice(values, first_index, extent, along_axis):
    return lax.slice_in_dim(values, first_index, first_index + extent, axis=along_axis)


def upwind_divergence(padded, motion, along_axis):
    length = padded.shape[along_axis] - 4
    face_count = length + 1
    behind = take_slice(padded, 0, face_count, along_axis)
    centre = take_slice(padded, 1, face_count, along_axis)
    onward = take_slice(padded, 2, face_count, along_axis)
    beyond = take_slice(padded, 3, face_count, along_axis)
    left_face = (6.0 * centre + 3.0 * onward - behind) * 0.125
    right_face = (3.0 * centre + 6.0 * onward - beyond) * 0.125
    face_speed = 0.5 * (
        take_slice(motion, 1, face_count, along_axis)
        + take_slice(motion, 2, face_count, along_axis)
    )
    fluxes = jnp.maximum(face_speed, 0.0) * left_face + jnp.minimum(face_speed, 0.0) * right_face
    return take_slice(fluxes, 1, length, along_axis) - take_slice(fluxes, 0, length, along_axis)


def substep(extended, speed_x, speed_y, sea_mask):
    across = upwind_divergence(extended, speed_x, 1)
    centre_part = extended[:, 2:-2]
    padding = ((0, 0), (0, 0), (2, 2))
    sideways = upwind_divergence(jnp.pad(centre_part, padding), jnp.pad(speed_y, padding), 2)
    return (centre_part - courant * (across + sideways)) * sea_mask


def direction_tables(directions):
    angles = jnp.arange(directions, dtype=jnp.float32) * (2.0 * jnp.pi / directions)
    return (jnp.cos(angles), jnp.sin(angles))


def source_term(values, wind_speed, growth, damping):
    return values * jnp.exp(wind_speed[:, None] * growth[None, :] - damping[None, :])


def velocities(stacked, freq_count):
    cosine_table, sine_table = direction_tables(DIR)
    celerity = stacked[:freq_count][:, None]
    shape_out = (freq_count * DIR,) + stacked.shape[1:]
    speed_x = (
        celerity * cosine_table[None, :, None, None] + stacked[freq_count][None, None]
    ).reshape(shape_out)
    speed_y = (
        celerity * sine_table[None, :, None, None] + stacked[freq_count + 1][None, None]
    ).reshape(shape_out)
    return (speed_x, speed_y)


def deliver(bulk_rows, small_rows):
    return (
        lax.all_to_all(bulk_rows, GROUP, split_axis=0, concat_axis=0, tiled=True),
        lax.all_to_all(small_rows, GROUP, split_axis=0, concat_axis=0, tiled=True),
    )


def tile_plan(spectra, wind, growth, damping, row_cell, land_mask, group_speed, current, turning):
    tile_count = lax.axis_size(GROUP)
    comp_width = spectra.shape[1]
    tile_rows, tile_cols = land_mask.shape
    cell_count = tile_rows * tile_cols
    capacity = cell_count // tile_count
    target = row_cell // cell_count
    local_cell = (row_cell - target * cell_count).astype(jnp.float32)
    matches = (target[:, None] == jnp.arange(tile_count, dtype=jnp.int32)[None, :]).astype(
        jnp.int32
    )
    bucket_slot = jnp.sum((jnp.cumsum(matches, axis=0) - 1) * matches, axis=1)

    def bucket(values, filler):
        shape_out = (tile_count, capacity) + values.shape[1:]
        return jnp.full(shape_out, filler, jnp.float32).at[target, bucket_slot].set(values)

    bulk_rows = bucket(source_term(spectra, wind, growth, damping), 0.0)
    small_rows = bucket(local_cell[:, None], float(cell_count))
    bulk_back, small_back = deliver(bulk_rows, small_rows)
    cell_index = small_back[:, :, 0].reshape(-1).astype(jnp.int32)
    flat_values = bulk_back.reshape((tile_count * capacity,) + bulk_back.shape[2:])
    tile_field = (
        jnp.zeros((cell_count,) + bulk_back.shape[2:], jnp.float32)
        .at[cell_index]
        .set(flat_values, mode="drop")
    )
    spectrum = tile_field.T.reshape(comp_width, tile_rows, tile_cols)
    freq_count = comp_width // DIR
    reach = 2 * SUBSTEPS
    stacked = jnp.concatenate([group_speed, current, land_mask.astype(jnp.float32)[None]], axis=0)
    rimmed = with_halo(stacked, ((GROUP, 1),), 2 * SUBSTEPS)
    speed_x, speed_y = velocities(rimmed, freq_count)
    sea_rim = rimmed[freq_count + 2 :]

    def window(values, margin):
        return lax.slice_in_dim(values, reach - margin, reach + tile_rows + margin, axis=1)

    for repeat in range(SUBSTEPS):
        extended = with_halo(spectrum, ((GROUP, 1),), 2)
        spectrum = substep(extended, window(speed_x, 2), window(speed_y, 0), window(sea_rim, 0)[0])
    blocks = spectrum.reshape(freq_count, DIR, tile_rows, tile_cols)
    wrapped = jnp.concatenate([blocks[:, -2:], blocks, blocks[:, :2]], axis=1)
    turning_full = jnp.broadcast_to(turning[None, None], wrapped.shape)
    blocks = blocks - upwind_divergence(wrapped, turning_full, 1)
    spectrum = blocks.reshape(comp_width, tile_rows, tile_cols)
    shipped = lax.all_to_all(spectrum, GROUP, split_axis=0, concat_axis=1, tiled=True)
    return shipped[None]


def pack_kernel(
    parts,
    freqs,
    spectra_ref,
    wind_ref,
    growth_ref,
    damping_ref,
    cell_ref,
    speed_ref,
    current_ref,
    turning_ref,
    out_ref,
):
    rows, comps = spectra_ref.shape
    half = LANES // 2
    full = rows // LANES
    spare = jnp.zeros((1, half), jnp.float32)
    wind_row = jnp.concatenate([wind_ref[...][None], spare], axis=1)
    wind_cols = jnp.broadcast_to(wind_row, (LANES, rows + half)).T
    low = lax.broadcasted_iota(jnp.int32, (8, LANES), 1) < half
    per_freq = DIR // 8
    span_rows = full * DIR + 16
    tails = []
    for block in range(comps // LANES):
        lanes = pl.ds(block * LANES, LANES)
        growth = growth_ref[lanes][None]
        damping = damping_ref[lanes][None]

        def source(first, count):
            span = pl.ds(first, count)
            return spectra_ref[span, lanes] * jnp.exp(
                wind_cols[first : first + count] * growth - damping
            )

        for chunk in range(full):
            turned = source(chunk * LANES, LANES).T
            for g in range(LANES // 8):
                freq, within = divmod(block * (LANES // 8) + g, per_freq)
                part, f = divmod(freq, freqs)
                at = f * span_rows + chunk * DIR + within * 8
                out_ref[part, pl.ds(at, 8), :] = turned[g * 8 : g * 8 + 8]
        tail = source(full * LANES, half)
        turned = jnp.concatenate([tail, tail], axis=0).T
        tails += [turned[g * 8 : g * 8 + 8] for g in range(LANES // 8)]
    cell_row = jnp.concatenate([cell_ref[...].astype(jnp.float32)[None], spare], axis=1)
    shared = jnp.concatenate(
        [current_ref[0], current_ref[1], turning_ref[...]]
        + [cell_row[:, c * LANES : (c + 1) * LANES] for c in range(full + 1)],
        axis=0,
    )
    for part in range(parts):
        for f in range(freqs):
            freq = part * freqs + f
            one, two, three = tails[freq * per_freq : (freq + 1) * per_freq]
            at = f * span_rows + full * DIR
            out_ref[part, pl.ds(at, 8), :] = jnp.where(low, one, two)
            folded = jnp.where(low, three, pltpu.roll(three, 4, 0))
            out_ref[part, pl.ds(at + 8, 8), :] = jnp.concatenate([folded[:4], speed_ref[freq]], axis=0)
        out_ref[part, pl.ds(freqs * span_rows, shared.shape[0]), :] = shared


BLOCK = 8
PER_STEP = 2


def slab_kernel(
    parts,
    tile_rows,
    full,
    freqs,
    recv_ref,
    out_ref,
    onehot,
    spread,
    first,
    second,
    table,
    faces_x,
    faces_y,
    moved_ref,
    done_ref,
    sems,
):
    slab_rows = parts * tile_rows
    half = LANES // 2
    span_rows = full * DIR + 16
    shared_base = freqs * span_rows
    highs = slab_rows // 2
    width = freqs * 2 * DIR
    low_lane = lax.broadcasted_iota(jnp.int32, (1, LANES), 1) < half
    low_lanes = lax.broadcasted_iota(jnp.int32, (8, LANES), 1) < half
    top_rows = lax.broadcasted_iota(jnp.int32, (8, LANES), 0) < 4
    cell_iota = lax.broadcasted_iota(jnp.int32, (2 * LANES, LANES), 0).astype(jnp.float32).astype(jnp.bfloat16)
    high_iota = lax.broadcasted_iota(jnp.int32, (highs, LANES), 0)

    def cells_of(owner, chunk):
        return recv_ref[owner, pl.ds(shared_base + 3 * tile_rows + chunk, 1), :].astype(jnp.int32)

    def place(index, cells, values):
        span = pl.ds(index * LANES, LANES)
        high = cells // (2 * LANES)
        low = (cells - high * (2 * LANES)).astype(jnp.float32)
        low = jnp.broadcast_to(low, (2 * LANES, LANES)).astype(jnp.bfloat16)
        onehot[:, span] = jnp.where(cell_iota == low, 1.0, 0.0).astype(jnp.bfloat16)
        pieces = []
        for value in values:
            head = value.astype(jnp.bfloat16).astype(jnp.float32)
            pieces += [head, value - head]
        both = jnp.concatenate(pieces, axis=0).astype(jnp.bfloat16)
        for h in range(highs):
            pick = jnp.broadcast_to((high == h).astype(jnp.float32), (width, LANES)).astype(jnp.bfloat16)
            spread[pl.ds(h * width, width), span] = both * pick
        spread[pl.ds(highs * width, highs), span] = (
            (high_iota == high).astype(jnp.float32).astype(jnp.bfloat16)
        )

    per_pair = 2 * full + 1
    for pair in range(parts // 2):
        even, odd = 2 * pair, 2 * pair + 1
        for side, owner in enumerate((even, odd)):
            for chunk in range(full):
                values = [
                    recv_ref[owner, pl.ds(f * span_rows + chunk * DIR, DIR), :] for f in range(freqs)
                ]
                place(pair * per_pair + side * full + chunk, cells_of(owner, chunk), values)

        def merged(offset):
            own, other = recv_ref[even, pl.ds(offset, 8), :], recv_ref[odd, pl.ds(offset, 8), :]
            return (
                jnp.where(low_lanes, own, pltpu.roll(other, half, 1)),
                jnp.where(low_lanes, pltpu.roll(own, half, 1), other),
            )

        values = []
        for f in range(freqs):
            one, two = merged(f * span_rows + full * DIR)
            three, four = merged(f * span_rows + full * DIR + 8)
            values.append(
                jnp.concatenate([one, two, jnp.where(top_rows, three, pltpu.roll(four, 4, 0))], axis=0)
            )
        cells = jnp.where(low_lane, cells_of(even, full), pltpu.roll(cells_of(odd, full), half, 1))
        place(pair * per_pair + 2 * full, cells, values)

    scattered = lax.dot_general(
        spread[...], onehot[...], (((1,), (1,)), ((), ())), preferred_element_type=jnp.float32
    )
    nothing = jnp.zeros((DIR, LANES), jnp.float32)
    for f in range(freqs):
        for field in (first, second):
            for edge in (0, 1, slab_rows + 2, slab_rows + 3):
                field[f, edge] = nothing
        for h in range(highs):
            at = h * width + f * 2 * DIR
            total = scattered[at : at + DIR] + scattered[at + DIR : at + 2 * DIR]
            first[f, 2 * h + 2] = total[:, :LANES]
            first[f, 2 * h + 3] = total[:, LANES:]

    lane = lax.broadcasted_iota(jnp.int32, (slab_rows, LANES), 1)
    zero_rows = jnp.zeros((8, LANES), jnp.float32)

    def gather(offset):
        return jnp.concatenate(
            [recv_ref[owner, pl.ds(offset, tile_rows), :] for owner in range(parts)], axis=0
        )

    gain = 0.5 * courant / 8.0
    slots = iter(range(table.shape[0]))

    def keep(rows):
        slot = next(slots)
        table[slot, pl.ds(8, rows.shape[0]), :] = rows
        return slot

    def face_x(rows):
        slot = next(slots)
        table[slot, pl.ds(0, 8), :] = zero_rows
        table[slot, pl.ds(8 + slab_rows, 8), :] = zero_rows
        table[slot, pl.ds(8, slab_rows), :] = rows
        faces = gain * (table[slot, pl.ds(7, slab_rows + 8), :] + table[slot, pl.ds(8, slab_rows + 8), :])
        table[slot, pl.ds(7, slab_rows + 8), :] = faces
        return slot

    def face_y(rows):
        after = jnp.where(lane < LANES - 1, pltpu.roll(rows, LANES - 1, 1), 0.0)
        before = jnp.where(lane > 0, pltpu.roll(rows, 1, 1), 0.0)
        return keep(gain * (rows + after)), keep(gain * (rows + before))

    speeds = [gather(f * span_rows + full * DIR + 12) for f in range(freqs)]
    current_x, current_y, turning = (gather(shared_base + kind * tile_rows) for kind in range(3))
    current_x_face, speed_x_face = face_x(current_x), [face_x(s) for s in speeds]
    current_y_faces, speed_y_faces = face_y(current_y), [face_y(s) for s in speeds]
    named = scattered[highs * width : highs * width + highs]
    land_slots = keep(named[:, :LANES]), keep(named[:, LANES:])
    ahead = jnp.maximum(turning, 0.0) * 0.125
    back = jnp.minimum(turning, 0.0) * 0.125
    bend_slots = [
        keep(rows)
        for rows in (
            -ahead,
            7.0 * ahead + 3.0 * back,
            1.0 - 3.0 * (ahead - back),
            -3.0 * ahead - 7.0 * back,
            back,
        )
    ]

    angles = lax.broadcasted_iota(jnp.int32, (DIR, LANES), 0).astype(jnp.float32) * (2.0 * math.pi / DIR)
    cosine = jnp.cos(angles)
    sine = jnp.sin(angles)
    lane_wide = lax.broadcasted_iota(jnp.int32, (DIR, LANES), 1)

    def row(slot, x):
        return table[slot, pl.ds(8 + x, 1), :]

    def flux(speed, behind, centre3, onward3, beyond):
        positive = speed > 0.0
        near = jnp.where(positive, centre3, onward3)
        far = jnp.where(positive, behind, beyond)
        return speed * ((centre3 + onward3) + (near - far))

    def advance(field, fresh, step, carry, finish):
        def speed_x(f, x):
            if fresh:
                faces_x[f, x + 1] = row(speed_x_face[f], x) * cosine + row(current_x_face, x)
            return faces_x[f, x + 1]

        def speed_y(f, side, x):
            if fresh:
                faces_y[f, side, x] = row(speed_y_faces[f][side], x) * sine + row(current_y_faces[side], x)
            return faces_y[f, side, x]

        carry = list(carry)
        for i in range(BLOCK):
            x = step * BLOCK + i
            sea = row(land_slots[i % 2], step * (BLOCK // 2) + i // 2)
            for f in range(freqs):
                entering, centre3 = carry[f]
                centre = field[f, x + 2]
                onward3 = 3.0 * field[f, x + 3]
                leaving = flux(speed_x(f, x), field[f, x + 1], centre3, onward3, field[f, x + 4])
                up1 = jnp.where(lane_wide < LANES - 1, pltpu.roll(centre, LANES - 1, 1), 0.0)
                up2 = jnp.where(lane_wide < LANES - 2, pltpu.roll(centre, LANES - 2, 1), 0.0)
                down1 = jnp.where(lane_wide > 0, pltpu.roll(centre, 1, 1), 0.0)
                down2 = jnp.where(lane_wide > 1, pltpu.roll(centre, 2, 1), 0.0)
                right = flux(speed_y(f, 0, x), down1, centre3, 3.0 * up1, up2)
                left = flux(speed_y(f, 1, x), down2, 3.0 * down1, centre3, up1)
                finish(f, x, (centre - (leaving - entering) - (right - left)) * sea)
                carry[f] = leaving, onward3
        return tuple(carry)

    def enter(field, fresh):
        carry = []
        for f in range(freqs):
            if fresh:
                faces_x[f, 0] = row(speed_x_face[f], -1) * cosine + row(current_x_face, -1)
            start3 = 3.0 * field[f, 2]
            carry.append((flux(faces_x[f, 0], nothing, nothing, start3, field[f, 3]), start3))
        return tuple(carry)

    def store(f, x, moved):
        second[f, x + 2] = moved

    def turn(f, x, moved):
        for g in range(DIR // 8):
            at = (f * DIR + g * 8) * slab_rows + x
            moved_ref[pl.ds(at, 8, stride=slab_rows), :] = moved[g * 8 : g * 8 + 8]

    def copy_out(step):
        part = pl.ds(pl.multiple_of(step * BLOCK, BLOCK), BLOCK)
        return pltpu.make_async_copy(done_ref.at[:, part, :], out_ref.at[:, part, :], sems.at[step])

    def final(block, carry):
        carry = advance(second, False, block, carry, turn)
        at = pl.multiple_of(block * BLOCK, BLOCK)
        weights = [table[slot, pl.ds(8 + at, BLOCK), :] for slot in bend_slots]
        for f in range(freqs):
            ring = [moved_ref[pl.ds((f * DIR + d) * slab_rows + at, BLOCK), :] for d in range(DIR)]
            for d in range(DIR):
                bent = weights[2] * ring[d]
                for k in (0, 1, 3, 4):
                    bent = bent + weights[k] * ring[(d + k - 2) % DIR]
                done_ref[f * DIR + d, pl.ds(at, BLOCK), :] = bent
        copy_out(block).start()
        return carry

    def sweep(one_block, carry):
        def body(step, carry):
            for i in range(PER_STEP):
                carry = one_block(step * PER_STEP + i, carry)
            return carry

        lax.fori_loop(0, slab_rows // BLOCK // PER_STEP, body, carry)

    sweep(lambda block, carry: advance(first, True, block, carry, store), enter(first, True))
    sweep(final, enter(second, False))
    for block in range(slab_rows // BLOCK):
        copy_out(block).wait()


def slab_plan(spectra, wind, growth, damping, row_cell, group_speed, current, turning):
    parts = lax.axis_size(GROUP)
    rows, comps = spectra.shape
    tile_rows = turning.shape[0]
    freqs = comps // parts // DIR
    full = rows // LANES
    slab_rows = parts * tile_rows
    depth = parts * rows
    highs = slab_rows // 2
    block_rows = -(-(freqs * (full * DIR + 16) + 3 * tile_rows + full + 1) // 8) * 8
    packed = pl.pallas_call(
        functools.partial(pack_kernel, parts, freqs),
        out_shape=pltpu.VMEM((parts, block_rows, LANES), jnp.float32),
        compiler_params=pltpu.CompilerParams(vmem_limit_bytes=56 * 1024 * 1024),
        name="pack",
    )(spectra, wind, growth, damping, row_cell, group_speed, current, turning)
    arrived = lax.all_to_all(packed, GROUP, split_axis=0, concat_axis=0, tiled=True)
    out = pl.pallas_call(
        functools.partial(slab_kernel, parts, tile_rows, full, freqs),
        out_shape=jax.ShapeDtypeStruct((freqs * DIR, slab_rows, LANES), jnp.float32),
        in_specs=[pl.BlockSpec(memory_space=pltpu.VMEM)],
        out_specs=pl.BlockSpec(memory_space=pl.ANY),
        scratch_shapes=[
            pltpu.VMEM((2 * LANES, depth), jnp.bfloat16),
            pltpu.VMEM((highs * (freqs * 2 * DIR + 1), depth), jnp.bfloat16),
            pltpu.VMEM((freqs, slab_rows + 4, DIR, LANES), jnp.float32),
            pltpu.VMEM((freqs, slab_rows + 4, DIR, LANES), jnp.float32),
            pltpu.VMEM((10 + 3 * freqs, slab_rows + 16, LANES), jnp.float32),
            pltpu.VMEM((freqs, slab_rows + 1, DIR, LANES), jnp.float32),
            pltpu.VMEM((freqs, 2, slab_rows, DIR, LANES), jnp.float32),
            pltpu.VMEM((freqs * DIR * slab_rows, LANES), jnp.float32),
            pltpu.VMEM((freqs * DIR, slab_rows, LANES), jnp.float32),
            pltpu.SemaphoreType.DMA((slab_rows // BLOCK,)),
        ],
        compiler_params=pltpu.CompilerParams(vmem_limit_bytes=32 * 1024 * 1024),
        name="slab",
    )(arrived)
    return out.reshape(1, freqs * DIR, slab_rows, LANES)


def shards(*arrays):
    spectra, land_mask = arrays[0], arrays[5]
    parts = lax.axis_size(GROUP)
    rows, comps = spectra.shape
    whole_frequencies = comps == parts * 2 * DIR
    fits = rows % LANES == LANES // 2 and land_mask.shape == (4, LANES) and parts % 2 == 0
    if whole_frequencies and fits:
        return slab_plan(*arrays[:5], *arrays[6:])
    return tile_plan(*arrays)


def solution(mesh):
    placed = (
        P(("groups", "pts", "comp"), "sub"),
        P(("groups", "pts", "comp")),
        P("sub"),
        P("sub"),
        P(("groups", "pts", "comp")),
        P(("groups", "pts", "comp"), None),
        P(("groups", "sub"), ("pts", "comp"), None),
        P("groups", ("pts", "comp"), None),
        P(("groups", "pts", "comp"), None),
    )
    return jax.shard_map(
        shards,
        mesh=mesh,
        in_specs=placed,
        out_specs=P("sub", ("pts", "comp"), "groups", None),
        check_vma=False,
    )
```

```python
import functools
import math
import jax
import jax.numpy as jnp
from jax import lax
from jax.experimental import pallas as pl
from jax.experimental.pallas import tpu as pltpu
from jax.sharding import PartitionSpec as P

DIR = 24
SUBSTEPS = 2
LANES = 128
GROUP = ("pts", "comp")


courant = 0.35


def with_halo(cells, sides, width):
    for axis, dim in sides:
        count = lax.axis_size(axis)
        ends = count - 1
        head = lax.slice_in_dim(cells, 0, width, axis=dim)
        tail = lax.slice_in_dim(cells, cells.shape[dim] - width, cells.shape[dim], axis=dim)
        cells = jnp.concatenate(
            [
                lax.ppermute(tail, axis, [(i, (i + 1) % count) for i in range(ends)]),
                cells,
                lax.ppermute(head, axis, [((i + 1) % count, i) for i in range(ends)]),
            ],
            axis=dim,
        )
    return cells


def take_slice(values, first_index, extent, along_axis):
    return lax.slice_in_dim(values, first_index, first_index + extent, axis=along_axis)


def upwind_divergence(padded, motion, along_axis):
    length = padded.shape[along_axis] - 4
    face_count = length + 1
    behind = take_slice(padded, 0, face_count, along_axis)
    centre = take_slice(padded, 1, face_count, along_axis)
    onward = take_slice(padded, 2, face_count, along_axis)
    beyond = take_slice(padded, 3, face_count, along_axis)
    left_face = (6.0 * centre + 3.0 * onward - behind) * 0.125
    right_face = (3.0 * centre + 6.0 * onward - beyond) * 0.125
    face_speed = 0.5 * (
        take_slice(motion, 1, face_count, along_axis)
        + take_slice(motion, 2, face_count, along_axis)
    )
    fluxes = jnp.maximum(face_speed, 0.0) * left_face + jnp.minimum(face_speed, 0.0) * right_face
    return take_slice(fluxes, 1, length, along_axis) - take_slice(fluxes, 0, length, along_axis)


def substep(extended, speed_x, speed_y, sea_mask):
    across = upwind_divergence(extended, speed_x, 1)
    centre_part = extended[:, 2:-2]
    padding = ((0, 0), (0, 0), (2, 2))
    sideways = upwind_divergence(jnp.pad(centre_part, padding), jnp.pad(speed_y, padding), 2)
    return (centre_part - courant * (across + sideways)) * sea_mask


def direction_tables(directions):
    angles = jnp.arange(directions, dtype=jnp.float32) * (2.0 * jnp.pi / directions)
    return (jnp.cos(angles), jnp.sin(angles))


def source_term(values, wind_speed, growth, damping):
    return values * jnp.exp(wind_speed[:, None] * growth[None, :] - damping[None, :])


def velocities(stacked, freq_count):
    cosine_table, sine_table = direction_tables(DIR)
    celerity = stacked[:freq_count][:, None]
    shape_out = (freq_count * DIR,) + stacked.shape[1:]
    speed_x = (
        celerity * cosine_table[None, :, None, None] + stacked[freq_count][None, None]
    ).reshape(shape_out)
    speed_y = (
        celerity * sine_table[None, :, None, None] + stacked[freq_count + 1][None, None]
    ).reshape(shape_out)
    return (speed_x, speed_y)


def deliver(bulk_rows, small_rows):
    return (
        lax.all_to_all(bulk_rows, GROUP, split_axis=0, concat_axis=0, tiled=True),
        lax.all_to_all(small_rows, GROUP, split_axis=0, concat_axis=0, tiled=True),
    )


def tile_plan(spectra, wind, growth, damping, row_cell, land_mask, group_speed, current, turning):
    tile_count = lax.axis_size(GROUP)
    comp_width = spectra.shape[1]
    tile_rows, tile_cols = land_mask.shape
    cell_count = tile_rows * tile_cols
    capacity = cell_count // tile_count
    target = row_cell // cell_count
    local_cell = (row_cell - target * cell_count).astype(jnp.float32)
    matches = (target[:, None] == jnp.arange(tile_count, dtype=jnp.int32)[None, :]).astype(
        jnp.int32
    )
    bucket_slot = jnp.sum((jnp.cumsum(matches, axis=0) - 1) * matches, axis=1)

    def bucket(values, filler):
        shape_out = (tile_count, capacity) + values.shape[1:]
        return jnp.full(shape_out, filler, jnp.float32).at[target, bucket_slot].set(values)

    bulk_rows = bucket(source_term(spectra, wind, growth, damping), 0.0)
    small_rows = bucket(local_cell[:, None], float(cell_count))
    bulk_back, small_back = deliver(bulk_rows, small_rows)
    cell_index = small_back[:, :, 0].reshape(-1).astype(jnp.int32)
    flat_values = bulk_back.reshape((tile_count * capacity,) + bulk_back.shape[2:])
    tile_field = (
        jnp.zeros((cell_count,) + bulk_back.shape[2:], jnp.float32)
        .at[cell_index]
        .set(flat_values, mode="drop")
    )
    spectrum = tile_field.T.reshape(comp_width, tile_rows, tile_cols)
    freq_count = comp_width // DIR
    reach = 2 * SUBSTEPS
    stacked = jnp.concatenate([group_speed, current, land_mask.astype(jnp.float32)[None]], axis=0)
    rimmed = with_halo(stacked, ((GROUP, 1),), 2 * SUBSTEPS)
    speed_x, speed_y = velocities(rimmed, freq_count)
    sea_rim = rimmed[freq_count + 2 :]

    def window(values, margin):
        return lax.slice_in_dim(values, reach - margin, reach + tile_rows + margin, axis=1)

    for repeat in range(SUBSTEPS):
        extended = with_halo(spectrum, ((GROUP, 1),), 2)
        spectrum = substep(extended, window(speed_x, 2), window(speed_y, 0), window(sea_rim, 0)[0])
    blocks = spectrum.reshape(freq_count, DIR, tile_rows, tile_cols)
    wrapped = jnp.concatenate([blocks[:, -2:], blocks, blocks[:, :2]], axis=1)
    turning_full = jnp.broadcast_to(turning[None, None], wrapped.shape)
    blocks = blocks - upwind_divergence(wrapped, turning_full, 1)
    spectrum = blocks.reshape(comp_width, tile_rows, tile_cols)
    shipped = lax.all_to_all(spectrum, GROUP, split_axis=0, concat_axis=1, tiled=True)
    return shipped[None]


def pack_kernel(
    parts,
    freqs,
    spectra_ref,
    wind_ref,
    growth_ref,
    damping_ref,
    cell_ref,
    land_ref,
    speed_ref,
    current_ref,
    turning_ref,
    rows_ref,
    small_ref,
):
    rows, comps = spectra_ref.shape
    half = LANES // 2
    full = rows // LANES
    width = freqs * DIR
    spare = jnp.zeros((1, half), jnp.float32)
    wind_row = jnp.concatenate([wind_ref[...][None], spare], axis=1)
    wind_cols = jnp.broadcast_to(wind_row, (LANES, rows + half)).T
    low = lax.broadcasted_iota(jnp.int32, (8, LANES), 1) < half
    tails = []
    for block in range(comps // LANES):
        lanes = pl.ds(block * LANES, LANES)
        growth = growth_ref[lanes][None]
        damping = damping_ref[lanes][None]

        def source(first, count):
            span = pl.ds(first, count)
            return spectra_ref[span, lanes] * jnp.exp(
                wind_cols[first : first + count] * growth - damping
            )

        for chunk in range(full):
            turned = source(chunk * LANES, LANES).T
            for g in range(LANES // 8):
                part, within = divmod(block * LANES + g * 8, width)
                rows_ref[part, pl.ds(chunk * width + within, 8), :] = turned[g * 8 : g * 8 + 8]
        tail = source(full * LANES, half)
        turned = jnp.concatenate([tail, tail], axis=0).T
        tails += [turned[g * 8 : g * 8 + 8] for g in range(LANES // 8)]
    for part in range(parts):
        for g in range(DIR // 8):
            one = tails[part * width // 8 + g]
            two = tails[(part * width + DIR) // 8 + g]
            rows_ref[part, pl.ds(full * width + g * 8, 8), :] = jnp.where(low, one, two)
    cell_row = jnp.concatenate([cell_ref[...].astype(jnp.float32)[None], spare], axis=1)
    small = jnp.concatenate(
        [speed_ref[f] for f in range(speed_ref.shape[0])]
        + [current_ref[0], current_ref[1], turning_ref[...], land_ref[...].astype(jnp.float32)]
        + [cell_row[:, c * LANES : (c + 1) * LANES] for c in range(full + 1)],
        axis=0,
    )
    spare_rows = jnp.zeros((small_ref.shape[0] - small.shape[0], LANES), jnp.float32)
    small_ref[...] = jnp.concatenate([small, spare_rows], axis=0)


def prepare_kernel(
    parts,
    tile_rows,
    full,
    freqs,
    me_ref,
    small_ref,
    onehot_ref,
    pick_ref,
    weight_ref,
    bend_ref,
    table,
):
    slab_rows = parts * tile_rows
    small_rows = small_ref.shape[0] // parts
    base = small_rows - 8 * -(-(4 * tile_rows + full + 1) // 8)
    half = LANES // 2
    highs = slab_rows // 2
    low_lane = lax.broadcasted_iota(jnp.int32, (1, LANES), 1) < half
    cell_iota = (
        lax.broadcasted_iota(jnp.int32, (2 * LANES, LANES), 0).astype(jnp.float32).astype(jnp.bfloat16)
    )

    def cells_of(owner, chunk):
        return small_ref[pl.ds(owner * small_rows + base + 4 * tile_rows + chunk, 1), :].astype(jnp.int32)

    def place(index, cells):
        span = pl.ds(index * LANES, LANES)
        high = cells // (2 * LANES)
        low = jnp.broadcast_to((cells - high * (2 * LANES)).astype(jnp.float32), (2 * LANES, LANES))
        hit = cell_iota == low.astype(jnp.bfloat16)
        onehot_ref[:, span] = jnp.where(hit, 1.0, 0.0).astype(jnp.bfloat16)
        for h in range(highs):
            pick = jnp.broadcast_to((high == h).astype(jnp.float32), (16, LANES))
            pick_ref[h, :, span] = pick.astype(jnp.bfloat16)

    per_pair = 2 * full + 1
    for pair in range(parts // 2):
        for side in range(2):
            for chunk in range(full):
                place(pair * per_pair + side * full + chunk, cells_of(2 * pair + side, chunk))
        even, odd = cells_of(2 * pair, full), cells_of(2 * pair + 1, full)
        place(pair * per_pair + 2 * full, jnp.where(low_lane, even, pltpu.roll(odd, half, 1)))

    lane = lax.broadcasted_iota(jnp.int32, (slab_rows, LANES), 1)
    zero_rows = jnp.zeros((8, LANES), jnp.float32)
    slots = iter(range(table.shape[0]))
    gain = 0.5 * courant / 8.0

    def keep(rows):
        slot = next(slots)
        table[slot, pl.ds(8, slab_rows), :] = rows
        return slot

    def face_x(rows):
        slot = next(slots)
        table[slot, pl.ds(0, 8), :] = zero_rows
        table[slot, pl.ds(8 + slab_rows, 8), :] = zero_rows
        table[slot, pl.ds(8, slab_rows), :] = rows
        faces = gain * (table[slot, pl.ds(7, slab_rows + 8), :] + table[slot, pl.ds(8, slab_rows + 8), :])
        table[slot, pl.ds(7, slab_rows + 8), :] = faces
        return slot

    def face_y(rows):
        after = jnp.where(lane < LANES - 1, pltpu.roll(rows, LANES - 1, 1), 0.0)
        before = jnp.where(lane > 0, pltpu.roll(rows, 1, 1), 0.0)
        return keep(gain * (rows + after)), keep(gain * (rows + before))

    def small(kind):
        return jnp.concatenate(
            [
                small_ref[pl.ds(owner * small_rows + base + kind * tile_rows, tile_rows), :]
                for owner in range(parts)
            ],
            axis=0,
        )

    mine = [
        small_ref[pl.ds(pl.multiple_of(owner * small_rows + me_ref[0] * 8, 8), 8), :] for owner in range(parts)
    ]
    speeds = [
        jnp.concatenate([m[f * tile_rows : (f + 1) * tile_rows] for m in mine], axis=0) for f in range(freqs)
    ]
    current_x, current_y, turning, land = (small(kind) for kind in range(4))
    current_x_face, speed_x_face = face_x(current_x), [face_x(s) for s in speeds]
    current_y_faces, speed_y_faces = face_y(current_y), [face_y(s) for s in speeds]
    land_slots = [
        keep(rows)
        for rows in (
            jnp.where(lane > 1, land, 0.0),
            jnp.where(lane > 0, land, 0.0),
            jnp.where(lane < LANES - 1, land, 0.0),
            jnp.where(lane < LANES - 2, land, 0.0),
            land,
        )
    ]
    ahead = jnp.maximum(turning, 0.0) * 0.125
    back = jnp.minimum(turning, 0.0) * 0.125
    bend_ref[0] = -ahead
    bend_ref[1] = 7.0 * ahead + 3.0 * back
    bend_ref[2] = 1.0 - 3.0 * (ahead - back)
    bend_ref[3] = -3.0 * ahead - 7.0 * back
    bend_ref[4] = back

    angles = lax.broadcasted_iota(jnp.int32, (DIR, LANES), 0).astype(jnp.float32) * (2.0 * math.pi / DIR)
    cosine = jnp.cos(angles)
    sine = jnp.sin(angles)

    def row(slot, x):
        return table[slot, pl.ds(8 + x, 1), :]

    def face(speed):
        plus, minus = jnp.maximum(speed, 0.0), jnp.minimum(speed, 0.0)
        return plus, minus, 6.0 * plus + 3.0 * minus, 3.0 * plus + 6.0 * minus

    def weights(right, left):
        plus, minus, centre, onward = right
        plus_l, minus_l, centre_l, onward_l = left
        return -plus_l, plus + centre_l, -onward - minus_l, minus, onward_l - centre

    def body(x, carry):
        seas = [row(slot, x) for slot in land_slots]
        leaving = []
        for f in range(freqs):
            right = face(row(speed_x_face[f], x) * cosine + row(current_x_face, x))
            along_x = weights(right, carry[f])
            along_y = weights(
                *(
                    face(row(speed_y_faces[f][side], x) * sine + row(current_y_faces[side], x))
                    for side in range(2)
                )
            )
            for k in range(4):
                weight_ref[k, f, x] = along_x[k] * seas[4]
                weight_ref[4 + k, f, x] = along_y[k] * seas[k]
            weight_ref[8, f, x] = (1.0 + along_x[4] + along_y[4]) * seas[4]
            leaving.append(right)
        return tuple(leaving)

    entering = tuple(
        face(row(speed_x_face[f], -1) * cosine + row(current_x_face, -1)) for f in range(freqs)
    )
    lax.fori_loop(0, slab_rows, body, entering)


BLOCK = 8
PER_STEP = 2


def slab_kernel(
    parts,
    tile_rows,
    full,
    freqs,
    recv_ref,
    onehot_ref,
    pick_ref,
    weight_ref,
    bend_ref,
    out_ref,
    spread,
    first,
    second,
    moved_ref,
    done_ref,
    sems,
):
    slab_rows = parts * tile_rows
    half = LANES // 2
    highs = slab_rows // 2
    width = freqs * DIR
    low_lanes = lax.broadcasted_iota(jnp.int32, (DIR, LANES), 1) < half

    def place(index, values):
        span = pl.ds(index * LANES, LANES)
        pieces = []
        for value in values:
            head = value.astype(jnp.bfloat16).astype(jnp.float32)
            pieces += [head, value - head]
        both = jnp.concatenate(pieces, axis=0).astype(jnp.bfloat16)
        for h in range(highs):
            pick = jnp.concatenate([pick_ref[h, :, span]] * (2 * width // 16), axis=0)
            spread[pl.ds(h * 2 * width, 2 * width), span] = both * pick

    per_pair = 2 * full + 1
    for pair in range(parts // 2):
        even, odd = 2 * pair, 2 * pair + 1
        for side, owner in enumerate((even, odd)):
            for chunk in range(full):
                values = [
                    recv_ref[owner, pl.ds(chunk * width + f * DIR, DIR), :] for f in range(freqs)
                ]
                place(pair * per_pair + side * full + chunk, values)
        own = recv_ref[even, pl.ds(full * width, DIR), :]
        other = recv_ref[odd, pl.ds(full * width, DIR), :]
        values = [
            jnp.where(low_lanes, own, pltpu.roll(other, half, 1)),
            jnp.where(low_lanes, pltpu.roll(own, half, 1), other),
        ]
        place(pair * per_pair + 2 * full, values)

    scattered = lax.dot_general(
        spread[...], onehot_ref[...], (((1,), (1,)), ((), ())), preferred_element_type=jnp.float32
    )
    nothing = jnp.zeros((DIR, LANES), jnp.float32)
    for f in range(freqs):
        for field in (first, second):
            for edge in (0, 1, slab_rows + 2, slab_rows + 3):
                field[f, edge] = nothing
        for h in range(highs):
            at = (h * freqs + f) * 2 * DIR
            total = scattered[at : at + DIR] + scattered[at + DIR : at + 2 * DIR]
            first[f, 2 * h + 2] = total[:, :LANES]
            first[f, 2 * h + 3] = total[:, LANES:]

    def advance(field, block, finish):
        for i in range(BLOCK):
            x = block * BLOCK + i
            for f in range(freqs):
                centre = field[f, x + 2]
                moved = weight_ref[8, f, x] * centre
                for k, there in enumerate((x, x + 1, x + 3, x + 4)):
                    moved = moved + weight_ref[k, f, x] * field[f, there]
                for k, shift in enumerate((2, 1, LANES - 1, LANES - 2)):
                    moved = moved + weight_ref[4 + k, f, x] * pltpu.roll(centre, shift, 1)
                finish(f, x, moved)

    def store(f, x, moved):
        second[f, x + 2] = moved

    def turn(f, x, moved):
        for g in range(DIR // 8):
            at = (f * DIR + g * 8) * slab_rows + x
            moved_ref[pl.ds(at, 8, stride=slab_rows), :] = moved[g * 8 : g * 8 + 8]

    def copy_out(block):
        part = pl.ds(pl.multiple_of(block * BLOCK, BLOCK), BLOCK)
        return pltpu.make_async_copy(done_ref.at[:, part, :], out_ref.at[:, part, :], sems.at[block])

    def final(block):
        advance(second, block, turn)
        at = pl.multiple_of(block * BLOCK, BLOCK)
        bends = [bend_ref[k, pl.ds(at, BLOCK), :] for k in range(5)]
        for f in range(freqs):
            ring = [moved_ref[pl.ds((f * DIR + d) * slab_rows + at, BLOCK), :] for d in range(DIR)]
            for d in range(DIR):
                bent = bends[2] * ring[d]
                for k in (0, 1, 3, 4):
                    bent = bent + bends[k] * ring[(d + k - 2) % DIR]
                done_ref[f * DIR + d, pl.ds(at, BLOCK), :] = bent
        copy_out(block).start()

    def sweep(one_block):
        def body(step, carry):
            for i in range(PER_STEP):
                one_block(step * PER_STEP + i)
            return carry

        lax.fori_loop(0, slab_rows // BLOCK // PER_STEP, body, 0)

    sweep(lambda block: advance(first, block, store))
    sweep(final)
    for block in range(slab_rows // BLOCK):
        copy_out(block).wait()


def slab_plan(spectra, wind, growth, damping, row_cell, land_mask, group_speed, current, turning):
    parts = lax.axis_size(GROUP)
    rows, comps = spectra.shape
    tile_rows = turning.shape[0]
    freqs = comps // parts // DIR
    width = freqs * DIR
    full = rows // LANES
    slab_rows = parts * tile_rows
    depth = parts * rows
    highs = slab_rows // 2
    small_rows = group_speed.shape[0] * tile_rows + 8 * -(-(4 * tile_rows + full + 1) // 8)
    megabyte = 1024 * 1024
    vmem = pl.BlockSpec(memory_space=pltpu.VMEM)
    packed, small = pl.pallas_call(
        functools.partial(pack_kernel, parts, freqs),
        out_shape=[
            pltpu.VMEM((parts, full * width + DIR, LANES), jnp.float32),
            jax.ShapeDtypeStruct((small_rows, LANES), jnp.float32),
        ],
        compiler_params=pltpu.CompilerParams(vmem_limit_bytes=56 * megabyte),
        name="pack",
    )(spectra, wind, growth, damping, row_cell, land_mask, group_speed, current, turning)
    gathered = lax.all_gather(small, GROUP, axis=0, tiled=True)
    arrived = lax.all_to_all(packed, GROUP, split_axis=0, concat_axis=0, tiled=True)
    me = lax.axis_index(GROUP).astype(jnp.int32)[None]
    prepared = pl.pallas_call(
        functools.partial(prepare_kernel, parts, tile_rows, full, freqs),
        out_shape=[
            pltpu.VMEM((2 * LANES, depth), jnp.bfloat16),
            pltpu.VMEM((highs, 16, depth), jnp.bfloat16),
            pltpu.VMEM((9, freqs, slab_rows, DIR, LANES), jnp.float32),
            pltpu.VMEM((5, slab_rows, LANES), jnp.float32),
        ],
        in_specs=[pl.BlockSpec(memory_space=pltpu.SMEM), vmem],
        scratch_shapes=[pltpu.VMEM((8 + 3 * freqs, slab_rows + 16, LANES), jnp.float32)],
        cost_estimate=pl.CostEstimate(flops=60 * 1000 * 1000, bytes_accessed=8 * megabyte, transcendentals=0),
        compiler_params=pltpu.CompilerParams(vmem_limit_bytes=16 * megabyte),
        name="prepare",
    )(me, gathered)
    out = pl.pallas_call(
        functools.partial(slab_kernel, parts, tile_rows, full, freqs),
        out_shape=jax.ShapeDtypeStruct((width, slab_rows, LANES), jnp.float32),
        in_specs=[vmem] * 5,
        out_specs=pl.BlockSpec(memory_space=pl.ANY),
        scratch_shapes=[
            pltpu.VMEM((highs * 2 * width, depth), jnp.bfloat16),
            pltpu.VMEM((freqs, slab_rows + 4, DIR, LANES), jnp.float32),
            pltpu.VMEM((freqs, slab_rows + 4, DIR, LANES), jnp.float32),
            pltpu.VMEM((width * slab_rows, LANES), jnp.float32),
            pltpu.VMEM((width, slab_rows, LANES), jnp.float32),
            pltpu.SemaphoreType.DMA((slab_rows // BLOCK,)),
        ],
        compiler_params=pltpu.CompilerParams(vmem_limit_bytes=32 * megabyte),
        name="slab",
    )(arrived, *prepared)
    return out.reshape(1, width, slab_rows, LANES)


def shards(*arrays):
    spectra, land_mask = arrays[0], arrays[5]
    parts = lax.axis_size(GROUP)
    rows, comps = spectra.shape
    whole_frequencies = comps == parts * 2 * DIR
    fits = rows % LANES == LANES // 2 and land_mask.shape == (4, LANES) and parts % 2 == 0
    if whole_frequencies and fits:
        return slab_plan(*arrays)
    return tile_plan(*arrays)


def solution(mesh):
    placed = (
        P(("groups", "pts", "comp"), "sub"),
        P(("groups", "pts", "comp")),
        P("sub"),
        P("sub"),
        P(("groups", "pts", "comp")),
        P(("groups", "pts", "comp"), None),
        P(("groups", "sub"), ("pts", "comp"), None),
        P("groups", ("pts", "comp"), None),
        P(("groups", "pts", "comp"), None),
    )
    return jax.shard_map(
        shards,
        mesh=mesh,
        in_specs=placed,
        out_specs=P("sub", ("pts", "comp"), "groups", None),
        check_vma=False,
    )
```

```python
import functools
import math
import jax
import jax.numpy as jnp
from jax import lax
from jax.experimental import pallas as pl
from jax.experimental.pallas import tpu as pltpu
from jax.sharding import PartitionSpec as P

DIR = 24
SUBSTEPS = 2
LANES = 128
GROUP = ("pts", "comp")


courant = 0.35


def with_halo(cells, sides, width):
    for axis, dim in sides:
        count = lax.axis_size(axis)
        ends = count - 1
        head = lax.slice_in_dim(cells, 0, width, axis=dim)
        tail = lax.slice_in_dim(cells, cells.shape[dim] - width, cells.shape[dim], axis=dim)
        cells = jnp.concatenate(
            [
                lax.ppermute(tail, axis, [(i, (i + 1) % count) for i in range(ends)]),
                cells,
                lax.ppermute(head, axis, [((i + 1) % count, i) for i in range(ends)]),
            ],
            axis=dim,
        )
    return cells


def take_slice(values, first_index, extent, along_axis):
    return lax.slice_in_dim(values, first_index, first_index + extent, axis=along_axis)


def upwind_divergence(padded, motion, along_axis):
    length = padded.shape[along_axis] - 4
    face_count = length + 1
    behind = take_slice(padded, 0, face_count, along_axis)
    centre = take_slice(padded, 1, face_count, along_axis)
    onward = take_slice(padded, 2, face_count, along_axis)
    beyond = take_slice(padded, 3, face_count, along_axis)
    left_face = (6.0 * centre + 3.0 * onward - behind) * 0.125
    right_face = (3.0 * centre + 6.0 * onward - beyond) * 0.125
    face_speed = 0.5 * (
        take_slice(motion, 1, face_count, along_axis)
        + take_slice(motion, 2, face_count, along_axis)
    )
    fluxes = jnp.maximum(face_speed, 0.0) * left_face + jnp.minimum(face_speed, 0.0) * right_face
    return take_slice(fluxes, 1, length, along_axis) - take_slice(fluxes, 0, length, along_axis)


def substep(extended, speed_x, speed_y, sea_mask):
    across = upwind_divergence(extended, speed_x, 1)
    centre_part = extended[:, 2:-2]
    padding = ((0, 0), (0, 0), (2, 2))
    sideways = upwind_divergence(jnp.pad(centre_part, padding), jnp.pad(speed_y, padding), 2)
    return (centre_part - courant * (across + sideways)) * sea_mask


def direction_tables(directions):
    angles = jnp.arange(directions, dtype=jnp.float32) * (2.0 * jnp.pi / directions)
    return (jnp.cos(angles), jnp.sin(angles))


def source_term(values, wind_speed, growth, damping):
    return values * jnp.exp(wind_speed[:, None] * growth[None, :] - damping[None, :])


def velocities(stacked, freq_count):
    cosine_table, sine_table = direction_tables(DIR)
    celerity = stacked[:freq_count][:, None]
    shape_out = (freq_count * DIR,) + stacked.shape[1:]
    speed_x = (
        celerity * cosine_table[None, :, None, None] + stacked[freq_count][None, None]
    ).reshape(shape_out)
    speed_y = (
        celerity * sine_table[None, :, None, None] + stacked[freq_count + 1][None, None]
    ).reshape(shape_out)
    return (speed_x, speed_y)


def deliver(bulk_rows, small_rows):
    return (
        lax.all_to_all(bulk_rows, GROUP, split_axis=0, concat_axis=0, tiled=True),
        lax.all_to_all(small_rows, GROUP, split_axis=0, concat_axis=0, tiled=True),
    )


def tile_plan(spectra, wind, growth, damping, row_cell, land_mask, group_speed, current, turning):
    tile_count = lax.axis_size(GROUP)
    comp_width = spectra.shape[1]
    tile_rows, tile_cols = land_mask.shape
    cell_count = tile_rows * tile_cols
    capacity = cell_count // tile_count
    target = row_cell // cell_count
    local_cell = (row_cell - target * cell_count).astype(jnp.float32)
    matches = (target[:, None] == jnp.arange(tile_count, dtype=jnp.int32)[None, :]).astype(
        jnp.int32
    )
    bucket_slot = jnp.sum((jnp.cumsum(matches, axis=0) - 1) * matches, axis=1)

    def bucket(values, filler):
        shape_out = (tile_count, capacity) + values.shape[1:]
        return jnp.full(shape_out, filler, jnp.float32).at[target, bucket_slot].set(values)

    bulk_rows = bucket(source_term(spectra, wind, growth, damping), 0.0)
    small_rows = bucket(local_cell[:, None], float(cell_count))
    bulk_back, small_back = deliver(bulk_rows, small_rows)
    cell_index = small_back[:, :, 0].reshape(-1).astype(jnp.int32)
    flat_values = bulk_back.reshape((tile_count * capacity,) + bulk_back.shape[2:])
    tile_field = (
        jnp.zeros((cell_count,) + bulk_back.shape[2:], jnp.float32)
        .at[cell_index]
        .set(flat_values, mode="drop")
    )
    spectrum = tile_field.T.reshape(comp_width, tile_rows, tile_cols)
    freq_count = comp_width // DIR
    reach = 2 * SUBSTEPS
    stacked = jnp.concatenate([group_speed, current, land_mask.astype(jnp.float32)[None]], axis=0)
    rimmed = with_halo(stacked, ((GROUP, 1),), 2 * SUBSTEPS)
    speed_x, speed_y = velocities(rimmed, freq_count)
    sea_rim = rimmed[freq_count + 2 :]

    def window(values, margin):
        return lax.slice_in_dim(values, reach - margin, reach + tile_rows + margin, axis=1)

    for repeat in range(SUBSTEPS):
        extended = with_halo(spectrum, ((GROUP, 1),), 2)
        spectrum = substep(extended, window(speed_x, 2), window(speed_y, 0), window(sea_rim, 0)[0])
    blocks = spectrum.reshape(freq_count, DIR, tile_rows, tile_cols)
    wrapped = jnp.concatenate([blocks[:, -2:], blocks, blocks[:, :2]], axis=1)
    turning_full = jnp.broadcast_to(turning[None, None], wrapped.shape)
    blocks = blocks - upwind_divergence(wrapped, turning_full, 1)
    spectrum = blocks.reshape(comp_width, tile_rows, tile_cols)
    shipped = lax.all_to_all(spectrum, GROUP, split_axis=0, concat_axis=1, tiled=True)
    return shipped[None]


def pack_kernel(
    parts,
    freqs,
    spectra_ref,
    wind_ref,
    growth_ref,
    damping_ref,
    cell_ref,
    speed_ref,
    current_ref,
    turning_ref,
    out_ref,
):
    rows, comps = spectra_ref.shape
    half = LANES // 2
    full = rows // LANES
    spare = jnp.zeros((1, half), jnp.float32)
    wind_row = jnp.concatenate([wind_ref[...][None], spare], axis=1)
    wind_cols = jnp.broadcast_to(wind_row, (LANES, rows + half)).T
    low = lax.broadcasted_iota(jnp.int32, (8, LANES), 1) < half
    per_freq = DIR // 8
    span_rows = full * DIR + 16
    tails = []
    for block in range(comps // LANES):
        lanes = pl.ds(block * LANES, LANES)
        growth = growth_ref[lanes][None]
        damping = damping_ref[lanes][None]

        def source(first, count):
            span = pl.ds(first, count)
            return spectra_ref[span, lanes] * jnp.exp(
                wind_cols[first : first + count] * growth - damping
            )

        for chunk in range(full):
            turned = source(chunk * LANES, LANES).T
            for g in range(LANES // 8):
                freq, within = divmod(block * (LANES // 8) + g, per_freq)
                part, f = divmod(freq, freqs)
                at = f * span_rows + chunk * DIR + within * 8
                out_ref[part, pl.ds(at, 8), :] = turned[g * 8 : g * 8 + 8]
        tail = source(full * LANES, half)
        turned = jnp.concatenate([tail, tail], axis=0).T
        tails += [turned[g * 8 : g * 8 + 8] for g in range(LANES // 8)]
    cell_row = jnp.concatenate([cell_ref[...].astype(jnp.float32)[None], spare], axis=1)
    shared = jnp.concatenate(
        [current_ref[0], current_ref[1], turning_ref[...]]
        + [cell_row[:, c * LANES : (c + 1) * LANES] for c in range(full + 1)],
        axis=0,
    )
    for part in range(parts):
        for f in range(freqs):
            freq = part * freqs + f
            one, two, three = tails[freq * per_freq : (freq + 1) * per_freq]
            at = f * span_rows + full * DIR
            out_ref[part, pl.ds(at, 8), :] = jnp.where(low, one, two)
            folded = jnp.where(low, three, pltpu.roll(three, 4, 0))
            out_ref[part, pl.ds(at + 8, 8), :] = jnp.concatenate([folded[:4], speed_ref[freq]], axis=0)
        out_ref[part, pl.ds(freqs * span_rows, shared.shape[0]), :] = shared


BLOCK = 8
PER_STEP = 2


def slab_kernel(
    parts,
    tile_rows,
    full,
    freqs,
    recv_ref,
    out_ref,
    onehot,
    first,
    second,
    table,
    faces_x,
    faces_y,
    moved_ref,
    done_ref,
    sems,
):
    slab_rows = parts * tile_rows
    half = LANES // 2
    span_rows = full * DIR + 16
    shared_base = freqs * span_rows
    highs = slab_rows // 2
    width = freqs * 2 * DIR
    low_lane = lax.broadcasted_iota(jnp.int32, (1, LANES), 1) < half
    low_lanes = lax.broadcasted_iota(jnp.int32, (8, LANES), 1) < half
    top_rows = lax.broadcasted_iota(jnp.int32, (8, LANES), 0) < 4
    cell_iota = lax.broadcasted_iota(jnp.int32, (2 * LANES, LANES), 0).astype(jnp.float32).astype(jnp.bfloat16)
    high_iota = lax.broadcasted_iota(jnp.int32, (highs, LANES), 0)

    def cells_of(owner, chunk):
        return recv_ref[owner, pl.ds(shared_base + 3 * tile_rows + chunk, 1), :].astype(jnp.int32)

    columns = []

    def place(index, cells, values):
        span = pl.ds(index * LANES, LANES)
        high = cells // (2 * LANES)
        low = (cells - high * (2 * LANES)).astype(jnp.float32)
        low = jnp.broadcast_to(low, (2 * LANES, LANES)).astype(jnp.bfloat16)
        onehot[:, span] = jnp.where(cell_iota == low, 1.0, 0.0).astype(jnp.bfloat16)
        pieces = []
        for value in values:
            head = value.astype(jnp.bfloat16).astype(jnp.float32)
            pieces += [head, value - head]
        both = jnp.concatenate(pieces, axis=0).astype(jnp.bfloat16)
        column = []
        for h in range(highs):
            pick = jnp.broadcast_to((high == h).astype(jnp.float32), (width, LANES)).astype(jnp.bfloat16)
            column.append(both * pick)
        column.append((high_iota == high).astype(jnp.float32).astype(jnp.bfloat16))
        columns.append(jnp.concatenate(column, axis=0))

    per_pair = 2 * full + 1
    for pair in range(parts // 2):
        even, odd = 2 * pair, 2 * pair + 1
        for side, owner in enumerate((even, odd)):
            for chunk in range(full):
                values = [
                    recv_ref[owner, pl.ds(f * span_rows + chunk * DIR, DIR), :] for f in range(freqs)
                ]
                place(pair * per_pair + side * full + chunk, cells_of(owner, chunk), values)

        def merged(offset):
            own, other = recv_ref[even, pl.ds(offset, 8), :], recv_ref[odd, pl.ds(offset, 8), :]
            return (
                jnp.where(low_lanes, own, pltpu.roll(other, half, 1)),
                jnp.where(low_lanes, pltpu.roll(own, half, 1), other),
            )

        values = []
        for f in range(freqs):
            one, two = merged(f * span_rows + full * DIR)
            three, four = merged(f * span_rows + full * DIR + 8)
            values.append(
                jnp.concatenate([one, two, jnp.where(top_rows, three, pltpu.roll(four, 4, 0))], axis=0)
            )
        cells = jnp.where(low_lane, cells_of(even, full), pltpu.roll(cells_of(odd, full), half, 1))
        place(pair * per_pair + 2 * full, cells, values)

    scattered = lax.dot_general(
        jnp.concatenate(columns, axis=1),
        onehot[...],
        (((1,), (1,)), ((), ())),
        preferred_element_type=jnp.float32,
    )
    nothing = jnp.zeros((DIR, LANES), jnp.float32)
    for f in range(freqs):
        for field in (first, second):
            for edge in (0, 1, slab_rows + 2, slab_rows + 3):
                field[f, edge] = nothing
        for h in range(highs):
            at = h * width + f * 2 * DIR
            total = scattered[at : at + DIR] + scattered[at + DIR : at + 2 * DIR]
            first[f, 2 * h + 2] = total[:, :LANES]
            first[f, 2 * h + 3] = total[:, LANES:]

    lane = lax.broadcasted_iota(jnp.int32, (slab_rows, LANES), 1)
    zero_rows = jnp.zeros((8, LANES), jnp.float32)

    def gather(offset):
        return jnp.concatenate(
            [recv_ref[owner, pl.ds(offset, tile_rows), :] for owner in range(parts)], axis=0
        )

    gain = 0.5 * courant / 8.0
    slots = iter(range(table.shape[0]))

    def keep(rows):
        slot = next(slots)
        table[slot, pl.ds(8, rows.shape[0]), :] = rows
        return slot

    def face_x(rows):
        slot = next(slots)
        table[slot, pl.ds(0, 8), :] = zero_rows
        table[slot, pl.ds(8 + slab_rows, 8), :] = zero_rows
        table[slot, pl.ds(8, slab_rows), :] = rows
        faces = gain * (table[slot, pl.ds(7, slab_rows + 8), :] + table[slot, pl.ds(8, slab_rows + 8), :])
        table[slot, pl.ds(7, slab_rows + 8), :] = faces
        return slot

    def face_y(rows):
        after = jnp.where(lane < LANES - 1, pltpu.roll(rows, LANES - 1, 1), 0.0)
        before = jnp.where(lane > 0, pltpu.roll(rows, 1, 1), 0.0)
        return keep(gain * (rows + after)), keep(gain * (rows + before))

    speeds = [gather(f * span_rows + full * DIR + 12) for f in range(freqs)]
    current_x, current_y, turning = (gather(shared_base + kind * tile_rows) for kind in range(3))
    current_x_face, speed_x_face = face_x(current_x), [face_x(s) for s in speeds]
    current_y_faces, speed_y_faces = face_y(current_y), [face_y(s) for s in speeds]
    named = scattered[highs * width : highs * width + highs]
    land_slots = keep(named[:, :LANES]), keep(named[:, LANES:])
    ahead = jnp.maximum(turning, 0.0) * 0.125
    back = jnp.minimum(turning, 0.0) * 0.125
    bend_slots = [
        keep(rows)
        for rows in (
            -ahead,
            7.0 * ahead + 3.0 * back,
            1.0 - 3.0 * (ahead - back),
            -3.0 * ahead - 7.0 * back,
            back,
        )
    ]

    angles = lax.broadcasted_iota(jnp.int32, (DIR, LANES), 0).astype(jnp.float32) * (2.0 * math.pi / DIR)
    cosine = jnp.cos(angles)
    sine = jnp.sin(angles)
    lane_wide = lax.broadcasted_iota(jnp.int32, (DIR, LANES), 1)

    def row(slot, x):
        return table[slot, pl.ds(8 + x, 1), :]

    def flux(speed, behind, centre3, onward3, beyond):
        positive = speed > 0.0
        near = jnp.where(positive, centre3, onward3)
        far = jnp.where(positive, behind, beyond)
        return speed * ((centre3 + onward3) + (near - far))

    def advance(field, fresh, step, carry, finish):
        def speed_x(f, x):
            if fresh:
                faces_x[f, x + 1] = row(speed_x_face[f], x) * cosine + row(current_x_face, x)
            return faces_x[f, x + 1]

        def speed_y(f, side, x):
            if fresh:
                faces_y[f, side, x] = row(speed_y_faces[f][side], x) * sine + row(current_y_faces[side], x)
            return faces_y[f, side, x]

        carry = list(carry)
        for i in range(BLOCK):
            x = step * BLOCK + i
            sea = row(land_slots[i % 2], step * (BLOCK // 2) + i // 2)
            for f in range(freqs):
                entering, centre3 = carry[f]
                centre = field[f, x + 2]
                onward3 = 3.0 * field[f, x + 3]
                leaving = flux(speed_x(f, x), field[f, x + 1], centre3, onward3, field[f, x + 4])
                up1 = jnp.where(lane_wide < LANES - 1, pltpu.roll(centre, LANES - 1, 1), 0.0)
                up2 = jnp.where(lane_wide < LANES - 2, pltpu.roll(centre, LANES - 2, 1), 0.0)
                down1 = jnp.where(lane_wide > 0, pltpu.roll(centre, 1, 1), 0.0)
                down2 = jnp.where(lane_wide > 1, pltpu.roll(centre, 2, 1), 0.0)
                right = flux(speed_y(f, 0, x), down1, centre3, 3.0 * up1, up2)
                left = flux(speed_y(f, 1, x), down2, 3.0 * down1, centre3, up1)
                finish(f, x, (centre - (leaving - entering) - (right - left)) * sea)
                carry[f] = leaving, onward3
        return tuple(carry)

    def enter(field, fresh):
        carry = []
        for f in range(freqs):
            if fresh:
                faces_x[f, 0] = row(speed_x_face[f], -1) * cosine + row(current_x_face, -1)
            start3 = 3.0 * field[f, 2]
            carry.append((flux(faces_x[f, 0], nothing, nothing, start3, field[f, 3]), start3))
        return tuple(carry)

    def store(f, x, moved):
        second[f, x + 2] = moved

    def turn(f, x, moved):
        for g in range(DIR // 8):
            at = (f * DIR + g * 8) * slab_rows + x
            moved_ref[pl.ds(at, 8, stride=slab_rows), :] = moved[g * 8 : g * 8 + 8]

    def copy_out(step):
        part = pl.ds(pl.multiple_of(step * BLOCK, BLOCK), BLOCK)
        return pltpu.make_async_copy(done_ref.at[:, part, :], out_ref.at[:, part, :], sems.at[step])

    def final(block, carry):
        carry = advance(second, False, block, carry, turn)
        at = pl.multiple_of(block * BLOCK, BLOCK)
        weights = [table[slot, pl.ds(8 + at, BLOCK), :] for slot in bend_slots]
        for f in range(freqs):
            ring = [moved_ref[pl.ds((f * DIR + d) * slab_rows + at, BLOCK), :] for d in range(DIR)]
            for d in range(DIR):
                bent = weights[2] * ring[d]
                for k in (0, 1, 3, 4):
                    bent = bent + weights[k] * ring[(d + k - 2) % DIR]
                done_ref[f * DIR + d, pl.ds(at, BLOCK), :] = bent
        copy_out(block).start()
        return carry

    def sweep(one_block, carry):
        def body(step, carry):
            for i in range(PER_STEP):
                carry = one_block(step * PER_STEP + i, carry)
            return carry

        lax.fori_loop(0, slab_rows // BLOCK // PER_STEP, body, carry)

    sweep(lambda block, carry: advance(first, True, block, carry, store), enter(first, True))
    sweep(final, enter(second, False))
    for block in range(slab_rows // BLOCK):
        copy_out(block).wait()


def slab_plan(spectra, wind, growth, damping, row_cell, group_speed, current, turning):
    parts = lax.axis_size(GROUP)
    rows, comps = spectra.shape
    tile_rows = turning.shape[0]
    freqs = comps // parts // DIR
    full = rows // LANES
    slab_rows = parts * tile_rows
    depth = parts * rows
    highs = slab_rows // 2
    block_rows = -(-(freqs * (full * DIR + 16) + 3 * tile_rows + full + 1) // 8) * 8
    packed = pl.pallas_call(
        functools.partial(pack_kernel, parts, freqs),
        out_shape=pltpu.VMEM((parts, block_rows, LANES), jnp.float32),
        compiler_params=pltpu.CompilerParams(vmem_limit_bytes=56 * 1024 * 1024),
        name="pack",
    )(spectra, wind, growth, damping, row_cell, group_speed, current, turning)
    arrived = lax.all_to_all(packed, GROUP, split_axis=0, concat_axis=0, tiled=True)
    out = pl.pallas_call(
        functools.partial(slab_kernel, parts, tile_rows, full, freqs),
        out_shape=jax.ShapeDtypeStruct((freqs * DIR, slab_rows, LANES), jnp.float32),
        in_specs=[pl.BlockSpec(memory_space=pltpu.VMEM)],
        out_specs=pl.BlockSpec(memory_space=pl.ANY),
        scratch_shapes=[
            pltpu.VMEM((2 * LANES, depth), jnp.bfloat16),
            pltpu.VMEM((freqs, slab_rows + 4, DIR, LANES), jnp.float32),
            pltpu.VMEM((freqs, slab_rows + 4, DIR, LANES), jnp.float32),
            pltpu.VMEM((10 + 3 * freqs, slab_rows + 16, LANES), jnp.float32),
            pltpu.VMEM((freqs, slab_rows + 1, DIR, LANES), jnp.float32),
            pltpu.VMEM((freqs, 2, slab_rows, DIR, LANES), jnp.float32),
            pltpu.VMEM((freqs * DIR * slab_rows, LANES), jnp.float32),
            pltpu.VMEM((freqs * DIR, slab_rows, LANES), jnp.float32),
            pltpu.SemaphoreType.DMA((slab_rows // BLOCK,)),
        ],
        compiler_params=pltpu.CompilerParams(vmem_limit_bytes=32 * 1024 * 1024),
        name="slab",
    )(arrived)
    return out.reshape(1, freqs * DIR, slab_rows, LANES)


def shards(*arrays):
    spectra, land_mask = arrays[0], arrays[5]
    parts = lax.axis_size(GROUP)
    rows, comps = spectra.shape
    whole_frequencies = comps == parts * 2 * DIR
    fits = rows % LANES == LANES // 2 and land_mask.shape == (4, LANES) and parts % 2 == 0
    if whole_frequencies and fits:
        return slab_plan(*arrays[:5], *arrays[6:])
    return tile_plan(*arrays)


def solution(mesh):
    placed = (
        P(("groups", "pts", "comp"), "sub"),
        P(("groups", "pts", "comp")),
        P("sub"),
        P("sub"),
        P(("groups", "pts", "comp")),
        P(("groups", "pts", "comp"), None),
        P(("groups", "sub"), ("pts", "comp"), None),
        P("groups", ("pts", "comp"), None),
        P(("groups", "pts", "comp"), None),
    )
    return jax.shard_map(
        shards,
        mesh=mesh,
        in_specs=placed,
        out_specs=P("sub", ("pts", "comp"), "groups", None),
        check_vma=False,
    )
```

```python
import functools
import math
import jax
import jax.numpy as jnp
from jax import lax
from jax.experimental import pallas as pl
from jax.experimental.pallas import tpu as pltpu
from jax.sharding import PartitionSpec as P

DIR = 24
SUBSTEPS = 2
LANES = 128
GROUP = ("pts", "comp")


courant = 0.35


def with_halo(cells, sides, width):
    for axis, dim in sides:
        count = lax.axis_size(axis)
        ends = count - 1
        head = lax.slice_in_dim(cells, 0, width, axis=dim)
        tail = lax.slice_in_dim(cells, cells.shape[dim] - width, cells.shape[dim], axis=dim)
        cells = jnp.concatenate(
            [
                lax.ppermute(tail, axis, [(i, (i + 1) % count) for i in range(ends)]),
                cells,
                lax.ppermute(head, axis, [((i + 1) % count, i) for i in range(ends)]),
            ],
            axis=dim,
        )
    return cells


def take_slice(values, first_index, extent, along_axis):
    return lax.slice_in_dim(values, first_index, first_index + extent, axis=along_axis)


def upwind_divergence(padded, motion, along_axis):
    length = padded.shape[along_axis] - 4
    face_count = length + 1
    behind = take_slice(padded, 0, face_count, along_axis)
    centre = take_slice(padded, 1, face_count, along_axis)
    onward = take_slice(padded, 2, face_count, along_axis)
    beyond = take_slice(padded, 3, face_count, along_axis)
    left_face = (6.0 * centre + 3.0 * onward - behind) * 0.125
    right_face = (3.0 * centre + 6.0 * onward - beyond) * 0.125
    face_speed = 0.5 * (
        take_slice(motion, 1, face_count, along_axis)
        + take_slice(motion, 2, face_count, along_axis)
    )
    fluxes = jnp.maximum(face_speed, 0.0) * left_face + jnp.minimum(face_speed, 0.0) * right_face
    return take_slice(fluxes, 1, length, along_axis) - take_slice(fluxes, 0, length, along_axis)


def substep(extended, speed_x, speed_y, sea_mask):
    across = upwind_divergence(extended, speed_x, 1)
    centre_part = extended[:, 2:-2]
    padding = ((0, 0), (0, 0), (2, 2))
    sideways = upwind_divergence(jnp.pad(centre_part, padding), jnp.pad(speed_y, padding), 2)
    return (centre_part - courant * (across + sideways)) * sea_mask


def direction_tables(directions):
    angles = jnp.arange(directions, dtype=jnp.float32) * (2.0 * jnp.pi / directions)
    return (jnp.cos(angles), jnp.sin(angles))


def source_term(values, wind_speed, growth, damping):
    return values * jnp.exp(wind_speed[:, None] * growth[None, :] - damping[None, :])


def velocities(stacked, freq_count):
    cosine_table, sine_table = direction_tables(DIR)
    celerity = stacked[:freq_count][:, None]
    shape_out = (freq_count * DIR,) + stacked.shape[1:]
    speed_x = (
        celerity * cosine_table[None, :, None, None] + stacked[freq_count][None, None]
    ).reshape(shape_out)
    speed_y = (
        celerity * sine_table[None, :, None, None] + stacked[freq_count + 1][None, None]
    ).reshape(shape_out)
    return (speed_x, speed_y)


def deliver(bulk_rows, small_rows):
    return (
        lax.all_to_all(bulk_rows, GROUP, split_axis=0, concat_axis=0, tiled=True),
        lax.all_to_all(small_rows, GROUP, split_axis=0, concat_axis=0, tiled=True),
    )


def tile_plan(spectra, wind, growth, damping, row_cell, land_mask, group_speed, current, turning):
    tile_count = lax.axis_size(GROUP)
    comp_width = spectra.shape[1]
    tile_rows, tile_cols = land_mask.shape
    cell_count = tile_rows * tile_cols
    capacity = cell_count // tile_count
    target = row_cell // cell_count
    local_cell = (row_cell - target * cell_count).astype(jnp.float32)
    matches = (target[:, None] == jnp.arange(tile_count, dtype=jnp.int32)[None, :]).astype(
        jnp.int32
    )
    bucket_slot = jnp.sum((jnp.cumsum(matches, axis=0) - 1) * matches, axis=1)

    def bucket(values, filler):
        shape_out = (tile_count, capacity) + values.shape[1:]
        return jnp.full(shape_out, filler, jnp.float32).at[target, bucket_slot].set(values)

    bulk_rows = bucket(source_term(spectra, wind, growth, damping), 0.0)
    small_rows = bucket(local_cell[:, None], float(cell_count))
    bulk_back, small_back = deliver(bulk_rows, small_rows)
    cell_index = small_back[:, :, 0].reshape(-1).astype(jnp.int32)
    flat_values = bulk_back.reshape((tile_count * capacity,) + bulk_back.shape[2:])
    tile_field = (
        jnp.zeros((cell_count,) + bulk_back.shape[2:], jnp.float32)
        .at[cell_index]
        .set(flat_values, mode="drop")
    )
    spectrum = tile_field.T.reshape(comp_width, tile_rows, tile_cols)
    freq_count = comp_width // DIR
    reach = 2 * SUBSTEPS
    stacked = jnp.concatenate([group_speed, current, land_mask.astype(jnp.float32)[None]], axis=0)
    rimmed = with_halo(stacked, ((GROUP, 1),), 2 * SUBSTEPS)
    speed_x, speed_y = velocities(rimmed, freq_count)
    sea_rim = rimmed[freq_count + 2 :]

    def window(values, margin):
        return lax.slice_in_dim(values, reach - margin, reach + tile_rows + margin, axis=1)

    for repeat in range(SUBSTEPS):
        extended = with_halo(spectrum, ((GROUP, 1),), 2)
        spectrum = substep(extended, window(speed_x, 2), window(speed_y, 0), window(sea_rim, 0)[0])
    blocks = spectrum.reshape(freq_count, DIR, tile_rows, tile_cols)
    wrapped = jnp.concatenate([blocks[:, -2:], blocks, blocks[:, :2]], axis=1)
    turning_full = jnp.broadcast_to(turning[None, None], wrapped.shape)
    blocks = blocks - upwind_divergence(wrapped, turning_full, 1)
    spectrum = blocks.reshape(comp_width, tile_rows, tile_cols)
    shipped = lax.all_to_all(spectrum, GROUP, split_axis=0, concat_axis=1, tiled=True)
    return shipped[None]


def pack_kernel(
    parts,
    freqs,
    spectra_ref,
    wind_ref,
    growth_ref,
    damping_ref,
    cell_ref,
    speed_ref,
    current_ref,
    turning_ref,
    out_ref,
):
    rows, comps = spectra_ref.shape
    half = LANES // 2
    full = rows // LANES
    padded = (full + 1) * LANES
    low = lax.broadcasted_iota(jnp.int32, (8, LANES), 1) < half
    per_freq = DIR // 8
    span_rows = full * DIR + 16

    def extended(row, filler):
        return jnp.concatenate([row[None], jnp.full((1, half), filler, jnp.float32)], axis=1)

    def as_columns(row):
        return jnp.broadcast_to(row, (LANES, padded)).T

    cells = cell_ref[...].astype(jnp.float32)
    keys = extended(cells, 1e9)
    key_cols = as_columns(keys)
    ranks = jnp.concatenate(
        [
            jnp.sum(
                jnp.where(key_cols < keys[:, c * LANES : (c + 1) * LANES], 1.0, 0.0), axis=0, keepdims=True
            )
            for c in range(full + 1)
        ],
        axis=1,
    )
    place = lax.broadcasted_iota(jnp.int32, (padded, padded), 0)
    place = jnp.where(place < rows, place, place - half).astype(jnp.float32)
    order = jnp.where(place == ranks, 1.0, 0.0).astype(jnp.bfloat16)

    wind_cols = as_columns(extended(wind_ref[...], 0.0))
    turned = []
    for block in range(comps // LANES):
        lanes = pl.ds(block * LANES, LANES)
        growth = growth_ref[lanes][None]
        damping = damping_ref[lanes][None]

        def source(first, count):
            span = pl.ds(first, count)
            return spectra_ref[span, lanes] * jnp.exp(
                wind_cols[first : first + count] * growth - damping
            )

        pieces = [source(c * LANES, LANES).T for c in range(full)]
        last = jnp.concatenate([source(full * LANES, half), jnp.zeros((half, LANES), jnp.float32)], axis=0)
        turned.append(jnp.concatenate(pieces + [last.T], axis=1))
    turned.append(jnp.broadcast_to(extended(cells, 0.0), (16, padded)))
    values = jnp.concatenate(turned, axis=0)
    head = values.astype(jnp.bfloat16)
    rest = (values - head.astype(jnp.float32)).astype(jnp.bfloat16)
    both = lax.dot_general(
        jnp.concatenate([head, rest], axis=0),
        order,
        (((1,), (1,)), ((), ())),
        preferred_element_type=jnp.float32,
    )

    def piece(first, count, chunk):
        lanes = slice(chunk * LANES, (chunk + 1) * LANES)
        return both[first : first + count, lanes] + both[comps + 16 + first : comps + 16 + first + count, lanes]

    shared = jnp.concatenate(
        [current_ref[0], current_ref[1], turning_ref[...]] + [piece(comps, 1, c) for c in range(full + 1)],
        axis=0,
    )
    for part in range(parts):
        for f in range(freqs):
            freq = part * freqs + f
            at = f * span_rows
            for chunk in range(full):
                out_ref[part, pl.ds(at + chunk * DIR, DIR), :] = piece(freq * DIR, DIR, chunk)
            at += full * DIR
            one, two, three = (piece(freq * DIR + g * 8, 8, full) for g in range(per_freq))
            out_ref[part, pl.ds(at, 8), :] = jnp.where(low, one, two)
            folded = jnp.where(low, three, pltpu.roll(three, 4, 0))
            out_ref[part, pl.ds(at + 8, 8), :] = jnp.concatenate([folded[:4], speed_ref[freq]], axis=0)
        out_ref[part, pl.ds(freqs * span_rows, shared.shape[0]), :] = shared


BLOCK = 8
PER_STEP = 2


def slab_kernel(
    parts,
    tile_rows,
    full,
    freqs,
    recv_ref,
    out_ref,
    onehot,
    first,
    second,
    table,
    faces_x,
    faces_y,
    moved_ref,
    done_ref,
    sems,
):
    slab_rows = parts * tile_rows
    half = LANES // 2
    span_rows = full * DIR + 16
    shared_base = freqs * span_rows
    highs = slab_rows // 2
    width = freqs * 2 * DIR
    low_lane = lax.broadcasted_iota(jnp.int32, (1, LANES), 1) < half
    low_lanes = lax.broadcasted_iota(jnp.int32, (8, LANES), 1) < half
    top_rows = lax.broadcasted_iota(jnp.int32, (8, LANES), 0) < 4
    cell_iota = lax.broadcasted_iota(jnp.int32, (2 * LANES, LANES), 0).astype(jnp.float32).astype(jnp.bfloat16)
    high_iota = lax.broadcasted_iota(jnp.int32, (highs, LANES), 0)

    def cells_of(owner, chunk):
        return recv_ref[owner, pl.ds(shared_base + 3 * tile_rows + chunk, 1), :].astype(jnp.int32)

    owner_rows = full * LANES + half
    capacity = tile_rows * LANES // parts
    spans = []
    for chunk in range(full + 1):
        begin, end = chunk * LANES, min((chunk + 1) * LANES, owner_rows)
        tiles = [
            t
            for t in range(parts)
            if owner_rows - capacity * (parts - t) < end and capacity * (t + 1) > begin
        ]
        spans.append(range(tiles[0] * tile_rows // 2, (tiles[-1] + 1) * tile_rows // 2))
    offsets = [parts * LANES * chunk for chunk in range(full + 1)]
    columns = [[] for _ in spans]

    def place(chunk, cells, values):
        span = pl.ds(offsets[chunk] + len(columns[chunk]) * LANES, LANES)
        high = cells // (2 * LANES)
        low = (cells - high * (2 * LANES)).astype(jnp.float32)
        low = jnp.broadcast_to(low, (2 * LANES, LANES)).astype(jnp.bfloat16)
        onehot[:, span] = jnp.where(cell_iota == low, 1.0, 0.0).astype(jnp.bfloat16)
        pieces = []
        for value in values:
            head = value.astype(jnp.bfloat16).astype(jnp.float32)
            pieces += [head, value - head]
        both = jnp.concatenate(pieces, axis=0).astype(jnp.bfloat16)
        column = []
        for h in spans[chunk]:
            pick = jnp.broadcast_to((high == h).astype(jnp.float32), (width, LANES)).astype(jnp.bfloat16)
            column.append(both * pick)
        column.append((high_iota == high).astype(jnp.float32).astype(jnp.bfloat16))
        columns[chunk].append(jnp.concatenate(column, axis=0))

    for pair in range(parts // 2):
        even, odd = 2 * pair, 2 * pair + 1
        for owner in (even, odd):
            for chunk in range(full):
                values = [
                    recv_ref[owner, pl.ds(f * span_rows + chunk * DIR, DIR), :] for f in range(freqs)
                ]
                place(chunk, cells_of(owner, chunk), values)

        def merged(offset):
            own, other = recv_ref[even, pl.ds(offset, 8), :], recv_ref[odd, pl.ds(offset, 8), :]
            return (
                jnp.where(low_lanes, own, pltpu.roll(other, half, 1)),
                jnp.where(low_lanes, pltpu.roll(own, half, 1), other),
            )

        values = []
        for f in range(freqs):
            one, two = merged(f * span_rows + full * DIR)
            three, four = merged(f * span_rows + full * DIR + 8)
            values.append(
                jnp.concatenate([one, two, jnp.where(top_rows, three, pltpu.roll(four, 4, 0))], axis=0)
            )
        place(full, jnp.where(low_lane, cells_of(even, full), cells_of(odd, full)), values)

    scattered = [
        lax.dot_general(
            jnp.concatenate(column, axis=1),
            onehot[:, pl.ds(offset, len(column) * LANES)],
            (((1,), (1,)), ((), ())),
            preferred_element_type=jnp.float32,
        )
        for offset, column in zip(offsets, columns)
    ]
    nothing = jnp.zeros((DIR, LANES), jnp.float32)
    for f in range(freqs):
        for field in (first, second):
            for edge in (0, 1, slab_rows + 2, slab_rows + 3):
                field[f, edge] = nothing
        for h in range(highs):
            terms = []
            for span, product in zip(spans, scattered):
                if h in span:
                    at = (h - span[0]) * width + f * 2 * DIR
                    terms += [product[at : at + DIR], product[at + DIR : at + 2 * DIR]]
            total = sum(terms[1:], terms[0])
            first[f, 2 * h + 2] = total[:, :LANES]
            first[f, 2 * h + 3] = total[:, LANES:]
    named = sum(product[len(span) * width :] for span, product in zip(spans, scattered))

    lane = lax.broadcasted_iota(jnp.int32, (slab_rows, LANES), 1)
    zero_rows = jnp.zeros((8, LANES), jnp.float32)

    def gather(offset):
        return jnp.concatenate(
            [recv_ref[owner, pl.ds(offset, tile_rows), :] for owner in range(parts)], axis=0
        )

    gain = 0.5 * courant / 8.0
    slots = iter(range(table.shape[0]))

    def keep(rows):
        slot = next(slots)
        table[slot, pl.ds(8, rows.shape[0]), :] = rows
        return slot

    def face_x(rows):
        slot = next(slots)
        table[slot, pl.ds(0, 8), :] = zero_rows
        table[slot, pl.ds(8 + slab_rows, 8), :] = zero_rows
        table[slot, pl.ds(8, slab_rows), :] = rows
        faces = gain * (table[slot, pl.ds(7, slab_rows + 8), :] + table[slot, pl.ds(8, slab_rows + 8), :])
        table[slot, pl.ds(7, slab_rows + 8), :] = faces
        return slot

    def face_y(rows):
        after = jnp.where(lane < LANES - 1, pltpu.roll(rows, LANES - 1, 1), 0.0)
        before = jnp.where(lane > 0, pltpu.roll(rows, 1, 1), 0.0)
        return keep(gain * (rows + after)), keep(gain * (rows + before))

    speeds = [gather(f * span_rows + full * DIR + 12) for f in range(freqs)]
    current_x, current_y, turning = (gather(shared_base + kind * tile_rows) for kind in range(3))
    current_x_face, speed_x_face = face_x(current_x), [face_x(s) for s in speeds]
    current_y_faces, speed_y_faces = face_y(current_y), [face_y(s) for s in speeds]
    land_slots = keep(named[:, :LANES]), keep(named[:, LANES:])
    ahead = jnp.maximum(turning, 0.0) * 0.125
    back = jnp.minimum(turning, 0.0) * 0.125
    bend_slots = [
        keep(rows)
        for rows in (
            -ahead,
            7.0 * ahead + 3.0 * back,
            1.0 - 3.0 * (ahead - back),
            -3.0 * ahead - 7.0 * back,
            back,
        )
    ]

    angles = lax.broadcasted_iota(jnp.int32, (DIR, LANES), 0).astype(jnp.float32) * (2.0 * math.pi / DIR)
    cosine = jnp.cos(angles)
    sine = jnp.sin(angles)
    lane_wide = lax.broadcasted_iota(jnp.int32, (DIR, LANES), 1)

    def row(slot, x):
        return table[slot, pl.ds(8 + x, 1), :]

    def flux(speed, behind, centre3, onward3, beyond):
        positive = speed > 0.0
        near = jnp.where(positive, centre3, onward3)
        far = jnp.where(positive, behind, beyond)
        return speed * ((centre3 + onward3) + (near - far))

    def advance(field, fresh, step, carry, finish):
        def speed_x(f, x):
            if fresh:
                faces_x[f, x + 1] = row(speed_x_face[f], x) * cosine + row(current_x_face, x)
            return faces_x[f, x + 1]

        def speed_y(f, side, x):
            if fresh:
                faces_y[f, side, x] = row(speed_y_faces[f][side], x) * sine + row(current_y_faces[side], x)
            return faces_y[f, side, x]

        carry = list(carry)
        for i in range(BLOCK):
            x = step * BLOCK + i
            sea = row(land_slots[i % 2], step * (BLOCK // 2) + i // 2)
            for f in range(freqs):
                entering, centre3 = carry[f]
                centre = field[f, x + 2]
                onward3 = 3.0 * field[f, x + 3]
                leaving = flux(speed_x(f, x), field[f, x + 1], centre3, onward3, field[f, x + 4])
                up1 = jnp.where(lane_wide < LANES - 1, pltpu.roll(centre, LANES - 1, 1), 0.0)
                up2 = jnp.where(lane_wide < LANES - 2, pltpu.roll(centre, LANES - 2, 1), 0.0)
                down1 = jnp.where(lane_wide > 0, pltpu.roll(centre, 1, 1), 0.0)
                down2 = jnp.where(lane_wide > 1, pltpu.roll(centre, 2, 1), 0.0)
                right = flux(speed_y(f, 0, x), down1, centre3, 3.0 * up1, up2)
                left = flux(speed_y(f, 1, x), down2, 3.0 * down1, centre3, up1)
                finish(f, x, (centre - (leaving - entering) - (right - left)) * sea)
                carry[f] = leaving, onward3
        return tuple(carry)

    def enter(field, fresh):
        carry = []
        for f in range(freqs):
            if fresh:
                faces_x[f, 0] = row(speed_x_face[f], -1) * cosine + row(current_x_face, -1)
            start3 = 3.0 * field[f, 2]
            carry.append((flux(faces_x[f, 0], nothing, nothing, start3, field[f, 3]), start3))
        return tuple(carry)

    def store(f, x, moved):
        second[f, x + 2] = moved

    def turn(f, x, moved):
        for g in range(DIR // 8):
            at = (f * DIR + g * 8) * slab_rows + x
            moved_ref[pl.ds(at, 8, stride=slab_rows), :] = moved[g * 8 : g * 8 + 8]

    def copy_out(step):
        part = pl.ds(pl.multiple_of(step * BLOCK, BLOCK), BLOCK)
        return pltpu.make_async_copy(done_ref.at[:, part, :], out_ref.at[:, part, :], sems.at[step])

    def final(block, carry):
        carry = advance(second, False, block, carry, turn)
        at = pl.multiple_of(block * BLOCK, BLOCK)
        weights = [table[slot, pl.ds(8 + at, BLOCK), :] for slot in bend_slots]
        for f in range(freqs):
            ring = [moved_ref[pl.ds((f * DIR + d) * slab_rows + at, BLOCK), :] for d in range(DIR)]
            for d in range(DIR):
                bent = weights[2] * ring[d]
                for k in (0, 1, 3, 4):
                    bent = bent + weights[k] * ring[(d + k - 2) % DIR]
                done_ref[f * DIR + d, pl.ds(at, BLOCK), :] = bent
        copy_out(block).start()
        return carry

    def sweep(one_block, carry):
        def body(step, carry):
            for i in range(PER_STEP):
                carry = one_block(step * PER_STEP + i, carry)
            return carry

        lax.fori_loop(0, slab_rows // BLOCK // PER_STEP, body, carry)

    sweep(lambda block, carry: advance(first, True, block, carry, store), enter(first, True))
    sweep(final, enter(second, False))
    for block in range(slab_rows // BLOCK):
        copy_out(block).wait()


def slab_plan(spectra, wind, growth, damping, row_cell, group_speed, current, turning):
    parts = lax.axis_size(GROUP)
    rows, comps = spectra.shape
    tile_rows = turning.shape[0]
    freqs = comps // parts // DIR
    full = rows // LANES
    slab_rows = parts * tile_rows
    depth = parts * rows
    highs = slab_rows // 2
    block_rows = -(-(freqs * (full * DIR + 16) + 3 * tile_rows + full + 1) // 8) * 8
    packed = pl.pallas_call(
        functools.partial(pack_kernel, parts, freqs),
        out_shape=pltpu.VMEM((parts, block_rows, LANES), jnp.float32),
        compiler_params=pltpu.CompilerParams(vmem_limit_bytes=56 * 1024 * 1024),
        name="pack",
    )(spectra, wind, growth, damping, row_cell, group_speed, current, turning)
    arrived = lax.all_to_all(packed, GROUP, split_axis=0, concat_axis=0, tiled=True)
    out = pl.pallas_call(
        functools.partial(slab_kernel, parts, tile_rows, full, freqs),
        out_shape=jax.ShapeDtypeStruct((freqs * DIR, slab_rows, LANES), jnp.float32),
        in_specs=[pl.BlockSpec(memory_space=pltpu.VMEM)],
        out_specs=pl.BlockSpec(memory_space=pl.ANY),
        scratch_shapes=[
            pltpu.VMEM((2 * LANES, depth), jnp.bfloat16),
            pltpu.VMEM((freqs, slab_rows + 4, DIR, LANES), jnp.float32),
            pltpu.VMEM((freqs, slab_rows + 4, DIR, LANES), jnp.float32),
            pltpu.VMEM((10 + 3 * freqs, slab_rows + 16, LANES), jnp.float32),
            pltpu.VMEM((freqs, slab_rows + 1, DIR, LANES), jnp.float32),
            pltpu.VMEM((freqs, 2, slab_rows, DIR, LANES), jnp.float32),
            pltpu.VMEM((freqs * DIR * slab_rows, LANES), jnp.float32),
            pltpu.VMEM((freqs * DIR, slab_rows, LANES), jnp.float32),
            pltpu.SemaphoreType.DMA((slab_rows // BLOCK,)),
        ],
        compiler_params=pltpu.CompilerParams(vmem_limit_bytes=32 * 1024 * 1024),
        name="slab",
    )(arrived)
    return out.reshape(1, freqs * DIR, slab_rows, LANES)


def shards(*arrays):
    spectra, land_mask = arrays[0], arrays[5]
    parts = lax.axis_size(GROUP)
    rows, comps = spectra.shape
    whole_frequencies = comps == parts * 2 * DIR
    fits = rows % LANES == LANES // 2 and land_mask.shape == (4, LANES) and parts % 2 == 0
    if whole_frequencies and fits:
        return slab_plan(*arrays[:5], *arrays[6:])
    return tile_plan(*arrays)


def solution(mesh):
    placed = (
        P(("groups", "pts", "comp"), "sub"),
        P(("groups", "pts", "comp")),
        P("sub"),
        P("sub"),
        P(("groups", "pts", "comp")),
        P(("groups", "pts", "comp"), None),
        P(("groups", "sub"), ("pts", "comp"), None),
        P("groups", ("pts", "comp"), None),
        P(("groups", "pts", "comp"), None),
    )
    return jax.shard_map(
        shards,
        mesh=mesh,
        in_specs=placed,
        out_specs=P("sub", ("pts", "comp"), "groups", None),
        check_vma=False,
    )
```

```python
import functools
import math
import jax
import jax.numpy as jnp
from jax import lax
from jax.experimental import pallas as pl
from jax.experimental.pallas import tpu as pltpu
from jax.sharding import PartitionSpec as P

DIR = 24
SUBSTEPS = 2
LANES = 128
GROUP = ("pts", "comp")


courant = 0.35


def with_halo(cells, sides, width):
    for axis, dim in sides:
        count = lax.axis_size(axis)
        ends = count - 1
        head = lax.slice_in_dim(cells, 0, width, axis=dim)
        tail = lax.slice_in_dim(cells, cells.shape[dim] - width, cells.shape[dim], axis=dim)
        cells = jnp.concatenate(
            [
                lax.ppermute(tail, axis, [(i, (i + 1) % count) for i in range(ends)]),
                cells,
                lax.ppermute(head, axis, [((i + 1) % count, i) for i in range(ends)]),
            ],
            axis=dim,
        )
    return cells


def take_slice(values, first_index, extent, along_axis):
    return lax.slice_in_dim(values, first_index, first_index + extent, axis=along_axis)


def upwind_divergence(padded, motion, along_axis):
    length = padded.shape[along_axis] - 4
    face_count = length + 1
    behind = take_slice(padded, 0, face_count, along_axis)
    centre = take_slice(padded, 1, face_count, along_axis)
    onward = take_slice(padded, 2, face_count, along_axis)
    beyond = take_slice(padded, 3, face_count, along_axis)
    left_face = (6.0 * centre + 3.0 * onward - behind) * 0.125
    right_face = (3.0 * centre + 6.0 * onward - beyond) * 0.125
    face_speed = 0.5 * (
        take_slice(motion, 1, face_count, along_axis)
        + take_slice(motion, 2, face_count, along_axis)
    )
    fluxes = jnp.maximum(face_speed, 0.0) * left_face + jnp.minimum(face_speed, 0.0) * right_face
    return take_slice(fluxes, 1, length, along_axis) - take_slice(fluxes, 0, length, along_axis)


def substep(extended, speed_x, speed_y, sea_mask):
    across = upwind_divergence(extended, speed_x, 1)
    centre_part = extended[:, 2:-2]
    padding = ((0, 0), (0, 0), (2, 2))
    sideways = upwind_divergence(jnp.pad(centre_part, padding), jnp.pad(speed_y, padding), 2)
    return (centre_part - courant * (across + sideways)) * sea_mask


def direction_tables(directions):
    angles = jnp.arange(directions, dtype=jnp.float32) * (2.0 * jnp.pi / directions)
    return (jnp.cos(angles), jnp.sin(angles))


def source_term(values, wind_speed, growth, damping):
    return values * jnp.exp(wind_speed[:, None] * growth[None, :] - damping[None, :])


def velocities(stacked, freq_count):
    cosine_table, sine_table = direction_tables(DIR)
    celerity = stacked[:freq_count][:, None]
    shape_out = (freq_count * DIR,) + stacked.shape[1:]
    speed_x = (
        celerity * cosine_table[None, :, None, None] + stacked[freq_count][None, None]
    ).reshape(shape_out)
    speed_y = (
        celerity * sine_table[None, :, None, None] + stacked[freq_count + 1][None, None]
    ).reshape(shape_out)
    return (speed_x, speed_y)


def deliver(bulk_rows, small_rows):
    return (
        lax.all_to_all(bulk_rows, GROUP, split_axis=0, concat_axis=0, tiled=True),
        lax.all_to_all(small_rows, GROUP, split_axis=0, concat_axis=0, tiled=True),
    )


def tile_plan(spectra, wind, growth, damping, row_cell, land_mask, group_speed, current, turning):
    tile_count = lax.axis_size(GROUP)
    comp_width = spectra.shape[1]
    tile_rows, tile_cols = land_mask.shape
    cell_count = tile_rows * tile_cols
    capacity = cell_count // tile_count
    target = row_cell // cell_count
    local_cell = (row_cell - target * cell_count).astype(jnp.float32)
    matches = (target[:, None] == jnp.arange(tile_count, dtype=jnp.int32)[None, :]).astype(
        jnp.int32
    )
    bucket_slot = jnp.sum((jnp.cumsum(matches, axis=0) - 1) * matches, axis=1)

    def bucket(values, filler):
        shape_out = (tile_count, capacity) + values.shape[1:]
        return jnp.full(shape_out, filler, jnp.float32).at[target, bucket_slot].set(values)

    bulk_rows = bucket(source_term(spectra, wind, growth, damping), 0.0)
    small_rows = bucket(local_cell[:, None], float(cell_count))
    bulk_back, small_back = deliver(bulk_rows, small_rows)
    cell_index = small_back[:, :, 0].reshape(-1).astype(jnp.int32)
    flat_values = bulk_back.reshape((tile_count * capacity,) + bulk_back.shape[2:])
    tile_field = (
        jnp.zeros((cell_count,) + bulk_back.shape[2:], jnp.float32)
        .at[cell_index]
        .set(flat_values, mode="drop")
    )
    spectrum = tile_field.T.reshape(comp_width, tile_rows, tile_cols)
    freq_count = comp_width // DIR
    reach = 2 * SUBSTEPS
    stacked = jnp.concatenate([group_speed, current, land_mask.astype(jnp.float32)[None]], axis=0)
    rimmed = with_halo(stacked, ((GROUP, 1),), 2 * SUBSTEPS)
    speed_x, speed_y = velocities(rimmed, freq_count)
    sea_rim = rimmed[freq_count + 2 :]

    def window(values, margin):
        return lax.slice_in_dim(values, reach - margin, reach + tile_rows + margin, axis=1)

    for repeat in range(SUBSTEPS):
        extended = with_halo(spectrum, ((GROUP, 1),), 2)
        spectrum = substep(extended, window(speed_x, 2), window(speed_y, 0), window(sea_rim, 0)[0])
    blocks = spectrum.reshape(freq_count, DIR, tile_rows, tile_cols)
    wrapped = jnp.concatenate([blocks[:, -2:], blocks, blocks[:, :2]], axis=1)
    turning_full = jnp.broadcast_to(turning[None, None], wrapped.shape)
    blocks = blocks - upwind_divergence(wrapped, turning_full, 1)
    spectrum = blocks.reshape(comp_width, tile_rows, tile_cols)
    shipped = lax.all_to_all(spectrum, GROUP, split_axis=0, concat_axis=1, tiled=True)
    return shipped[None]


def pack_kernel(
    parts,
    freqs,
    spectra_ref,
    wind_ref,
    growth_ref,
    damping_ref,
    cell_ref,
    speed_ref,
    current_ref,
    turning_ref,
    out_ref,
):
    rows, comps = spectra_ref.shape
    half = LANES // 2
    full = rows // LANES
    padded = (full + 1) * LANES
    low = lax.broadcasted_iota(jnp.int32, (8, LANES), 1) < half
    per_freq = DIR // 8
    span_rows = full * DIR + 16

    def extended(row, filler):
        return jnp.concatenate([row[None], jnp.full((1, half), filler, jnp.float32)], axis=1)

    def as_columns(row):
        return jnp.broadcast_to(row, (LANES, padded)).T

    cells = cell_ref[...].astype(jnp.float32)
    keys = extended(cells, 1e9)
    key_cols = as_columns(keys)
    ranks = jnp.concatenate(
        [
            jnp.sum(
                jnp.where(key_cols < keys[:, c * LANES : (c + 1) * LANES], 1.0, 0.0), axis=0, keepdims=True
            )
            for c in range(full + 1)
        ],
        axis=1,
    )
    place = lax.broadcasted_iota(jnp.int32, (padded, padded), 0)
    odd = lax.axis_index(GROUP) % 2 == 1
    swapped = jnp.where(place % LANES < half, place + half, place - half)
    place = jnp.where((place < full * LANES) & odd, swapped, place)
    place = jnp.where(place < rows, place, place - half).astype(jnp.float32)
    order = jnp.where(place == ranks, 1.0, 0.0).astype(jnp.bfloat16)

    wind_cols = as_columns(extended(wind_ref[...], 0.0))
    turned = []
    for block in range(comps // LANES):
        lanes = pl.ds(block * LANES, LANES)
        growth = growth_ref[lanes][None]
        damping = damping_ref[lanes][None]

        def source(first, count):
            span = pl.ds(first, count)
            return spectra_ref[span, lanes] * jnp.exp(
                wind_cols[first : first + count] * growth - damping
            )

        pieces = [source(c * LANES, LANES).T for c in range(full)]
        last = jnp.concatenate([source(full * LANES, half), jnp.zeros((half, LANES), jnp.float32)], axis=0)
        turned.append(jnp.concatenate(pieces + [last.T], axis=1))
    turned.append(jnp.broadcast_to(extended(cells, 0.0), (16, padded)))
    values = jnp.concatenate(turned, axis=0)
    head = values.astype(jnp.bfloat16)
    rest = (values - head.astype(jnp.float32)).astype(jnp.bfloat16)
    both = lax.dot_general(
        jnp.concatenate([head, rest], axis=0),
        order,
        (((1,), (1,)), ((), ())),
        preferred_element_type=jnp.float32,
    )

    def piece(first, count, chunk):
        lanes = slice(chunk * LANES, (chunk + 1) * LANES)
        return both[first : first + count, lanes] + both[comps + 16 + first : comps + 16 + first + count, lanes]

    shared = jnp.concatenate(
        [current_ref[0], current_ref[1], turning_ref[...]] + [piece(comps, 1, c) for c in range(full + 1)],
        axis=0,
    )
    for part in range(parts):
        for f in range(freqs):
            freq = part * freqs + f
            at = f * span_rows
            for chunk in range(full):
                out_ref[part, pl.ds(at + chunk * DIR, DIR), :] = piece(freq * DIR, DIR, chunk)
            at += full * DIR
            one, two, three = (piece(freq * DIR + g * 8, 8, full) for g in range(per_freq))
            out_ref[part, pl.ds(at, 8), :] = jnp.where(low, one, two)
            folded = jnp.where(low, three, pltpu.roll(three, 4, 0))
            out_ref[part, pl.ds(at + 8, 8), :] = jnp.concatenate([folded[:4], speed_ref[freq]], axis=0)
        out_ref[part, pl.ds(freqs * span_rows, shared.shape[0]), :] = shared


BLOCK = 8
PER_STEP = 2


def slab_kernel(
    parts,
    tile_rows,
    full,
    freqs,
    recv_ref,
    out_ref,
    onehot,
    first,
    second,
    table,
    faces_x,
    faces_y,
    moved_ref,
    done_ref,
    sems,
):
    slab_rows = parts * tile_rows
    half = LANES // 2
    span_rows = full * DIR + 16
    shared_base = freqs * span_rows
    highs = slab_rows // 2
    width = freqs * 2 * DIR
    low_lane = lax.broadcasted_iota(jnp.int32, (1, LANES), 1) < half
    low_lanes = lax.broadcasted_iota(jnp.int32, (8, LANES), 1) < half
    low_wide = lax.broadcasted_iota(jnp.int32, (DIR, LANES), 1) < half
    top_rows = lax.broadcasted_iota(jnp.int32, (8, LANES), 0) < 4
    cell_iota = lax.broadcasted_iota(jnp.int32, (2 * LANES, LANES), 0).astype(jnp.float32).astype(jnp.bfloat16)
    high_iota = lax.broadcasted_iota(jnp.int32, (highs, LANES), 0)

    def cells_of(owner, chunk):
        return recv_ref[owner, pl.ds(shared_base + 3 * tile_rows + chunk, 1), :].astype(jnp.int32)

    owner_rows = full * LANES + half
    capacity = tile_rows * LANES // parts
    spans = []
    for begin in range(0, owner_rows, half):
        tiles = [
            t
            for t in range(parts)
            if owner_rows - capacity * (parts - t) < begin + half and capacity * (t + 1) > begin
        ]
        spans.append(range(tiles[0] * tile_rows // 2, (tiles[-1] + 1) * tile_rows // 2))
    offsets = [parts // 2 * LANES * chunk for chunk in range(len(spans))]
    columns = [[] for _ in spans]

    def place(chunk, cells, values):
        span = pl.ds(offsets[chunk] + len(columns[chunk]) * LANES, LANES)
        high = cells // (2 * LANES)
        low = (cells - high * (2 * LANES)).astype(jnp.float32)
        low = jnp.broadcast_to(low, (2 * LANES, LANES)).astype(jnp.bfloat16)
        onehot[:, span] = jnp.where(cell_iota == low, 1.0, 0.0).astype(jnp.bfloat16)
        pieces = []
        for value in values:
            head = value.astype(jnp.bfloat16).astype(jnp.float32)
            pieces += [head, value - head]
        both = jnp.concatenate(pieces, axis=0).astype(jnp.bfloat16)
        column = []
        for h in spans[chunk]:
            pick = jnp.broadcast_to((high == h).astype(jnp.float32), (width, LANES)).astype(jnp.bfloat16)
            column.append(both * pick)
        column.append((high_iota == high).astype(jnp.float32).astype(jnp.bfloat16))
        columns[chunk].append(jnp.concatenate(column, axis=0))

    for pair in range(parts // 2):
        even, odd = 2 * pair, 2 * pair + 1
        for chunk in range(full):
            here, there = (
                [recv_ref[owner, pl.ds(f * span_rows + chunk * DIR, DIR), :] for f in range(freqs)]
                for owner in (even, odd)
            )
            cells, cells_there = cells_of(even, chunk), cells_of(odd, chunk)
            for side in range(2):
                place(
                    2 * chunk + side,
                    jnp.where(low_lane, cells, cells_there),
                    [jnp.where(low_wide, a, b) for a, b in zip(here, there)],
                )
                here, there, cells, cells_there = there, here, cells_there, cells

        def merged(offset):
            own, other = recv_ref[even, pl.ds(offset, 8), :], recv_ref[odd, pl.ds(offset, 8), :]
            return (
                jnp.where(low_lanes, own, pltpu.roll(other, half, 1)),
                jnp.where(low_lanes, pltpu.roll(own, half, 1), other),
            )

        values = []
        for f in range(freqs):
            one, two = merged(f * span_rows + full * DIR)
            three, four = merged(f * span_rows + full * DIR + 8)
            values.append(
                jnp.concatenate([one, two, jnp.where(top_rows, three, pltpu.roll(four, 4, 0))], axis=0)
            )
        place(2 * full, jnp.where(low_lane, cells_of(even, full), cells_of(odd, full)), values)

    lane = lax.broadcasted_iota(jnp.int32, (slab_rows, LANES), 1)
    zero_rows = jnp.zeros((8, LANES), jnp.float32)

    def gather(offset):
        return jnp.concatenate(
            [recv_ref[owner, pl.ds(offset, tile_rows), :] for owner in range(parts)], axis=0
        )

    gain = 0.5 * courant / 8.0
    slots = iter(range(table.shape[0]))

    def keep(rows):
        slot = next(slots)
        table[slot, pl.ds(8, rows.shape[0]), :] = rows
        return slot

    def face_x(rows):
        slot = next(slots)
        table[slot, pl.ds(0, 8), :] = zero_rows
        table[slot, pl.ds(8 + slab_rows, 8), :] = zero_rows
        table[slot, pl.ds(8, slab_rows), :] = rows
        faces = gain * (table[slot, pl.ds(7, slab_rows + 8), :] + table[slot, pl.ds(8, slab_rows + 8), :])
        table[slot, pl.ds(7, slab_rows + 8), :] = faces
        return slot

    def face_y(rows):
        after = jnp.where(lane < LANES - 1, pltpu.roll(rows, LANES - 1, 1), 0.0)
        before = jnp.where(lane > 0, pltpu.roll(rows, 1, 1), 0.0)
        return keep(gain * (rows + after)), keep(gain * (rows + before))

    speeds = [gather(f * span_rows + full * DIR + 12) for f in range(freqs)]
    current_x, current_y, turning = (gather(shared_base + kind * tile_rows) for kind in range(3))
    current_x_face, speed_x_face = face_x(current_x), [face_x(s) for s in speeds]
    current_y_faces, speed_y_faces = face_y(current_y), [face_y(s) for s in speeds]
    step_angle = 2.0 * math.pi / DIR
    sublane = lax.broadcasted_iota(jnp.int32, (8, LANES), 0)
    cosine0 = jnp.ones((8, LANES), jnp.float32)
    sine0 = jnp.zeros((8, LANES), jnp.float32)
    for d in range(1, 8):
        cosine0 = jnp.where(sublane == d, math.cos(d * step_angle), cosine0)
        sine0 = jnp.where(sublane == d, math.sin(d * step_angle), sine0)
    turns = [(math.cos(g * 8 * step_angle), math.sin(g * 8 * step_angle)) for g in range(DIR // 8)]
    cosine = jnp.concatenate([c * cosine0 - t * sine0 for c, t in turns], axis=0)
    sine = jnp.concatenate([c * sine0 + t * cosine0 for c, t in turns], axis=0)

    def row(slot, x):
        return table[slot, pl.ds(8 + x, 1), :]

    for f in range(freqs):
        for x in range(-1, slab_rows):
            faces_x[f, x + 1] = row(speed_x_face[f], x) * cosine + row(current_x_face, x)
        for x in range(slab_rows):
            for side in range(2):
                faces_y[f, side, x] = row(speed_y_faces[f][side], x) * sine + row(current_y_faces[side], x)

    scattered = [
        lax.dot_general(
            jnp.concatenate(column, axis=1),
            onehot[:, pl.ds(offset, len(column) * LANES)],
            (((1,), (1,)), ((), ())),
            preferred_element_type=jnp.float32,
        )
        for offset, column in zip(offsets, columns)
    ]
    nothing = jnp.zeros((DIR, LANES), jnp.float32)
    for f in range(freqs):
        for field in (first, second):
            for edge in (0, 1, slab_rows + 2, slab_rows + 3):
                field[f, edge] = nothing
        for h in range(highs):
            terms = []
            for span, product in zip(spans, scattered):
                if h in span:
                    at = (h - span[0]) * width + f * 2 * DIR
                    terms += [product[at : at + DIR], product[at + DIR : at + 2 * DIR]]
            total = sum(terms[1:], terms[0])
            first[f, 2 * h + 2] = total[:, :LANES]
            first[f, 2 * h + 3] = total[:, LANES:]
    named = sum(product[len(span) * width :] for span, product in zip(spans, scattered))

    land_slots = keep(named[:, :LANES]), keep(named[:, LANES:])
    ahead = jnp.maximum(turning, 0.0) * 0.125
    back = jnp.minimum(turning, 0.0) * 0.125
    bend_slots = [
        keep(rows)
        for rows in (
            -ahead,
            7.0 * ahead + 3.0 * back,
            1.0 - 3.0 * (ahead - back),
            -3.0 * ahead - 7.0 * back,
            back,
        )
    ]

    lane_wide = lax.broadcasted_iota(jnp.int32, (DIR, LANES), 1)

    def flux(speed, behind, centre3, onward3, beyond):
        positive = speed > 0.0
        near = jnp.where(positive, centre3, onward3)
        far = jnp.where(positive, behind, beyond)
        return speed * ((centre3 + onward3) + (near - far))

    def advance(field, step, carry, finish):
        carry = list(carry)
        for i in range(BLOCK):
            x = step * BLOCK + i
            sea = row(land_slots[i % 2], step * (BLOCK // 2) + i // 2)
            for f in range(freqs):
                entering, centre3 = carry[f]
                centre = field[f, x + 2]
                onward3 = 3.0 * field[f, x + 3]
                leaving = flux(faces_x[f, x + 1], field[f, x + 1], centre3, onward3, field[f, x + 4])
                up1 = jnp.where(lane_wide < LANES - 1, pltpu.roll(centre, LANES - 1, 1), 0.0)
                up2 = jnp.where(lane_wide < LANES - 2, pltpu.roll(centre, LANES - 2, 1), 0.0)
                down1 = jnp.where(lane_wide > 0, pltpu.roll(centre, 1, 1), 0.0)
                down2 = jnp.where(lane_wide > 1, pltpu.roll(centre, 2, 1), 0.0)
                right = flux(faces_y[f, 0, x], down1, centre3, 3.0 * up1, up2)
                left = flux(faces_y[f, 1, x], down2, 3.0 * down1, centre3, up1)
                finish(f, x, (centre - (leaving - entering) - (right - left)) * sea)
                carry[f] = leaving, onward3
        return tuple(carry)

    def enter(field):
        carry = []
        for f in range(freqs):
            start3 = 3.0 * field[f, 2]
            carry.append((flux(faces_x[f, 0], nothing, nothing, start3, field[f, 3]), start3))
        return tuple(carry)

    def store(f, x, moved):
        second[f, x + 2] = moved

    def turn(f, x, moved):
        for g in range(DIR // 8):
            at = (f * DIR + g * 8) * slab_rows + x
            moved_ref[pl.ds(at, 8, stride=slab_rows), :] = moved[g * 8 : g * 8 + 8]

    def copy_out(step):
        part = pl.ds(pl.multiple_of(step * BLOCK, BLOCK), BLOCK)
        return pltpu.make_async_copy(done_ref.at[:, part, :], out_ref.at[:, part, :], sems.at[step])

    def final(block, carry):
        carry = advance(second, block, carry, turn)
        at = pl.multiple_of(block * BLOCK, BLOCK)
        weights = [table[slot, pl.ds(8 + at, BLOCK), :] for slot in bend_slots]
        for f in range(freqs):
            ring = [moved_ref[pl.ds((f * DIR + d) * slab_rows + at, BLOCK), :] for d in range(DIR)]
            for d in range(DIR):
                bent = weights[2] * ring[d]
                for k in (0, 1, 3, 4):
                    bent = bent + weights[k] * ring[(d + k - 2) % DIR]
                done_ref[f * DIR + d, pl.ds(at, BLOCK), :] = bent
        copy_out(block).start()
        return carry

    def sweep(one_block, carry):
        def body(step, carry):
            for i in range(PER_STEP):
                carry = one_block(step * PER_STEP + i, carry)
            return carry

        lax.fori_loop(0, slab_rows // BLOCK // PER_STEP, body, carry)

    sweep(lambda block, carry: advance(first, block, carry, store), enter(first))
    sweep(final, enter(second))
    for block in range(slab_rows // BLOCK):
        copy_out(block).wait()


def slab_plan(spectra, wind, growth, damping, row_cell, group_speed, current, turning):
    parts = lax.axis_size(GROUP)
    rows, comps = spectra.shape
    tile_rows = turning.shape[0]
    freqs = comps // parts // DIR
    full = rows // LANES
    slab_rows = parts * tile_rows
    depth = parts * rows
    highs = slab_rows // 2
    block_rows = -(-(freqs * (full * DIR + 16) + 3 * tile_rows + full + 1) // 8) * 8
    packed = pl.pallas_call(
        functools.partial(pack_kernel, parts, freqs),
        out_shape=pltpu.VMEM((parts, block_rows, LANES), jnp.float32),
        compiler_params=pltpu.CompilerParams(vmem_limit_bytes=56 * 1024 * 1024),
        name="pack",
    )(spectra, wind, growth, damping, row_cell, group_speed, current, turning)
    arrived = lax.all_to_all(packed, GROUP, split_axis=0, concat_axis=0, tiled=True)
    out = pl.pallas_call(
        functools.partial(slab_kernel, parts, tile_rows, full, freqs),
        out_shape=jax.ShapeDtypeStruct((freqs * DIR, slab_rows, LANES), jnp.float32),
        in_specs=[pl.BlockSpec(memory_space=pltpu.VMEM)],
        out_specs=pl.BlockSpec(memory_space=pl.ANY),
        scratch_shapes=[
            pltpu.VMEM((2 * LANES, depth), jnp.bfloat16),
            pltpu.VMEM((freqs, slab_rows + 4, DIR, LANES), jnp.float32),
            pltpu.VMEM((freqs, slab_rows + 4, DIR, LANES), jnp.float32),
            pltpu.VMEM((10 + 3 * freqs, slab_rows + 16, LANES), jnp.float32),
            pltpu.VMEM((freqs, slab_rows + 1, DIR, LANES), jnp.float32),
            pltpu.VMEM((freqs, 2, slab_rows, DIR, LANES), jnp.float32),
            pltpu.VMEM((freqs * DIR * slab_rows, LANES), jnp.float32),
            pltpu.VMEM((freqs * DIR, slab_rows, LANES), jnp.float32),
            pltpu.SemaphoreType.DMA((slab_rows // BLOCK,)),
        ],
        compiler_params=pltpu.CompilerParams(vmem_limit_bytes=32 * 1024 * 1024),
        name="slab",
    )(arrived)
    return out.reshape(1, freqs * DIR, slab_rows, LANES)


def shards(*arrays):
    spectra, land_mask = arrays[0], arrays[5]
    parts = lax.axis_size(GROUP)
    rows, comps = spectra.shape
    whole_frequencies = comps == parts * 2 * DIR
    fits = rows % LANES == LANES // 2 and land_mask.shape == (4, LANES) and parts % 2 == 0
    if whole_frequencies and fits:
        return slab_plan(*arrays[:5], *arrays[6:])
    return tile_plan(*arrays)


def solution(mesh):
    placed = (
        P(("groups", "pts", "comp"), "sub"),
        P(("groups", "pts", "comp")),
        P("sub"),
        P("sub"),
        P(("groups", "pts", "comp")),
        P(("groups", "pts", "comp"), None),
        P(("groups", "sub"), ("pts", "comp"), None),
        P("groups", ("pts", "comp"), None),
        P(("groups", "pts", "comp"), None),
    )
    return jax.shard_map(
        shards,
        mesh=mesh,
        in_specs=placed,
        out_specs=P("sub", ("pts", "comp"), "groups", None),
        check_vma=False,
    )
```

```python
import functools
import math
import jax
import jax.numpy as jnp
from jax import lax
from jax.experimental import pallas as pl
from jax.experimental.pallas import tpu as pltpu
from jax.sharding import PartitionSpec as P

DIR = 24
SUBSTEPS = 2
LANES = 128
GROUP = ("pts", "comp")


courant = 0.35


def with_halo(cells, sides, width):
    for axis, dim in sides:
        count = lax.axis_size(axis)
        ends = count - 1
        head = lax.slice_in_dim(cells, 0, width, axis=dim)
        tail = lax.slice_in_dim(cells, cells.shape[dim] - width, cells.shape[dim], axis=dim)
        cells = jnp.concatenate(
            [
                lax.ppermute(tail, axis, [(i, (i + 1) % count) for i in range(ends)]),
                cells,
                lax.ppermute(head, axis, [((i + 1) % count, i) for i in range(ends)]),
            ],
            axis=dim,
        )
    return cells


def take_slice(values, first_index, extent, along_axis):
    return lax.slice_in_dim(values, first_index, first_index + extent, axis=along_axis)


def upwind_divergence(padded, motion, along_axis):
    length = padded.shape[along_axis] - 4
    face_count = length + 1
    behind = take_slice(padded, 0, face_count, along_axis)
    centre = take_slice(padded, 1, face_count, along_axis)
    onward = take_slice(padded, 2, face_count, along_axis)
    beyond = take_slice(padded, 3, face_count, along_axis)
    left_face = (6.0 * centre + 3.0 * onward - behind) * 0.125
    right_face = (3.0 * centre + 6.0 * onward - beyond) * 0.125
    face_speed = 0.5 * (
        take_slice(motion, 1, face_count, along_axis)
        + take_slice(motion, 2, face_count, along_axis)
    )
    fluxes = jnp.maximum(face_speed, 0.0) * left_face + jnp.minimum(face_speed, 0.0) * right_face
    return take_slice(fluxes, 1, length, along_axis) - take_slice(fluxes, 0, length, along_axis)


def substep(extended, speed_x, speed_y, sea_mask):
    across = upwind_divergence(extended, speed_x, 1)
    centre_part = extended[:, 2:-2]
    padding = ((0, 0), (0, 0), (2, 2))
    sideways = upwind_divergence(jnp.pad(centre_part, padding), jnp.pad(speed_y, padding), 2)
    return (centre_part - courant * (across + sideways)) * sea_mask


def direction_tables(directions):
    angles = jnp.arange(directions, dtype=jnp.float32) * (2.0 * jnp.pi / directions)
    return (jnp.cos(angles), jnp.sin(angles))


def source_term(values, wind_speed, growth, damping):
    return values * jnp.exp(wind_speed[:, None] * growth[None, :] - damping[None, :])


def velocities(stacked, freq_count):
    cosine_table, sine_table = direction_tables(DIR)
    celerity = stacked[:freq_count][:, None]
    shape_out = (freq_count * DIR,) + stacked.shape[1:]
    speed_x = (
        celerity * cosine_table[None, :, None, None] + stacked[freq_count][None, None]
    ).reshape(shape_out)
    speed_y = (
        celerity * sine_table[None, :, None, None] + stacked[freq_count + 1][None, None]
    ).reshape(shape_out)
    return (speed_x, speed_y)


def deliver(bulk_rows, small_rows):
    return (
        lax.all_to_all(bulk_rows, GROUP, split_axis=0, concat_axis=0, tiled=True),
        lax.all_to_all(small_rows, GROUP, split_axis=0, concat_axis=0, tiled=True),
    )


def tile_plan(spectra, wind, growth, damping, row_cell, land_mask, group_speed, current, turning):
    tile_count = lax.axis_size(GROUP)
    comp_width = spectra.shape[1]
    tile_rows, tile_cols = land_mask.shape
    cell_count = tile_rows * tile_cols
    capacity = cell_count // tile_count
    target = row_cell // cell_count
    local_cell = (row_cell - target * cell_count).astype(jnp.float32)
    matches = (target[:, None] == jnp.arange(tile_count, dtype=jnp.int32)[None, :]).astype(
        jnp.int32
    )
    bucket_slot = jnp.sum((jnp.cumsum(matches, axis=0) - 1) * matches, axis=1)

    def bucket(values, filler):
        shape_out = (tile_count, capacity) + values.shape[1:]
        return jnp.full(shape_out, filler, jnp.float32).at[target, bucket_slot].set(values)

    bulk_rows = bucket(source_term(spectra, wind, growth, damping), 0.0)
    small_rows = bucket(local_cell[:, None], float(cell_count))
    bulk_back, small_back = deliver(bulk_rows, small_rows)
    cell_index = small_back[:, :, 0].reshape(-1).astype(jnp.int32)
    flat_values = bulk_back.reshape((tile_count * capacity,) + bulk_back.shape[2:])
    tile_field = (
        jnp.zeros((cell_count,) + bulk_back.shape[2:], jnp.float32)
        .at[cell_index]
        .set(flat_values, mode="drop")
    )
    spectrum = tile_field.T.reshape(comp_width, tile_rows, tile_cols)
    freq_count = comp_width // DIR
    reach = 2 * SUBSTEPS
    stacked = jnp.concatenate([group_speed, current, land_mask.astype(jnp.float32)[None]], axis=0)
    rimmed = with_halo(stacked, ((GROUP, 1),), 2 * SUBSTEPS)
    speed_x, speed_y = velocities(rimmed, freq_count)
    sea_rim = rimmed[freq_count + 2 :]

    def window(values, margin):
        return lax.slice_in_dim(values, reach - margin, reach + tile_rows + margin, axis=1)

    for repeat in range(SUBSTEPS):
        extended = with_halo(spectrum, ((GROUP, 1),), 2)
        spectrum = substep(extended, window(speed_x, 2), window(speed_y, 0), window(sea_rim, 0)[0])
    blocks = spectrum.reshape(freq_count, DIR, tile_rows, tile_cols)
    wrapped = jnp.concatenate([blocks[:, -2:], blocks, blocks[:, :2]], axis=1)
    turning_full = jnp.broadcast_to(turning[None, None], wrapped.shape)
    blocks = blocks - upwind_divergence(wrapped, turning_full, 1)
    spectrum = blocks.reshape(comp_width, tile_rows, tile_cols)
    shipped = lax.all_to_all(spectrum, GROUP, split_axis=0, concat_axis=1, tiled=True)
    return shipped[None]


def pack_kernel(
    parts,
    freqs,
    spectra_ref,
    wind_ref,
    growth_ref,
    damping_ref,
    cell_ref,
    speed_ref,
    current_ref,
    turning_ref,
    out_ref,
):
    rows, comps = spectra_ref.shape
    half = LANES // 2
    full = rows // LANES
    padded = (full + 1) * LANES
    low = lax.broadcasted_iota(jnp.int32, (8, LANES), 1) < half
    per_freq = DIR // 8
    span_rows = full * DIR + 16

    def extended(row, filler):
        return jnp.concatenate([row[None], jnp.full((1, half), filler, jnp.float32)], axis=1)

    def as_columns(row):
        return jnp.broadcast_to(row, (LANES, padded)).T

    cells = cell_ref[...].astype(jnp.float32)
    keys = extended(cells, 1e9)
    key_cols = as_columns(keys)
    ranks = jnp.concatenate(
        [
            jnp.sum(
                jnp.where(key_cols < keys[:, c * LANES : (c + 1) * LANES], 1.0, 0.0), axis=0, keepdims=True
            )
            for c in range(full + 1)
        ],
        axis=1,
    )
    place = lax.broadcasted_iota(jnp.int32, (padded, padded), 0)
    odd = lax.axis_index(GROUP) % 2 == 1
    swapped = jnp.where(place % LANES < half, place + half, place - half)
    place = jnp.where((place < full * LANES) & odd, swapped, place)
    place = jnp.where(place < rows, place, place - half).astype(jnp.float32)
    order = jnp.where(place == ranks, 1.0, 0.0).astype(jnp.bfloat16)

    wind_cols = as_columns(extended(wind_ref[...], 0.0))
    turned = []
    for block in range(comps // LANES):
        lanes = pl.ds(block * LANES, LANES)
        growth = growth_ref[lanes][None]
        damping = damping_ref[lanes][None]

        def source(first, count):
            span = pl.ds(first, count)
            return spectra_ref[span, lanes] * jnp.exp(
                wind_cols[first : first + count] * growth - damping
            )

        pieces = [source(c * LANES, LANES).T for c in range(full)]
        last = jnp.concatenate([source(full * LANES, half), jnp.zeros((half, LANES), jnp.float32)], axis=0)
        turned.append(jnp.concatenate(pieces + [last.T], axis=1))
    turned.append(jnp.broadcast_to(extended(cells, 0.0), (16, padded)))
    values = jnp.concatenate(turned, axis=0)
    head = values.astype(jnp.bfloat16)
    rest = (values - head.astype(jnp.float32)).astype(jnp.bfloat16)
    both = lax.dot_general(
        jnp.concatenate([head, rest], axis=0),
        order,
        (((1,), (1,)), ((), ())),
        preferred_element_type=jnp.float32,
    )

    def piece(first, count, chunk):
        lanes = slice(chunk * LANES, (chunk + 1) * LANES)
        return both[first : first + count, lanes] + both[comps + 16 + first : comps + 16 + first + count, lanes]

    shared = jnp.concatenate(
        [current_ref[0], current_ref[1], turning_ref[...]] + [piece(comps, 1, c) for c in range(full + 1)],
        axis=0,
    )
    for part in range(parts):
        for f in range(freqs):
            freq = part * freqs + f
            at = f * span_rows
            for chunk in range(full):
                out_ref[part, pl.ds(at + chunk * DIR, DIR), :] = piece(freq * DIR, DIR, chunk)
            at += full * DIR
            one, two, three = (piece(freq * DIR + g * 8, 8, full) for g in range(per_freq))
            out_ref[part, pl.ds(at, 8), :] = jnp.where(low, one, two)
            folded = jnp.where(low, three, pltpu.roll(three, 4, 0))
            out_ref[part, pl.ds(at + 8, 8), :] = jnp.concatenate([folded[:4], speed_ref[freq]], axis=0)
        out_ref[part, pl.ds(freqs * span_rows, shared.shape[0]), :] = shared


BLOCK = 8
PER_STEP = 4


def slab_kernel(
    parts,
    tile_rows,
    full,
    freqs,
    recv_ref,
    out_ref,
    onehot,
    first,
    second,
    table,
    faces_x,
    faces_y,
    moved_ref,
    done_ref,
    sems,
):
    slab_rows = parts * tile_rows
    half = LANES // 2
    span_rows = full * DIR + 16
    shared_base = freqs * span_rows
    highs = slab_rows // 2
    width = freqs * 2 * DIR
    low_lane = lax.broadcasted_iota(jnp.int32, (1, LANES), 1) < half
    low_lanes = lax.broadcasted_iota(jnp.int32, (8, LANES), 1) < half
    low_wide = lax.broadcasted_iota(jnp.int32, (DIR, LANES), 1) < half
    top_rows = lax.broadcasted_iota(jnp.int32, (8, LANES), 0) < 4
    cell_iota = lax.broadcasted_iota(jnp.int32, (2 * LANES, LANES), 0).astype(jnp.float32).astype(jnp.bfloat16)
    high_iota = lax.broadcasted_iota(jnp.int32, (highs, LANES), 0)

    def cells_of(owner, chunk):
        return recv_ref[owner, pl.ds(shared_base + 3 * tile_rows + chunk, 1), :].astype(jnp.int32)

    owner_rows = full * LANES + half
    capacity = tile_rows * LANES // parts
    spans = []
    for begin in range(0, owner_rows, half):
        tiles = [
            t
            for t in range(parts)
            if owner_rows - capacity * (parts - t) < begin + half and capacity * (t + 1) > begin
        ]
        spans.append(range(tiles[0] * tile_rows // 2, (tiles[-1] + 1) * tile_rows // 2))
    offsets = [parts // 2 * LANES * chunk for chunk in range(len(spans))]
    columns = [[] for _ in spans]

    def place(chunk, cells, values):
        span = pl.ds(offsets[chunk] + len(columns[chunk]) * LANES, LANES)
        high = cells // (2 * LANES)
        low = (cells - high * (2 * LANES)).astype(jnp.float32)
        low = jnp.broadcast_to(low, (2 * LANES, LANES)).astype(jnp.bfloat16)
        onehot[:, span] = jnp.where(cell_iota == low, 1.0, 0.0).astype(jnp.bfloat16)
        pieces = []
        for value in values:
            head = value.astype(jnp.bfloat16).astype(jnp.float32)
            pieces += [head, value - head]
        both = jnp.concatenate(pieces, axis=0).astype(jnp.bfloat16)
        column = []
        for h in spans[chunk]:
            pick = jnp.broadcast_to((high == h).astype(jnp.float32), (width, LANES)).astype(jnp.bfloat16)
            column.append(both * pick)
        column.append((high_iota == high).astype(jnp.float32).astype(jnp.bfloat16))
        columns[chunk].append(jnp.concatenate(column, axis=0))

    for pair in range(parts // 2):
        even, odd = 2 * pair, 2 * pair + 1
        for chunk in range(full):
            here, there = (
                [recv_ref[owner, pl.ds(f * span_rows + chunk * DIR, DIR), :] for f in range(freqs)]
                for owner in (even, odd)
            )
            cells, cells_there = cells_of(even, chunk), cells_of(odd, chunk)
            for side in range(2):
                place(
                    2 * chunk + side,
                    jnp.where(low_lane, cells, cells_there),
                    [jnp.where(low_wide, a, b) for a, b in zip(here, there)],
                )
                here, there, cells, cells_there = there, here, cells_there, cells

        def merged(offset):
            own, other = recv_ref[even, pl.ds(offset, 8), :], recv_ref[odd, pl.ds(offset, 8), :]
            return (
                jnp.where(low_lanes, own, pltpu.roll(other, half, 1)),
                jnp.where(low_lanes, pltpu.roll(own, half, 1), other),
            )

        values = []
        for f in range(freqs):
            one, two = merged(f * span_rows + full * DIR)
            three, four = merged(f * span_rows + full * DIR + 8)
            values.append(
                jnp.concatenate([one, two, jnp.where(top_rows, three, pltpu.roll(four, 4, 0))], axis=0)
            )
        place(2 * full, jnp.where(low_lane, cells_of(even, full), cells_of(odd, full)), values)

    lane = lax.broadcasted_iota(jnp.int32, (slab_rows, LANES), 1)
    zero_rows = jnp.zeros((8, LANES), jnp.float32)

    def gather(offset):
        return jnp.concatenate(
            [recv_ref[owner, pl.ds(offset, tile_rows), :] for owner in range(parts)], axis=0
        )

    gain = 0.5 * courant / 8.0
    slots = iter(range(table.shape[0]))

    def keep(rows):
        slot = next(slots)
        table[slot, pl.ds(8, rows.shape[0]), :] = rows
        return slot

    def face_x(rows):
        slot = next(slots)
        table[slot, pl.ds(0, 8), :] = zero_rows
        table[slot, pl.ds(8 + slab_rows, 8), :] = zero_rows
        table[slot, pl.ds(8, slab_rows), :] = rows
        faces = gain * (table[slot, pl.ds(7, slab_rows + 8), :] + table[slot, pl.ds(8, slab_rows + 8), :])
        table[slot, pl.ds(7, slab_rows + 8), :] = faces
        return slot

    def face_y(rows):
        after = jnp.where(lane < LANES - 1, pltpu.roll(rows, LANES - 1, 1), 0.0)
        before = jnp.where(lane > 0, pltpu.roll(rows, 1, 1), 0.0)
        return keep(gain * (rows + after)), keep(gain * (rows + before))

    speeds = [gather(f * span_rows + full * DIR + 12) for f in range(freqs)]
    current_x, current_y, turning = (gather(shared_base + kind * tile_rows) for kind in range(3))
    current_x_face, speed_x_face = face_x(current_x), [face_x(s) for s in speeds]
    current_y_faces, speed_y_faces = face_y(current_y), [face_y(s) for s in speeds]
    step_angle = 2.0 * math.pi / DIR
    sublane = lax.broadcasted_iota(jnp.int32, (8, LANES), 0)
    cosine0 = jnp.ones((8, LANES), jnp.float32)
    sine0 = jnp.zeros((8, LANES), jnp.float32)
    for d in range(1, 8):
        cosine0 = jnp.where(sublane == d, math.cos(d * step_angle), cosine0)
        sine0 = jnp.where(sublane == d, math.sin(d * step_angle), sine0)
    turns = [(math.cos(g * 8 * step_angle), math.sin(g * 8 * step_angle)) for g in range(DIR // 8)]
    cosine = jnp.concatenate([c * cosine0 - t * sine0 for c, t in turns], axis=0)
    sine = jnp.concatenate([c * sine0 + t * cosine0 for c, t in turns], axis=0)

    def row(slot, x):
        return table[slot, pl.ds(8 + x, 1), :]

    for f in range(freqs):
        for x in range(-1, slab_rows):
            faces_x[f, x + 1] = row(speed_x_face[f], x) * cosine + row(current_x_face, x)
        for x in range(slab_rows):
            for side in range(2):
                faces_y[f, side, x] = row(speed_y_faces[f][side], x) * sine + row(current_y_faces[side], x)

    scattered = [
        lax.dot_general(
            jnp.concatenate(column, axis=1),
            onehot[:, pl.ds(offset, len(column) * LANES)],
            (((1,), (1,)), ((), ())),
            preferred_element_type=jnp.float32,
        )
        for offset, column in zip(offsets, columns)
    ]
    nothing = jnp.zeros((DIR, LANES), jnp.float32)
    for f in range(freqs):
        for field in (first, second):
            for edge in (0, 1, slab_rows + 2, slab_rows + 3):
                field[f, edge] = nothing
        for h in range(highs):
            terms = []
            for span, product in zip(spans, scattered):
                if h in span:
                    at = (h - span[0]) * width + f * 2 * DIR
                    terms += [product[at : at + DIR], product[at + DIR : at + 2 * DIR]]
            total = sum(terms[1:], terms[0])
            first[f, 2 * h + 2] = total[:, :LANES]
            first[f, 2 * h + 3] = total[:, LANES:]
    named = sum(product[len(span) * width :] for span, product in zip(spans, scattered))

    land_slots = keep(named[:, :LANES]), keep(named[:, LANES:])
    ahead = jnp.maximum(turning, 0.0) * 0.125
    back = jnp.minimum(turning, 0.0) * 0.125
    bend_slots = [
        keep(rows)
        for rows in (
            -ahead,
            7.0 * ahead + 3.0 * back,
            1.0 - 3.0 * (ahead - back),
            -3.0 * ahead - 7.0 * back,
            back,
        )
    ]

    lane_wide = lax.broadcasted_iota(jnp.int32, (DIR, LANES), 1)

    def flux(speed, behind, centre3, onward3, beyond):
        positive = speed > 0.0
        near = jnp.where(positive, centre3, onward3)
        far = jnp.where(positive, behind, beyond)
        return speed * ((centre3 + onward3) + (near - far))

    def advance(field, step, carry, finish):
        carry = list(carry)
        for i in range(BLOCK):
            x = step * BLOCK + i
            sea = row(land_slots[i % 2], step * (BLOCK // 2) + i // 2)
            for f in range(freqs):
                entering, centre3 = carry[f]
                centre = field[f, x + 2]
                onward3 = 3.0 * field[f, x + 3]
                leaving = flux(faces_x[f, x + 1], field[f, x + 1], centre3, onward3, field[f, x + 4])
                up1 = jnp.where(lane_wide < LANES - 1, pltpu.roll(centre, LANES - 1, 1), 0.0)
                up2 = jnp.where(lane_wide < LANES - 2, pltpu.roll(centre, LANES - 2, 1), 0.0)
                down1 = jnp.where(lane_wide > 0, pltpu.roll(centre, 1, 1), 0.0)
                down2 = jnp.where(lane_wide > 1, pltpu.roll(centre, 2, 1), 0.0)
                right = flux(faces_y[f, 0, x], down1, centre3, 3.0 * up1, up2)
                left = flux(faces_y[f, 1, x], down2, 3.0 * down1, centre3, up1)
                finish(f, x, (centre - (leaving - entering) - (right - left)) * sea)
                carry[f] = leaving, onward3
        return tuple(carry)

    def enter(field):
        carry = []
        for f in range(freqs):
            start3 = 3.0 * field[f, 2]
            carry.append((flux(faces_x[f, 0], nothing, nothing, start3, field[f, 3]), start3))
        return tuple(carry)

    def store(f, x, moved):
        second[f, x + 2] = moved

    def turn(f, x, moved):
        for g in range(DIR // 8):
            at = (f * DIR + g * 8) * slab_rows + x
            moved_ref[pl.ds(at, 8, stride=slab_rows), :] = moved[g * 8 : g * 8 + 8]

    def copy_out(step):
        part = pl.ds(pl.multiple_of(step * BLOCK, BLOCK), BLOCK)
        return pltpu.make_async_copy(done_ref.at[:, part, :], out_ref.at[:, part, :], sems.at[step])

    def final(block, carry):
        carry = advance(second, block, carry, turn)
        at = pl.multiple_of(block * BLOCK, BLOCK)
        weights = [table[slot, pl.ds(8 + at, BLOCK), :] for slot in bend_slots]
        for f in range(freqs):
            ring = [moved_ref[pl.ds((f * DIR + d) * slab_rows + at, BLOCK), :] for d in range(DIR)]
            for d in range(DIR):
                bent = weights[2] * ring[d]
                for k in (0, 1, 3, 4):
                    bent = bent + weights[k] * ring[(d + k - 2) % DIR]
                done_ref[f * DIR + d, pl.ds(at, BLOCK), :] = bent
        copy_out(block).start()
        return carry

    def sweep(one_block, carry):
        def body(step, carry):
            for i in range(PER_STEP):
                carry = one_block(step * PER_STEP + i, carry)
            return carry

        lax.fori_loop(0, slab_rows // BLOCK // PER_STEP, body, carry)

    sweep(lambda block, carry: advance(first, block, carry, store), enter(first))
    sweep(final, enter(second))
    for block in range(slab_rows // BLOCK):
        copy_out(block).wait()


def slab_plan(spectra, wind, growth, damping, row_cell, group_speed, current, turning):
    parts = lax.axis_size(GROUP)
    rows, comps = spectra.shape
    tile_rows = turning.shape[0]
    freqs = comps // parts // DIR
    full = rows // LANES
    slab_rows = parts * tile_rows
    depth = parts * rows
    highs = slab_rows // 2
    block_rows = -(-(freqs * (full * DIR + 16) + 3 * tile_rows + full + 1) // 8) * 8
    packed = pl.pallas_call(
        functools.partial(pack_kernel, parts, freqs),
        out_shape=pltpu.VMEM((parts, block_rows, LANES), jnp.float32),
        compiler_params=pltpu.CompilerParams(vmem_limit_bytes=56 * 1024 * 1024),
        name="pack",
    )(spectra, wind, growth, damping, row_cell, group_speed, current, turning)
    arrived = lax.all_to_all(packed, GROUP, split_axis=0, concat_axis=0, tiled=True)
    out = pl.pallas_call(
        functools.partial(slab_kernel, parts, tile_rows, full, freqs),
        out_shape=jax.ShapeDtypeStruct((freqs * DIR, slab_rows, LANES), jnp.float32),
        in_specs=[pl.BlockSpec(memory_space=pltpu.VMEM)],
        out_specs=pl.BlockSpec(memory_space=pl.ANY),
        scratch_shapes=[
            pltpu.VMEM((2 * LANES, depth), jnp.bfloat16),
            pltpu.VMEM((freqs, slab_rows + 4, DIR, LANES), jnp.float32),
            pltpu.VMEM((freqs, slab_rows + 4, DIR, LANES), jnp.float32),
            pltpu.VMEM((10 + 3 * freqs, slab_rows + 16, LANES), jnp.float32),
            pltpu.VMEM((freqs, slab_rows + 1, DIR, LANES), jnp.float32),
            pltpu.VMEM((freqs, 2, slab_rows, DIR, LANES), jnp.float32),
            pltpu.VMEM((freqs * DIR * slab_rows, LANES), jnp.float32),
            pltpu.VMEM((freqs * DIR, slab_rows, LANES), jnp.float32),
            pltpu.SemaphoreType.DMA((slab_rows // BLOCK,)),
        ],
        compiler_params=pltpu.CompilerParams(vmem_limit_bytes=32 * 1024 * 1024),
        name="slab",
    )(arrived)
    return out.reshape(1, freqs * DIR, slab_rows, LANES)


def shards(*arrays):
    spectra, land_mask = arrays[0], arrays[5]
    parts = lax.axis_size(GROUP)
    rows, comps = spectra.shape
    whole_frequencies = comps == parts * 2 * DIR
    fits = rows % LANES == LANES // 2 and land_mask.shape == (4, LANES) and parts % 2 == 0
    if whole_frequencies and fits:
        return slab_plan(*arrays[:5], *arrays[6:])
    return tile_plan(*arrays)


def solution(mesh):
    placed = (
        P(("groups", "pts", "comp"), "sub"),
        P(("groups", "pts", "comp")),
        P("sub"),
        P("sub"),
        P(("groups", "pts", "comp")),
        P(("groups", "pts", "comp"), None),
        P(("groups", "sub"), ("pts", "comp"), None),
        P("groups", ("pts", "comp"), None),
        P(("groups", "pts", "comp"), None),
    )
    return jax.shard_map(
        shards,
        mesh=mesh,
        in_specs=placed,
        out_specs=P("sub", ("pts", "comp"), "groups", None),
        check_vma=False,
    )
```

```python
import functools
import math
import jax
import jax.numpy as jnp
from jax import lax
from jax.experimental import pallas as pl
from jax.experimental.pallas import tpu as pltpu
from jax.sharding import PartitionSpec as P

DIR = 24
SUBSTEPS = 2
LANES = 128
GROUP = ("pts", "comp")


courant = 0.35


def with_halo(cells, sides, width):
    for axis, dim in sides:
        count = lax.axis_size(axis)
        ends = count - 1
        head = lax.slice_in_dim(cells, 0, width, axis=dim)
        tail = lax.slice_in_dim(cells, cells.shape[dim] - width, cells.shape[dim], axis=dim)
        cells = jnp.concatenate(
            [
                lax.ppermute(tail, axis, [(i, (i + 1) % count) for i in range(ends)]),
                cells,
                lax.ppermute(head, axis, [((i + 1) % count, i) for i in range(ends)]),
            ],
            axis=dim,
        )
    return cells


def take_slice(values, first_index, extent, along_axis):
    return lax.slice_in_dim(values, first_index, first_index + extent, axis=along_axis)


def upwind_divergence(padded, motion, along_axis):
    length = padded.shape[along_axis] - 4
    face_count = length + 1
    behind = take_slice(padded, 0, face_count, along_axis)
    centre = take_slice(padded, 1, face_count, along_axis)
    onward = take_slice(padded, 2, face_count, along_axis)
    beyond = take_slice(padded, 3, face_count, along_axis)
    left_face = (6.0 * centre + 3.0 * onward - behind) * 0.125
    right_face = (3.0 * centre + 6.0 * onward - beyond) * 0.125
    face_speed = 0.5 * (
        take_slice(motion, 1, face_count, along_axis)
        + take_slice(motion, 2, face_count, along_axis)
    )
    fluxes = jnp.maximum(face_speed, 0.0) * left_face + jnp.minimum(face_speed, 0.0) * right_face
    return take_slice(fluxes, 1, length, along_axis) - take_slice(fluxes, 0, length, along_axis)


def substep(extended, speed_x, speed_y, sea_mask):
    across = upwind_divergence(extended, speed_x, 1)
    centre_part = extended[:, 2:-2]
    padding = ((0, 0), (0, 0), (2, 2))
    sideways = upwind_divergence(jnp.pad(centre_part, padding), jnp.pad(speed_y, padding), 2)
    return (centre_part - courant * (across + sideways)) * sea_mask


def direction_tables(directions):
    angles = jnp.arange(directions, dtype=jnp.float32) * (2.0 * jnp.pi / directions)
    return (jnp.cos(angles), jnp.sin(angles))


def source_term(values, wind_speed, growth, damping):
    return values * jnp.exp(wind_speed[:, None] * growth[None, :] - damping[None, :])


def velocities(stacked, freq_count):
    cosine_table, sine_table = direction_tables(DIR)
    celerity = stacked[:freq_count][:, None]
    shape_out = (freq_count * DIR,) + stacked.shape[1:]
    speed_x = (
        celerity * cosine_table[None, :, None, None] + stacked[freq_count][None, None]
    ).reshape(shape_out)
    speed_y = (
        celerity * sine_table[None, :, None, None] + stacked[freq_count + 1][None, None]
    ).reshape(shape_out)
    return (speed_x, speed_y)


def deliver(bulk_rows, small_rows):
    return (
        lax.all_to_all(bulk_rows, GROUP, split_axis=0, concat_axis=0, tiled=True),
        lax.all_to_all(small_rows, GROUP, split_axis=0, concat_axis=0, tiled=True),
    )


def tile_plan(spectra, wind, growth, damping, row_cell, land_mask, group_speed, current, turning):
    tile_count = lax.axis_size(GROUP)
    comp_width = spectra.shape[1]
    tile_rows, tile_cols = land_mask.shape
    cell_count = tile_rows * tile_cols
    capacity = cell_count // tile_count
    target = row_cell // cell_count
    local_cell = (row_cell - target * cell_count).astype(jnp.float32)
    matches = (target[:, None] == jnp.arange(tile_count, dtype=jnp.int32)[None, :]).astype(
        jnp.int32
    )
    bucket_slot = jnp.sum((jnp.cumsum(matches, axis=0) - 1) * matches, axis=1)

    def bucket(values, filler):
        shape_out = (tile_count, capacity) + values.shape[1:]
        return jnp.full(shape_out, filler, jnp.float32).at[target, bucket_slot].set(values)

    bulk_rows = bucket(source_term(spectra, wind, growth, damping), 0.0)
    small_rows = bucket(local_cell[:, None], float(cell_count))
    bulk_back, small_back = deliver(bulk_rows, small_rows)
    cell_index = small_back[:, :, 0].reshape(-1).astype(jnp.int32)
    flat_values = bulk_back.reshape((tile_count * capacity,) + bulk_back.shape[2:])
    tile_field = (
        jnp.zeros((cell_count,) + bulk_back.shape[2:], jnp.float32)
        .at[cell_index]
        .set(flat_values, mode="drop")
    )
    spectrum = tile_field.T.reshape(comp_width, tile_rows, tile_cols)
    freq_count = comp_width // DIR
    reach = 2 * SUBSTEPS
    stacked = jnp.concatenate([group_speed, current, land_mask.astype(jnp.float32)[None]], axis=0)
    rimmed = with_halo(stacked, ((GROUP, 1),), 2 * SUBSTEPS)
    speed_x, speed_y = velocities(rimmed, freq_count)
    sea_rim = rimmed[freq_count + 2 :]

    def window(values, margin):
        return lax.slice_in_dim(values, reach - margin, reach + tile_rows + margin, axis=1)

    for repeat in range(SUBSTEPS):
        extended = with_halo(spectrum, ((GROUP, 1),), 2)
        spectrum = substep(extended, window(speed_x, 2), window(speed_y, 0), window(sea_rim, 0)[0])
    blocks = spectrum.reshape(freq_count, DIR, tile_rows, tile_cols)
    wrapped = jnp.concatenate([blocks[:, -2:], blocks, blocks[:, :2]], axis=1)
    turning_full = jnp.broadcast_to(turning[None, None], wrapped.shape)
    blocks = blocks - upwind_divergence(wrapped, turning_full, 1)
    spectrum = blocks.reshape(comp_width, tile_rows, tile_cols)
    shipped = lax.all_to_all(spectrum, GROUP, split_axis=0, concat_axis=1, tiled=True)
    return shipped[None]


def pack_kernel(
    parts,
    freqs,
    spectra_ref,
    wind_ref,
    growth_ref,
    damping_ref,
    cell_ref,
    speed_ref,
    current_ref,
    turning_ref,
    out_ref,
):
    rows, comps = spectra_ref.shape
    half = LANES // 2
    full = rows // LANES
    padded = (full + 1) * LANES
    low = lax.broadcasted_iota(jnp.int32, (8, LANES), 1) < half
    per_freq = DIR // 8
    span_rows = full * DIR + 16

    def extended(row, filler):
        return jnp.concatenate([row[None], jnp.full((1, half), filler, jnp.float32)], axis=1)

    def as_columns(row):
        return jnp.broadcast_to(row, (LANES, padded)).T

    cells = cell_ref[...].astype(jnp.float32)
    keys = extended(cells, 1e9)
    key_cols = as_columns(keys)
    ranks = jnp.concatenate(
        [
            jnp.sum(
                jnp.where(key_cols < keys[:, c * LANES : (c + 1) * LANES], 1.0, 0.0), axis=0, keepdims=True
            )
            for c in range(full + 1)
        ],
        axis=1,
    )
    place = lax.broadcasted_iota(jnp.int32, (padded, padded), 0)
    odd = lax.axis_index(GROUP) % 2 == 1
    swapped = jnp.where(place % LANES < half, place + half, place - half)
    place = jnp.where((place < full * LANES) & odd, swapped, place)
    place = jnp.where(place < rows, place, place - half).astype(jnp.float32)
    order = jnp.where(place == ranks, 1.0, 0.0).astype(jnp.bfloat16)

    wind_cols = as_columns(extended(wind_ref[...], 0.0))
    turned = []
    for block in range(comps // LANES):
        lanes = pl.ds(block * LANES, LANES)
        growth = growth_ref[lanes][None]
        damping = damping_ref[lanes][None]

        def source(first, count):
            span = pl.ds(first, count)
            return spectra_ref[span, lanes] * jnp.exp(
                wind_cols[first : first + count] * growth - damping
            )

        pieces = [source(c * LANES, LANES).T for c in range(full)]
        last = jnp.concatenate([source(full * LANES, half), jnp.zeros((half, LANES), jnp.float32)], axis=0)
        turned.append(jnp.concatenate(pieces + [last.T], axis=1))
    turned.append(jnp.broadcast_to(extended(cells, 0.0), (16, padded)))
    values = jnp.concatenate(turned, axis=0)
    head = values.astype(jnp.bfloat16)
    rest = (values - head.astype(jnp.float32)).astype(jnp.bfloat16)
    both = lax.dot_general(
        jnp.concatenate([head, rest], axis=0),
        order,
        (((1,), (1,)), ((), ())),
        preferred_element_type=jnp.float32,
    )

    def piece(first, count, chunk):
        lanes = slice(chunk * LANES, (chunk + 1) * LANES)
        return both[first : first + count, lanes] + both[comps + 16 + first : comps + 16 + first + count, lanes]

    shared = jnp.concatenate(
        [current_ref[0], current_ref[1], turning_ref[...]] + [piece(comps, 1, c) for c in range(full + 1)],
        axis=0,
    )
    for part in range(parts):
        for f in range(freqs):
            freq = part * freqs + f
            at = f * span_rows
            for chunk in range(full):
                out_ref[part, pl.ds(at + chunk * DIR, DIR), :] = piece(freq * DIR, DIR, chunk)
            at += full * DIR
            one, two, three = (piece(freq * DIR + g * 8, 8, full) for g in range(per_freq))
            out_ref[part, pl.ds(at, 8), :] = jnp.where(low, one, two)
            folded = jnp.where(low, three, pltpu.roll(three, 4, 0))
            out_ref[part, pl.ds(at + 8, 8), :] = jnp.concatenate([folded[:4], speed_ref[freq]], axis=0)
        out_ref[part, pl.ds(freqs * span_rows, shared.shape[0]), :] = shared


BLOCK = 8


def slab_kernel(
    parts,
    tile_rows,
    full,
    freqs,
    recv_ref,
    out_ref,
    onehot,
    first,
    second,
    table,
    faces_x,
    faces_y,
    moved_ref,
    done_ref,
    sems,
):
    slab_rows = parts * tile_rows
    half = LANES // 2
    span_rows = full * DIR + 16
    shared_base = freqs * span_rows
    highs = slab_rows // 2
    width = freqs * 2 * DIR
    low_lane = lax.broadcasted_iota(jnp.int32, (1, LANES), 1) < half
    low_lanes = lax.broadcasted_iota(jnp.int32, (8, LANES), 1) < half
    low_wide = lax.broadcasted_iota(jnp.int32, (DIR, LANES), 1) < half
    top_rows = lax.broadcasted_iota(jnp.int32, (8, LANES), 0) < 4
    cell_iota = lax.broadcasted_iota(jnp.int32, (2 * LANES, LANES), 0).astype(jnp.float32).astype(jnp.bfloat16)
    high_iota = lax.broadcasted_iota(jnp.int32, (highs, LANES), 0)

    def cells_of(owner, chunk):
        return recv_ref[owner, pl.ds(shared_base + 3 * tile_rows + chunk, 1), :].astype(jnp.int32)

    owner_rows = full * LANES + half
    capacity = tile_rows * LANES // parts
    spans = []
    for begin in range(0, owner_rows, half):
        tiles = [
            t
            for t in range(parts)
            if owner_rows - capacity * (parts - t) < begin + half and capacity * (t + 1) > begin
        ]
        spans.append(range(tiles[0] * tile_rows // 2, (tiles[-1] + 1) * tile_rows // 2))
    offsets = [parts // 2 * LANES * chunk for chunk in range(len(spans))]
    columns = [[] for _ in spans]

    def place(chunk, cells, values):
        span = pl.ds(offsets[chunk] + len(columns[chunk]) * LANES, LANES)
        high = cells // (2 * LANES)
        low = (cells - high * (2 * LANES)).astype(jnp.float32)
        low = jnp.broadcast_to(low, (2 * LANES, LANES)).astype(jnp.bfloat16)
        onehot[:, span] = jnp.where(cell_iota == low, 1.0, 0.0).astype(jnp.bfloat16)
        pieces = []
        for value in values:
            head = value.astype(jnp.bfloat16).astype(jnp.float32)
            pieces += [head, value - head]
        both = jnp.concatenate(pieces, axis=0).astype(jnp.bfloat16)
        column = []
        for h in spans[chunk]:
            pick = jnp.broadcast_to((high == h).astype(jnp.float32), (width, LANES)).astype(jnp.bfloat16)
            column.append(both * pick)
        column.append((high_iota == high).astype(jnp.float32).astype(jnp.bfloat16))
        columns[chunk].append(jnp.concatenate(column, axis=0))

    for pair in range(parts // 2):
        even, odd = 2 * pair, 2 * pair + 1
        for chunk in range(full):
            here, there = (
                [recv_ref[owner, pl.ds(f * span_rows + chunk * DIR, DIR), :] for f in range(freqs)]
                for owner in (even, odd)
            )
            cells, cells_there = cells_of(even, chunk), cells_of(odd, chunk)
            for side in range(2):
                place(
                    2 * chunk + side,
                    jnp.where(low_lane, cells, cells_there),
                    [jnp.where(low_wide, a, b) for a, b in zip(here, there)],
                )
                here, there, cells, cells_there = there, here, cells_there, cells

        def merged(offset):
            own, other = recv_ref[even, pl.ds(offset, 8), :], recv_ref[odd, pl.ds(offset, 8), :]
            return (
                jnp.where(low_lanes, own, pltpu.roll(other, half, 1)),
                jnp.where(low_lanes, pltpu.roll(own, half, 1), other),
            )

        values = []
        for f in range(freqs):
            one, two = merged(f * span_rows + full * DIR)
            three, four = merged(f * span_rows + full * DIR + 8)
            values.append(
                jnp.concatenate([one, two, jnp.where(top_rows, three, pltpu.roll(four, 4, 0))], axis=0)
            )
        place(2 * full, jnp.where(low_lane, cells_of(even, full), cells_of(odd, full)), values)

    lane = lax.broadcasted_iota(jnp.int32, (slab_rows, LANES), 1)
    zero_rows = jnp.zeros((8, LANES), jnp.float32)

    def gather(offset):
        return jnp.concatenate(
            [recv_ref[owner, pl.ds(offset, tile_rows), :] for owner in range(parts)], axis=0
        )

    gain = 0.5 * courant / 8.0
    slots = iter(range(table.shape[0]))

    def keep(rows):
        slot = next(slots)
        table[slot, pl.ds(8, rows.shape[0]), :] = rows
        return slot

    def face_x(rows):
        slot = next(slots)
        table[slot, pl.ds(0, 8), :] = zero_rows
        table[slot, pl.ds(8 + slab_rows, 8), :] = zero_rows
        table[slot, pl.ds(8, slab_rows), :] = rows
        faces = gain * (table[slot, pl.ds(7, slab_rows + 8), :] + table[slot, pl.ds(8, slab_rows + 8), :])
        table[slot, pl.ds(7, slab_rows + 8), :] = faces
        return slot

    def face_y(rows):
        after = jnp.where(lane < LANES - 1, pltpu.roll(rows, LANES - 1, 1), 0.0)
        before = jnp.where(lane > 0, pltpu.roll(rows, 1, 1), 0.0)
        return keep(gain * (rows + after)), keep(gain * (rows + before))

    speeds = [gather(f * span_rows + full * DIR + 12) for f in range(freqs)]
    current_x, current_y, turning = (gather(shared_base + kind * tile_rows) for kind in range(3))
    current_x_face, speed_x_face = face_x(current_x), [face_x(s) for s in speeds]
    current_y_faces, speed_y_faces = face_y(current_y), [face_y(s) for s in speeds]
    step_angle = 2.0 * math.pi / DIR
    sublane = lax.broadcasted_iota(jnp.int32, (8, LANES), 0)
    cosine0 = jnp.ones((8, LANES), jnp.float32)
    sine0 = jnp.zeros((8, LANES), jnp.float32)
    for d in range(1, 8):
        cosine0 = jnp.where(sublane == d, math.cos(d * step_angle), cosine0)
        sine0 = jnp.where(sublane == d, math.sin(d * step_angle), sine0)
    turns = [(math.cos(g * 8 * step_angle), math.sin(g * 8 * step_angle)) for g in range(DIR // 8)]
    cosine = jnp.concatenate([c * cosine0 - t * sine0 for c, t in turns], axis=0)
    sine = jnp.concatenate([c * sine0 + t * cosine0 for c, t in turns], axis=0)

    def row(slot, x):
        return table[slot, pl.ds(8 + x, 1), :]

    for f in range(freqs):
        for x in range(-1, slab_rows):
            faces_x[f, x + 1] = row(speed_x_face[f], x) * cosine + row(current_x_face, x)
        for x in range(slab_rows):
            for side in range(2):
                faces_y[f, side, x] = row(speed_y_faces[f][side], x) * sine + row(current_y_faces[side], x)

    ahead = jnp.maximum(turning, 0.0) * 0.125
    back = jnp.minimum(turning, 0.0) * 0.125
    bend_slots = [
        keep(rows)
        for rows in (
            -ahead,
            7.0 * ahead + 3.0 * back,
            1.0 - 3.0 * (ahead - back),
            -3.0 * ahead - 7.0 * back,
            back,
        )
    ]
    land_slots = next(slots), next(slots)
    nothing = jnp.zeros((DIR, LANES), jnp.float32)
    for f in range(freqs):
        for field in (first, second):
            for edge in (0, 1, slab_rows + 2, slab_rows + 3):
                field[f, edge] = nothing
    lane_wide = lax.broadcasted_iota(jnp.int32, (DIR, LANES), 1)

    def flux(speed, behind, centre3, onward3, beyond):
        positive = speed > 0.0
        near = jnp.where(positive, centre3, onward3)
        far = jnp.where(positive, behind, beyond)
        return speed * ((centre3 + onward3) + (near - far))

    def advance(field, x, carry, finish):
        sea = row(land_slots[x % 2], x // 2)
        for f in range(freqs):
            if x == 0:
                start3 = 3.0 * field[f, 2]
                carry[f] = flux(faces_x[f, 0], nothing, nothing, start3, field[f, 3]), start3
            entering, centre3 = carry[f]
            centre = field[f, x + 2]
            onward3 = 3.0 * field[f, x + 3]
            leaving = flux(faces_x[f, x + 1], field[f, x + 1], centre3, onward3, field[f, x + 4])
            up1 = jnp.where(lane_wide < LANES - 1, pltpu.roll(centre, LANES - 1, 1), 0.0)
            up2 = jnp.where(lane_wide < LANES - 2, pltpu.roll(centre, LANES - 2, 1), 0.0)
            down1 = jnp.where(lane_wide > 0, pltpu.roll(centre, 1, 1), 0.0)
            down2 = jnp.where(lane_wide > 1, pltpu.roll(centre, 2, 1), 0.0)
            right = flux(faces_y[f, 0, x], down1, centre3, 3.0 * up1, up2)
            left = flux(faces_y[f, 1, x], down2, 3.0 * down1, centre3, up1)
            finish(f, x, (centre - (leaving - entering) - (right - left)) * sea)
            carry[f] = leaving, onward3

    def store(f, x, moved):
        second[f, x + 2] = moved

    def turn(f, x, moved):
        for g in range(DIR // 8):
            at = (f * DIR + g * 8) * slab_rows + x
            moved_ref[pl.ds(at, 8, stride=slab_rows), :] = moved[g * 8 : g * 8 + 8]

    def copy_out(block):
        part = pl.ds(block * BLOCK, BLOCK)
        return pltpu.make_async_copy(done_ref.at[:, part, :], out_ref.at[:, part, :], sems.at[block])

    def refract(block):
        at = block * BLOCK
        weights = [table[slot, pl.ds(8 + at, BLOCK), :] for slot in bend_slots]
        for f in range(freqs):
            ring = [moved_ref[pl.ds((f * DIR + d) * slab_rows + at, BLOCK), :] for d in range(DIR)]
            for d in range(DIR):
                bent = weights[2] * ring[d]
                for k in (0, 1, 3, 4):
                    bent = bent + weights[k] * ring[(d + k - 2) % DIR]
                done_ref[f * DIR + d, pl.ds(at, BLOCK), :] = bent
        copy_out(block).start()

    sums = [None] * highs
    named = [None, None]
    complete = 0
    reached = [0, 0, 0]
    carries = [[None] * freqs, [None] * freqs]
    for part, (span, offset, column) in enumerate(zip(spans, offsets, columns)):
        product = lax.dot_general(
            jnp.concatenate(column, axis=1),
            onehot[:, pl.ds(offset, len(column) * LANES)],
            (((1,), (1,)), ((), ())),
            preferred_element_type=jnp.float32,
        )
        for h in span:
            at = (h - span[0]) * width
            for f in range(freqs):
                here = at + f * 2 * DIR
                term = product[here : here + DIR] + product[here + DIR : here + 2 * DIR]
                sums[h] = sums[h] or []
                if len(sums[h]) > f:
                    sums[h][f] = sums[h][f] + term
                else:
                    sums[h].append(term)
        for side in range(2):
            hit = product[len(span) * width :, side * LANES : (side + 1) * LANES]
            named[side] = hit if part == 0 else named[side] + hit
            table[land_slots[side], pl.ds(8, highs), :] = named[side]
        until = highs if part + 1 == len(spans) else spans[part + 1][0]
        for h in range(complete, until):
            for f in range(freqs):
                first[f, 2 * h + 2] = sums[h][f][:, :LANES]
                first[f, 2 * h + 3] = sums[h][f][:, LANES:]
        complete = until
        ready = 2 * complete
        for stage, (field, finish) in enumerate(((first, store), (second, turn))):
            ready = slab_rows if ready == slab_rows else max(ready - 2, 0)
            for x in range(reached[stage], ready):
                advance(field, x, carries[stage], finish)
            reached[stage] = ready
        for block in range(reached[2], ready // BLOCK):
            refract(block)
        reached[2] = ready // BLOCK
    for block in range(slab_rows // BLOCK):
        copy_out(block).wait()


def slab_plan(spectra, wind, growth, damping, row_cell, group_speed, current, turning):
    parts = lax.axis_size(GROUP)
    rows, comps = spectra.shape
    tile_rows = turning.shape[0]
    freqs = comps // parts // DIR
    full = rows // LANES
    slab_rows = parts * tile_rows
    depth = parts * rows
    highs = slab_rows // 2
    block_rows = -(-(freqs * (full * DIR + 16) + 3 * tile_rows + full + 1) // 8) * 8
    packed = pl.pallas_call(
        functools.partial(pack_kernel, parts, freqs),
        out_shape=pltpu.VMEM((parts, block_rows, LANES), jnp.float32),
        compiler_params=pltpu.CompilerParams(vmem_limit_bytes=56 * 1024 * 1024),
        name="pack",
    )(spectra, wind, growth, damping, row_cell, group_speed, current, turning)
    arrived = lax.all_to_all(packed, GROUP, split_axis=0, concat_axis=0, tiled=True)
    out = pl.pallas_call(
        functools.partial(slab_kernel, parts, tile_rows, full, freqs),
        out_shape=jax.ShapeDtypeStruct((freqs * DIR, slab_rows, LANES), jnp.float32),
        in_specs=[pl.BlockSpec(memory_space=pltpu.VMEM)],
        out_specs=pl.BlockSpec(memory_space=pl.ANY),
        scratch_shapes=[
            pltpu.VMEM((2 * LANES, depth), jnp.bfloat16),
            pltpu.VMEM((freqs, slab_rows + 4, DIR, LANES), jnp.float32),
            pltpu.VMEM((freqs, slab_rows + 4, DIR, LANES), jnp.float32),
            pltpu.VMEM((10 + 3 * freqs, slab_rows + 16, LANES), jnp.float32),
            pltpu.VMEM((freqs, slab_rows + 1, DIR, LANES), jnp.float32),
            pltpu.VMEM((freqs, 2, slab_rows, DIR, LANES), jnp.float32),
            pltpu.VMEM((freqs * DIR * slab_rows, LANES), jnp.float32),
            pltpu.VMEM((freqs * DIR, slab_rows, LANES), jnp.float32),
            pltpu.SemaphoreType.DMA((slab_rows // BLOCK,)),
        ],
        compiler_params=pltpu.CompilerParams(vmem_limit_bytes=32 * 1024 * 1024),
        name="slab",
    )(arrived)
    return out.reshape(1, freqs * DIR, slab_rows, LANES)


def shards(*arrays):
    spectra, land_mask = arrays[0], arrays[5]
    parts = lax.axis_size(GROUP)
    rows, comps = spectra.shape
    whole_frequencies = comps == parts * 2 * DIR
    fits = rows % LANES == LANES // 2 and land_mask.shape == (4, LANES) and parts % 2 == 0
    if whole_frequencies and fits:
        return slab_plan(*arrays[:5], *arrays[6:])
    return tile_plan(*arrays)


def solution(mesh):
    placed = (
        P(("groups", "pts", "comp"), "sub"),
        P(("groups", "pts", "comp")),
        P("sub"),
        P("sub"),
        P(("groups", "pts", "comp")),
        P(("groups", "pts", "comp"), None),
        P(("groups", "sub"), ("pts", "comp"), None),
        P("groups", ("pts", "comp"), None),
        P(("groups", "pts", "comp"), None),
    )
    return jax.shard_map(
        shards,
        mesh=mesh,
        in_specs=placed,
        out_specs=P("sub", ("pts", "comp"), "groups", None),
        check_vma=False,
    )
```

```python
import functools
import math
import jax
import jax.numpy as jnp
from jax import lax
from jax.experimental import pallas as pl
from jax.experimental.pallas import tpu as pltpu
from jax.sharding import PartitionSpec as P

DIR = 24
SUBSTEPS = 2
LANES = 128
GROUP = ("pts", "comp")


courant = 0.35


def with_halo(cells, sides, width):
    for axis, dim in sides:
        count = lax.axis_size(axis)
        ends = count - 1
        head = lax.slice_in_dim(cells, 0, width, axis=dim)
        tail = lax.slice_in_dim(cells, cells.shape[dim] - width, cells.shape[dim], axis=dim)
        cells = jnp.concatenate(
            [
                lax.ppermute(tail, axis, [(i, (i + 1) % count) for i in range(ends)]),
                cells,
                lax.ppermute(head, axis, [((i + 1) % count, i) for i in range(ends)]),
            ],
            axis=dim,
        )
    return cells


def take_slice(values, first_index, extent, along_axis):
    return lax.slice_in_dim(values, first_index, first_index + extent, axis=along_axis)


def upwind_divergence(padded, motion, along_axis):
    length = padded.shape[along_axis] - 4
    face_count = length + 1
    behind = take_slice(padded, 0, face_count, along_axis)
    centre = take_slice(padded, 1, face_count, along_axis)
    onward = take_slice(padded, 2, face_count, along_axis)
    beyond = take_slice(padded, 3, face_count, along_axis)
    left_face = (6.0 * centre + 3.0 * onward - behind) * 0.125
    right_face = (3.0 * centre + 6.0 * onward - beyond) * 0.125
    face_speed = 0.5 * (
        take_slice(motion, 1, face_count, along_axis)
        + take_slice(motion, 2, face_count, along_axis)
    )
    fluxes = jnp.maximum(face_speed, 0.0) * left_face + jnp.minimum(face_speed, 0.0) * right_face
    return take_slice(fluxes, 1, length, along_axis) - take_slice(fluxes, 0, length, along_axis)


def substep(extended, speed_x, speed_y, sea_mask):
    across = upwind_divergence(extended, speed_x, 1)
    centre_part = extended[:, 2:-2]
    padding = ((0, 0), (0, 0), (2, 2))
    sideways = upwind_divergence(jnp.pad(centre_part, padding), jnp.pad(speed_y, padding), 2)
    return (centre_part - courant * (across + sideways)) * sea_mask


def direction_tables(directions):
    angles = jnp.arange(directions, dtype=jnp.float32) * (2.0 * jnp.pi / directions)
    return (jnp.cos(angles), jnp.sin(angles))


def source_term(values, wind_speed, growth, damping):
    return values * jnp.exp(wind_speed[:, None] * growth[None, :] - damping[None, :])


def velocities(stacked, freq_count):
    cosine_table, sine_table = direction_tables(DIR)
    celerity = stacked[:freq_count][:, None]
    shape_out = (freq_count * DIR,) + stacked.shape[1:]
    speed_x = (
        celerity * cosine_table[None, :, None, None] + stacked[freq_count][None, None]
    ).reshape(shape_out)
    speed_y = (
        celerity * sine_table[None, :, None, None] + stacked[freq_count + 1][None, None]
    ).reshape(shape_out)
    return (speed_x, speed_y)


def deliver(bulk_rows, small_rows):
    return (
        lax.all_to_all(bulk_rows, GROUP, split_axis=0, concat_axis=0, tiled=True),
        lax.all_to_all(small_rows, GROUP, split_axis=0, concat_axis=0, tiled=True),
    )


def tile_plan(spectra, wind, growth, damping, row_cell, land_mask, group_speed, current, turning):
    tile_count = lax.axis_size(GROUP)
    comp_width = spectra.shape[1]
    tile_rows, tile_cols = land_mask.shape
    cell_count = tile_rows * tile_cols
    capacity = cell_count // tile_count
    target = row_cell // cell_count
    local_cell = (row_cell - target * cell_count).astype(jnp.float32)
    matches = (target[:, None] == jnp.arange(tile_count, dtype=jnp.int32)[None, :]).astype(
        jnp.int32
    )
    bucket_slot = jnp.sum((jnp.cumsum(matches, axis=0) - 1) * matches, axis=1)

    def bucket(values, filler):
        shape_out = (tile_count, capacity) + values.shape[1:]
        return jnp.full(shape_out, filler, jnp.float32).at[target, bucket_slot].set(values)

    bulk_rows = bucket(source_term(spectra, wind, growth, damping), 0.0)
    small_rows = bucket(local_cell[:, None], float(cell_count))
    bulk_back, small_back = deliver(bulk_rows, small_rows)
    cell_index = small_back[:, :, 0].reshape(-1).astype(jnp.int32)
    flat_values = bulk_back.reshape((tile_count * capacity,) + bulk_back.shape[2:])
    tile_field = (
        jnp.zeros((cell_count,) + bulk_back.shape[2:], jnp.float32)
        .at[cell_index]
        .set(flat_values, mode="drop")
    )
    spectrum = tile_field.T.reshape(comp_width, tile_rows, tile_cols)
    freq_count = comp_width // DIR
    reach = 2 * SUBSTEPS
    stacked = jnp.concatenate([group_speed, current, land_mask.astype(jnp.float32)[None]], axis=0)
    rimmed = with_halo(stacked, ((GROUP, 1),), 2 * SUBSTEPS)
    speed_x, speed_y = velocities(rimmed, freq_count)
    sea_rim = rimmed[freq_count + 2 :]

    def window(values, margin):
        return lax.slice_in_dim(values, reach - margin, reach + tile_rows + margin, axis=1)

    for repeat in range(SUBSTEPS):
        extended = with_halo(spectrum, ((GROUP, 1),), 2)
        spectrum = substep(extended, window(speed_x, 2), window(speed_y, 0), window(sea_rim, 0)[0])
    blocks = spectrum.reshape(freq_count, DIR, tile_rows, tile_cols)
    wrapped = jnp.concatenate([blocks[:, -2:], blocks, blocks[:, :2]], axis=1)
    turning_full = jnp.broadcast_to(turning[None, None], wrapped.shape)
    blocks = blocks - upwind_divergence(wrapped, turning_full, 1)
    spectrum = blocks.reshape(comp_width, tile_rows, tile_cols)
    shipped = lax.all_to_all(spectrum, GROUP, split_axis=0, concat_axis=1, tiled=True)
    return shipped[None]


def pack_kernel(
    parts,
    freqs,
    spectra_ref,
    wind_ref,
    growth_ref,
    damping_ref,
    cell_ref,
    speed_ref,
    current_ref,
    turning_ref,
    out_ref,
):
    rows, comps = spectra_ref.shape
    half = LANES // 2
    full = rows // LANES
    padded = (full + 1) * LANES
    low = lax.broadcasted_iota(jnp.int32, (8, LANES), 1) < half
    per_freq = DIR // 8
    span_rows = full * DIR + 16

    def extended(row, filler):
        return jnp.concatenate([row[None], jnp.full((1, half), filler, jnp.float32)], axis=1)

    def as_columns(row):
        return jnp.broadcast_to(row, (LANES, padded)).T

    cells = cell_ref[...].astype(jnp.float32)
    keys = extended(cells, 1e9)
    key_cols = as_columns(keys)
    ranks = jnp.concatenate(
        [
            jnp.sum(
                jnp.where(key_cols < keys[:, c * LANES : (c + 1) * LANES], 1.0, 0.0), axis=0, keepdims=True
            )
            for c in range(full + 1)
        ],
        axis=1,
    )
    place = lax.broadcasted_iota(jnp.int32, (padded, padded), 0)
    odd = lax.axis_index(GROUP) % 2 == 1
    swapped = jnp.where(place % LANES < half, place + half, place - half)
    place = jnp.where((place < full * LANES) & odd, swapped, place)
    place = jnp.where(place < rows, place, place - half).astype(jnp.float32)
    order = jnp.where(place == ranks, 1.0, 0.0).astype(jnp.bfloat16)

    wind_cols = as_columns(extended(wind_ref[...], 0.0))
    turned = []
    for block in range(comps // LANES):
        lanes = pl.ds(block * LANES, LANES)
        growth = growth_ref[lanes][None]
        damping = damping_ref[lanes][None]

        def source(first, count):
            span = pl.ds(first, count)
            return spectra_ref[span, lanes] * jnp.exp(
                wind_cols[first : first + count] * growth - damping
            )

        pieces = [source(c * LANES, LANES).T for c in range(full)]
        last = jnp.concatenate([source(full * LANES, half), jnp.zeros((half, LANES), jnp.float32)], axis=0)
        turned.append(jnp.concatenate(pieces + [last.T], axis=1))
    turned.append(jnp.broadcast_to(extended(cells, 0.0), (16, padded)))
    values = jnp.concatenate(turned, axis=0)
    head = values.astype(jnp.bfloat16)
    rest = (values - head.astype(jnp.float32)).astype(jnp.bfloat16)
    both = lax.dot_general(
        jnp.concatenate([head, rest], axis=0),
        order,
        (((1,), (1,)), ((), ())),
        preferred_element_type=jnp.float32,
    )

    def piece(first, count, chunk):
        lanes = slice(chunk * LANES, (chunk + 1) * LANES)
        return both[first : first + count, lanes] + both[comps + 16 + first : comps + 16 + first + count, lanes]

    shared = jnp.concatenate(
        [current_ref[0], current_ref[1], turning_ref[...]] + [piece(comps, 1, c) for c in range(full + 1)],
        axis=0,
    )
    for part in range(parts):
        for f in range(freqs):
            freq = part * freqs + f
            at = f * span_rows
            for chunk in range(full):
                out_ref[part, pl.ds(at + chunk * DIR, DIR), :] = piece(freq * DIR, DIR, chunk)
            at += full * DIR
            one, two, three = (piece(freq * DIR + g * 8, 8, full) for g in range(per_freq))
            out_ref[part, pl.ds(at, 8), :] = jnp.where(low, one, two)
            folded = jnp.where(low, three, pltpu.roll(three, 4, 0))
            out_ref[part, pl.ds(at + 8, 8), :] = jnp.concatenate([folded[:4], speed_ref[freq]], axis=0)
        out_ref[part, pl.ds(freqs * span_rows, shared.shape[0]), :] = shared


BLOCK = 8


def slab_kernel(
    parts,
    tile_rows,
    full,
    freqs,
    recv_ref,
    out_ref,
    onehot,
    first,
    second,
    table,
    faces_x,
    faces_y,
    moved_ref,
    done_ref,
    sems,
):
    slab_rows = parts * tile_rows
    half = LANES // 2
    span_rows = full * DIR + 16
    shared_base = freqs * span_rows
    highs = slab_rows // 2
    width = freqs * 2 * DIR
    low_lane = lax.broadcasted_iota(jnp.int32, (1, LANES), 1) < half
    low_lanes = lax.broadcasted_iota(jnp.int32, (8, LANES), 1) < half
    low_wide = lax.broadcasted_iota(jnp.int32, (DIR, LANES), 1) < half
    top_rows = lax.broadcasted_iota(jnp.int32, (8, LANES), 0) < 4
    cell_iota = lax.broadcasted_iota(jnp.int32, (2 * LANES, LANES), 0).astype(jnp.float32).astype(jnp.bfloat16)
    high_iota = lax.broadcasted_iota(jnp.int32, (highs, LANES), 0)

    def cells_of(owner, chunk):
        return recv_ref[owner, pl.ds(shared_base + 3 * tile_rows + chunk, 1), :].astype(jnp.int32)

    owner_rows = full * LANES + half
    capacity = tile_rows * LANES // parts
    spans = []
    for begin in range(0, owner_rows, half):
        tiles = [
            t
            for t in range(parts)
            if owner_rows - capacity * (parts - t) < begin + half and capacity * (t + 1) > begin
        ]
        spans.append(range(tiles[0] * tile_rows // 2, (tiles[-1] + 1) * tile_rows // 2))
    offsets = [parts // 2 * LANES * chunk for chunk in range(len(spans))]
    columns = [[] for _ in spans]

    def place(chunk, cells, values):
        span = pl.ds(offsets[chunk] + len(columns[chunk]) * LANES, LANES)
        high = cells // (2 * LANES)
        low = (cells - high * (2 * LANES)).astype(jnp.float32)
        low = jnp.broadcast_to(low, (2 * LANES, LANES)).astype(jnp.bfloat16)
        onehot[:, span] = jnp.where(cell_iota == low, 1.0, 0.0).astype(jnp.bfloat16)
        pieces = []
        for value in values:
            head = value.astype(jnp.bfloat16).astype(jnp.float32)
            pieces += [head, value - head]
        both = jnp.concatenate(pieces, axis=0).astype(jnp.bfloat16)
        column = []
        for h in spans[chunk]:
            pick = jnp.broadcast_to((high == h).astype(jnp.float32), (width, LANES)).astype(jnp.bfloat16)
            column.append(both * pick)
        column.append((high_iota == high).astype(jnp.float32).astype(jnp.bfloat16))
        columns[chunk].append(jnp.concatenate(column, axis=0))

    for pair in range(parts // 2):
        even, odd = 2 * pair, 2 * pair + 1
        for chunk in range(full):
            here, there = (
                [recv_ref[owner, pl.ds(f * span_rows + chunk * DIR, DIR), :] for f in range(freqs)]
                for owner in (even, odd)
            )
            cells, cells_there = cells_of(even, chunk), cells_of(odd, chunk)
            for side in range(2):
                place(
                    2 * chunk + side,
                    jnp.where(low_lane, cells, cells_there),
                    [jnp.where(low_wide, a, b) for a, b in zip(here, there)],
                )
                here, there, cells, cells_there = there, here, cells_there, cells

        def merged(offset):
            own, other = recv_ref[even, pl.ds(offset, 8), :], recv_ref[odd, pl.ds(offset, 8), :]
            return (
                jnp.where(low_lanes, own, pltpu.roll(other, half, 1)),
                jnp.where(low_lanes, pltpu.roll(own, half, 1), other),
            )

        values = []
        for f in range(freqs):
            one, two = merged(f * span_rows + full * DIR)
            three, four = merged(f * span_rows + full * DIR + 8)
            values.append(
                jnp.concatenate([one, two, jnp.where(top_rows, three, pltpu.roll(four, 4, 0))], axis=0)
            )
        place(2 * full, jnp.where(low_lane, cells_of(even, full), cells_of(odd, full)), values)

    lane = lax.broadcasted_iota(jnp.int32, (slab_rows, LANES), 1)
    zero_rows = jnp.zeros((8, LANES), jnp.float32)

    def gather(offset):
        return jnp.concatenate(
            [recv_ref[owner, pl.ds(offset, tile_rows), :] for owner in range(parts)], axis=0
        )

    gain = 0.5 * courant / 8.0
    slots = iter(range(table.shape[0]))

    def keep(rows):
        slot = next(slots)
        table[slot, pl.ds(8, rows.shape[0]), :] = rows
        return slot

    def face_x(rows):
        slot = next(slots)
        table[slot, pl.ds(0, 8), :] = zero_rows
        table[slot, pl.ds(8 + slab_rows, 8), :] = zero_rows
        table[slot, pl.ds(8, slab_rows), :] = rows
        faces = gain * (table[slot, pl.ds(7, slab_rows + 8), :] + table[slot, pl.ds(8, slab_rows + 8), :])
        table[slot, pl.ds(7, slab_rows + 8), :] = faces
        return slot

    def face_y(rows):
        after = jnp.where(lane < LANES - 1, pltpu.roll(rows, LANES - 1, 1), 0.0)
        before = jnp.where(lane > 0, pltpu.roll(rows, 1, 1), 0.0)
        return keep(gain * (rows + after)), keep(gain * (rows + before))

    speeds = [gather(f * span_rows + full * DIR + 12) for f in range(freqs)]
    current_x, current_y, turning = (gather(shared_base + kind * tile_rows) for kind in range(3))
    current_x_face, speed_x_face = face_x(current_x), [face_x(s) for s in speeds]
    current_y_faces, speed_y_faces = face_y(current_y), [face_y(s) for s in speeds]
    step_angle = 2.0 * math.pi / DIR
    sublane = lax.broadcasted_iota(jnp.int32, (8, LANES), 0)
    cosine0 = jnp.ones((8, LANES), jnp.float32)
    sine0 = jnp.zeros((8, LANES), jnp.float32)
    for d in range(1, 8):
        cosine0 = jnp.where(sublane == d, math.cos(d * step_angle), cosine0)
        sine0 = jnp.where(sublane == d, math.sin(d * step_angle), sine0)
    turns = [(math.cos(g * 8 * step_angle), math.sin(g * 8 * step_angle)) for g in range(DIR // 8)]
    cosine = jnp.concatenate([c * cosine0 - t * sine0 for c, t in turns], axis=0)
    sine = jnp.concatenate([c * sine0 + t * cosine0 for c, t in turns], axis=0)

    def row(slot, x):
        return table[slot, pl.ds(8 + x, 1), :]

    for f in range(freqs):
        for x in range(-1, slab_rows):
            faces_x[f, x + 1] = row(speed_x_face[f], x) * cosine + row(current_x_face, x)
        for x in range(slab_rows):
            for side in range(2):
                faces_y[f, side, x] = row(speed_y_faces[f][side], x) * sine + row(current_y_faces[side], x)

    scattered = [
        lax.dot_general(
            jnp.concatenate(column, axis=1),
            onehot[:, pl.ds(offset, len(column) * LANES)],
            (((1,), (1,)), ((), ())),
            preferred_element_type=jnp.float32,
        )
        for offset, column in zip(offsets, columns)
    ]
    nothing = jnp.zeros((DIR, LANES), jnp.float32)
    for f in range(freqs):
        for field in (first, second):
            for edge in (0, 1, slab_rows + 2, slab_rows + 3):
                field[f, edge] = nothing
        for h in range(highs):
            terms = []
            for span, product in zip(spans, scattered):
                if h in span:
                    at = (h - span[0]) * width + f * 2 * DIR
                    terms += [product[at : at + DIR], product[at + DIR : at + 2 * DIR]]
            total = sum(terms[1:], terms[0])
            first[f, 2 * h + 2] = total[:, :LANES]
            first[f, 2 * h + 3] = total[:, LANES:]
    named = sum(product[len(span) * width :] for span, product in zip(spans, scattered))

    land_slots = keep(named[:, :LANES]), keep(named[:, LANES:])
    ahead = jnp.maximum(turning, 0.0) * 0.125
    back = jnp.minimum(turning, 0.0) * 0.125
    bend_slots = [
        keep(rows)
        for rows in (
            -ahead,
            7.0 * ahead + 3.0 * back,
            1.0 - 3.0 * (ahead - back),
            -3.0 * ahead - 7.0 * back,
            back,
        )
    ]

    gap = lax.broadcasted_iota(jnp.int32, (LANES, LANES), 0) - lax.broadcasted_iota(
        jnp.int32, (LANES, LANES), 1
    )

    def band(first_gap, values):
        out = jnp.zeros((LANES, LANES), jnp.float32)
        for i, value in enumerate(values):
            out = jnp.where(gap == first_gap + i, value, out)
        return out

    left_values, right_values = (-1.0, 6.0, 3.0), (3.0, 6.0, -1.0)
    bands = jnp.concatenate(
        [band(-1, left_values), band(0, right_values), band(-2, left_values), band(-1, right_values)], axis=1
    ).astype(jnp.bfloat16)
    bands = jnp.concatenate([bands, bands], axis=0)

    def flux(speed, behind, centre3, onward3, beyond):
        positive = speed > 0.0
        near = jnp.where(positive, centre3, onward3)
        far = jnp.where(positive, behind, beyond)
        return speed * ((centre3 + onward3) + (near - far))

    def along_y(field):
        rows = jnp.concatenate(
            [field[f, 2 : slab_rows + 2].reshape(slab_rows * DIR, LANES) for f in range(freqs)], axis=0
        )
        head = rows.astype(jnp.bfloat16)
        rest = (rows - head.astype(jnp.float32)).astype(jnp.bfloat16)
        return lax.dot_general(
            jnp.concatenate([head, rest], axis=1),
            bands,
            (((1,), (0,)), ((), ())),
            preferred_element_type=jnp.float32,
        )

    def upwind(speed, values):
        return speed * jnp.where(speed > 0.0, values[:, :LANES], values[:, LANES:])

    def advance(field, finish, after_block):
        values = along_y(field)
        carry = []
        for f in range(freqs):
            start3 = 3.0 * field[f, 2]
            carry.append((flux(faces_x[f, 0], nothing, nothing, start3, field[f, 3]), start3))
        for x in range(slab_rows):
            sea = row(land_slots[x % 2], x // 2)
            for f in range(freqs):
                entering, centre3 = carry[f]
                onward3 = 3.0 * field[f, x + 3]
                leaving = flux(faces_x[f, x + 1], field[f, x + 1], centre3, onward3, field[f, x + 4])
                at = (f * slab_rows + x) * DIR
                right = upwind(faces_y[f, 0, x], values[at : at + DIR, : 2 * LANES])
                left = upwind(faces_y[f, 1, x], values[at : at + DIR, 2 * LANES :])
                finish(f, x, (field[f, x + 2] - (leaving - entering) - (right - left)) * sea)
                carry[f] = leaving, onward3
            if (x + 1) % BLOCK == 0:
                after_block(x // BLOCK)

    def store(f, x, moved):
        second[f, x + 2] = moved

    def turn(f, x, moved):
        for g in range(DIR // 8):
            at = (f * DIR + g * 8) * slab_rows + x
            moved_ref[pl.ds(at, 8, stride=slab_rows), :] = moved[g * 8 : g * 8 + 8]

    def copy_out(step):
        part = pl.ds(pl.multiple_of(step * BLOCK, BLOCK), BLOCK)
        return pltpu.make_async_copy(done_ref.at[:, part, :], out_ref.at[:, part, :], sems.at[step])

    def refract(block):
        at = block * BLOCK
        weights = [table[slot, pl.ds(8 + at, BLOCK), :] for slot in bend_slots]
        for f in range(freqs):
            ring = [moved_ref[pl.ds((f * DIR + d) * slab_rows + at, BLOCK), :] for d in range(DIR)]
            for d in range(DIR):
                bent = weights[2] * ring[d]
                for k in (0, 1, 3, 4):
                    bent = bent + weights[k] * ring[(d + k - 2) % DIR]
                done_ref[f * DIR + d, pl.ds(at, BLOCK), :] = bent
        copy_out(block).start()

    advance(first, store, lambda block: None)
    advance(second, turn, refract)
    for block in range(slab_rows // BLOCK):
        copy_out(block).wait()


def slab_plan(spectra, wind, growth, damping, row_cell, group_speed, current, turning):
    parts = lax.axis_size(GROUP)
    rows, comps = spectra.shape
    tile_rows = turning.shape[0]
    freqs = comps // parts // DIR
    full = rows // LANES
    slab_rows = parts * tile_rows
    depth = parts * rows
    highs = slab_rows // 2
    block_rows = -(-(freqs * (full * DIR + 16) + 3 * tile_rows + full + 1) // 8) * 8
    packed = pl.pallas_call(
        functools.partial(pack_kernel, parts, freqs),
        out_shape=pltpu.VMEM((parts, block_rows, LANES), jnp.float32),
        compiler_params=pltpu.CompilerParams(vmem_limit_bytes=56 * 1024 * 1024),
        name="pack",
    )(spectra, wind, growth, damping, row_cell, group_speed, current, turning)
    arrived = lax.all_to_all(packed, GROUP, split_axis=0, concat_axis=0, tiled=True)
    out = pl.pallas_call(
        functools.partial(slab_kernel, parts, tile_rows, full, freqs),
        out_shape=jax.ShapeDtypeStruct((freqs * DIR, slab_rows, LANES), jnp.float32),
        in_specs=[pl.BlockSpec(memory_space=pltpu.VMEM)],
        out_specs=pl.BlockSpec(memory_space=pl.ANY),
        scratch_shapes=[
            pltpu.VMEM((2 * LANES, depth), jnp.bfloat16),
            pltpu.VMEM((freqs, slab_rows + 4, DIR, LANES), jnp.float32),
            pltpu.VMEM((freqs, slab_rows + 4, DIR, LANES), jnp.float32),
            pltpu.VMEM((10 + 3 * freqs, slab_rows + 16, LANES), jnp.float32),
            pltpu.VMEM((freqs, slab_rows + 1, DIR, LANES), jnp.float32),
            pltpu.VMEM((freqs, 2, slab_rows, DIR, LANES), jnp.float32),
            pltpu.VMEM((freqs * DIR * slab_rows, LANES), jnp.float32),
            pltpu.VMEM((freqs * DIR, slab_rows, LANES), jnp.float32),
            pltpu.SemaphoreType.DMA((slab_rows // BLOCK,)),
        ],
        compiler_params=pltpu.CompilerParams(vmem_limit_bytes=32 * 1024 * 1024),
        name="slab",
    )(arrived)
    return out.reshape(1, freqs * DIR, slab_rows, LANES)


def shards(*arrays):
    spectra, land_mask = arrays[0], arrays[5]
    parts = lax.axis_size(GROUP)
    rows, comps = spectra.shape
    whole_frequencies = comps == parts * 2 * DIR
    fits = rows % LANES == LANES // 2 and land_mask.shape == (4, LANES) and parts % 2 == 0
    if whole_frequencies and fits:
        return slab_plan(*arrays[:5], *arrays[6:])
    return tile_plan(*arrays)


def solution(mesh):
    placed = (
        P(("groups", "pts", "comp"), "sub"),
        P(("groups", "pts", "comp")),
        P("sub"),
        P("sub"),
        P(("groups", "pts", "comp")),
        P(("groups", "pts", "comp"), None),
        P(("groups", "sub"), ("pts", "comp"), None),
        P("groups", ("pts", "comp"), None),
        P(("groups", "pts", "comp"), None),
    )
    return jax.shard_map(
        shards,
        mesh=mesh,
        in_specs=placed,
        out_specs=P("sub", ("pts", "comp"), "groups", None),
        check_vma=False,
    )
```

```python
import functools
import math
import jax
import jax.numpy as jnp
from jax import lax
from jax.experimental import pallas as pl
from jax.experimental.pallas import tpu as pltpu
from jax.sharding import PartitionSpec as P

DIR = 24
SUBSTEPS = 2
LANES = 128
GROUP = ("pts", "comp")


courant = 0.35


def with_halo(cells, sides, width):
    for axis, dim in sides:
        count = lax.axis_size(axis)
        ends = count - 1
        head = lax.slice_in_dim(cells, 0, width, axis=dim)
        tail = lax.slice_in_dim(cells, cells.shape[dim] - width, cells.shape[dim], axis=dim)
        cells = jnp.concatenate(
            [
                lax.ppermute(tail, axis, [(i, (i + 1) % count) for i in range(ends)]),
                cells,
                lax.ppermute(head, axis, [((i + 1) % count, i) for i in range(ends)]),
            ],
            axis=dim,
        )
    return cells


def take_slice(values, first_index, extent, along_axis):
    return lax.slice_in_dim(values, first_index, first_index + extent, axis=along_axis)


def upwind_divergence(padded, motion, along_axis):
    length = padded.shape[along_axis] - 4
    face_count = length + 1
    behind = take_slice(padded, 0, face_count, along_axis)
    centre = take_slice(padded, 1, face_count, along_axis)
    onward = take_slice(padded, 2, face_count, along_axis)
    beyond = take_slice(padded, 3, face_count, along_axis)
    left_face = (6.0 * centre + 3.0 * onward - behind) * 0.125
    right_face = (3.0 * centre + 6.0 * onward - beyond) * 0.125
    face_speed = 0.5 * (
        take_slice(motion, 1, face_count, along_axis)
        + take_slice(motion, 2, face_count, along_axis)
    )
    fluxes = jnp.maximum(face_speed, 0.0) * left_face + jnp.minimum(face_speed, 0.0) * right_face
    return take_slice(fluxes, 1, length, along_axis) - take_slice(fluxes, 0, length, along_axis)


def substep(extended, speed_x, speed_y, sea_mask):
    across = upwind_divergence(extended, speed_x, 1)
    centre_part = extended[:, 2:-2]
    padding = ((0, 0), (0, 0), (2, 2))
    sideways = upwind_divergence(jnp.pad(centre_part, padding), jnp.pad(speed_y, padding), 2)
    return (centre_part - courant * (across + sideways)) * sea_mask


def direction_tables(directions):
    angles = jnp.arange(directions, dtype=jnp.float32) * (2.0 * jnp.pi / directions)
    return (jnp.cos(angles), jnp.sin(angles))


def source_term(values, wind_speed, growth, damping):
    return values * jnp.exp(wind_speed[:, None] * growth[None, :] - damping[None, :])


def velocities(stacked, freq_count):
    cosine_table, sine_table = direction_tables(DIR)
    celerity = stacked[:freq_count][:, None]
    shape_out = (freq_count * DIR,) + stacked.shape[1:]
    speed_x = (
        celerity * cosine_table[None, :, None, None] + stacked[freq_count][None, None]
    ).reshape(shape_out)
    speed_y = (
        celerity * sine_table[None, :, None, None] + stacked[freq_count + 1][None, None]
    ).reshape(shape_out)
    return (speed_x, speed_y)


def deliver(bulk_rows, small_rows):
    return (
        lax.all_to_all(bulk_rows, GROUP, split_axis=0, concat_axis=0, tiled=True),
        lax.all_to_all(small_rows, GROUP, split_axis=0, concat_axis=0, tiled=True),
    )


def tile_plan(spectra, wind, growth, damping, row_cell, land_mask, group_speed, current, turning):
    tile_count = lax.axis_size(GROUP)
    comp_width = spectra.shape[1]
    tile_rows, tile_cols = land_mask.shape
    cell_count = tile_rows * tile_cols
    capacity = cell_count // tile_count
    target = row_cell // cell_count
    local_cell = (row_cell - target * cell_count).astype(jnp.float32)
    matches = (target[:, None] == jnp.arange(tile_count, dtype=jnp.int32)[None, :]).astype(
        jnp.int32
    )
    bucket_slot = jnp.sum((jnp.cumsum(matches, axis=0) - 1) * matches, axis=1)

    def bucket(values, filler):
        shape_out = (tile_count, capacity) + values.shape[1:]
        return jnp.full(shape_out, filler, jnp.float32).at[target, bucket_slot].set(values)

    bulk_rows = bucket(source_term(spectra, wind, growth, damping), 0.0)
    small_rows = bucket(local_cell[:, None], float(cell_count))
    bulk_back, small_back = deliver(bulk_rows, small_rows)
    cell_index = small_back[:, :, 0].reshape(-1).astype(jnp.int32)
    flat_values = bulk_back.reshape((tile_count * capacity,) + bulk_back.shape[2:])
    tile_field = (
        jnp.zeros((cell_count,) + bulk_back.shape[2:], jnp.float32)
        .at[cell_index]
        .set(flat_values, mode="drop")
    )
    spectrum = tile_field.T.reshape(comp_width, tile_rows, tile_cols)
    freq_count = comp_width // DIR
    reach = 2 * SUBSTEPS
    stacked = jnp.concatenate([group_speed, current, land_mask.astype(jnp.float32)[None]], axis=0)
    rimmed = with_halo(stacked, ((GROUP, 1),), 2 * SUBSTEPS)
    speed_x, speed_y = velocities(rimmed, freq_count)
    sea_rim = rimmed[freq_count + 2 :]

    def window(values, margin):
        return lax.slice_in_dim(values, reach - margin, reach + tile_rows + margin, axis=1)

    for repeat in range(SUBSTEPS):
        extended = with_halo(spectrum, ((GROUP, 1),), 2)
        spectrum = substep(extended, window(speed_x, 2), window(speed_y, 0), window(sea_rim, 0)[0])
    blocks = spectrum.reshape(freq_count, DIR, tile_rows, tile_cols)
    wrapped = jnp.concatenate([blocks[:, -2:], blocks, blocks[:, :2]], axis=1)
    turning_full = jnp.broadcast_to(turning[None, None], wrapped.shape)
    blocks = blocks - upwind_divergence(wrapped, turning_full, 1)
    spectrum = blocks.reshape(comp_width, tile_rows, tile_cols)
    shipped = lax.all_to_all(spectrum, GROUP, split_axis=0, concat_axis=1, tiled=True)
    return shipped[None]


def pack_kernel(
    parts,
    freqs,
    spectra_ref,
    wind_ref,
    growth_ref,
    damping_ref,
    cell_ref,
    speed_ref,
    current_ref,
    turning_ref,
    out_ref,
):
    rows, comps = spectra_ref.shape
    half = LANES // 2
    full = rows // LANES
    padded = (full + 1) * LANES
    low = lax.broadcasted_iota(jnp.int32, (8, LANES), 1) < half
    per_freq = DIR // 8
    span_rows = full * DIR + 16

    def extended(row, filler):
        return jnp.concatenate([row[None], jnp.full((1, half), filler, jnp.float32)], axis=1)

    def as_columns(row):
        return jnp.broadcast_to(row, (LANES, padded)).T

    cells = cell_ref[...].astype(jnp.float32)
    keys = extended(cells, 1e9)
    key_cols = as_columns(keys)
    ranks = jnp.concatenate(
        [
            jnp.sum(
                jnp.where(key_cols < keys[:, c * LANES : (c + 1) * LANES], 1.0, 0.0), axis=0, keepdims=True
            )
            for c in range(full + 1)
        ],
        axis=1,
    )
    place = lax.broadcasted_iota(jnp.int32, (padded, padded), 0)
    odd = lax.axis_index(GROUP) % 2 == 1
    swapped = jnp.where(place % LANES < half, place + half, place - half)
    place = jnp.where((place < full * LANES) & odd, swapped, place)
    place = jnp.where(place < rows, place, place - half).astype(jnp.float32)
    order = jnp.where(place == ranks, 1.0, 0.0).astype(jnp.bfloat16)

    wind_cols = as_columns(extended(wind_ref[...], 0.0))
    turned = []
    for block in range(comps // LANES):
        lanes = pl.ds(block * LANES, LANES)
        growth = growth_ref[lanes][None]
        damping = damping_ref[lanes][None]

        def source(first, count):
            span = pl.ds(first, count)
            return spectra_ref[span, lanes] * jnp.exp(
                wind_cols[first : first + count] * growth - damping
            )

        pieces = [source(c * LANES, LANES).T for c in range(full)]
        last = jnp.concatenate([source(full * LANES, half), jnp.zeros((half, LANES), jnp.float32)], axis=0)
        turned.append(jnp.concatenate(pieces + [last.T], axis=1))
    turned.append(jnp.broadcast_to(extended(cells, 0.0), (16, padded)))
    values = jnp.concatenate(turned, axis=0)
    head = values.astype(jnp.bfloat16)
    rest = (values - head.astype(jnp.float32)).astype(jnp.bfloat16)
    both = lax.dot_general(
        jnp.concatenate([head, rest], axis=0),
        order,
        (((1,), (1,)), ((), ())),
        preferred_element_type=jnp.float32,
    )

    def piece(first, count, chunk):
        lanes = slice(chunk * LANES, (chunk + 1) * LANES)
        return both[first : first + count, lanes] + both[comps + 16 + first : comps + 16 + first + count, lanes]

    shared = jnp.concatenate(
        [current_ref[0], current_ref[1], turning_ref[...]] + [piece(comps, 1, c) for c in range(full + 1)],
        axis=0,
    )
    for part in range(parts):
        for f in range(freqs):
            freq = part * freqs + f
            at = f * span_rows
            for chunk in range(full):
                out_ref[part, pl.ds(at + chunk * DIR, DIR), :] = piece(freq * DIR, DIR, chunk)
            at += full * DIR
            one, two, three = (piece(freq * DIR + g * 8, 8, full) for g in range(per_freq))
            out_ref[part, pl.ds(at, 8), :] = jnp.where(low, one, two)
            folded = jnp.where(low, three, pltpu.roll(three, 4, 0))
            out_ref[part, pl.ds(at + 8, 8), :] = jnp.concatenate([folded[:4], speed_ref[freq]], axis=0)
        out_ref[part, pl.ds(freqs * span_rows, shared.shape[0]), :] = shared


BLOCK = 8
PER_STEP = 4


def slab_kernel(
    parts,
    tile_rows,
    full,
    freqs,
    recv_ref,
    out_ref,
    first,
    second,
    table,
    faces_x,
    faces_y,
    moved_ref,
    done_ref,
    sems,
):
    slab_rows = parts * tile_rows
    half = LANES // 2
    span_rows = full * DIR + 16
    shared_base = freqs * span_rows
    highs = slab_rows // 2
    width = freqs * 2 * DIR
    low_lane = lax.broadcasted_iota(jnp.int32, (1, LANES), 1) < half
    low_lanes = lax.broadcasted_iota(jnp.int32, (8, LANES), 1) < half
    low_wide = lax.broadcasted_iota(jnp.int32, (DIR, LANES), 1) < half
    top_rows = lax.broadcasted_iota(jnp.int32, (8, LANES), 0) < 4
    cell_iota = lax.broadcasted_iota(jnp.int32, (2 * LANES, LANES), 0).astype(jnp.float32).astype(jnp.bfloat16)
    high_iota = lax.broadcasted_iota(jnp.int32, (highs, LANES), 0)

    def cells_of(owner, chunk):
        return recv_ref[owner, pl.ds(shared_base + 3 * tile_rows + chunk, 1), :].astype(jnp.int32)

    owner_rows = full * LANES + half
    capacity = tile_rows * LANES // parts
    spans = []
    for begin in range(0, owner_rows, half):
        tiles = [
            t
            for t in range(parts)
            if owner_rows - capacity * (parts - t) < begin + half and capacity * (t + 1) > begin
        ]
        spans.append(range(tiles[0] * tile_rows // 2, (tiles[-1] + 1) * tile_rows // 2))
    columns = [[] for _ in spans]
    hots = [[] for _ in spans]

    def repeated(line, count):
        tile = jnp.broadcast_to(line, (16, LANES)).astype(jnp.bfloat16)
        return jnp.concatenate([tile] * (count // 16), axis=0)

    def place(chunk, cells, values):
        high = cells // (2 * LANES)
        low = (cells - high * (2 * LANES)).astype(jnp.float32)
        low = repeated(low, 2 * LANES)
        hots[chunk].append(jnp.where(cell_iota == low, 1.0, 0.0).astype(jnp.bfloat16))
        pieces = []
        for value in values:
            head = value.astype(jnp.bfloat16).astype(jnp.float32)
            pieces += [head, value - head]
        both = jnp.concatenate(pieces, axis=0).astype(jnp.bfloat16)
        column = []
        for h in spans[chunk]:
            column.append(both * repeated((high == h).astype(jnp.float32), width))
        column.append((high_iota == high).astype(jnp.float32).astype(jnp.bfloat16))
        columns[chunk].append(jnp.concatenate(column, axis=0))

    for pair in range(parts // 2):
        even, odd = 2 * pair, 2 * pair + 1
        for chunk in range(full):
            here, there = (
                [recv_ref[owner, pl.ds(f * span_rows + chunk * DIR, DIR), :] for f in range(freqs)]
                for owner in (even, odd)
            )
            cells, cells_there = cells_of(even, chunk), cells_of(odd, chunk)
            for side in range(2):
                place(
                    2 * chunk + side,
                    jnp.where(low_lane, cells, cells_there),
                    [jnp.where(low_wide, a, b) for a, b in zip(here, there)],
                )
                here, there, cells, cells_there = there, here, cells_there, cells

        def merged(offset):
            own, other = recv_ref[even, pl.ds(offset, 8), :], recv_ref[odd, pl.ds(offset, 8), :]
            return (
                jnp.where(low_lanes, own, pltpu.roll(other, half, 1)),
                jnp.where(low_lanes, pltpu.roll(own, half, 1), other),
            )

        values = []
        for f in range(freqs):
            one, two = merged(f * span_rows + full * DIR)
            three, four = merged(f * span_rows + full * DIR + 8)
            values.append(
                jnp.concatenate([one, two, jnp.where(top_rows, three, pltpu.roll(four, 4, 0))], axis=0)
            )
        place(2 * full, jnp.where(low_lane, cells_of(even, full), cells_of(odd, full)), values)

    lane = lax.broadcasted_iota(jnp.int32, (slab_rows, LANES), 1)
    zero_rows = jnp.zeros((8, LANES), jnp.float32)

    def gather(offset):
        return jnp.concatenate(
            [recv_ref[owner, pl.ds(offset, tile_rows), :] for owner in range(parts)], axis=0
        )

    gain = 0.5 * courant / 8.0
    slots = iter(range(table.shape[0]))

    def keep(rows):
        slot = next(slots)
        table[slot, pl.ds(8, rows.shape[0]), :] = rows
        return slot

    def face_x(rows):
        slot = next(slots)
        table[slot, pl.ds(0, 8), :] = zero_rows
        table[slot, pl.ds(8 + slab_rows, 8), :] = zero_rows
        table[slot, pl.ds(8, slab_rows), :] = rows
        faces = gain * (table[slot, pl.ds(7, slab_rows + 8), :] + table[slot, pl.ds(8, slab_rows + 8), :])
        table[slot, pl.ds(7, slab_rows + 8), :] = faces
        return slot

    def face_y(rows):
        after = jnp.where(lane < LANES - 1, pltpu.roll(rows, LANES - 1, 1), 0.0)
        before = jnp.where(lane > 0, pltpu.roll(rows, 1, 1), 0.0)
        return keep(gain * (rows + after)), keep(gain * (rows + before))

    speeds = [gather(f * span_rows + full * DIR + 12) for f in range(freqs)]
    current_x, current_y, turning = (gather(shared_base + kind * tile_rows) for kind in range(3))
    current_x_face, speed_x_face = face_x(current_x), [face_x(s) for s in speeds]
    current_y_faces, speed_y_faces = face_y(current_y), [face_y(s) for s in speeds]
    step_angle = 2.0 * math.pi / DIR
    sublane = lax.broadcasted_iota(jnp.int32, (8, LANES), 0)
    cosine0 = jnp.ones((8, LANES), jnp.float32)
    sine0 = jnp.zeros((8, LANES), jnp.float32)
    for d in range(1, 8):
        cosine0 = jnp.where(sublane == d, math.cos(d * step_angle), cosine0)
        sine0 = jnp.where(sublane == d, math.sin(d * step_angle), sine0)
    turns = [(math.cos(g * 8 * step_angle), math.sin(g * 8 * step_angle)) for g in range(DIR // 8)]
    cosine = jnp.concatenate([c * cosine0 - t * sine0 for c, t in turns], axis=0)
    sine = jnp.concatenate([c * sine0 + t * cosine0 for c, t in turns], axis=0)

    def row(slot, x):
        return table[slot, pl.ds(8 + x, 1), :]

    for f in range(freqs):
        for x in range(-1, slab_rows):
            faces_x[f, x + 1] = row(speed_x_face[f], x) * cosine + row(current_x_face, x)
        for x in range(slab_rows):
            for side in range(2):
                faces_y[f, side, x] = row(speed_y_faces[f][side], x) * sine + row(current_y_faces[side], x)

    scattered = [
        lax.dot_general(
            jnp.concatenate(column, axis=1),
            jnp.concatenate(hot, axis=1),
            (((1,), (1,)), ((), ())),
            preferred_element_type=jnp.float32,
        )
        for hot, column in zip(hots, columns)
    ]
    nothing = jnp.zeros((DIR, LANES), jnp.float32)
    for f in range(freqs):
        for field in (first, second):
            for edge in (0, 1, slab_rows + 2, slab_rows + 3):
                field[f, edge] = nothing
        for h in range(highs):
            terms = []
            for span, product in zip(spans, scattered):
                if h in span:
                    at = (h - span[0]) * width + f * 2 * DIR
                    terms += [product[at : at + DIR], product[at + DIR : at + 2 * DIR]]
            total = sum(terms[1:], terms[0])
            first[f, 2 * h + 2] = total[:, :LANES]
            first[f, 2 * h + 3] = total[:, LANES:]
    named = sum(product[len(span) * width :] for span, product in zip(spans, scattered))

    land_slots = keep(named[:, :LANES]), keep(named[:, LANES:])
    ahead = jnp.maximum(turning, 0.0) * 0.125
    back = jnp.minimum(turning, 0.0) * 0.125
    bend_slots = [
        keep(rows)
        for rows in (
            -ahead,
            7.0 * ahead + 3.0 * back,
            1.0 - 3.0 * (ahead - back),
            -3.0 * ahead - 7.0 * back,
            back,
        )
    ]

    lane_wide = lax.broadcasted_iota(jnp.int32, (DIR, LANES), 1)

    def flux(speed, behind, centre3, onward3, beyond):
        positive = speed > 0.0
        near = jnp.where(positive, centre3, onward3)
        far = jnp.where(positive, behind, beyond)
        return speed * ((centre3 + onward3) + (near - far))

    def advance(field, step, carry, finish):
        carry = list(carry)
        for i in range(BLOCK):
            x = step * BLOCK + i
            sea = row(land_slots[i % 2], step * (BLOCK // 2) + i // 2)
            for f in range(freqs):
                entering, centre3 = carry[f]
                centre = field[f, x + 2]
                onward3 = 3.0 * field[f, x + 3]
                leaving = flux(faces_x[f, x + 1], field[f, x + 1], centre3, onward3, field[f, x + 4])
                up1 = jnp.where(lane_wide < LANES - 1, pltpu.roll(centre, LANES - 1, 1), 0.0)
                up2 = jnp.where(lane_wide < LANES - 2, pltpu.roll(centre, LANES - 2, 1), 0.0)
                down1 = jnp.where(lane_wide > 0, pltpu.roll(centre, 1, 1), 0.0)
                down2 = jnp.where(lane_wide > 1, pltpu.roll(centre, 2, 1), 0.0)
                right = flux(faces_y[f, 0, x], down1, centre3, 3.0 * up1, up2)
                left = flux(faces_y[f, 1, x], down2, 3.0 * down1, centre3, up1)
                finish(f, x, (centre - (leaving - entering) - (right - left)) * sea)
                carry[f] = leaving, onward3
        return tuple(carry)

    def enter(field):
        carry = []
        for f in range(freqs):
            start3 = 3.0 * field[f, 2]
            carry.append((flux(faces_x[f, 0], nothing, nothing, start3, field[f, 3]), start3))
        return tuple(carry)

    def store(f, x, moved):
        second[f, x + 2] = moved

    def turn(f, x, moved):
        for g in range(DIR // 8):
            at = (f * DIR + g * 8) * slab_rows + x
            moved_ref[pl.ds(at, 8, stride=slab_rows), :] = moved[g * 8 : g * 8 + 8]

    def copy_out(step):
        part = pl.ds(pl.multiple_of(step * BLOCK, BLOCK), BLOCK)
        return pltpu.make_async_copy(done_ref.at[:, part, :], out_ref.at[:, part, :], sems.at[step])

    def final(block, carry):
        carry = advance(second, block, carry, turn)
        at = pl.multiple_of(block * BLOCK, BLOCK)
        weights = [table[slot, pl.ds(8 + at, BLOCK), :] for slot in bend_slots]
        for f in range(freqs):
            ring = [moved_ref[pl.ds((f * DIR + d) * slab_rows + at, BLOCK), :] for d in range(DIR)]
            for d in range(DIR):
                bent = weights[2] * ring[d]
                for k in (0, 1, 3, 4):
                    bent = bent + weights[k] * ring[(d + k - 2) % DIR]
                done_ref[f * DIR + d, pl.ds(at, BLOCK), :] = bent
        copy_out(block).start()
        return carry

    def sweep(one_block, carry):
        def body(step, carry):
            for i in range(PER_STEP):
                carry = one_block(step * PER_STEP + i, carry)
            return carry

        lax.fori_loop(0, slab_rows // BLOCK // PER_STEP, body, carry)

    sweep(lambda block, carry: advance(first, block, carry, store), enter(first))
    sweep(final, enter(second))
    for block in range(slab_rows // BLOCK):
        copy_out(block).wait()


def slab_plan(spectra, wind, growth, damping, row_cell, group_speed, current, turning):
    parts = lax.axis_size(GROUP)
    rows, comps = spectra.shape
    tile_rows = turning.shape[0]
    freqs = comps // parts // DIR
    full = rows // LANES
    slab_rows = parts * tile_rows
    highs = slab_rows // 2
    block_rows = -(-(freqs * (full * DIR + 16) + 3 * tile_rows + full + 1) // 8) * 8
    packed = pl.pallas_call(
        functools.partial(pack_kernel, parts, freqs),
        out_shape=pltpu.VMEM((parts, block_rows, LANES), jnp.float32),
        compiler_params=pltpu.CompilerParams(vmem_limit_bytes=56 * 1024 * 1024),
        name="pack",
    )(spectra, wind, growth, damping, row_cell, group_speed, current, turning)
    arrived = lax.all_to_all(packed, GROUP, split_axis=0, concat_axis=0, tiled=True)
    out = pl.pallas_call(
        functools.partial(slab_kernel, parts, tile_rows, full, freqs),
        out_shape=jax.ShapeDtypeStruct((freqs * DIR, slab_rows, LANES), jnp.float32),
        in_specs=[pl.BlockSpec(memory_space=pltpu.VMEM)],
        out_specs=pl.BlockSpec(memory_space=pl.ANY),
        scratch_shapes=[
            pltpu.VMEM((freqs, slab_rows + 4, DIR, LANES), jnp.float32),
            pltpu.VMEM((freqs, slab_rows + 4, DIR, LANES), jnp.float32),
            pltpu.VMEM((10 + 3 * freqs, slab_rows + 16, LANES), jnp.float32),
            pltpu.VMEM((freqs, slab_rows + 1, DIR, LANES), jnp.float32),
            pltpu.VMEM((freqs, 2, slab_rows, DIR, LANES), jnp.float32),
            pltpu.VMEM((freqs * DIR * slab_rows, LANES), jnp.float32),
            pltpu.VMEM((freqs * DIR, slab_rows, LANES), jnp.float32),
            pltpu.SemaphoreType.DMA((slab_rows // BLOCK,)),
        ],
        compiler_params=pltpu.CompilerParams(vmem_limit_bytes=32 * 1024 * 1024),
        name="slab",
    )(arrived)
    return out.reshape(1, freqs * DIR, slab_rows, LANES)


def shards(*arrays):
    spectra, land_mask = arrays[0], arrays[5]
    parts = lax.axis_size(GROUP)
    rows, comps = spectra.shape
    whole_frequencies = comps == parts * 2 * DIR
    fits = rows % LANES == LANES // 2 and land_mask.shape == (4, LANES) and parts % 2 == 0
    if whole_frequencies and fits:
        return slab_plan(*arrays[:5], *arrays[6:])
    return tile_plan(*arrays)


def solution(mesh):
    placed = (
        P(("groups", "pts", "comp"), "sub"),
        P(("groups", "pts", "comp")),
        P("sub"),
        P("sub"),
        P(("groups", "pts", "comp")),
        P(("groups", "pts", "comp"), None),
        P(("groups", "sub"), ("pts", "comp"), None),
        P("groups", ("pts", "comp"), None),
        P(("groups", "pts", "comp"), None),
    )
    return jax.shard_map(
        shards,
        mesh=mesh,
        in_specs=placed,
        out_specs=P("sub", ("pts", "comp"), "groups", None),
        check_vma=False,
    )
```

```python
import functools
import math
import jax
import jax.numpy as jnp
from jax import lax
from jax.experimental import pallas as pl
from jax.experimental.pallas import tpu as pltpu
from jax.sharding import PartitionSpec as P

DIR = 24
SUBSTEPS = 2
LANES = 128
GROUP = ("pts", "comp")


courant = 0.35


def with_halo(cells, sides, width):
    for axis, dim in sides:
        count = lax.axis_size(axis)
        ends = count - 1
        head = lax.slice_in_dim(cells, 0, width, axis=dim)
        tail = lax.slice_in_dim(cells, cells.shape[dim] - width, cells.shape[dim], axis=dim)
        cells = jnp.concatenate(
            [
                lax.ppermute(tail, axis, [(i, (i + 1) % count) for i in range(ends)]),
                cells,
                lax.ppermute(head, axis, [((i + 1) % count, i) for i in range(ends)]),
            ],
            axis=dim,
        )
    return cells


def take_slice(values, first_index, extent, along_axis):
    return lax.slice_in_dim(values, first_index, first_index + extent, axis=along_axis)


def upwind_divergence(padded, motion, along_axis):
    length = padded.shape[along_axis] - 4
    face_count = length + 1
    behind = take_slice(padded, 0, face_count, along_axis)
    centre = take_slice(padded, 1, face_count, along_axis)
    onward = take_slice(padded, 2, face_count, along_axis)
    beyond = take_slice(padded, 3, face_count, along_axis)
    left_face = (6.0 * centre + 3.0 * onward - behind) * 0.125
    right_face = (3.0 * centre + 6.0 * onward - beyond) * 0.125
    face_speed = 0.5 * (
        take_slice(motion, 1, face_count, along_axis)
        + take_slice(motion, 2, face_count, along_axis)
    )
    fluxes = jnp.maximum(face_speed, 0.0) * left_face + jnp.minimum(face_speed, 0.0) * right_face
    return take_slice(fluxes, 1, length, along_axis) - take_slice(fluxes, 0, length, along_axis)


def substep(extended, speed_x, speed_y, sea_mask):
    across = upwind_divergence(extended, speed_x, 1)
    centre_part = extended[:, 2:-2]
    padding = ((0, 0), (0, 0), (2, 2))
    sideways = upwind_divergence(jnp.pad(centre_part, padding), jnp.pad(speed_y, padding), 2)
    return (centre_part - courant * (across + sideways)) * sea_mask


def direction_tables(directions):
    angles = jnp.arange(directions, dtype=jnp.float32) * (2.0 * jnp.pi / directions)
    return (jnp.cos(angles), jnp.sin(angles))


def source_term(values, wind_speed, growth, damping):
    return values * jnp.exp(wind_speed[:, None] * growth[None, :] - damping[None, :])


def velocities(stacked, freq_count):
    cosine_table, sine_table = direction_tables(DIR)
    celerity = stacked[:freq_count][:, None]
    shape_out = (freq_count * DIR,) + stacked.shape[1:]
    speed_x = (
        celerity * cosine_table[None, :, None, None] + stacked[freq_count][None, None]
    ).reshape(shape_out)
    speed_y = (
        celerity * sine_table[None, :, None, None] + stacked[freq_count + 1][None, None]
    ).reshape(shape_out)
    return (speed_x, speed_y)


def deliver(bulk_rows, small_rows):
    return (
        lax.all_to_all(bulk_rows, GROUP, split_axis=0, concat_axis=0, tiled=True),
        lax.all_to_all(small_rows, GROUP, split_axis=0, concat_axis=0, tiled=True),
    )


def tile_plan(spectra, wind, growth, damping, row_cell, land_mask, group_speed, current, turning):
    tile_count = lax.axis_size(GROUP)
    comp_width = spectra.shape[1]
    tile_rows, tile_cols = land_mask.shape
    cell_count = tile_rows * tile_cols
    capacity = cell_count // tile_count
    target = row_cell // cell_count
    local_cell = (row_cell - target * cell_count).astype(jnp.float32)
    matches = (target[:, None] == jnp.arange(tile_count, dtype=jnp.int32)[None, :]).astype(
        jnp.int32
    )
    bucket_slot = jnp.sum((jnp.cumsum(matches, axis=0) - 1) * matches, axis=1)

    def bucket(values, filler):
        shape_out = (tile_count, capacity) + values.shape[1:]
        return jnp.full(shape_out, filler, jnp.float32).at[target, bucket_slot].set(values)

    bulk_rows = bucket(source_term(spectra, wind, growth, damping), 0.0)
    small_rows = bucket(local_cell[:, None], float(cell_count))
    bulk_back, small_back = deliver(bulk_rows, small_rows)
    cell_index = small_back[:, :, 0].reshape(-1).astype(jnp.int32)
    flat_values = bulk_back.reshape((tile_count * capacity,) + bulk_back.shape[2:])
    tile_field = (
        jnp.zeros((cell_count,) + bulk_back.shape[2:], jnp.float32)
        .at[cell_index]
        .set(flat_values, mode="drop")
    )
    spectrum = tile_field.T.reshape(comp_width, tile_rows, tile_cols)
    freq_count = comp_width // DIR
    reach = 2 * SUBSTEPS
    stacked = jnp.concatenate([group_speed, current, land_mask.astype(jnp.float32)[None]], axis=0)
    rimmed = with_halo(stacked, ((GROUP, 1),), 2 * SUBSTEPS)
    speed_x, speed_y = velocities(rimmed, freq_count)
    sea_rim = rimmed[freq_count + 2 :]

    def window(values, margin):
        return lax.slice_in_dim(values, reach - margin, reach + tile_rows + margin, axis=1)

    for repeat in range(SUBSTEPS):
        extended = with_halo(spectrum, ((GROUP, 1),), 2)
        spectrum = substep(extended, window(speed_x, 2), window(speed_y, 0), window(sea_rim, 0)[0])
    blocks = spectrum.reshape(freq_count, DIR, tile_rows, tile_cols)
    wrapped = jnp.concatenate([blocks[:, -2:], blocks, blocks[:, :2]], axis=1)
    turning_full = jnp.broadcast_to(turning[None, None], wrapped.shape)
    blocks = blocks - upwind_divergence(wrapped, turning_full, 1)
    spectrum = blocks.reshape(comp_width, tile_rows, tile_cols)
    shipped = lax.all_to_all(spectrum, GROUP, split_axis=0, concat_axis=1, tiled=True)
    return shipped[None]


def pack_kernel(
    parts,
    freqs,
    spectra_ref,
    wind_ref,
    growth_ref,
    damping_ref,
    cell_ref,
    speed_ref,
    current_ref,
    turning_ref,
    out_ref,
):
    rows, comps = spectra_ref.shape
    half = LANES // 2
    full = rows // LANES
    padded = (full + 1) * LANES
    low = lax.broadcasted_iota(jnp.int32, (8, LANES), 1) < half
    per_freq = DIR // 8
    span_rows = full * DIR + 16

    def extended(row, filler):
        return jnp.concatenate([row[None], jnp.full((1, half), filler, jnp.float32)], axis=1)

    def as_columns(row):
        return jnp.broadcast_to(row, (LANES, padded)).T

    cells = cell_ref[...].astype(jnp.float32)
    keys = extended(cells, 1e9)
    key_cols = as_columns(keys)
    ranks = jnp.concatenate(
        [
            jnp.sum(
                jnp.where(key_cols < keys[:, c * LANES : (c + 1) * LANES], 1.0, 0.0), axis=0, keepdims=True
            )
            for c in range(full + 1)
        ],
        axis=1,
    )
    place = lax.broadcasted_iota(jnp.int32, (padded, padded), 0)
    odd = lax.axis_index(GROUP) % 2 == 1
    swapped = jnp.where(place % LANES < half, place + half, place - half)
    place = jnp.where((place < full * LANES) & odd, swapped, place)
    place = jnp.where(place < rows, place, place - half).astype(jnp.float32)
    order = jnp.where(place == ranks, 1.0, 0.0).astype(jnp.bfloat16)

    wind_cols = as_columns(extended(wind_ref[...], 0.0))
    turned = []
    for block in range(comps // LANES):
        lanes = pl.ds(block * LANES, LANES)
        growth = growth_ref[lanes][None]
        damping = damping_ref[lanes][None]

        def source(first, count):
            span = pl.ds(first, count)
            return spectra_ref[span, lanes] * jnp.exp(
                wind_cols[first : first + count] * growth - damping
            )

        pieces = [source(c * LANES, LANES).T for c in range(full)]
        last = jnp.concatenate([source(full * LANES, half), jnp.zeros((half, LANES), jnp.float32)], axis=0)
        turned.append(jnp.concatenate(pieces + [last.T], axis=1))
    turned.append(jnp.broadcast_to(extended(cells, 0.0), (16, padded)))
    values = jnp.concatenate(turned, axis=0)
    head = values.astype(jnp.bfloat16)
    rest = (values - head.astype(jnp.float32)).astype(jnp.bfloat16)
    both = lax.dot_general(
        jnp.concatenate([head, rest], axis=0),
        order,
        (((1,), (1,)), ((), ())),
        preferred_element_type=jnp.float32,
    )

    def piece(first, count, chunk):
        lanes = slice(chunk * LANES, (chunk + 1) * LANES)
        return both[first : first + count, lanes] + both[comps + 16 + first : comps + 16 + first + count, lanes]

    shared = jnp.concatenate(
        [current_ref[0], current_ref[1], turning_ref[...]] + [piece(comps, 1, c) for c in range(full + 1)],
        axis=0,
    )
    for part in range(parts):
        for f in range(freqs):
            freq = part * freqs + f
            at = f * span_rows
            for chunk in range(full):
                out_ref[part, pl.ds(at + chunk * DIR, DIR), :] = piece(freq * DIR, DIR, chunk)
            at += full * DIR
            one, two, three = (piece(freq * DIR + g * 8, 8, full) for g in range(per_freq))
            out_ref[part, pl.ds(at, 8), :] = jnp.where(low, one, two)
            folded = jnp.where(low, three, pltpu.roll(three, 4, 0))
            out_ref[part, pl.ds(at + 8, 8), :] = jnp.concatenate([folded[:4], speed_ref[freq]], axis=0)
        out_ref[part, pl.ds(freqs * span_rows, shared.shape[0]), :] = shared


BLOCK = 8
PER_STEP = 4


def slab_kernel(
    parts,
    tile_rows,
    full,
    freqs,
    recv_ref,
    out_ref,
    first,
    second,
    table,
    faces_x,
    faces_y,
    moved_ref,
    done_ref,
    sems,
):
    slab_rows = parts * tile_rows
    half = LANES // 2
    span_rows = full * DIR + 16
    shared_base = freqs * span_rows
    highs = slab_rows // 2
    width = freqs * 2 * DIR
    low_lane = lax.broadcasted_iota(jnp.int32, (1, LANES), 1) < half
    low_lanes = lax.broadcasted_iota(jnp.int32, (8, LANES), 1) < half
    low_wide = lax.broadcasted_iota(jnp.int32, (DIR, LANES), 1) < half
    top_rows = lax.broadcasted_iota(jnp.int32, (8, LANES), 0) < 4
    cell_iota = lax.broadcasted_iota(jnp.int32, (2 * LANES, LANES), 0).astype(jnp.float32).astype(jnp.bfloat16)
    high_iota = lax.broadcasted_iota(jnp.int32, (highs, LANES), 0)

    def cells_of(owner, chunk):
        return recv_ref[owner, pl.ds(shared_base + 3 * tile_rows + chunk, 1), :].astype(jnp.int32)

    owner_rows = full * LANES + half
    capacity = tile_rows * LANES // parts
    spans = []
    for begin in range(0, owner_rows, half):
        tiles = [
            t
            for t in range(parts)
            if owner_rows - capacity * (parts - t) < begin + half and capacity * (t + 1) > begin
        ]
        spans.append(range(tiles[0] * tile_rows // 2, (tiles[-1] + 1) * tile_rows // 2))
    columns = [[] for _ in spans]
    hots = [[] for _ in spans]

    def repeated(line, count):
        tile = jnp.broadcast_to(line, (16, LANES)).astype(jnp.bfloat16)
        return jnp.concatenate([tile] * (count // 16), axis=0)

    def place(chunk, cells, values):
        high = cells // (2 * LANES)
        low = (cells - high * (2 * LANES)).astype(jnp.float32)
        low = repeated(low, 2 * LANES)
        hots[chunk].append(jnp.where(cell_iota == low, 1.0, 0.0).astype(jnp.bfloat16))
        pieces = []
        for value in values:
            head = value.astype(jnp.bfloat16).astype(jnp.float32)
            pieces += [head, value - head]
        both = jnp.concatenate(pieces, axis=0).astype(jnp.bfloat16)
        column = []
        for h in spans[chunk]:
            column.append(both * repeated((high == h).astype(jnp.float32), width))
        column.append((high_iota == high).astype(jnp.float32).astype(jnp.bfloat16))
        columns[chunk].append(jnp.concatenate(column, axis=0))

    for pair in range(parts // 2):
        even, odd = 2 * pair, 2 * pair + 1
        for chunk in range(full):
            here, there = (
                [recv_ref[owner, pl.ds(f * span_rows + chunk * DIR, DIR), :] for f in range(freqs)]
                for owner in (even, odd)
            )
            cells, cells_there = cells_of(even, chunk), cells_of(odd, chunk)
            for side in range(2):
                place(
                    2 * chunk + side,
                    jnp.where(low_lane, cells, cells_there),
                    [jnp.where(low_wide, a, b) for a, b in zip(here, there)],
                )
                here, there, cells, cells_there = there, here, cells_there, cells

        def merged(offset):
            own, other = recv_ref[even, pl.ds(offset, 8), :], recv_ref[odd, pl.ds(offset, 8), :]
            return (
                jnp.where(low_lanes, own, pltpu.roll(other, half, 1)),
                jnp.where(low_lanes, pltpu.roll(own, half, 1), other),
            )

        values = []
        for f in range(freqs):
            one, two = merged(f * span_rows + full * DIR)
            three, four = merged(f * span_rows + full * DIR + 8)
            values.append(
                jnp.concatenate([one, two, jnp.where(top_rows, three, pltpu.roll(four, 4, 0))], axis=0)
            )
        place(2 * full, jnp.where(low_lane, cells_of(even, full), cells_of(odd, full)), values)

    lane = lax.broadcasted_iota(jnp.int32, (slab_rows, LANES), 1)
    zero_rows = jnp.zeros((8, LANES), jnp.float32)

    def gather(offset):
        return jnp.concatenate(
            [recv_ref[owner, pl.ds(offset, tile_rows), :] for owner in range(parts)], axis=0
        )

    gain = 0.5 * courant / 8.0
    slots = iter(range(table.shape[0]))

    def keep(rows):
        slot = next(slots)
        table[slot, pl.ds(8, rows.shape[0]), :] = rows
        return slot

    def face_x(rows):
        slot = next(slots)
        table[slot, pl.ds(0, 8), :] = zero_rows
        table[slot, pl.ds(8 + slab_rows, 8), :] = zero_rows
        table[slot, pl.ds(8, slab_rows), :] = rows
        faces = gain * (table[slot, pl.ds(7, slab_rows + 8), :] + table[slot, pl.ds(8, slab_rows + 8), :])
        table[slot, pl.ds(7, slab_rows + 8), :] = faces
        return slot

    def face_y(rows):
        after = jnp.where(lane < LANES - 1, pltpu.roll(rows, LANES - 1, 1), 0.0)
        before = jnp.where(lane > 0, pltpu.roll(rows, 1, 1), 0.0)
        return keep(gain * (rows + after)), keep(gain * (rows + before))

    speeds = [gather(f * span_rows + full * DIR + 12) for f in range(freqs)]
    current_x, current_y, turning = (gather(shared_base + kind * tile_rows) for kind in range(3))
    current_x_face, speed_x_face = face_x(current_x), [face_x(s) for s in speeds]
    current_y_faces, speed_y_faces = face_y(current_y), [face_y(s) for s in speeds]
    step_angle = 2.0 * math.pi / DIR
    sublane = lax.broadcasted_iota(jnp.int32, (8, LANES), 0)
    cosine0 = jnp.ones((8, LANES), jnp.float32)
    sine0 = jnp.zeros((8, LANES), jnp.float32)
    for d in range(1, 8):
        cosine0 = jnp.where(sublane == d, math.cos(d * step_angle), cosine0)
        sine0 = jnp.where(sublane == d, math.sin(d * step_angle), sine0)
    turns = [(math.cos(g * 8 * step_angle), math.sin(g * 8 * step_angle)) for g in range(DIR // 8)]
    cosine = jnp.concatenate([c * cosine0 - t * sine0 for c, t in turns], axis=0)
    sine = jnp.concatenate([c * sine0 + t * cosine0 for c, t in turns], axis=0)

    def row(slot, x):
        return table[slot, pl.ds(8 + x, 1), :]

    for f in range(freqs):
        for x in range(-1, slab_rows):
            faces_x[f, x + 1] = row(speed_x_face[f], x) * cosine + row(current_x_face, x)
        for x in range(slab_rows):
            for side in range(2):
                faces_y[f, side, x] = row(speed_y_faces[f][side], x) * sine + row(current_y_faces[side], x)

    scattered = [
        lax.dot_general(
            jnp.concatenate(column, axis=1),
            jnp.concatenate(hot, axis=1),
            (((1,), (1,)), ((), ())),
            preferred_element_type=jnp.float32,
        )
        for hot, column in zip(hots, columns)
    ]
    nothing = jnp.zeros((DIR, LANES), jnp.float32)
    for f in range(freqs):
        for field in (first, second):
            for edge in (0, 1, slab_rows + 2, slab_rows + 3):
                field[f, edge] = nothing
        for h in range(highs):
            terms = []
            for span, product in zip(spans, scattered):
                if h in span:
                    at = (h - span[0]) * width + f * 2 * DIR
                    terms += [product[at : at + DIR], product[at + DIR : at + 2 * DIR]]
            total = sum(terms[1:], terms[0])
            first[f, 2 * h + 2] = total[:, :LANES]
            first[f, 2 * h + 3] = total[:, LANES:]
    named = sum(product[len(span) * width :] for span, product in zip(spans, scattered))

    land_slots = keep(named[:, :LANES]), keep(named[:, LANES:])
    ahead = jnp.maximum(turning, 0.0) * 0.125
    back = jnp.minimum(turning, 0.0) * 0.125
    bend_slots = [
        keep(rows)
        for rows in (
            -ahead,
            7.0 * ahead + 3.0 * back,
            1.0 - 3.0 * (ahead - back),
            -3.0 * ahead - 7.0 * back,
            back,
        )
    ]

    lane_wide = lax.broadcasted_iota(jnp.int32, (DIR, LANES), 1)

    def flux(speed, behind, centre3, onward3, beyond):
        positive = speed > 0.0
        near = jnp.where(positive, centre3, onward3)
        far = jnp.where(positive, behind, beyond)
        return speed * ((centre3 + onward3) + (near - far))

    def advance(field, step, carry, finish):
        carry = list(carry)
        for i in range(BLOCK):
            x = step * BLOCK + i
            sea = row(land_slots[i % 2], step * (BLOCK // 2) + i // 2)
            for f in range(freqs):
                entering, centre3 = carry[f]
                centre = field[f, x + 2]
                onward3 = 3.0 * field[f, x + 3]
                leaving = flux(faces_x[f, x + 1], field[f, x + 1], centre3, onward3, field[f, x + 4])
                up1 = jnp.where(lane_wide < LANES - 1, pltpu.roll(centre, LANES - 1, 1), 0.0)
                up2 = jnp.where(lane_wide < LANES - 2, pltpu.roll(centre, LANES - 2, 1), 0.0)
                down1 = jnp.where(lane_wide > 0, pltpu.roll(centre, 1, 1), 0.0)
                down2 = jnp.where(lane_wide > 1, pltpu.roll(centre, 2, 1), 0.0)
                right = flux(faces_y[f, 0, x], down1, centre3, 3.0 * up1, up2)
                left = flux(faces_y[f, 1, x], down2, 3.0 * down1, centre3, up1)
                finish(f, x, (centre - (leaving - entering) - (right - left)) * sea)
                carry[f] = leaving, onward3
        return tuple(carry)

    def enter(field):
        carry = []
        for f in range(freqs):
            start3 = 3.0 * field[f, 2]
            carry.append((flux(faces_x[f, 0], nothing, nothing, start3, field[f, 3]), start3))
        return tuple(carry)

    def store(f, x, moved):
        second[f, x + 2] = moved

    pitch = slab_rows + 1

    def turn(f, x, moved):
        for g in range(DIR // 8):
            at = (f * DIR + g * 8) * pitch + x
            moved_ref[pl.ds(at, 8, stride=pitch), :] = moved[g * 8 : g * 8 + 8]

    def copy_out(step):
        part = pl.ds(pl.multiple_of(step * BLOCK, BLOCK), BLOCK)
        return pltpu.make_async_copy(done_ref.at[:, part, :], out_ref.at[:, part, :], sems.at[step])

    def final(block, carry):
        carry = advance(second, block, carry, turn)
        at = pl.multiple_of(block * BLOCK, BLOCK)
        weights = [table[slot, pl.ds(8 + at, BLOCK), :] for slot in bend_slots]
        for f in range(freqs):
            ring = [moved_ref[pl.ds((f * DIR + d) * pitch + at, BLOCK), :] for d in range(DIR)]
            for d in range(DIR):
                bent = weights[2] * ring[d]
                for k in (0, 1, 3, 4):
                    bent = bent + weights[k] * ring[(d + k - 2) % DIR]
                done_ref[f * DIR + d, pl.ds(at, BLOCK), :] = bent
        copy_out(block).start()
        return carry

    def sweep(one_block, carry):
        def body(step, carry):
            for i in range(PER_STEP):
                carry = one_block(step * PER_STEP + i, carry)
            return carry

        lax.fori_loop(0, slab_rows // BLOCK // PER_STEP, body, carry)

    sweep(lambda block, carry: advance(first, block, carry, store), enter(first))
    sweep(final, enter(second))
    for block in range(slab_rows // BLOCK):
        copy_out(block).wait()


def slab_plan(spectra, wind, growth, damping, row_cell, group_speed, current, turning):
    parts = lax.axis_size(GROUP)
    rows, comps = spectra.shape
    tile_rows = turning.shape[0]
    freqs = comps // parts // DIR
    full = rows // LANES
    slab_rows = parts * tile_rows
    highs = slab_rows // 2
    block_rows = -(-(freqs * (full * DIR + 16) + 3 * tile_rows + full + 1) // 8) * 8
    packed = pl.pallas_call(
        functools.partial(pack_kernel, parts, freqs),
        out_shape=pltpu.VMEM((parts, block_rows, LANES), jnp.float32),
        compiler_params=pltpu.CompilerParams(vmem_limit_bytes=56 * 1024 * 1024),
        name="pack",
    )(spectra, wind, growth, damping, row_cell, group_speed, current, turning)
    arrived = lax.all_to_all(packed, GROUP, split_axis=0, concat_axis=0, tiled=True)
    out = pl.pallas_call(
        functools.partial(slab_kernel, parts, tile_rows, full, freqs),
        out_shape=jax.ShapeDtypeStruct((freqs * DIR, slab_rows, LANES), jnp.float32),
        in_specs=[pl.BlockSpec(memory_space=pltpu.VMEM)],
        out_specs=pl.BlockSpec(memory_space=pl.ANY),
        scratch_shapes=[
            pltpu.VMEM((freqs, slab_rows + 4, DIR, LANES), jnp.float32),
            pltpu.VMEM((freqs, slab_rows + 4, DIR, LANES), jnp.float32),
            pltpu.VMEM((10 + 3 * freqs, slab_rows + 16, LANES), jnp.float32),
            pltpu.VMEM((freqs, slab_rows + 1, DIR, LANES), jnp.float32),
            pltpu.VMEM((freqs, 2, slab_rows, DIR, LANES), jnp.float32),
            pltpu.VMEM((freqs * DIR * (slab_rows + 1), LANES), jnp.float32),
            pltpu.VMEM((freqs * DIR, slab_rows, LANES), jnp.float32),
            pltpu.SemaphoreType.DMA((slab_rows // BLOCK,)),
        ],
        compiler_params=pltpu.CompilerParams(vmem_limit_bytes=32 * 1024 * 1024),
        name="slab",
    )(arrived)
    return out.reshape(1, freqs * DIR, slab_rows, LANES)


def shards(*arrays):
    spectra, land_mask = arrays[0], arrays[5]
    parts = lax.axis_size(GROUP)
    rows, comps = spectra.shape
    whole_frequencies = comps == parts * 2 * DIR
    fits = rows % LANES == LANES // 2 and land_mask.shape == (4, LANES) and parts % 2 == 0
    if whole_frequencies and fits:
        return slab_plan(*arrays[:5], *arrays[6:])
    return tile_plan(*arrays)


def solution(mesh):
    placed = (
        P(("groups", "pts", "comp"), "sub"),
        P(("groups", "pts", "comp")),
        P("sub"),
        P("sub"),
        P(("groups", "pts", "comp")),
        P(("groups", "pts", "comp"), None),
        P(("groups", "sub"), ("pts", "comp"), None),
        P("groups", ("pts", "comp"), None),
        P(("groups", "pts", "comp"), None),
    )
    return jax.shard_map(
        shards,
        mesh=mesh,
        in_specs=placed,
        out_specs=P("sub", ("pts", "comp"), "groups", None),
        check_vma=False,
    )
```

```python
import functools
import math
import jax
import jax.numpy as jnp
from jax import lax
from jax.experimental import pallas as pl
from jax.experimental.pallas import tpu as pltpu
from jax.sharding import PartitionSpec as P

DIR = 24
SUBSTEPS = 2
LANES = 128
GROUP = ("pts", "comp")


courant = 0.35


def with_halo(cells, sides, width):
    for axis, dim in sides:
        count = lax.axis_size(axis)
        ends = count - 1
        head = lax.slice_in_dim(cells, 0, width, axis=dim)
        tail = lax.slice_in_dim(cells, cells.shape[dim] - width, cells.shape[dim], axis=dim)
        cells = jnp.concatenate(
            [
                lax.ppermute(tail, axis, [(i, (i + 1) % count) for i in range(ends)]),
                cells,
                lax.ppermute(head, axis, [((i + 1) % count, i) for i in range(ends)]),
            ],
            axis=dim,
        )
    return cells


def take_slice(values, first_index, extent, along_axis):
    return lax.slice_in_dim(values, first_index, first_index + extent, axis=along_axis)


def upwind_divergence(padded, motion, along_axis):
    length = padded.shape[along_axis] - 4
    face_count = length + 1
    behind = take_slice(padded, 0, face_count, along_axis)
    centre = take_slice(padded, 1, face_count, along_axis)
    onward = take_slice(padded, 2, face_count, along_axis)
    beyond = take_slice(padded, 3, face_count, along_axis)
    left_face = (6.0 * centre + 3.0 * onward - behind) * 0.125
    right_face = (3.0 * centre + 6.0 * onward - beyond) * 0.125
    face_speed = 0.5 * (
        take_slice(motion, 1, face_count, along_axis)
        + take_slice(motion, 2, face_count, along_axis)
    )
    fluxes = jnp.maximum(face_speed, 0.0) * left_face + jnp.minimum(face_speed, 0.0) * right_face
    return take_slice(fluxes, 1, length, along_axis) - take_slice(fluxes, 0, length, along_axis)


def substep(extended, speed_x, speed_y, sea_mask):
    across = upwind_divergence(extended, speed_x, 1)
    centre_part = extended[:, 2:-2]
    padding = ((0, 0), (0, 0), (2, 2))
    sideways = upwind_divergence(jnp.pad(centre_part, padding), jnp.pad(speed_y, padding), 2)
    return (centre_part - courant * (across + sideways)) * sea_mask


def direction_tables(directions):
    angles = jnp.arange(directions, dtype=jnp.float32) * (2.0 * jnp.pi / directions)
    return (jnp.cos(angles), jnp.sin(angles))


def source_term(values, wind_speed, growth, damping):
    return values * jnp.exp(wind_speed[:, None] * growth[None, :] - damping[None, :])


def velocities(stacked, freq_count):
    cosine_table, sine_table = direction_tables(DIR)
    celerity = stacked[:freq_count][:, None]
    shape_out = (freq_count * DIR,) + stacked.shape[1:]
    speed_x = (
        celerity * cosine_table[None, :, None, None] + stacked[freq_count][None, None]
    ).reshape(shape_out)
    speed_y = (
        celerity * sine_table[None, :, None, None] + stacked[freq_count + 1][None, None]
    ).reshape(shape_out)
    return (speed_x, speed_y)


def deliver(bulk_rows, small_rows):
    return (
        lax.all_to_all(bulk_rows, GROUP, split_axis=0, concat_axis=0, tiled=True),
        lax.all_to_all(small_rows, GROUP, split_axis=0, concat_axis=0, tiled=True),
    )


def tile_plan(spectra, wind, growth, damping, row_cell, land_mask, group_speed, current, turning):
    tile_count = lax.axis_size(GROUP)
    comp_width = spectra.shape[1]
    tile_rows, tile_cols = land_mask.shape
    cell_count = tile_rows * tile_cols
    capacity = cell_count // tile_count
    target = row_cell // cell_count
    local_cell = (row_cell - target * cell_count).astype(jnp.float32)
    matches = (target[:, None] == jnp.arange(tile_count, dtype=jnp.int32)[None, :]).astype(
        jnp.int32
    )
    bucket_slot = jnp.sum((jnp.cumsum(matches, axis=0) - 1) * matches, axis=1)

    def bucket(values, filler):
        shape_out = (tile_count, capacity) + values.shape[1:]
        return jnp.full(shape_out, filler, jnp.float32).at[target, bucket_slot].set(values)

    bulk_rows = bucket(source_term(spectra, wind, growth, damping), 0.0)
    small_rows = bucket(local_cell[:, None], float(cell_count))
    bulk_back, small_back = deliver(bulk_rows, small_rows)
    cell_index = small_back[:, :, 0].reshape(-1).astype(jnp.int32)
    flat_values = bulk_back.reshape((tile_count * capacity,) + bulk_back.shape[2:])
    tile_field = (
        jnp.zeros((cell_count,) + bulk_back.shape[2:], jnp.float32)
        .at[cell_index]
        .set(flat_values, mode="drop")
    )
    spectrum = tile_field.T.reshape(comp_width, tile_rows, tile_cols)
    freq_count = comp_width // DIR
    reach = 2 * SUBSTEPS
    stacked = jnp.concatenate([group_speed, current, land_mask.astype(jnp.float32)[None]], axis=0)
    rimmed = with_halo(stacked, ((GROUP, 1),), 2 * SUBSTEPS)
    speed_x, speed_y = velocities(rimmed, freq_count)
    sea_rim = rimmed[freq_count + 2 :]

    def window(values, margin):
        return lax.slice_in_dim(values, reach - margin, reach + tile_rows + margin, axis=1)

    for repeat in range(SUBSTEPS):
        extended = with_halo(spectrum, ((GROUP, 1),), 2)
        spectrum = substep(extended, window(speed_x, 2), window(speed_y, 0), window(sea_rim, 0)[0])
    blocks = spectrum.reshape(freq_count, DIR, tile_rows, tile_cols)
    wrapped = jnp.concatenate([blocks[:, -2:], blocks, blocks[:, :2]], axis=1)
    turning_full = jnp.broadcast_to(turning[None, None], wrapped.shape)
    blocks = blocks - upwind_divergence(wrapped, turning_full, 1)
    spectrum = blocks.reshape(comp_width, tile_rows, tile_cols)
    shipped = lax.all_to_all(spectrum, GROUP, split_axis=0, concat_axis=1, tiled=True)
    return shipped[None]


def pack_kernel(
    parts,
    freqs,
    spectra_ref,
    wind_ref,
    growth_ref,
    damping_ref,
    cell_ref,
    speed_ref,
    current_ref,
    turning_ref,
    out_ref,
):
    rows, comps = spectra_ref.shape
    half = LANES // 2
    full = rows // LANES
    padded = (full + 1) * LANES
    low = lax.broadcasted_iota(jnp.int32, (8, LANES), 1) < half
    per_freq = DIR // 8
    span_rows = full * DIR + 16

    def extended(row, filler):
        return jnp.concatenate([row[None], jnp.full((1, half), filler, jnp.float32)], axis=1)

    def as_columns(row):
        return jnp.broadcast_to(row, (LANES, padded)).T

    cells = cell_ref[...].astype(jnp.float32)
    keys = extended(cells, 1e9)
    key_cols = as_columns(keys)
    ranks = jnp.concatenate(
        [
            jnp.sum(
                jnp.where(key_cols < keys[:, c * LANES : (c + 1) * LANES], 1.0, 0.0), axis=0, keepdims=True
            )
            for c in range(full + 1)
        ],
        axis=1,
    )
    place = lax.broadcasted_iota(jnp.int32, (padded, padded), 0)
    odd = lax.axis_index(GROUP) % 2 == 1
    swapped = jnp.where(place % LANES < half, place + half, place - half)
    place = jnp.where((place < full * LANES) & odd, swapped, place)
    place = jnp.where(place < rows, place, place - half).astype(jnp.float32)
    order = jnp.where(place == ranks, 1.0, 0.0).astype(jnp.bfloat16)

    wind_cols = as_columns(extended(wind_ref[...], 0.0))
    turned = []
    for block in range(comps // LANES):
        lanes = pl.ds(block * LANES, LANES)
        growth = growth_ref[lanes][None]
        damping = damping_ref[lanes][None]

        def source(first, count):
            span = pl.ds(first, count)
            return spectra_ref[span, lanes] * jnp.exp(
                wind_cols[first : first + count] * growth - damping
            )

        pieces = [source(c * LANES, LANES).T for c in range(full)]
        last = jnp.concatenate([source(full * LANES, half), jnp.zeros((half, LANES), jnp.float32)], axis=0)
        turned.append(jnp.concatenate(pieces + [last.T], axis=1))
    turned.append(jnp.broadcast_to(extended(cells, 0.0), (16, padded)))
    values = jnp.concatenate(turned, axis=0)
    head = values.astype(jnp.bfloat16)
    rest = (values - head.astype(jnp.float32)).astype(jnp.bfloat16)
    both = lax.dot_general(
        jnp.concatenate([head, rest], axis=0),
        order,
        (((1,), (1,)), ((), ())),
        preferred_element_type=jnp.float32,
    )

    def piece(first, count, chunk):
        lanes = slice(chunk * LANES, (chunk + 1) * LANES)
        return both[first : first + count, lanes] + both[comps + 16 + first : comps + 16 + first + count, lanes]

    shared = jnp.concatenate(
        [current_ref[0], current_ref[1], turning_ref[...]] + [piece(comps, 1, c) for c in range(full + 1)],
        axis=0,
    )
    for part in range(parts):
        for f in range(freqs):
            freq = part * freqs + f
            at = f * span_rows
            for chunk in range(full):
                out_ref[part, pl.ds(at + chunk * DIR, DIR), :] = piece(freq * DIR, DIR, chunk)
            at += full * DIR
            one, two, three = (piece(freq * DIR + g * 8, 8, full) for g in range(per_freq))
            out_ref[part, pl.ds(at, 8), :] = jnp.where(low, one, two)
            folded = jnp.where(low, three, pltpu.roll(three, 4, 0))
            out_ref[part, pl.ds(at + 8, 8), :] = jnp.concatenate([folded[:4], speed_ref[freq]], axis=0)
        out_ref[part, pl.ds(freqs * span_rows, shared.shape[0]), :] = shared


BLOCK = 8


def slab_kernel(
    parts,
    tile_rows,
    full,
    freqs,
    recv_ref,
    out_ref,
    first,
    second,
    table,
    faces_x,
    faces_y,
    moved_ref,
    done_ref,
    sems,
):
    slab_rows = parts * tile_rows
    half = LANES // 2
    span_rows = full * DIR + 16
    shared_base = freqs * span_rows
    highs = slab_rows // 2
    width = freqs * 2 * DIR
    low_lane = lax.broadcasted_iota(jnp.int32, (1, LANES), 1) < half
    low_lanes = lax.broadcasted_iota(jnp.int32, (8, LANES), 1) < half
    low_wide = lax.broadcasted_iota(jnp.int32, (DIR, LANES), 1) < half
    top_rows = lax.broadcasted_iota(jnp.int32, (8, LANES), 0) < 4
    cell_iota = lax.broadcasted_iota(jnp.int32, (2 * LANES, LANES), 0).astype(jnp.float32).astype(jnp.bfloat16)
    high_iota = lax.broadcasted_iota(jnp.int32, (highs, LANES), 0)

    def cells_of(owner, chunk):
        return recv_ref[owner, pl.ds(shared_base + 3 * tile_rows + chunk, 1), :].astype(jnp.int32)

    owner_rows = full * LANES + half
    capacity = tile_rows * LANES // parts
    spans = []
    for begin in range(0, owner_rows, half):
        tiles = [
            t
            for t in range(parts)
            if owner_rows - capacity * (parts - t) < begin + half and capacity * (t + 1) > begin
        ]
        spans.append(range(tiles[0] * tile_rows // 2, (tiles[-1] + 1) * tile_rows // 2))
    columns = [[] for _ in spans]
    hots = [[] for _ in spans]

    def repeated(line, count):
        tile = jnp.broadcast_to(line, (16, LANES)).astype(jnp.bfloat16)
        return jnp.concatenate([tile] * (count // 16), axis=0)

    def place(chunk, cells, values):
        high = cells // (2 * LANES)
        low = (cells - high * (2 * LANES)).astype(jnp.float32)
        low = repeated(low, 2 * LANES)
        hots[chunk].append(jnp.where(cell_iota == low, 1.0, 0.0).astype(jnp.bfloat16))
        pieces = []
        for value in values:
            head = value.astype(jnp.bfloat16).astype(jnp.float32)
            pieces += [head, value - head]
        both = jnp.concatenate(pieces, axis=0).astype(jnp.bfloat16)
        column = []
        for h in spans[chunk]:
            column.append(both * repeated((high == h).astype(jnp.float32), width))
        column.append((high_iota == high).astype(jnp.float32).astype(jnp.bfloat16))
        columns[chunk].append(jnp.concatenate(column, axis=0))

    for pair in range(parts // 2):
        even, odd = 2 * pair, 2 * pair + 1
        for chunk in range(full):
            here, there = (
                [recv_ref[owner, pl.ds(f * span_rows + chunk * DIR, DIR), :] for f in range(freqs)]
                for owner in (even, odd)
            )
            cells, cells_there = cells_of(even, chunk), cells_of(odd, chunk)
            for side in range(2):
                place(
                    2 * chunk + side,
                    jnp.where(low_lane, cells, cells_there),
                    [jnp.where(low_wide, a, b) for a, b in zip(here, there)],
                )
                here, there, cells, cells_there = there, here, cells_there, cells

        def merged(offset):
            own, other = recv_ref[even, pl.ds(offset, 8), :], recv_ref[odd, pl.ds(offset, 8), :]
            return (
                jnp.where(low_lanes, own, pltpu.roll(other, half, 1)),
                jnp.where(low_lanes, pltpu.roll(own, half, 1), other),
            )

        values = []
        for f in range(freqs):
            one, two = merged(f * span_rows + full * DIR)
            three, four = merged(f * span_rows + full * DIR + 8)
            values.append(
                jnp.concatenate([one, two, jnp.where(top_rows, three, pltpu.roll(four, 4, 0))], axis=0)
            )
        place(2 * full, jnp.where(low_lane, cells_of(even, full), cells_of(odd, full)), values)

    lane = lax.broadcasted_iota(jnp.int32, (slab_rows, LANES), 1)
    zero_rows = jnp.zeros((8, LANES), jnp.float32)

    def gather(offset):
        return jnp.concatenate(
            [recv_ref[owner, pl.ds(offset, tile_rows), :] for owner in range(parts)], axis=0
        )

    gain = 0.5 * courant / 8.0
    slots = iter(range(table.shape[0]))

    def keep(rows):
        slot = next(slots)
        table[slot, pl.ds(8, rows.shape[0]), :] = rows
        return slot

    def face_x(rows):
        slot = next(slots)
        table[slot, pl.ds(0, 8), :] = zero_rows
        table[slot, pl.ds(8 + slab_rows, 8), :] = zero_rows
        table[slot, pl.ds(8, slab_rows), :] = rows
        faces = gain * (table[slot, pl.ds(7, slab_rows + 8), :] + table[slot, pl.ds(8, slab_rows + 8), :])
        table[slot, pl.ds(7, slab_rows + 8), :] = faces
        return slot

    def face_y(rows):
        after = jnp.where(lane < LANES - 1, pltpu.roll(rows, LANES - 1, 1), 0.0)
        before = jnp.where(lane > 0, pltpu.roll(rows, 1, 1), 0.0)
        return keep(gain * (rows + after)), keep(gain * (rows + before))

    speeds = [gather(f * span_rows + full * DIR + 12) for f in range(freqs)]
    current_x, current_y, turning = (gather(shared_base + kind * tile_rows) for kind in range(3))
    current_x_face, speed_x_face = face_x(current_x), [face_x(s) for s in speeds]
    current_y_faces, speed_y_faces = face_y(current_y), [face_y(s) for s in speeds]
    step_angle = 2.0 * math.pi / DIR
    sublane = lax.broadcasted_iota(jnp.int32, (8, LANES), 0)
    cosine0 = jnp.ones((8, LANES), jnp.float32)
    sine0 = jnp.zeros((8, LANES), jnp.float32)
    for d in range(1, 8):
        cosine0 = jnp.where(sublane == d, math.cos(d * step_angle), cosine0)
        sine0 = jnp.where(sublane == d, math.sin(d * step_angle), sine0)
    turns = [(math.cos(g * 8 * step_angle), math.sin(g * 8 * step_angle)) for g in range(DIR // 8)]
    cosine = jnp.concatenate([c * cosine0 - t * sine0 for c, t in turns], axis=0)
    sine = jnp.concatenate([c * sine0 + t * cosine0 for c, t in turns], axis=0)

    def row(slot, x):
        return table[slot, pl.ds(8 + x, 1), :]

    for f in range(freqs):
        for x in range(-1, slab_rows):
            faces_x[f, x + 1] = row(speed_x_face[f], x) * cosine + row(current_x_face, x)
        for x in range(slab_rows):
            for side in range(2):
                faces_y[f, side, x] = row(speed_y_faces[f][side], x) * sine + row(current_y_faces[side], x)

    ahead = jnp.maximum(turning, 0.0) * 0.125
    back = jnp.minimum(turning, 0.0) * 0.125
    bend_slots = [
        keep(rows)
        for rows in (
            -ahead,
            7.0 * ahead + 3.0 * back,
            1.0 - 3.0 * (ahead - back),
            -3.0 * ahead - 7.0 * back,
            back,
        )
    ]
    land_slots = next(slots), next(slots)
    nothing = jnp.zeros((DIR, LANES), jnp.float32)
    for f in range(freqs):
        for field in (first, second):
            for edge in (0, 1, slab_rows + 2, slab_rows + 3):
                field[f, edge] = nothing
    lane_wide = lax.broadcasted_iota(jnp.int32, (DIR, LANES), 1)

    def flux(speed, behind, centre3, onward3, beyond):
        positive = speed > 0.0
        near = jnp.where(positive, centre3, onward3)
        far = jnp.where(positive, behind, beyond)
        return speed * ((centre3 + onward3) + (near - far))

    def advance(field, x, carry, finish):
        sea = row(land_slots[x % 2], x // 2)
        for f in range(freqs):
            if x == 0:
                start3 = 3.0 * field[f, 2]
                carry[f] = flux(faces_x[f, 0], nothing, nothing, start3, field[f, 3]), start3
            entering, centre3 = carry[f]
            centre = field[f, x + 2]
            onward3 = 3.0 * field[f, x + 3]
            leaving = flux(faces_x[f, x + 1], field[f, x + 1], centre3, onward3, field[f, x + 4])
            up1 = jnp.where(lane_wide < LANES - 1, pltpu.roll(centre, LANES - 1, 1), 0.0)
            up2 = jnp.where(lane_wide < LANES - 2, pltpu.roll(centre, LANES - 2, 1), 0.0)
            down1 = jnp.where(lane_wide > 0, pltpu.roll(centre, 1, 1), 0.0)
            down2 = jnp.where(lane_wide > 1, pltpu.roll(centre, 2, 1), 0.0)
            right = flux(faces_y[f, 0, x], down1, centre3, 3.0 * up1, up2)
            left = flux(faces_y[f, 1, x], down2, 3.0 * down1, centre3, up1)
            finish(f, x, (centre - (leaving - entering) - (right - left)) * sea)
            carry[f] = leaving, onward3

    def store(f, x, moved):
        second[f, x + 2] = moved

    pitch = slab_rows + 1

    def turn(f, x, moved):
        for g in range(DIR // 8):
            at = (f * DIR + g * 8) * pitch + x
            moved_ref[pl.ds(at, 8, stride=pitch), :] = moved[g * 8 : g * 8 + 8]

    def copy_out(block):
        part = pl.ds(block * BLOCK, BLOCK)
        return pltpu.make_async_copy(done_ref.at[:, part, :], out_ref.at[:, part, :], sems.at[block])

    def refract(block):
        at = block * BLOCK
        weights = [table[slot, pl.ds(8 + at, BLOCK), :] for slot in bend_slots]
        for f in range(freqs):
            ring = [moved_ref[pl.ds((f * DIR + d) * pitch + at, BLOCK), :] for d in range(DIR)]
            for d in range(DIR):
                bent = weights[2] * ring[d]
                for k in (0, 1, 3, 4):
                    bent = bent + weights[k] * ring[(d + k - 2) % DIR]
                done_ref[f * DIR + d, pl.ds(at, BLOCK), :] = bent
        copy_out(block).start()

    sums = [None] * highs
    named = [None, None]
    complete = 0
    reached = [0, 0, 0]
    carries = [[None] * freqs, [None] * freqs]
    for part, (span, hot, column) in enumerate(zip(spans, hots, columns)):
        product = lax.dot_general(
            jnp.concatenate(column, axis=1),
            jnp.concatenate(hot, axis=1),
            (((1,), (1,)), ((), ())),
            preferred_element_type=jnp.float32,
        )
        for h in span:
            at = (h - span[0]) * width
            for f in range(freqs):
                here = at + f * 2 * DIR
                term = product[here : here + DIR] + product[here + DIR : here + 2 * DIR]
                sums[h] = sums[h] or []
                if len(sums[h]) > f:
                    sums[h][f] = sums[h][f] + term
                else:
                    sums[h].append(term)
        for side in range(2):
            hit = product[len(span) * width :, side * LANES : (side + 1) * LANES]
            named[side] = hit if part == 0 else named[side] + hit
            table[land_slots[side], pl.ds(8, highs), :] = named[side]
        until = highs if part + 1 == len(spans) else spans[part + 1][0]
        for h in range(complete, until):
            for f in range(freqs):
                first[f, 2 * h + 2] = sums[h][f][:, :LANES]
                first[f, 2 * h + 3] = sums[h][f][:, LANES:]
        complete = until
        ready = 2 * complete
        for stage, (field, finish) in enumerate(((first, store), (second, turn))):
            ready = slab_rows if ready == slab_rows else max(ready - 2, 0)
            for x in range(reached[stage], ready):
                advance(field, x, carries[stage], finish)
            reached[stage] = ready
        for block in range(reached[2], ready // BLOCK):
            refract(block)
        reached[2] = ready // BLOCK
    for block in range(slab_rows // BLOCK):
        copy_out(block).wait()


def slab_plan(spectra, wind, growth, damping, row_cell, group_speed, current, turning):
    parts = lax.axis_size(GROUP)
    rows, comps = spectra.shape
    tile_rows = turning.shape[0]
    freqs = comps // parts // DIR
    full = rows // LANES
    slab_rows = parts * tile_rows
    highs = slab_rows // 2
    block_rows = -(-(freqs * (full * DIR + 16) + 3 * tile_rows + full + 1) // 8) * 8
    packed = pl.pallas_call(
        functools.partial(pack_kernel, parts, freqs),
        out_shape=pltpu.VMEM((parts, block_rows, LANES), jnp.float32),
        compiler_params=pltpu.CompilerParams(vmem_limit_bytes=56 * 1024 * 1024),
        name="pack",
    )(spectra, wind, growth, damping, row_cell, group_speed, current, turning)
    arrived = lax.all_to_all(packed, GROUP, split_axis=0, concat_axis=0, tiled=True)
    out = pl.pallas_call(
        functools.partial(slab_kernel, parts, tile_rows, full, freqs),
        out_shape=jax.ShapeDtypeStruct((freqs * DIR, slab_rows, LANES), jnp.float32),
        in_specs=[pl.BlockSpec(memory_space=pltpu.VMEM)],
        out_specs=pl.BlockSpec(memory_space=pl.ANY),
        scratch_shapes=[
            pltpu.VMEM((freqs, slab_rows + 4, DIR, LANES), jnp.float32),
            pltpu.VMEM((freqs, slab_rows + 4, DIR, LANES), jnp.float32),
            pltpu.VMEM((10 + 3 * freqs, slab_rows + 16, LANES), jnp.float32),
            pltpu.VMEM((freqs, slab_rows + 1, DIR, LANES), jnp.float32),
            pltpu.VMEM((freqs, 2, slab_rows, DIR, LANES), jnp.float32),
            pltpu.VMEM((freqs * DIR * (slab_rows + 1), LANES), jnp.float32),
            pltpu.VMEM((freqs * DIR, slab_rows, LANES), jnp.float32),
            pltpu.SemaphoreType.DMA((slab_rows // BLOCK,)),
        ],
        compiler_params=pltpu.CompilerParams(vmem_limit_bytes=32 * 1024 * 1024),
        name="slab",
    )(arrived)
    return out.reshape(1, freqs * DIR, slab_rows, LANES)


def shards(*arrays):
    spectra, land_mask = arrays[0], arrays[5]
    parts = lax.axis_size(GROUP)
    rows, comps = spectra.shape
    whole_frequencies = comps == parts * 2 * DIR
    fits = rows % LANES == LANES // 2 and land_mask.shape == (4, LANES) and parts % 2 == 0
    if whole_frequencies and fits:
        return slab_plan(*arrays[:5], *arrays[6:])
    return tile_plan(*arrays)


def solution(mesh):
    placed = (
        P(("groups", "pts", "comp"), "sub"),
        P(("groups", "pts", "comp")),
        P("sub"),
        P("sub"),
        P(("groups", "pts", "comp")),
        P(("groups", "pts", "comp"), None),
        P(("groups", "sub"), ("pts", "comp"), None),
        P("groups", ("pts", "comp"), None),
        P(("groups", "pts", "comp"), None),
    )
    return jax.shard_map(
        shards,
        mesh=mesh,
        in_specs=placed,
        out_specs=P("sub", ("pts", "comp"), "groups", None),
        check_vma=False,
    )
```

```python
import functools
import math
import jax
import jax.numpy as jnp
from jax import lax
from jax.experimental import pallas as pl
from jax.experimental.pallas import tpu as pltpu
from jax.sharding import PartitionSpec as P

DIR = 24
SUBSTEPS = 2
LANES = 128
GROUP = ("pts", "comp")


courant = 0.35


def with_halo(cells, sides, width):
    for axis, dim in sides:
        count = lax.axis_size(axis)
        ends = count - 1
        head = lax.slice_in_dim(cells, 0, width, axis=dim)
        tail = lax.slice_in_dim(cells, cells.shape[dim] - width, cells.shape[dim], axis=dim)
        cells = jnp.concatenate(
            [
                lax.ppermute(tail, axis, [(i, (i + 1) % count) for i in range(ends)]),
                cells,
                lax.ppermute(head, axis, [((i + 1) % count, i) for i in range(ends)]),
            ],
            axis=dim,
        )
    return cells


def take_slice(values, first_index, extent, along_axis):
    return lax.slice_in_dim(values, first_index, first_index + extent, axis=along_axis)


def upwind_divergence(padded, motion, along_axis):
    length = padded.shape[along_axis] - 4
    face_count = length + 1
    behind = take_slice(padded, 0, face_count, along_axis)
    centre = take_slice(padded, 1, face_count, along_axis)
    onward = take_slice(padded, 2, face_count, along_axis)
    beyond = take_slice(padded, 3, face_count, along_axis)
    left_face = (6.0 * centre + 3.0 * onward - behind) * 0.125
    right_face = (3.0 * centre + 6.0 * onward - beyond) * 0.125
    face_speed = 0.5 * (
        take_slice(motion, 1, face_count, along_axis)
        + take_slice(motion, 2, face_count, along_axis)
    )
    fluxes = jnp.maximum(face_speed, 0.0) * left_face + jnp.minimum(face_speed, 0.0) * right_face
    return take_slice(fluxes, 1, length, along_axis) - take_slice(fluxes, 0, length, along_axis)


def substep(extended, speed_x, speed_y, sea_mask):
    across = upwind_divergence(extended, speed_x, 1)
    centre_part = extended[:, 2:-2]
    padding = ((0, 0), (0, 0), (2, 2))
    sideways = upwind_divergence(jnp.pad(centre_part, padding), jnp.pad(speed_y, padding), 2)
    return (centre_part - courant * (across + sideways)) * sea_mask


def direction_tables(directions):
    angles = jnp.arange(directions, dtype=jnp.float32) * (2.0 * jnp.pi / directions)
    return (jnp.cos(angles), jnp.sin(angles))


def source_term(values, wind_speed, growth, damping):
    return values * jnp.exp(wind_speed[:, None] * growth[None, :] - damping[None, :])


def velocities(stacked, freq_count):
    cosine_table, sine_table = direction_tables(DIR)
    celerity = stacked[:freq_count][:, None]
    shape_out = (freq_count * DIR,) + stacked.shape[1:]
    speed_x = (
        celerity * cosine_table[None, :, None, None] + stacked[freq_count][None, None]
    ).reshape(shape_out)
    speed_y = (
        celerity * sine_table[None, :, None, None] + stacked[freq_count + 1][None, None]
    ).reshape(shape_out)
    return (speed_x, speed_y)


def deliver(bulk_rows, small_rows):
    return (
        lax.all_to_all(bulk_rows, GROUP, split_axis=0, concat_axis=0, tiled=True),
        lax.all_to_all(small_rows, GROUP, split_axis=0, concat_axis=0, tiled=True),
    )


def tile_plan(spectra, wind, growth, damping, row_cell, land_mask, group_speed, current, turning):
    tile_count = lax.axis_size(GROUP)
    comp_width = spectra.shape[1]
    tile_rows, tile_cols = land_mask.shape
    cell_count = tile_rows * tile_cols
    capacity = cell_count // tile_count
    target = row_cell // cell_count
    local_cell = (row_cell - target * cell_count).astype(jnp.float32)
    matches = (target[:, None] == jnp.arange(tile_count, dtype=jnp.int32)[None, :]).astype(
        jnp.int32
    )
    bucket_slot = jnp.sum((jnp.cumsum(matches, axis=0) - 1) * matches, axis=1)

    def bucket(values, filler):
        shape_out = (tile_count, capacity) + values.shape[1:]
        return jnp.full(shape_out, filler, jnp.float32).at[target, bucket_slot].set(values)

    bulk_rows = bucket(source_term(spectra, wind, growth, damping), 0.0)
    small_rows = bucket(local_cell[:, None], float(cell_count))
    bulk_back, small_back = deliver(bulk_rows, small_rows)
    cell_index = small_back[:, :, 0].reshape(-1).astype(jnp.int32)
    flat_values = bulk_back.reshape((tile_count * capacity,) + bulk_back.shape[2:])
    tile_field = (
        jnp.zeros((cell_count,) + bulk_back.shape[2:], jnp.float32)
        .at[cell_index]
        .set(flat_values, mode="drop")
    )
    spectrum = tile_field.T.reshape(comp_width, tile_rows, tile_cols)
    freq_count = comp_width // DIR
    reach = 2 * SUBSTEPS
    stacked = jnp.concatenate([group_speed, current, land_mask.astype(jnp.float32)[None]], axis=0)
    rimmed = with_halo(stacked, ((GROUP, 1),), 2 * SUBSTEPS)
    speed_x, speed_y = velocities(rimmed, freq_count)
    sea_rim = rimmed[freq_count + 2 :]

    def window(values, margin):
        return lax.slice_in_dim(values, reach - margin, reach + tile_rows + margin, axis=1)

    for repeat in range(SUBSTEPS):
        extended = with_halo(spectrum, ((GROUP, 1),), 2)
        spectrum = substep(extended, window(speed_x, 2), window(speed_y, 0), window(sea_rim, 0)[0])
    blocks = spectrum.reshape(freq_count, DIR, tile_rows, tile_cols)
    wrapped = jnp.concatenate([blocks[:, -2:], blocks, blocks[:, :2]], axis=1)
    turning_full = jnp.broadcast_to(turning[None, None], wrapped.shape)
    blocks = blocks - upwind_divergence(wrapped, turning_full, 1)
    spectrum = blocks.reshape(comp_width, tile_rows, tile_cols)
    shipped = lax.all_to_all(spectrum, GROUP, split_axis=0, concat_axis=1, tiled=True)
    return shipped[None]


def pack_kernel(
    parts,
    freqs,
    spectra_ref,
    wind_ref,
    growth_ref,
    damping_ref,
    cell_ref,
    speed_ref,
    current_ref,
    turning_ref,
    out_ref,
):
    rows, comps = spectra_ref.shape
    half = LANES // 2
    full = rows // LANES
    padded = (full + 1) * LANES
    low = lax.broadcasted_iota(jnp.int32, (8, LANES), 1) < half
    per_freq = DIR // 8
    span_rows = full * DIR + 16

    def extended(row, filler):
        return jnp.concatenate([row[None], jnp.full((1, half), filler, jnp.float32)], axis=1)

    def as_columns(row):
        return jnp.broadcast_to(row, (LANES, padded)).T

    cells = cell_ref[...].astype(jnp.float32)
    keys = extended(cells, 1e9)
    key_cols = as_columns(keys)
    ranks = jnp.concatenate(
        [
            jnp.sum(
                jnp.where(key_cols < keys[:, c * LANES : (c + 1) * LANES], 1.0, 0.0), axis=0, keepdims=True
            )
            for c in range(full + 1)
        ],
        axis=1,
    )
    place = lax.broadcasted_iota(jnp.int32, (padded, padded), 0)
    odd = lax.axis_index(GROUP) % 2 == 1
    swapped = jnp.where(place % LANES < half, place + half, place - half)
    place = jnp.where((place < full * LANES) & odd, swapped, place)
    place = jnp.where(place < rows, place, place - half).astype(jnp.float32)
    order = jnp.where(place == ranks, 1.0, 0.0).astype(jnp.bfloat16)

    wind_cols = as_columns(extended(wind_ref[...], 0.0))
    turned = []
    for block in range(comps // LANES):
        lanes = pl.ds(block * LANES, LANES)
        growth = growth_ref[lanes][None]
        damping = damping_ref[lanes][None]

        def source(first, count):
            span = pl.ds(first, count)
            return spectra_ref[span, lanes] * jnp.exp(
                wind_cols[first : first + count] * growth - damping
            )

        pieces = [source(c * LANES, LANES).T for c in range(full)]
        last = jnp.concatenate([source(full * LANES, half), jnp.zeros((half, LANES), jnp.float32)], axis=0)
        turned.append(jnp.concatenate(pieces + [last.T], axis=1))
    turned.append(jnp.broadcast_to(extended(cells, 0.0), (16, padded)))
    values = jnp.concatenate(turned, axis=0)
    head = values.astype(jnp.bfloat16)
    rest = (values - head.astype(jnp.float32)).astype(jnp.bfloat16)
    both = lax.dot_general(
        jnp.concatenate([head, rest], axis=0),
        order,
        (((1,), (1,)), ((), ())),
        preferred_element_type=jnp.float32,
    )

    def piece(first, count, chunk):
        lanes = slice(chunk * LANES, (chunk + 1) * LANES)
        return both[first : first + count, lanes] + both[comps + 16 + first : comps + 16 + first + count, lanes]

    shared = jnp.concatenate(
        [current_ref[0], current_ref[1], turning_ref[...]] + [piece(comps, 1, c) for c in range(full + 1)],
        axis=0,
    )
    for part in range(parts):
        for f in range(freqs):
            freq = part * freqs + f
            at = f * span_rows
            for chunk in range(full):
                out_ref[part, pl.ds(at + chunk * DIR, DIR), :] = piece(freq * DIR, DIR, chunk)
            at += full * DIR
            one, two, three = (piece(freq * DIR + g * 8, 8, full) for g in range(per_freq))
            out_ref[part, pl.ds(at, 8), :] = jnp.where(low, one, two)
            folded = jnp.where(low, three, pltpu.roll(three, 4, 0))
            out_ref[part, pl.ds(at + 8, 8), :] = jnp.concatenate([folded[:4], speed_ref[freq]], axis=0)
        out_ref[part, pl.ds(freqs * span_rows, shared.shape[0]), :] = shared


BLOCK = 8
PER_STEP = 4


def slab_kernel(
    parts,
    tile_rows,
    full,
    freqs,
    recv_ref,
    out_ref,
    first,
    second,
    table,
    faces_x,
    faces_y,
    moved_ref,
    done_ref,
    sems,
):
    slab_rows = parts * tile_rows
    half = LANES // 2
    span_rows = full * DIR + 16
    shared_base = freqs * span_rows
    highs = slab_rows // 2
    width = freqs * 2 * DIR
    low_lane = lax.broadcasted_iota(jnp.int32, (1, LANES), 1) < half
    low_lanes = lax.broadcasted_iota(jnp.int32, (8, LANES), 1) < half
    low_wide = lax.broadcasted_iota(jnp.int32, (DIR, LANES), 1) < half
    top_rows = lax.broadcasted_iota(jnp.int32, (8, LANES), 0) < 4
    cell_iota = lax.broadcasted_iota(jnp.int32, (2 * LANES, LANES), 0).astype(jnp.float32).astype(jnp.bfloat16)
    high_iota = lax.broadcasted_iota(jnp.int32, (highs, LANES), 0)

    def cells_of(owner, chunk):
        return recv_ref[owner, pl.ds(shared_base + 3 * tile_rows + chunk, 1), :].astype(jnp.int32)

    owner_rows = full * LANES + half
    capacity = tile_rows * LANES // parts
    spans = []
    for begin in range(0, owner_rows, half):
        tiles = [
            t
            for t in range(parts)
            if owner_rows - capacity * (parts - t) < begin + half and capacity * (t + 1) > begin
        ]
        spans.append(range(tiles[0] * tile_rows // 2, (tiles[-1] + 1) * tile_rows // 2))
    columns = [[] for _ in spans]
    hots = [[] for _ in spans]

    def repeated(line, count):
        tile = jnp.broadcast_to(line, (16, LANES)).astype(jnp.bfloat16)
        return jnp.concatenate([tile] * (count // 16), axis=0)

    def place(chunk, cells, values):
        high = cells // (2 * LANES)
        low = (cells - high * (2 * LANES)).astype(jnp.float32)
        low = repeated(low, 2 * LANES)
        hots[chunk].append(jnp.where(cell_iota == low, 1.0, 0.0).astype(jnp.bfloat16))
        pieces = []
        for value in values:
            head = value.astype(jnp.bfloat16).astype(jnp.float32)
            pieces += [head, value - head]
        both = jnp.concatenate(pieces, axis=0).astype(jnp.bfloat16)
        column = []
        for h in spans[chunk]:
            column.append(both * repeated((high == h).astype(jnp.float32), width))
        column.append((high_iota == high).astype(jnp.float32).astype(jnp.bfloat16))
        columns[chunk].append(jnp.concatenate(column, axis=0))

    for pair in range(parts // 2):
        even, odd = 2 * pair, 2 * pair + 1
        for chunk in range(full):
            here, there = (
                [recv_ref[owner, pl.ds(f * span_rows + chunk * DIR, DIR), :] for f in range(freqs)]
                for owner in (even, odd)
            )
            cells, cells_there = cells_of(even, chunk), cells_of(odd, chunk)
            for side in range(2):
                place(
                    2 * chunk + side,
                    jnp.where(low_lane, cells, cells_there),
                    [jnp.where(low_wide, a, b) for a, b in zip(here, there)],
                )
                here, there, cells, cells_there = there, here, cells_there, cells

        def merged(offset):
            own, other = recv_ref[even, pl.ds(offset, 8), :], recv_ref[odd, pl.ds(offset, 8), :]
            return (
                jnp.where(low_lanes, own, pltpu.roll(other, half, 1)),
                jnp.where(low_lanes, pltpu.roll(own, half, 1), other),
            )

        values = []
        for f in range(freqs):
            one, two = merged(f * span_rows + full * DIR)
            three, four = merged(f * span_rows + full * DIR + 8)
            values.append(
                jnp.concatenate([one, two, jnp.where(top_rows, three, pltpu.roll(four, 4, 0))], axis=0)
            )
        place(2 * full, jnp.where(low_lane, cells_of(even, full), cells_of(odd, full)), values)

    lane = lax.broadcasted_iota(jnp.int32, (slab_rows, LANES), 1)
    zero_rows = jnp.zeros((8, LANES), jnp.float32)

    def gather(offset):
        return jnp.concatenate(
            [recv_ref[owner, pl.ds(offset, tile_rows), :] for owner in range(parts)], axis=0
        )

    gain = 0.5 * courant / 8.0
    slots = iter(range(table.shape[0]))

    def keep(rows):
        slot = next(slots)
        table[slot, pl.ds(8, rows.shape[0]), :] = rows
        return slot

    def face_x(rows):
        slot = next(slots)
        table[slot, pl.ds(0, 8), :] = zero_rows
        table[slot, pl.ds(8 + slab_rows, 8), :] = zero_rows
        table[slot, pl.ds(8, slab_rows), :] = rows
        faces = gain * (table[slot, pl.ds(7, slab_rows + 8), :] + table[slot, pl.ds(8, slab_rows + 8), :])
        table[slot, pl.ds(7, slab_rows + 8), :] = faces
        return slot

    def face_y(rows):
        after = jnp.where(lane < LANES - 1, pltpu.roll(rows, LANES - 1, 1), 0.0)
        before = jnp.where(lane > 0, pltpu.roll(rows, 1, 1), 0.0)
        return keep(gain * (rows + after)), keep(gain * (rows + before))

    speeds = [gather(f * span_rows + full * DIR + 12) for f in range(freqs)]
    current_x, current_y, turning = (gather(shared_base + kind * tile_rows) for kind in range(3))
    current_x_face, speed_x_face = face_x(current_x), [face_x(s) for s in speeds]
    current_y_faces, speed_y_faces = face_y(current_y), [face_y(s) for s in speeds]
    step_angle = 2.0 * math.pi / DIR
    sublane = lax.broadcasted_iota(jnp.int32, (8, LANES), 0)
    cosine0 = jnp.ones((8, LANES), jnp.float32)
    sine0 = jnp.zeros((8, LANES), jnp.float32)
    for d in range(1, 8):
        cosine0 = jnp.where(sublane == d, math.cos(d * step_angle), cosine0)
        sine0 = jnp.where(sublane == d, math.sin(d * step_angle), sine0)
    turns = [(math.cos(g * 8 * step_angle), math.sin(g * 8 * step_angle)) for g in range(DIR // 8)]
    cosine = jnp.concatenate([c * cosine0 - t * sine0 for c, t in turns], axis=0)
    sine = jnp.concatenate([c * sine0 + t * cosine0 for c, t in turns], axis=0)

    def row(slot, x):
        return table[slot, pl.ds(8 + x, 1), :]

    for f in range(freqs):
        for x in range(-1, slab_rows):
            faces_x[f, x + 1] = row(speed_x_face[f], x) * cosine + row(current_x_face, x)
        for x in range(slab_rows):
            for side in range(2):
                faces_y[f, side, x] = row(speed_y_faces[f][side], x) * sine + row(current_y_faces[side], x)

    scattered = [
        lax.dot_general(
            jnp.concatenate(column, axis=1),
            jnp.concatenate(hot, axis=1),
            (((1,), (1,)), ((), ())),
            preferred_element_type=jnp.float32,
        )
        for hot, column in zip(hots, columns)
    ]
    nothing = jnp.zeros((DIR, LANES), jnp.float32)
    for f in range(freqs):
        for field in (first, second):
            for edge in (0, 1, slab_rows + 2, slab_rows + 3):
                field[f, edge] = nothing
        for h in range(highs):
            terms = []
            for span, product in zip(spans, scattered):
                if h in span:
                    at = (h - span[0]) * width + f * 2 * DIR
                    terms += [product[at : at + DIR], product[at + DIR : at + 2 * DIR]]
            total = sum(terms[1:], terms[0])
            first[f, 2 * h + 2] = total[:, :LANES]
            first[f, 2 * h + 3] = total[:, LANES:]
    named = sum(product[len(span) * width :] for span, product in zip(spans, scattered))

    land_slots = keep(named[:, :LANES]), keep(named[:, LANES:])
    ahead = jnp.maximum(turning, 0.0) * 0.125
    back = jnp.minimum(turning, 0.0) * 0.125
    bend_slots = [
        keep(rows)
        for rows in (
            -ahead,
            7.0 * ahead + 3.0 * back,
            1.0 - 3.0 * (ahead - back),
            -3.0 * ahead - 7.0 * back,
            back,
        )
    ]

    lane_wide = lax.broadcasted_iota(jnp.int32, (DIR, LANES), 1)

    not_first, not_last = lane_wide > 0, lane_wide < LANES - 1

    def upwind(speed, shared, from_left, from_right):
        return speed * (shared + jnp.where(speed > 0.0, from_left, from_right))

    def flux(speed, behind, centre3, onward3, beyond):
        return upwind(speed, centre3 + onward3, centre3 - behind, onward3 - beyond)

    def advance(field, step, carry, finish):
        carry = list(carry)
        for i in range(BLOCK):
            x = step * BLOCK + i
            sea = row(land_slots[i % 2], step * (BLOCK // 2) + i // 2)
            for f in range(freqs):
                entering, centre3 = carry[f]
                centre = field[f, x + 2]
                onward3 = 3.0 * field[f, x + 3]
                leaving = flux(faces_x[f, x + 1], field[f, x + 1], centre3, onward3, field[f, x + 4])
                up = jnp.where(not_last, pltpu.roll(centre, LANES - 1, 1), 0.0)
                down = jnp.where(not_first, pltpu.roll(centre, 1, 1), 0.0)
                from_left, from_right = centre3 - down, centre3 - up
                next_right = jnp.where(not_last, pltpu.roll(from_right, LANES - 1, 1), 0.0)
                last_left = jnp.where(not_first, pltpu.roll(from_left, 1, 1), 0.0)
                right = upwind(faces_y[f, 0, x], centre3 + 3.0 * up, from_left, next_right)
                left = upwind(faces_y[f, 1, x], centre3 + 3.0 * down, last_left, from_right)
                finish(f, x, (centre - (leaving - entering) - (right - left)) * sea)
                carry[f] = leaving, onward3
        return tuple(carry)

    def enter(field):
        carry = []
        for f in range(freqs):
            start3 = 3.0 * field[f, 2]
            carry.append((flux(faces_x[f, 0], nothing, nothing, start3, field[f, 3]), start3))
        return tuple(carry)

    def store(f, x, moved):
        second[f, x + 2] = moved

    pitch = slab_rows + 1

    def turn(f, x, moved):
        for g in range(DIR // 8):
            at = (f * DIR + g * 8) * pitch + x
            moved_ref[pl.ds(at, 8, stride=pitch), :] = moved[g * 8 : g * 8 + 8]

    def copy_out(f, block):
        comps = pl.ds(f * DIR, DIR)
        part = pl.ds(pl.multiple_of(block * BLOCK, BLOCK), BLOCK)
        return pltpu.make_async_copy(
            done_ref.at[comps, part, :], out_ref.at[comps, part, :], sems.at[f, block]
        )

    def final(block, carry):
        carry = advance(second, block, carry, turn)
        at = pl.multiple_of(block * BLOCK, BLOCK)
        weights = [table[slot, pl.ds(8 + at, BLOCK), :] for slot in bend_slots]
        for f in range(freqs):
            ring = [moved_ref[pl.ds((f * DIR + d) * pitch + at, BLOCK), :] for d in range(DIR)]
            for d in range(DIR):
                bent = weights[2] * ring[d]
                for k in (0, 1, 3, 4):
                    bent = bent + weights[k] * ring[(d + k - 2) % DIR]
                done_ref[f * DIR + d, pl.ds(at, BLOCK), :] = bent
            copy_out(f, block).start()
        return carry

    def sweep(one_block, carry):
        def body(step, carry):
            for i in range(PER_STEP):
                carry = one_block(step * PER_STEP + i, carry)
            return carry

        lax.fori_loop(0, slab_rows // BLOCK // PER_STEP, body, carry)

    sweep(lambda block, carry: advance(first, block, carry, store), enter(first))
    sweep(final, enter(second))
    for block in range(slab_rows // BLOCK):
        for f in range(freqs):
            copy_out(f, block).wait()


def slab_plan(spectra, wind, growth, damping, row_cell, group_speed, current, turning):
    parts = lax.axis_size(GROUP)
    rows, comps = spectra.shape
    tile_rows = turning.shape[0]
    freqs = comps // parts // DIR
    full = rows // LANES
    slab_rows = parts * tile_rows
    highs = slab_rows // 2
    block_rows = -(-(freqs * (full * DIR + 16) + 3 * tile_rows + full + 1) // 8) * 8
    packed = pl.pallas_call(
        functools.partial(pack_kernel, parts, freqs),
        out_shape=pltpu.VMEM((parts, block_rows, LANES), jnp.float32),
        compiler_params=pltpu.CompilerParams(vmem_limit_bytes=56 * 1024 * 1024),
        name="pack",
    )(spectra, wind, growth, damping, row_cell, group_speed, current, turning)
    arrived = lax.all_to_all(packed, GROUP, split_axis=0, concat_axis=0, tiled=True)
    out = pl.pallas_call(
        functools.partial(slab_kernel, parts, tile_rows, full, freqs),
        out_shape=jax.ShapeDtypeStruct((freqs * DIR, slab_rows, LANES), jnp.float32),
        in_specs=[pl.BlockSpec(memory_space=pltpu.VMEM)],
        out_specs=pl.BlockSpec(memory_space=pl.ANY),
        scratch_shapes=[
            pltpu.VMEM((freqs, slab_rows + 4, DIR, LANES), jnp.float32),
            pltpu.VMEM((freqs, slab_rows + 4, DIR, LANES), jnp.float32),
            pltpu.VMEM((10 + 3 * freqs, slab_rows + 16, LANES), jnp.float32),
            pltpu.VMEM((freqs, slab_rows + 1, DIR, LANES), jnp.float32),
            pltpu.VMEM((freqs, 2, slab_rows, DIR, LANES), jnp.float32),
            pltpu.VMEM((freqs * DIR * (slab_rows + 1), LANES), jnp.float32),
            pltpu.VMEM((freqs * DIR, slab_rows, LANES), jnp.float32),
            pltpu.SemaphoreType.DMA((freqs, slab_rows // BLOCK)),
        ],
        compiler_params=pltpu.CompilerParams(vmem_limit_bytes=32 * 1024 * 1024),
        name="slab",
    )(arrived)
    return out.reshape(1, freqs * DIR, slab_rows, LANES)


def shards(*arrays):
    spectra, land_mask = arrays[0], arrays[5]
    parts = lax.axis_size(GROUP)
    rows, comps = spectra.shape
    whole_frequencies = comps == parts * 2 * DIR
    fits = rows % LANES == LANES // 2 and land_mask.shape == (4, LANES) and parts % 2 == 0
    if whole_frequencies and fits:
        return slab_plan(*arrays[:5], *arrays[6:])
    return tile_plan(*arrays)


def solution(mesh):
    placed = (
        P(("groups", "pts", "comp"), "sub"),
        P(("groups", "pts", "comp")),
        P("sub"),
        P("sub"),
        P(("groups", "pts", "comp")),
        P(("groups", "pts", "comp"), None),
        P(("groups", "sub"), ("pts", "comp"), None),
        P("groups", ("pts", "comp"), None),
        P(("groups", "pts", "comp"), None),
    )
    return jax.shard_map(
        shards,
        mesh=mesh,
        in_specs=placed,
        out_specs=P("sub", ("pts", "comp"), "groups", None),
        check_vma=False,
    )
```

```python
import functools
import math
import jax
import jax.numpy as jnp
from jax import lax
from jax.experimental import pallas as pl
from jax.experimental.pallas import tpu as pltpu
from jax.sharding import PartitionSpec as P

DIR = 24
SUBSTEPS = 2
LANES = 128
GROUP = ("pts", "comp")


courant = 0.35


def with_halo(cells, sides, width):
    for axis, dim in sides:
        count = lax.axis_size(axis)
        ends = count - 1
        head = lax.slice_in_dim(cells, 0, width, axis=dim)
        tail = lax.slice_in_dim(cells, cells.shape[dim] - width, cells.shape[dim], axis=dim)
        cells = jnp.concatenate(
            [
                lax.ppermute(tail, axis, [(i, (i + 1) % count) for i in range(ends)]),
                cells,
                lax.ppermute(head, axis, [((i + 1) % count, i) for i in range(ends)]),
            ],
            axis=dim,
        )
    return cells


def take_slice(values, first_index, extent, along_axis):
    return lax.slice_in_dim(values, first_index, first_index + extent, axis=along_axis)


def upwind_divergence(padded, motion, along_axis):
    length = padded.shape[along_axis] - 4
    face_count = length + 1
    behind = take_slice(padded, 0, face_count, along_axis)
    centre = take_slice(padded, 1, face_count, along_axis)
    onward = take_slice(padded, 2, face_count, along_axis)
    beyond = take_slice(padded, 3, face_count, along_axis)
    left_face = (6.0 * centre + 3.0 * onward - behind) * 0.125
    right_face = (3.0 * centre + 6.0 * onward - beyond) * 0.125
    face_speed = 0.5 * (
        take_slice(motion, 1, face_count, along_axis)
        + take_slice(motion, 2, face_count, along_axis)
    )
    fluxes = jnp.maximum(face_speed, 0.0) * left_face + jnp.minimum(face_speed, 0.0) * right_face
    return take_slice(fluxes, 1, length, along_axis) - take_slice(fluxes, 0, length, along_axis)


def substep(extended, speed_x, speed_y, sea_mask):
    across = upwind_divergence(extended, speed_x, 1)
    centre_part = extended[:, 2:-2]
    padding = ((0, 0), (0, 0), (2, 2))
    sideways = upwind_divergence(jnp.pad(centre_part, padding), jnp.pad(speed_y, padding), 2)
    return (centre_part - courant * (across + sideways)) * sea_mask


def direction_tables(directions):
    angles = jnp.arange(directions, dtype=jnp.float32) * (2.0 * jnp.pi / directions)
    return (jnp.cos(angles), jnp.sin(angles))


def source_term(values, wind_speed, growth, damping):
    return values * jnp.exp(wind_speed[:, None] * growth[None, :] - damping[None, :])


def velocities(stacked, freq_count):
    cosine_table, sine_table = direction_tables(DIR)
    celerity = stacked[:freq_count][:, None]
    shape_out = (freq_count * DIR,) + stacked.shape[1:]
    speed_x = (
        celerity * cosine_table[None, :, None, None] + stacked[freq_count][None, None]
    ).reshape(shape_out)
    speed_y = (
        celerity * sine_table[None, :, None, None] + stacked[freq_count + 1][None, None]
    ).reshape(shape_out)
    return (speed_x, speed_y)


def deliver(bulk_rows, small_rows):
    return (
        lax.all_to_all(bulk_rows, GROUP, split_axis=0, concat_axis=0, tiled=True),
        lax.all_to_all(small_rows, GROUP, split_axis=0, concat_axis=0, tiled=True),
    )


def tile_plan(spectra, wind, growth, damping, row_cell, land_mask, group_speed, current, turning):
    tile_count = lax.axis_size(GROUP)
    comp_width = spectra.shape[1]
    tile_rows, tile_cols = land_mask.shape
    cell_count = tile_rows * tile_cols
    capacity = cell_count // tile_count
    target = row_cell // cell_count
    local_cell = (row_cell - target * cell_count).astype(jnp.float32)
    matches = (target[:, None] == jnp.arange(tile_count, dtype=jnp.int32)[None, :]).astype(
        jnp.int32
    )
    bucket_slot = jnp.sum((jnp.cumsum(matches, axis=0) - 1) * matches, axis=1)

    def bucket(values, filler):
        shape_out = (tile_count, capacity) + values.shape[1:]
        return jnp.full(shape_out, filler, jnp.float32).at[target, bucket_slot].set(values)

    bulk_rows = bucket(source_term(spectra, wind, growth, damping), 0.0)
    small_rows = bucket(local_cell[:, None], float(cell_count))
    bulk_back, small_back = deliver(bulk_rows, small_rows)
    cell_index = small_back[:, :, 0].reshape(-1).astype(jnp.int32)
    flat_values = bulk_back.reshape((tile_count * capacity,) + bulk_back.shape[2:])
    tile_field = (
        jnp.zeros((cell_count,) + bulk_back.shape[2:], jnp.float32)
        .at[cell_index]
        .set(flat_values, mode="drop")
    )
    spectrum = tile_field.T.reshape(comp_width, tile_rows, tile_cols)
    freq_count = comp_width // DIR
    reach = 2 * SUBSTEPS
    stacked = jnp.concatenate([group_speed, current, land_mask.astype(jnp.float32)[None]], axis=0)
    rimmed = with_halo(stacked, ((GROUP, 1),), 2 * SUBSTEPS)
    speed_x, speed_y = velocities(rimmed, freq_count)
    sea_rim = rimmed[freq_count + 2 :]

    def window(values, margin):
        return lax.slice_in_dim(values, reach - margin, reach + tile_rows + margin, axis=1)

    for repeat in range(SUBSTEPS):
        extended = with_halo(spectrum, ((GROUP, 1),), 2)
        spectrum = substep(extended, window(speed_x, 2), window(speed_y, 0), window(sea_rim, 0)[0])
    blocks = spectrum.reshape(freq_count, DIR, tile_rows, tile_cols)
    wrapped = jnp.concatenate([blocks[:, -2:], blocks, blocks[:, :2]], axis=1)
    turning_full = jnp.broadcast_to(turning[None, None], wrapped.shape)
    blocks = blocks - upwind_divergence(wrapped, turning_full, 1)
    spectrum = blocks.reshape(comp_width, tile_rows, tile_cols)
    shipped = lax.all_to_all(spectrum, GROUP, split_axis=0, concat_axis=1, tiled=True)
    return shipped[None]


def pack_kernel(
    parts,
    freqs,
    spectra_ref,
    wind_ref,
    growth_ref,
    damping_ref,
    cell_ref,
    speed_ref,
    current_ref,
    turning_ref,
    out_ref,
):
    rows, comps = spectra_ref.shape
    half = LANES // 2
    full = rows // LANES
    padded = (full + 1) * LANES
    low = lax.broadcasted_iota(jnp.int32, (8, LANES), 1) < half
    per_freq = DIR // 8
    span_rows = full * DIR + 16

    def extended(row, filler):
        return jnp.concatenate([row[None], jnp.full((1, half), filler, jnp.float32)], axis=1)

    def as_columns(row):
        return jnp.broadcast_to(row, (LANES, padded)).T

    cells = cell_ref[...].astype(jnp.float32)
    keys = extended(cells, 1e9)
    key_cols = as_columns(keys)
    ranks = jnp.concatenate(
        [
            jnp.sum(
                jnp.where(key_cols < keys[:, c * LANES : (c + 1) * LANES], 1.0, 0.0), axis=0, keepdims=True
            )
            for c in range(full + 1)
        ],
        axis=1,
    )
    place = lax.broadcasted_iota(jnp.int32, (padded, padded), 0)
    odd = lax.axis_index(GROUP) % 2 == 1
    swapped = jnp.where(place % LANES < half, place + half, place - half)
    place = jnp.where((place < full * LANES) & odd, swapped, place)
    place = jnp.where(place < rows, place, place - half).astype(jnp.float32)
    order = jnp.where(place == ranks, 1.0, 0.0).astype(jnp.bfloat16)

    wind_cols = as_columns(extended(wind_ref[...], 0.0))
    turned = []
    for block in range(comps // LANES):
        lanes = pl.ds(block * LANES, LANES)
        growth = growth_ref[lanes][None]
        damping = damping_ref[lanes][None]

        def source(first, count):
            span = pl.ds(first, count)
            return spectra_ref[span, lanes] * jnp.exp(
                wind_cols[first : first + count] * growth - damping
            )

        pieces = [source(c * LANES, LANES).T for c in range(full)]
        last = jnp.concatenate([source(full * LANES, half), jnp.zeros((half, LANES), jnp.float32)], axis=0)
        turned.append(jnp.concatenate(pieces + [last.T], axis=1))
    turned.append(jnp.broadcast_to(extended(cells, 0.0), (16, padded)))
    values = jnp.concatenate(turned, axis=0)
    head = values.astype(jnp.bfloat16)
    rest = (values - head.astype(jnp.float32)).astype(jnp.bfloat16)
    both = lax.dot_general(
        jnp.concatenate([head, rest], axis=0),
        order,
        (((1,), (1,)), ((), ())),
        preferred_element_type=jnp.float32,
    )

    def piece(first, count, chunk):
        lanes = slice(chunk * LANES, (chunk + 1) * LANES)
        return both[first : first + count, lanes] + both[comps + 16 + first : comps + 16 + first + count, lanes]

    shared = jnp.concatenate(
        [current_ref[0], current_ref[1], turning_ref[...]] + [piece(comps, 1, c) for c in range(full + 1)],
        axis=0,
    )
    for part in range(parts):
        for f in range(freqs):
            freq = part * freqs + f
            at = f * span_rows
            for chunk in range(full):
                out_ref[part, pl.ds(at + chunk * DIR, DIR), :] = piece(freq * DIR, DIR, chunk)
            at += full * DIR
            one, two, three = (piece(freq * DIR + g * 8, 8, full) for g in range(per_freq))
            out_ref[part, pl.ds(at, 8), :] = jnp.where(low, one, two)
            folded = jnp.where(low, three, pltpu.roll(three, 4, 0))
            out_ref[part, pl.ds(at + 8, 8), :] = jnp.concatenate([folded[:4], speed_ref[freq]], axis=0)
        out_ref[part, pl.ds(freqs * span_rows, shared.shape[0]), :] = shared


BLOCK = 8
PER_STEP = 4


def slab_kernel(
    parts,
    tile_rows,
    full,
    freqs,
    recv_ref,
    out_ref,
    first,
    second,
    table,
    faces_x,
    faces_y,
    moved_ref,
    done_ref,
    sems,
):
    slab_rows = parts * tile_rows
    half = LANES // 2
    span_rows = full * DIR + 16
    shared_base = freqs * span_rows
    highs = slab_rows // 2
    width = freqs * 2 * DIR
    low_lane = lax.broadcasted_iota(jnp.int32, (1, LANES), 1) < half
    low_lanes = lax.broadcasted_iota(jnp.int32, (8, LANES), 1) < half
    low_wide = lax.broadcasted_iota(jnp.int32, (DIR, LANES), 1) < half
    top_rows = lax.broadcasted_iota(jnp.int32, (8, LANES), 0) < 4
    cell_iota = lax.broadcasted_iota(jnp.int32, (2 * LANES, LANES), 0).astype(jnp.float32).astype(jnp.bfloat16)
    high_iota = lax.broadcasted_iota(jnp.int32, (highs, LANES), 0)

    def cells_of(owner, chunk):
        return recv_ref[owner, pl.ds(shared_base + 3 * tile_rows + chunk, 1), :].astype(jnp.int32)

    owner_rows = full * LANES + half
    capacity = tile_rows * LANES // parts
    spans = []
    for begin in range(0, owner_rows, half):
        tiles = [
            t
            for t in range(parts)
            if owner_rows - capacity * (parts - t) < begin + half and capacity * (t + 1) > begin
        ]
        spans.append(range(tiles[0] * tile_rows // 2, (tiles[-1] + 1) * tile_rows // 2))
    columns = [[] for _ in spans]
    hots = [[] for _ in spans]

    def repeated(line, count):
        tile = jnp.broadcast_to(line, (16, LANES)).astype(jnp.bfloat16)
        return jnp.concatenate([tile] * (count // 16), axis=0)

    def place(chunk, cells, values):
        high = cells // (2 * LANES)
        low = (cells - high * (2 * LANES)).astype(jnp.float32)
        low = repeated(low, 2 * LANES)
        hots[chunk].append(jnp.where(cell_iota == low, 1.0, 0.0).astype(jnp.bfloat16))
        pieces = []
        for value in values:
            head = value.astype(jnp.bfloat16).astype(jnp.float32)
            pieces += [head, value - head]
        both = jnp.concatenate(pieces, axis=0).astype(jnp.bfloat16)
        column = []
        for h in spans[chunk]:
            column.append(both * repeated((high == h).astype(jnp.float32), width))
        column.append((high_iota == high).astype(jnp.float32).astype(jnp.bfloat16))
        columns[chunk].append(jnp.concatenate(column, axis=0))

    for pair in range(parts // 2):
        even, odd = 2 * pair, 2 * pair + 1
        for chunk in range(full):
            here, there = (
                [recv_ref[owner, pl.ds(f * span_rows + chunk * DIR, DIR), :] for f in range(freqs)]
                for owner in (even, odd)
            )
            cells, cells_there = cells_of(even, chunk), cells_of(odd, chunk)
            for side in range(2):
                place(
                    2 * chunk + side,
                    jnp.where(low_lane, cells, cells_there),
                    [jnp.where(low_wide, a, b) for a, b in zip(here, there)],
                )
                here, there, cells, cells_there = there, here, cells_there, cells

        def merged(offset):
            own, other = recv_ref[even, pl.ds(offset, 8), :], recv_ref[odd, pl.ds(offset, 8), :]
            return (
                jnp.where(low_lanes, own, pltpu.roll(other, half, 1)),
                jnp.where(low_lanes, pltpu.roll(own, half, 1), other),
            )

        values = []
        for f in range(freqs):
            one, two = merged(f * span_rows + full * DIR)
            three, four = merged(f * span_rows + full * DIR + 8)
            values.append(
                jnp.concatenate([one, two, jnp.where(top_rows, three, pltpu.roll(four, 4, 0))], axis=0)
            )
        place(2 * full, jnp.where(low_lane, cells_of(even, full), cells_of(odd, full)), values)

    lane = lax.broadcasted_iota(jnp.int32, (slab_rows, LANES), 1)
    zero_rows = jnp.zeros((8, LANES), jnp.float32)

    def gather(offset):
        return jnp.concatenate(
            [recv_ref[owner, pl.ds(offset, tile_rows), :] for owner in range(parts)], axis=0
        )

    gain = 0.5 * courant / 8.0
    slots = iter(range(table.shape[0]))

    def keep(rows):
        slot = next(slots)
        table[slot, pl.ds(8, rows.shape[0]), :] = rows
        return slot

    def face_x(rows):
        slot = next(slots)
        table[slot, pl.ds(0, 8), :] = zero_rows
        table[slot, pl.ds(8 + slab_rows, 8), :] = zero_rows
        table[slot, pl.ds(8, slab_rows), :] = rows
        faces = gain * (table[slot, pl.ds(7, slab_rows + 8), :] + table[slot, pl.ds(8, slab_rows + 8), :])
        table[slot, pl.ds(7, slab_rows + 8), :] = faces
        return slot

    def face_y(rows):
        after = jnp.where(lane < LANES - 1, pltpu.roll(rows, LANES - 1, 1), 0.0)
        before = jnp.where(lane > 0, pltpu.roll(rows, 1, 1), 0.0)
        return keep(gain * (rows + after)), keep(gain * (rows + before))

    speeds = [gather(f * span_rows + full * DIR + 12) for f in range(freqs)]
    current_x, current_y, turning = (gather(shared_base + kind * tile_rows) for kind in range(3))
    current_x_face, speed_x_face = face_x(current_x), [face_x(s) for s in speeds]
    current_y_faces, speed_y_faces = face_y(current_y), [face_y(s) for s in speeds]
    step_angle = 2.0 * math.pi / DIR
    sublane = lax.broadcasted_iota(jnp.int32, (8, LANES), 0)
    cosine0 = jnp.ones((8, LANES), jnp.float32)
    sine0 = jnp.zeros((8, LANES), jnp.float32)
    for d in range(1, 8):
        cosine0 = jnp.where(sublane == d, math.cos(d * step_angle), cosine0)
        sine0 = jnp.where(sublane == d, math.sin(d * step_angle), sine0)
    turns = [(math.cos(g * 8 * step_angle), math.sin(g * 8 * step_angle)) for g in range(DIR // 8)]
    cosine = jnp.concatenate([c * cosine0 - t * sine0 for c, t in turns], axis=0)
    sine = jnp.concatenate([c * sine0 + t * cosine0 for c, t in turns], axis=0)

    def row(slot, x):
        return table[slot, pl.ds(8 + x, 1), :]

    for f in range(freqs):
        for x in range(-1, slab_rows):
            faces_x[f, x + 1] = row(speed_x_face[f], x) * cosine + row(current_x_face, x)
        for x in range(slab_rows):
            for side in range(2):
                faces_y[f, side, x] = row(speed_y_faces[f][side], x) * sine + row(current_y_faces[side], x)

    scattered = [
        lax.dot_general(
            jnp.concatenate(column, axis=1),
            jnp.concatenate(hot, axis=1),
            (((1,), (1,)), ((), ())),
            preferred_element_type=jnp.float32,
        )
        for hot, column in zip(hots, columns)
    ]
    nothing = jnp.zeros((DIR, LANES), jnp.float32)
    for f in range(freqs):
        for field in (first, second):
            for edge in (0, 1, slab_rows + 2, slab_rows + 3):
                field[f, edge] = nothing
        for h in range(highs):
            terms = []
            for span, product in zip(spans, scattered):
                if h in span:
                    at = (h - span[0]) * width + f * 2 * DIR
                    terms += [product[at : at + DIR], product[at + DIR : at + 2 * DIR]]
            total = sum(terms[1:], terms[0])
            first[f, 2 * h + 2] = total[:, :LANES]
            first[f, 2 * h + 3] = total[:, LANES:]
    named = sum(product[len(span) * width :] for span, product in zip(spans, scattered))

    land_slots = keep(named[:, :LANES]), keep(named[:, LANES:])
    ahead = jnp.maximum(turning, 0.0) * 0.125
    back = jnp.minimum(turning, 0.0) * 0.125
    bend_slots = [
        keep(rows)
        for rows in (
            -ahead,
            7.0 * ahead + 3.0 * back,
            1.0 - 3.0 * (ahead - back),
            -3.0 * ahead - 7.0 * back,
            back,
        )
    ]

    lane_wide = lax.broadcasted_iota(jnp.int32, (DIR, LANES), 1)

    def flux(speed, behind, centre3, onward3, beyond):
        positive = speed > 0.0
        near = jnp.where(positive, centre3, onward3)
        far = jnp.where(positive, behind, beyond)
        return speed * ((centre3 + onward3) + (near - far))

    def advance(field, step, carry, finish):
        carry = list(carry)
        order = [(i, f) for i in range(BLOCK) for f in range(freqs)]

        def rotations(i, f):
            centre = field[f, step * BLOCK + i + 2]
            return [centre] + [pltpu.roll(centre, k, 1) for k in (LANES - 1, LANES - 2, 1, 2)]

        ahead = [rotations(*order[0]), rotations(*order[1])]
        for at, (i, f) in enumerate(order):
            x = step * BLOCK + i
            if at + 2 < len(order):
                ahead.append(rotations(*order[at + 2]))
            centre, up1, up2, down1, down2 = ahead.pop(0)
            sea = row(land_slots[i % 2], step * (BLOCK // 2) + i // 2)
            entering, centre3 = carry[f]
            onward3 = 3.0 * field[f, x + 3]
            leaving = flux(faces_x[f, x + 1], field[f, x + 1], centre3, onward3, field[f, x + 4])
            up1 = jnp.where(lane_wide < LANES - 1, up1, 0.0)
            up2 = jnp.where(lane_wide < LANES - 2, up2, 0.0)
            down1 = jnp.where(lane_wide > 0, down1, 0.0)
            down2 = jnp.where(lane_wide > 1, down2, 0.0)
            right = flux(faces_y[f, 0, x], down1, centre3, 3.0 * up1, up2)
            left = flux(faces_y[f, 1, x], down2, 3.0 * down1, centre3, up1)
            finish(f, x, (centre - (leaving - entering) - (right - left)) * sea)
            carry[f] = leaving, onward3
        return tuple(carry)

    def enter(field):
        carry = []
        for f in range(freqs):
            start3 = 3.0 * field[f, 2]
            carry.append((flux(faces_x[f, 0], nothing, nothing, start3, field[f, 3]), start3))
        return tuple(carry)

    def store(f, x, moved):
        second[f, x + 2] = moved

    pitch = slab_rows + 1

    def turn(f, x, moved):
        for g in range(DIR // 8):
            at = (f * DIR + g * 8) * pitch + x
            moved_ref[pl.ds(at, 8, stride=pitch), :] = moved[g * 8 : g * 8 + 8]

    def copy_out(step):
        part = pl.ds(pl.multiple_of(step * BLOCK, BLOCK), BLOCK)
        return pltpu.make_async_copy(done_ref.at[:, part, :], out_ref.at[:, part, :], sems.at[step])

    def final(block, carry):
        carry = advance(second, block, carry, turn)
        at = pl.multiple_of(block * BLOCK, BLOCK)
        weights = [table[slot, pl.ds(8 + at, BLOCK), :] for slot in bend_slots]
        for f in range(freqs):
            ring = [moved_ref[pl.ds((f * DIR + d) * pitch + at, BLOCK), :] for d in range(DIR)]
            for d in range(DIR):
                bent = weights[2] * ring[d]
                for k in (0, 1, 3, 4):
                    bent = bent + weights[k] * ring[(d + k - 2) % DIR]
                done_ref[f * DIR + d, pl.ds(at, BLOCK), :] = bent
        copy_out(block).start()
        return carry

    def sweep(one_block, carry):
        def body(step, carry):
            for i in range(PER_STEP):
                carry = one_block(step * PER_STEP + i, carry)
            return carry

        lax.fori_loop(0, slab_rows // BLOCK // PER_STEP, body, carry)

    sweep(lambda block, carry: advance(first, block, carry, store), enter(first))
    sweep(final, enter(second))
    for block in range(slab_rows // BLOCK):
        copy_out(block).wait()


def slab_plan(spectra, wind, growth, damping, row_cell, group_speed, current, turning):
    parts = lax.axis_size(GROUP)
    rows, comps = spectra.shape
    tile_rows = turning.shape[0]
    freqs = comps // parts // DIR
    full = rows // LANES
    slab_rows = parts * tile_rows
    highs = slab_rows // 2
    block_rows = -(-(freqs * (full * DIR + 16) + 3 * tile_rows + full + 1) // 8) * 8
    packed = pl.pallas_call(
        functools.partial(pack_kernel, parts, freqs),
        out_shape=pltpu.VMEM((parts, block_rows, LANES), jnp.float32),
        compiler_params=pltpu.CompilerParams(vmem_limit_bytes=56 * 1024 * 1024),
        name="pack",
    )(spectra, wind, growth, damping, row_cell, group_speed, current, turning)
    arrived = lax.all_to_all(packed, GROUP, split_axis=0, concat_axis=0, tiled=True)
    out = pl.pallas_call(
        functools.partial(slab_kernel, parts, tile_rows, full, freqs),
        out_shape=jax.ShapeDtypeStruct((freqs * DIR, slab_rows, LANES), jnp.float32),
        in_specs=[pl.BlockSpec(memory_space=pltpu.VMEM)],
        out_specs=pl.BlockSpec(memory_space=pl.ANY),
        scratch_shapes=[
            pltpu.VMEM((freqs, slab_rows + 4, DIR, LANES), jnp.float32),
            pltpu.VMEM((freqs, slab_rows + 4, DIR, LANES), jnp.float32),
            pltpu.VMEM((10 + 3 * freqs, slab_rows + 16, LANES), jnp.float32),
            pltpu.VMEM((freqs, slab_rows + 1, DIR, LANES), jnp.float32),
            pltpu.VMEM((freqs, 2, slab_rows, DIR, LANES), jnp.float32),
            pltpu.VMEM((freqs * DIR * (slab_rows + 1), LANES), jnp.float32),
            pltpu.VMEM((freqs * DIR, slab_rows, LANES), jnp.float32),
            pltpu.SemaphoreType.DMA((slab_rows // BLOCK,)),
        ],
        compiler_params=pltpu.CompilerParams(vmem_limit_bytes=32 * 1024 * 1024),
        name="slab",
    )(arrived)
    return out.reshape(1, freqs * DIR, slab_rows, LANES)


def shards(*arrays):
    spectra, land_mask = arrays[0], arrays[5]
    parts = lax.axis_size(GROUP)
    rows, comps = spectra.shape
    whole_frequencies = comps == parts * 2 * DIR
    fits = rows % LANES == LANES // 2 and land_mask.shape == (4, LANES) and parts % 2 == 0
    if whole_frequencies and fits:
        return slab_plan(*arrays[:5], *arrays[6:])
    return tile_plan(*arrays)


def solution(mesh):
    placed = (
        P(("groups", "pts", "comp"), "sub"),
        P(("groups", "pts", "comp")),
        P("sub"),
        P("sub"),
        P(("groups", "pts", "comp")),
        P(("groups", "pts", "comp"), None),
        P(("groups", "sub"), ("pts", "comp"), None),
        P("groups", ("pts", "comp"), None),
        P(("groups", "pts", "comp"), None),
    )
    return jax.shard_map(
        shards,
        mesh=mesh,
        in_specs=placed,
        out_specs=P("sub", ("pts", "comp"), "groups", None),
        check_vma=False,
    )
```

```python
import functools
import math
import jax
import jax.numpy as jnp
from jax import lax
from jax.experimental import pallas as pl
from jax.experimental.pallas import tpu as pltpu
from jax.sharding import PartitionSpec as P

DIR = 24
SUBSTEPS = 2
LANES = 128
GROUP = ("pts", "comp")


courant = 0.35


def with_halo(cells, sides, width):
    for axis, dim in sides:
        count = lax.axis_size(axis)
        ends = count - 1
        head = lax.slice_in_dim(cells, 0, width, axis=dim)
        tail = lax.slice_in_dim(cells, cells.shape[dim] - width, cells.shape[dim], axis=dim)
        cells = jnp.concatenate(
            [
                lax.ppermute(tail, axis, [(i, (i + 1) % count) for i in range(ends)]),
                cells,
                lax.ppermute(head, axis, [((i + 1) % count, i) for i in range(ends)]),
            ],
            axis=dim,
        )
    return cells


def take_slice(values, first_index, extent, along_axis):
    return lax.slice_in_dim(values, first_index, first_index + extent, axis=along_axis)


def upwind_divergence(padded, motion, along_axis):
    length = padded.shape[along_axis] - 4
    face_count = length + 1
    behind = take_slice(padded, 0, face_count, along_axis)
    centre = take_slice(padded, 1, face_count, along_axis)
    onward = take_slice(padded, 2, face_count, along_axis)
    beyond = take_slice(padded, 3, face_count, along_axis)
    left_face = (6.0 * centre + 3.0 * onward - behind) * 0.125
    right_face = (3.0 * centre + 6.0 * onward - beyond) * 0.125
    face_speed = 0.5 * (
        take_slice(motion, 1, face_count, along_axis)
        + take_slice(motion, 2, face_count, along_axis)
    )
    fluxes = jnp.maximum(face_speed, 0.0) * left_face + jnp.minimum(face_speed, 0.0) * right_face
    return take_slice(fluxes, 1, length, along_axis) - take_slice(fluxes, 0, length, along_axis)


def substep(extended, speed_x, speed_y, sea_mask):
    across = upwind_divergence(extended, speed_x, 1)
    centre_part = extended[:, 2:-2]
    padding = ((0, 0), (0, 0), (2, 2))
    sideways = upwind_divergence(jnp.pad(centre_part, padding), jnp.pad(speed_y, padding), 2)
    return (centre_part - courant * (across + sideways)) * sea_mask


def direction_tables(directions):
    angles = jnp.arange(directions, dtype=jnp.float32) * (2.0 * jnp.pi / directions)
    return (jnp.cos(angles), jnp.sin(angles))


def source_term(values, wind_speed, growth, damping):
    return values * jnp.exp(wind_speed[:, None] * growth[None, :] - damping[None, :])


def velocities(stacked, freq_count):
    cosine_table, sine_table = direction_tables(DIR)
    celerity = stacked[:freq_count][:, None]
    shape_out = (freq_count * DIR,) + stacked.shape[1:]
    speed_x = (
        celerity * cosine_table[None, :, None, None] + stacked[freq_count][None, None]
    ).reshape(shape_out)
    speed_y = (
        celerity * sine_table[None, :, None, None] + stacked[freq_count + 1][None, None]
    ).reshape(shape_out)
    return (speed_x, speed_y)


def deliver(bulk_rows, small_rows):
    return (
        lax.all_to_all(bulk_rows, GROUP, split_axis=0, concat_axis=0, tiled=True),
        lax.all_to_all(small_rows, GROUP, split_axis=0, concat_axis=0, tiled=True),
    )


def tile_plan(spectra, wind, growth, damping, row_cell, land_mask, group_speed, current, turning):
    tile_count = lax.axis_size(GROUP)
    comp_width = spectra.shape[1]
    tile_rows, tile_cols = land_mask.shape
    cell_count = tile_rows * tile_cols
    capacity = cell_count // tile_count
    target = row_cell // cell_count
    local_cell = (row_cell - target * cell_count).astype(jnp.float32)
    matches = (target[:, None] == jnp.arange(tile_count, dtype=jnp.int32)[None, :]).astype(
        jnp.int32
    )
    bucket_slot = jnp.sum((jnp.cumsum(matches, axis=0) - 1) * matches, axis=1)

    def bucket(values, filler):
        shape_out = (tile_count, capacity) + values.shape[1:]
        return jnp.full(shape_out, filler, jnp.float32).at[target, bucket_slot].set(values)

    bulk_rows = bucket(source_term(spectra, wind, growth, damping), 0.0)
    small_rows = bucket(local_cell[:, None], float(cell_count))
    bulk_back, small_back = deliver(bulk_rows, small_rows)
    cell_index = small_back[:, :, 0].reshape(-1).astype(jnp.int32)
    flat_values = bulk_back.reshape((tile_count * capacity,) + bulk_back.shape[2:])
    tile_field = (
        jnp.zeros((cell_count,) + bulk_back.shape[2:], jnp.float32)
        .at[cell_index]
        .set(flat_values, mode="drop")
    )
    spectrum = tile_field.T.reshape(comp_width, tile_rows, tile_cols)
    freq_count = comp_width // DIR
    reach = 2 * SUBSTEPS
    stacked = jnp.concatenate([group_speed, current, land_mask.astype(jnp.float32)[None]], axis=0)
    rimmed = with_halo(stacked, ((GROUP, 1),), 2 * SUBSTEPS)
    speed_x, speed_y = velocities(rimmed, freq_count)
    sea_rim = rimmed[freq_count + 2 :]

    def window(values, margin):
        return lax.slice_in_dim(values, reach - margin, reach + tile_rows + margin, axis=1)

    for repeat in range(SUBSTEPS):
        extended = with_halo(spectrum, ((GROUP, 1),), 2)
        spectrum = substep(extended, window(speed_x, 2), window(speed_y, 0), window(sea_rim, 0)[0])
    blocks = spectrum.reshape(freq_count, DIR, tile_rows, tile_cols)
    wrapped = jnp.concatenate([blocks[:, -2:], blocks, blocks[:, :2]], axis=1)
    turning_full = jnp.broadcast_to(turning[None, None], wrapped.shape)
    blocks = blocks - upwind_divergence(wrapped, turning_full, 1)
    spectrum = blocks.reshape(comp_width, tile_rows, tile_cols)
    shipped = lax.all_to_all(spectrum, GROUP, split_axis=0, concat_axis=1, tiled=True)
    return shipped[None]


def pack_kernel(
    parts,
    freqs,
    spectra_ref,
    wind_ref,
    growth_ref,
    damping_ref,
    cell_ref,
    speed_ref,
    current_ref,
    turning_ref,
    out_ref,
):
    rows, comps = spectra_ref.shape
    half = LANES // 2
    full = rows // LANES
    padded = (full + 1) * LANES
    low = lax.broadcasted_iota(jnp.int32, (8, LANES), 1) < half
    per_freq = DIR // 8
    span_rows = full * DIR + 16

    def extended(row, filler):
        return jnp.concatenate([row[None], jnp.full((1, half), filler, jnp.float32)], axis=1)

    def as_columns(row):
        return jnp.broadcast_to(row, (LANES, padded)).T

    cells = cell_ref[...].astype(jnp.float32)
    keys = extended(cells, 1e9)
    key_cols = as_columns(keys)
    ranks = jnp.concatenate(
        [
            jnp.sum(
                jnp.where(key_cols < keys[:, c * LANES : (c + 1) * LANES], 1.0, 0.0), axis=0, keepdims=True
            )
            for c in range(full + 1)
        ],
        axis=1,
    )
    place = lax.broadcasted_iota(jnp.int32, (padded, padded), 0)
    odd = lax.axis_index(GROUP) % 2 == 1
    swapped = jnp.where(place % LANES < half, place + half, place - half)
    place = jnp.where((place < full * LANES) & odd, swapped, place)
    place = jnp.where(place < rows, place, place - half).astype(jnp.float32)
    order = jnp.where(place == ranks, 1.0, 0.0).astype(jnp.bfloat16)

    wind_cols = as_columns(extended(wind_ref[...], 0.0))
    turned = []
    for block in range(comps // LANES):
        lanes = pl.ds(block * LANES, LANES)
        growth = growth_ref[lanes][None]
        damping = damping_ref[lanes][None]

        def source(first, count):
            span = pl.ds(first, count)
            return spectra_ref[span, lanes] * jnp.exp(
                wind_cols[first : first + count] * growth - damping
            )

        pieces = [source(c * LANES, LANES).T for c in range(full)]
        last = jnp.concatenate([source(full * LANES, half), jnp.zeros((half, LANES), jnp.float32)], axis=0)
        turned.append(jnp.concatenate(pieces + [last.T], axis=1))
    turned.append(jnp.broadcast_to(extended(cells, 0.0), (16, padded)))
    values = jnp.concatenate(turned, axis=0)
    head = values.astype(jnp.bfloat16)
    rest = (values - head.astype(jnp.float32)).astype(jnp.bfloat16)
    both = lax.dot_general(
        jnp.concatenate([head, rest], axis=0),
        order,
        (((1,), (1,)), ((), ())),
        preferred_element_type=jnp.float32,
    )

    def piece(first, count, chunk):
        lanes = slice(chunk * LANES, (chunk + 1) * LANES)
        return both[first : first + count, lanes] + both[comps + 16 + first : comps + 16 + first + count, lanes]

    shared = jnp.concatenate(
        [current_ref[0], current_ref[1], turning_ref[...]] + [piece(comps, 1, c) for c in range(full + 1)],
        axis=0,
    )
    for part in range(parts):
        for f in range(freqs):
            freq = part * freqs + f
            at = f * span_rows
            for chunk in range(full):
                out_ref[part, pl.ds(at + chunk * DIR, DIR), :] = piece(freq * DIR, DIR, chunk)
            at += full * DIR
            one, two, three = (piece(freq * DIR + g * 8, 8, full) for g in range(per_freq))
            out_ref[part, pl.ds(at, 8), :] = jnp.where(low, one, two)
            folded = jnp.where(low, three, pltpu.roll(three, 4, 0))
            out_ref[part, pl.ds(at + 8, 8), :] = jnp.concatenate([folded[:4], speed_ref[freq]], axis=0)
        out_ref[part, pl.ds(freqs * span_rows, shared.shape[0]), :] = shared


BLOCK = 8
PER_STEP = 4


def slab_kernel(
    parts,
    tile_rows,
    full,
    freqs,
    recv_ref,
    out_ref,
    first,
    second,
    table,
    faces_x,
    faces_y,
    moved_ref,
    done_ref,
    sems,
):
    slab_rows = parts * tile_rows
    half = LANES // 2
    span_rows = full * DIR + 16
    shared_base = freqs * span_rows
    highs = slab_rows // 2
    width = freqs * 2 * DIR
    low_lane = lax.broadcasted_iota(jnp.int32, (1, LANES), 1) < half
    low_lanes = lax.broadcasted_iota(jnp.int32, (8, LANES), 1) < half
    low_wide = lax.broadcasted_iota(jnp.int32, (DIR, LANES), 1) < half
    top_rows = lax.broadcasted_iota(jnp.int32, (8, LANES), 0) < 4
    cell_iota = lax.broadcasted_iota(jnp.int32, (2 * LANES, LANES), 0).astype(jnp.float32).astype(jnp.bfloat16)
    high_iota = lax.broadcasted_iota(jnp.int32, (highs, LANES), 0)

    def cells_of(owner, chunk):
        return recv_ref[owner, pl.ds(shared_base + 3 * tile_rows + chunk, 1), :].astype(jnp.int32)

    owner_rows = full * LANES + half
    capacity = tile_rows * LANES // parts
    spans = []
    for begin in range(0, owner_rows, half):
        tiles = [
            t
            for t in range(parts)
            if owner_rows - capacity * (parts - t) < begin + half and capacity * (t + 1) > begin
        ]
        spans.append(range(tiles[0] * tile_rows // 2, (tiles[-1] + 1) * tile_rows // 2))
    columns = [[] for _ in spans]
    hots = [[] for _ in spans]

    def repeated(line, count):
        tile = jnp.broadcast_to(line, (16, LANES)).astype(jnp.bfloat16)
        return jnp.concatenate([tile] * (count // 16), axis=0)

    def place(chunk, cells, values):
        high = cells // (2 * LANES)
        low = (cells - high * (2 * LANES)).astype(jnp.float32)
        low = repeated(low, 2 * LANES)
        hots[chunk].append(jnp.where(cell_iota == low, 1.0, 0.0).astype(jnp.bfloat16))
        pieces = []
        for value in values:
            head = value.astype(jnp.bfloat16).astype(jnp.float32)
            pieces += [head, value - head]
        both = jnp.concatenate(pieces, axis=0).astype(jnp.bfloat16)
        column = []
        for h in spans[chunk]:
            column.append(both * repeated((high == h).astype(jnp.float32), width))
        column.append((high_iota == high).astype(jnp.float32).astype(jnp.bfloat16))
        columns[chunk].append(jnp.concatenate(column, axis=0))

    for pair in range(parts // 2):
        even, odd = 2 * pair, 2 * pair + 1
        for chunk in range(full):
            here, there = (
                [recv_ref[owner, pl.ds(f * span_rows + chunk * DIR, DIR), :] for f in range(freqs)]
                for owner in (even, odd)
            )
            cells, cells_there = cells_of(even, chunk), cells_of(odd, chunk)
            for side in range(2):
                place(
                    2 * chunk + side,
                    jnp.where(low_lane, cells, cells_there),
                    [jnp.where(low_wide, a, b) for a, b in zip(here, there)],
                )
                here, there, cells, cells_there = there, here, cells_there, cells

        def merged(offset):
            own, other = recv_ref[even, pl.ds(offset, 8), :], recv_ref[odd, pl.ds(offset, 8), :]
            return (
                jnp.where(low_lanes, own, pltpu.roll(other, half, 1)),
                jnp.where(low_lanes, pltpu.roll(own, half, 1), other),
            )

        values = []
        for f in range(freqs):
            one, two = merged(f * span_rows + full * DIR)
            three, four = merged(f * span_rows + full * DIR + 8)
            values.append(
                jnp.concatenate([one, two, jnp.where(top_rows, three, pltpu.roll(four, 4, 0))], axis=0)
            )
        place(2 * full, jnp.where(low_lane, cells_of(even, full), cells_of(odd, full)), values)

    lane = lax.broadcasted_iota(jnp.int32, (slab_rows, LANES), 1)
    zero_rows = jnp.zeros((8, LANES), jnp.float32)

    def gather(offset):
        return jnp.concatenate(
            [recv_ref[owner, pl.ds(offset, tile_rows), :] for owner in range(parts)], axis=0
        )

    gain = 0.5 * courant / 8.0
    slots = iter(range(table.shape[0]))

    def keep(rows):
        slot = next(slots)
        table[slot, pl.ds(8, rows.shape[0]), :] = rows
        return slot

    def face_x(rows):
        slot = next(slots)
        table[slot, pl.ds(0, 8), :] = zero_rows
        table[slot, pl.ds(8 + slab_rows, 8), :] = zero_rows
        table[slot, pl.ds(8, slab_rows), :] = rows
        faces = gain * (table[slot, pl.ds(7, slab_rows + 8), :] + table[slot, pl.ds(8, slab_rows + 8), :])
        table[slot, pl.ds(7, slab_rows + 8), :] = faces
        return slot

    def face_y(rows):
        after = jnp.where(lane < LANES - 1, pltpu.roll(rows, LANES - 1, 1), 0.0)
        before = jnp.where(lane > 0, pltpu.roll(rows, 1, 1), 0.0)
        return keep(gain * (rows + after)), keep(gain * (rows + before))

    speeds = [gather(f * span_rows + full * DIR + 12) for f in range(freqs)]
    current_x, current_y, turning = (gather(shared_base + kind * tile_rows) for kind in range(3))
    current_x_face, speed_x_face = face_x(current_x), [face_x(s) for s in speeds]
    current_y_faces, speed_y_faces = face_y(current_y), [face_y(s) for s in speeds]
    step_angle = 2.0 * math.pi / DIR
    sublane = lax.broadcasted_iota(jnp.int32, (8, LANES), 0)
    cosine0 = jnp.ones((8, LANES), jnp.float32)
    sine0 = jnp.zeros((8, LANES), jnp.float32)
    for d in range(1, 8):
        cosine0 = jnp.where(sublane == d, math.cos(d * step_angle), cosine0)
        sine0 = jnp.where(sublane == d, math.sin(d * step_angle), sine0)
    turns = [(math.cos(g * 8 * step_angle), math.sin(g * 8 * step_angle)) for g in range(DIR // 8)]
    cosine = jnp.concatenate([c * cosine0 - t * sine0 for c, t in turns], axis=0)
    sine = jnp.concatenate([c * sine0 + t * cosine0 for c, t in turns], axis=0)

    def row(slot, x):
        return table[slot, pl.ds(8 + x, 1), :]

    for f in range(freqs):
        for x in range(-1, slab_rows):
            faces_x[f, x + 1] = row(speed_x_face[f], x) * cosine + row(current_x_face, x)
        for x in range(slab_rows):
            for side in range(2):
                faces_y[f, side, x] = row(speed_y_faces[f][side], x) * sine + row(current_y_faces[side], x)

    scattered = [
        lax.dot_general(
            jnp.concatenate(column, axis=1),
            jnp.concatenate(hot, axis=1),
            (((1,), (1,)), ((), ())),
            preferred_element_type=jnp.float32,
        )
        for hot, column in zip(hots, columns)
    ]
    nothing = jnp.zeros((DIR, LANES), jnp.float32)
    for f in range(freqs):
        for field in (first, second):
            for edge in (0, 1, slab_rows + 2, slab_rows + 3):
                field[f, edge] = nothing
        for h in range(highs):
            terms = []
            for span, product in zip(spans, scattered):
                if h in span:
                    at = (h - span[0]) * width + f * 2 * DIR
                    terms += [product[at : at + DIR], product[at + DIR : at + 2 * DIR]]
            total = sum(terms[1:], terms[0])
            first[f, 2 * h + 2] = total[:, :LANES]
            first[f, 2 * h + 3] = total[:, LANES:]
    named = sum(product[len(span) * width :] for span, product in zip(spans, scattered))

    land_slots = keep(named[:, :LANES]), keep(named[:, LANES:])
    ahead = jnp.maximum(turning, 0.0) * 0.125
    back = jnp.minimum(turning, 0.0) * 0.125
    bend_slots = [
        keep(rows)
        for rows in (
            -ahead,
            7.0 * ahead + 3.0 * back,
            1.0 - 3.0 * (ahead - back),
            -3.0 * ahead - 7.0 * back,
            back,
        )
    ]

    lane_wide = lax.broadcasted_iota(jnp.int32, (DIR, LANES), 1)

    def flux(speed, behind, centre3, onward3, beyond):
        positive = speed > 0.0
        near = jnp.where(positive, centre3, onward3)
        far = jnp.where(positive, behind, beyond)
        return speed * ((centre3 + onward3) + (near - far))

    def advance(field, step, carry, finish):
        carry = list(carry)
        for i in range(BLOCK):
            x = step * BLOCK + i
            sea = row(land_slots[i % 2], step * (BLOCK // 2) + i // 2)
            for f in range(freqs):
                entering, centre3 = carry[f]
                centre = field[f, x + 2]
                onward3 = 3.0 * field[f, x + 3]
                leaving = flux(faces_x[f, x + 1], field[f, x + 1], centre3, onward3, field[f, x + 4])
                up1 = jnp.where(lane_wide < LANES - 1, pltpu.roll(centre, LANES - 1, 1), 0.0)
                up2 = jnp.where(lane_wide < LANES - 2, pltpu.roll(centre, LANES - 2, 1), 0.0)
                down1 = jnp.where(lane_wide > 0, pltpu.roll(centre, 1, 1), 0.0)
                down2 = jnp.where(lane_wide > 1, pltpu.roll(centre, 2, 1), 0.0)
                right = flux(faces_y[f, 0, x], down1, centre3, 3.0 * up1, up2)
                left = flux(faces_y[f, 1, x], down2, 3.0 * down1, centre3, up1)
                finish(f, x, (centre - (leaving - entering) - (right - left)) * sea)
                carry[f] = leaving, onward3
        return tuple(carry)

    def enter(field):
        carry = []
        for f in range(freqs):
            start3 = 3.0 * field[f, 2]
            carry.append((flux(faces_x[f, 0], nothing, nothing, start3, field[f, 3]), start3))
        return tuple(carry)

    def store(f, x, moved):
        second[f, x + 2] = moved

    pitch = slab_rows + 1

    def turn(f, x, moved):
        for g in range(DIR // 8):
            at = (f * DIR + g * 8) * pitch + x
            moved_ref[pl.ds(at, 8, stride=pitch), :] = moved[g * 8 : g * 8 + 8]

    def copy_out(f, block):
        comps = pl.ds(f * DIR, DIR)
        part = pl.ds(pl.multiple_of(block * BLOCK, BLOCK), BLOCK)
        return pltpu.make_async_copy(
            done_ref.at[comps, part, :], out_ref.at[comps, part, :], sems.at[f, block]
        )

    def final(block, carry):
        carry = advance(second, block, carry, turn)
        at = pl.multiple_of(block * BLOCK, BLOCK)
        weights = [table[slot, pl.ds(8 + at, BLOCK), :] for slot in bend_slots]
        for f in range(freqs):
            ring = [moved_ref[pl.ds((f * DIR + d) * pitch + at, BLOCK), :] for d in range(DIR)]
            for d in range(DIR):
                bent = weights[2] * ring[d]
                for k in (0, 1, 3, 4):
                    bent = bent + weights[k] * ring[(d + k - 2) % DIR]
                done_ref[f * DIR + d, pl.ds(at, BLOCK), :] = bent
            copy_out(f, block).start()
        return carry

    def sweep(one_block, carry):
        def body(step, carry):
            for i in range(PER_STEP):
                carry = one_block(step * PER_STEP + i, carry)
            return carry

        lax.fori_loop(0, slab_rows // BLOCK // PER_STEP, body, carry)

    sweep(lambda block, carry: advance(first, block, carry, store), enter(first))
    sweep(final, enter(second))
    for block in range(slab_rows // BLOCK):
        for f in range(freqs):
            copy_out(f, block).wait()


def slab_plan(spectra, wind, growth, damping, row_cell, group_speed, current, turning):
    parts = lax.axis_size(GROUP)
    rows, comps = spectra.shape
    tile_rows = turning.shape[0]
    freqs = comps // parts // DIR
    full = rows // LANES
    slab_rows = parts * tile_rows
    highs = slab_rows // 2
    block_rows = -(-(freqs * (full * DIR + 16) + 3 * tile_rows + full + 1) // 8) * 8
    packed = pl.pallas_call(
        functools.partial(pack_kernel, parts, freqs),
        out_shape=pltpu.VMEM((parts, block_rows, LANES), jnp.float32),
        compiler_params=pltpu.CompilerParams(vmem_limit_bytes=56 * 1024 * 1024),
        name="pack",
    )(spectra, wind, growth, damping, row_cell, group_speed, current, turning)
    arrived = lax.all_to_all(packed, GROUP, split_axis=0, concat_axis=0, tiled=True)
    out = pl.pallas_call(
        functools.partial(slab_kernel, parts, tile_rows, full, freqs),
        out_shape=jax.ShapeDtypeStruct((freqs * DIR, slab_rows, LANES), jnp.float32),
        in_specs=[pl.BlockSpec(memory_space=pltpu.VMEM)],
        out_specs=pl.BlockSpec(memory_space=pl.ANY),
        scratch_shapes=[
            pltpu.VMEM((freqs, slab_rows + 4, DIR, LANES), jnp.float32),
            pltpu.VMEM((freqs, slab_rows + 4, DIR, LANES), jnp.float32),
            pltpu.VMEM((10 + 3 * freqs, slab_rows + 16, LANES), jnp.float32),
            pltpu.VMEM((freqs, slab_rows + 1, DIR, LANES), jnp.float32),
            pltpu.VMEM((freqs, 2, slab_rows, DIR, LANES), jnp.float32),
            pltpu.VMEM((freqs * DIR * (slab_rows + 1), LANES), jnp.float32),
            pltpu.VMEM((freqs * DIR, slab_rows, LANES), jnp.float32),
            pltpu.SemaphoreType.DMA((freqs, slab_rows // BLOCK)),
        ],
        compiler_params=pltpu.CompilerParams(vmem_limit_bytes=32 * 1024 * 1024),
        name="slab",
    )(arrived)
    return out.reshape(1, freqs * DIR, slab_rows, LANES)


def shards(*arrays):
    spectra, land_mask = arrays[0], arrays[5]
    parts = lax.axis_size(GROUP)
    rows, comps = spectra.shape
    whole_frequencies = comps == parts * 2 * DIR
    fits = rows % LANES == LANES // 2 and land_mask.shape == (4, LANES) and parts % 2 == 0
    if whole_frequencies and fits:
        return slab_plan(*arrays[:5], *arrays[6:])
    return tile_plan(*arrays)


def solution(mesh):
    placed = (
        P(("groups", "pts", "comp"), "sub"),
        P(("groups", "pts", "comp")),
        P("sub"),
        P("sub"),
        P(("groups", "pts", "comp")),
        P(("groups", "pts", "comp"), None),
        P(("groups", "sub"), ("pts", "comp"), None),
        P("groups", ("pts", "comp"), None),
        P(("groups", "pts", "comp"), None),
    )
    return jax.shard_map(
        shards,
        mesh=mesh,
        in_specs=placed,
        out_specs=P("sub", ("pts", "comp"), "groups", None),
        check_vma=False,
    )
```
